512 devices in a mesh: gx: 16 (over z), gy: 8 (over y, core), gz: 4 (over x).
Axes of the slice: x: 4, y: 4, z: 16, core: 2. Of those that a mesh axis runs over, the one named last changes fastest.
Arguments:
- pressure_source: float32 [128, 128, 512], P('gx', 'gy', 'gz'), may hold values from -40 to 40
- conductivity: float32 [128, 128, 512], P('gx', 'gy', 'gz'), may hold values from 0.25 to 4
Outputs:
- pressure: float32 [128, 128, 512], P('gx', 'gy', 'gz')
The draws below stay inside these ranges and needn't reach their ends.
All inputs are finite; a program needn't handle non-finite values.
Results may differ from the reference program's by a relative error of at most 0.0001.
Values sent between devices are 32-bit elements; how exact they have to be, the bound alone decides.
A program may use at most 64 MiB of HBM per device.

```python
import math
import jax
import jax.numpy as jnp

LEVELS = 4
DEGREE = 3
NX = 128
NY = 128
NZ = 512


def draw_pressure_source(key, part):
    key = jax.random.fold_in(key, 11)
    return jnp.clip(8.0 * jax.random.normal(key, (NX, NY, NZ), jnp.float32), -40.0, 40.0)


def steps_of(rng, dims, cuts, low, largest):
    def one(position, blocks):
        heights = jax.random.uniform(jax.random.fold_in(jax.random.fold_in(rng, 6), position), (blocks,), jnp.float32, low / len(cuts), largest / len(cuts))
        return jnp.repeat(jnp.exp(heights), dims[position] // blocks).reshape((-1,) + (1,) * (len(dims) - position - 1))

    level = one(*cuts[0])
    for cut in cuts[1:]:
        level = level * one(*cut)
    return level


def setup_inputs(seed: int = 0) -> dict:
    keys = jax.random.split(jax.random.key(seed), 3)
    pressure_source = draw_pressure_source(jax.random.fold_in(keys[2], 71), 0)
    conductivity = jnp.clip(jnp.exp(math.log(4.0) - 2.7725887 * jax.random.uniform(keys[1], (NX, NY, NZ), jnp.float32) ** steps_of(keys[1], (NX, NY, NZ), ((0, 16), (1, 8), (2, 4)), -0.2, 0.2)), 0.25, 4.0)
    return {"pressure_source": pressure_source, "conductivity": conductivity}


center_value = 1.125
radius_value = 0.875


def wrap_pad(field_in):
    return jnp.pad(field_in, 1, mode="wrap")


def harmonic(one_side, other_side):
    return 2.0 * one_side * other_side / (one_side + other_side)


def fine_faces(padded):
    middle = padded[1:-1, 1:-1, 1:-1]
    return jnp.stack([
        harmonic(middle, padded[:-2, 1:-1, 1:-1]),
        harmonic(middle, padded[1:-1, :-2, 1:-1]),
        harmonic(middle, padded[1:-1, 1:-1, :-2]),
        harmonic(middle, padded[2:, 1:-1, 1:-1]),
        harmonic(middle, padded[1:-1, 2:, 1:-1]),
        harmonic(middle, padded[1:-1, 1:-1, 2:])])


def apply_operator(padded, face_terms):
    middle = padded[1:-1, 1:-1, 1:-1]
    result = face_terms[0] * (middle - padded[:-2, 1:-1, 1:-1]) + face_terms[3] * (middle - padded[2:, 1:-1, 1:-1])
    result = result + face_terms[1] * (middle - padded[1:-1, :-2, 1:-1]) + face_terms[4] * (middle - padded[1:-1, 2:, 1:-1])
    result = result + face_terms[2] * (middle - padded[1:-1, 1:-1, :-2]) + face_terms[5] * (middle - padded[1:-1, 1:-1, 2:])
    return result


def inverse_diagonal(face_terms):
    return 1.0 / (((face_terms[0] + face_terms[3]) + (face_terms[1] + face_terms[4])) + (face_terms[2] + face_terms[5]))


def coarsen_faces(face_terms):
    size_x = face_terms.shape[1] // 2
    size_y = face_terms.shape[2] // 2
    size_z = face_terms.shape[3] // 2
    blocks = face_terms.reshape(6, size_x, 2, size_y, 2, size_z, 2)
    return 0.125 * jnp.stack([
        blocks[0][:, 0].sum(axis=(2, 4)),
        blocks[1][:, :, :, 0].sum(axis=(1, 4)),
        blocks[2][..., 0].sum(axis=(1, 3)),
        blocks[3][:, 1].sum(axis=(2, 4)),
        blocks[4][:, :, :, 1].sum(axis=(1, 4)),
        blocks[5][..., 1].sum(axis=(1, 3))])


def restrict(field_in):
    size_x, size_y, size_z = field_in.shape
    blocks = field_in.reshape(size_x // 2, 2, size_y // 2, 2, size_z // 2, 2)
    return blocks.sum(axis=(1, 3, 5)) * 0.125


def prolong(field_in):
    size_x, size_y, size_z = field_in.shape
    spread = jnp.broadcast_to(field_in[:, None, :, None, :, None], (size_x, 2, size_y, 2, size_z, 2))
    return spread.reshape(2 * size_x, 2 * size_y, 2 * size_z)


def chebyshev(right_side, start, residual, face_terms, inverse, pad_field):
    ratio = center_value / radius_value
    rho_old = 1.0 / ratio
    direction = inverse * residual / center_value
    estimate = direction if start is None else start + direction
    for step_index in range(DEGREE - 1):
        residual = right_side - apply_operator(pad_field(estimate), face_terms)
        rho_new = 1.0 / (2.0 * ratio - rho_old)
        direction = rho_new * rho_old * direction + (2.0 * rho_new / radius_value) * inverse * residual
        estimate = estimate + direction
        rho_old = rho_new
    return estimate


def reference(pressure_source, conductivity):
    face_terms = fine_faces(wrap_pad(conductivity))
    right_side = pressure_source
    saved = []
    for level_index in range(LEVELS - 1):
        inverse = inverse_diagonal(face_terms)
        estimate = chebyshev(right_side, None, right_side, face_terms, inverse, wrap_pad)
        residual = right_side - apply_operator(wrap_pad(estimate), face_terms)
        saved.append((right_side, face_terms, inverse, estimate))
        right_side = restrict(residual)
        face_terms = coarsen_faces(face_terms)
    correction = chebyshev(right_side, None, right_side, face_terms, inverse_diagonal(face_terms), wrap_pad)
    for level_index in range(LEVELS - 2, -1, -1):
        right_side, face_terms, inverse, estimate = saved[level_index]
        estimate = estimate + prolong(correction)
        residual = right_side - apply_operator(wrap_pad(estimate), face_terms)
        correction = chebyshev(right_side, estimate, residual, face_terms, inverse, wrap_pad)
    return correction
```

```python
import functools

import jax
import jax.numpy as jnp
from jax import lax
from jax.experimental import pallas as pl
from jax.experimental.pallas import tpu as pltpu
from jax.sharding import PartitionSpec as P

MESH = pl.DeviceIdType.MESH
F32 = jnp.float32

CENTER = 1.125
RADIUS = 0.875
RATIO = CENTER / RADIUS
RHO0 = 1.0 / RATIO
RHO1 = 1.0 / (2.0 * RATIO - RHO0)
RHO2 = 1.0 / (2.0 * RATIO - RHO1)
STEPS = ((RHO1 * RHO0, 2.0 * RHO1 / RADIUS), (RHO2 * RHO1, 2.0 * RHO2 / RADIUS))


def roll(value, shift, axis):
    return pltpu.roll(value, shift % value.shape[axis], axis)


def lane_of(shape):
    return lax.broadcasted_iota(jnp.int32, shape, len(shape) - 1)


def select_matrix(target):
    row = lax.broadcasted_iota(jnp.int32, (128, 128), 0)
    column = lax.broadcasted_iota(jnp.int32, (128, 128), 1)
    return jnp.where(row == target(column), 1.0, 0.0).astype(F32)


def dot(a, b):
    return jnp.dot(a, b, precision=lax.Precision.HIGHEST, preferred_element_type=F32)


def harmonic(one_side, other_side):
    return 2.0 * one_side * other_side / (one_side + other_side)


def chunks(low, high, size):
    return [(start, min(start + size, high)) for start in range(low, high, size)]


def operator_0(field, faces, low, high):
    face_x, face_y, face_z = faces
    result = []
    cells = []
    for t in range(2):
        v = field[low - 1 : high + 1, t]
        flux = face_x[low : high + 1, t] * (v[1:] - v[:-1])
        c = v[1:-1]
        g = flux[:-1] - flux[1:]
        flux = face_y[low:high, t] * (c - roll(c, 1, 1))
        g = g + (flux - roll(flux, -1, 1))
        cells.append(c)
        result.append(g)
    even = face_z[low:high, 0] * (cells[0] - roll(cells[1], 1, 2))
    odd = face_z[low:high, 1] * (cells[1] - cells[0])
    return [result[0] + (even - odd), result[1] + (odd - roll(even, -1, 2))]


def operator_1(field, faces, low, high):
    v = field[low - 1 : high + 1]
    flux = faces[low : high + 1, 0] * (v[1:] - v[:-1])
    c = v[1:-1]
    g = flux[:-1] - flux[1:]
    flux = faces[low:high, 1] * (c - roll(c, 1, 1))
    g = g + (flux - roll(flux, -1, 1))
    flux = faces[low:high, 2] * (c - roll(c, 1, 2))
    return g + (flux - roll(flux, -1, 2))


def rows(ref, low, high):
    pieces = []
    at = low
    while at < high:
        start = at % 16
        stop = min(16, start + high - at)
        pieces.append(ref[start:stop])
        at += stop - start
    return pieces[0] if len(pieces) == 1 else jnp.concatenate(pieces, axis=0)


def put_rows(ref, low, high, value):
    at = low
    while at < high:
        start = at % 16
        stop = min(16, start + high - at)
        ref[start:stop] = value[at - low : at - low + stop - start]
        at += stop - start


def operator_2(field, faces, low, high):
    face_x, face_y, face_z = faces
    v = rows(field, low - 1, high + 1)
    half = lane_of(v[:-1].shape) < 64
    turned = roll(v, 64, 2)
    flux = rows(face_x, low, high + 1) * (v[1:] - jnp.where(half, turned[:-1], turned[1:]))
    turned = roll(flux, 64, 2)
    g = flux[:-1] - jnp.where(half[1:], turned[:-1], turned[1:])
    c = v[1:-1]
    flux = rows(face_y, low, high) * (c - roll(c, 1, 1))
    g = g + (flux - roll(flux, -1, 1))
    flux = rows(face_z, low, high) * (c - roll(c, 1, 2))
    return g + (flux - roll(flux, -1, 2))


def operator_3(field, faces, low, high):
    face_x, face_y, face_z = faces
    v = rows(field, low - 1, high + 1)
    flux = rows(face_x, low, high + 1) * (v[1:] - v[:-1])
    g = flux[:-1] - flux[1:]
    c = v[1:-1]
    flux = rows(face_y, low, high) * (c - roll(c, 1, 1))
    g = g + (flux - roll(flux, -1, 1))
    flux = rows(face_z, low, high) * (c - roll(c, 2, 2))
    return g + (flux - roll(flux, -2, 2))


def kernel(
    sizes,
    source_hbm,
    cond_hbm,
    out_ref,
    staged,
    own,
    z_send,
    z_recv,
    win,
    y_send,
    y_recv,
    fx,
    fy,
    fz,
    inv,
    xa,
    xb,
    dd,
    tmp0,
    f1,
    b1,
    inv1,
    x1a,
    x1b,
    d1,
    tmp1,
    dup1,
    g2f,
    g2b,
    f2,
    b2,
    inv2,
    x2a,
    x2b,
    d2,
    tmp2,
    f3,
    b3,
    inv3,
    x3a,
    x3b,
    d3,
    dup2,
    dup21,
    in_sem,
    z_sems,
    x_sems,
    y_sems,
    f1x_sems,
    f1y_sems,
    b1x_sems,
    b1y_sems,
    gfx_sems,
    gfy_sems,
    gbx_sems,
    gby_sems,
):
    count_x, count_y, count_z = sizes
    me_x, me_y, me_z = lax.axis_index("gx"), lax.axis_index("gy"), lax.axis_index("gz")

    def at_x(step):
        return {"gx": lax.rem(me_x + (step + count_x), count_x)}

    def at_y(step):
        return {"gy": lax.rem(me_y + (step + count_y), count_y)}

    def at_z(step):
        return {"gz": lax.rem(me_z + (step + count_z), count_z)}

    loads = [
        pltpu.make_async_copy(cond_hbm, staged.at[0], in_sem.at[0]),
        pltpu.make_async_copy(source_hbm, staged.at[1], in_sem.at[1]),
    ]
    for load in loads:
        load.start()

    barrier = pltpu.get_barrier_semaphore()
    partners = [at_z(1), at_z(-1)]
    partners += [at_x(step) for step in range(1, count_x)]
    partners += [at_y(step) for step in range(1, count_y)]
    for partner in partners:
        pl.semaphore_signal(barrier, inc=1, device_id=partner, device_id_type=MESH)

    pending = []

    def send(source, target, sems, slot, device):
        copy = pltpu.make_async_remote_copy(
            src_ref=source,
            dst_ref=target,
            send_sem=sems.at[0, slot],
            recv_sem=sems.at[1, slot],
            device_id=device,
            device_id_type=MESH,
        )
        copy.start()
        pending.append(copy)
        return copy

    keep = select_matrix(lambda l: jnp.where(l < 64, 2 * l, 2 * (l - 64) + 1))
    down_a = select_matrix(
        lambda l: jnp.where(l < 64, -1, jnp.where(l < 96, 2 * (l - 64), 2 * (l - 96) + 1))
    )
    down_b = select_matrix(
        lambda l: jnp.where(l >= 64, -1, jnp.where(l < 32, 2 * l, 2 * (l - 32) + 1))
    )
    up_a = select_matrix(
        lambda l: jnp.where(l < 64, -1, jnp.where(l >= 96, 64 + 2 * (l - 96), 64 + 2 * (l - 64) + 1))
    )
    up_b = select_matrix(
        lambda l: jnp.where(l >= 64, -1, jnp.where(l >= 32, 64 + 2 * (l - 32), 64 + 2 * l + 1))
    )
    z_copies = []
    for f in range(2):
        loads[f].wait()
        cells = staged[f].reshape(128, 128)
        z_send[f, 0] = (dot(cells[:64], down_a) + dot(cells[64:], down_b)).reshape(4, 16, 128)
        z_send[f, 1] = (dot(cells[:64], up_a) + dot(cells[64:], up_b)).reshape(4, 16, 128)
        if f == 0:
            pl.semaphore_wait(barrier, len(partners))
        z_copies.append(
            [
                send(z_send.at[f, way], z_recv.at[f, way], z_sems, 2 * f + way, at_z((-1, 1)[way]))
                for way in range(2)
            ]
        )
        own[f] = dot(cells, keep).reshape(8, 16, 128)

    def send_x(f):
        return [
            send(
                win.at[f, 4:8, :, 0:16, :],
                win.at[f, 12:16, :, 0:16, :],
                x_sems,
                2 * f,
                at_x(-1),
            ),
            send(
                win.at[f, 8:12, :, 0:16, :],
                win.at[f, 0:4, :, 0:16, :],
                x_sems,
                2 * f + 1,
                at_x(1),
            ),
        ]

    def send_y(f):
        y_send[f, 0] = win[f, :, :, 0:4, :]
        y_send[f, 1] = win[f, :, :, 12:16, :]
        return [
            send(y_send.at[f, way], y_recv.at[f, way], y_sems, 2 * f + way, at_y((-1, 1)[way]))
            for way in range(2)
        ]

    def place_y(f, copies):
        for copy in copies:
            copy.wait_recv()
        win[f, :, :, 16:20, :] = y_recv[f, 0]
        win[f, :, :, 20:24, :] = y_recv[f, 1]

    x_copies = []
    for f in range(2):
        for copy in z_copies[f]:
            copy.wait_recv()
        lane = lane_of((4, 16, 128))
        for part in range(2):
            mine = own[f, 4 * part : 4 * part + 4]
            above, below = z_recv[f, 0], z_recv[f, 1]
            for t in range(2):
                turn_above = ((0, 96), (64, 32))[part][t]
                turn_below = ((0, 32), (64, 96))[part][t]
                halo = jnp.where(
                    lane < 96,
                    roll(above, turn_above, 2) if turn_above else above,
                    roll(below, turn_below, 2) if turn_below else below,
                )
                win[f, 4 + 4 * part : 8 + 4 * part, t, 0:16, :] = jnp.where(
                    lane < 64, roll(mine, 64, 2) if t else mine, halo
                )
        x_copies.append(send_x(f))
    y_copies = []
    for f in range(2):
        for copy in x_copies[f]:
            copy.wait_recv()
        y_copies.append(send_y(f))
    place_y(0, y_copies[0])

    cond, source, best = win.at[0], win.at[1], win.at[2]
    faces0 = (fx, fy, fz)
    for low, high in chunks(1, 16, 4):
        for t in range(2):
            k = cond[low - 1 : high, t]
            fx[low:high, t] = harmonic(k[1:], k[:-1])
    for low, high in chunks(1, 15, 4):
        k0, k1 = cond[low:high, 0], cond[low:high, 1]
        fy[low:high, 0] = harmonic(k0, roll(k0, 1, 1))
        fy[low:high, 1] = harmonic(k1, roll(k1, 1, 1))
        fz[low:high, 0] = harmonic(k0, roll(k1, 1, 2))
        fz[low:high, 1] = harmonic(k1, k0)

    for i in range(4):
        tmp0[0, i] = fx[4 + 2 * i, 0, 0:16, :] + fx[4 + 2 * i, 1, 0:16, :]
        tmp0[1, i] = (fy[4 + 2 * i, 0, 0:16, :] + fy[4 + 2 * i, 1, 0:16, :]) + (
            fy[5 + 2 * i, 0, 0:16, :] + fy[5 + 2 * i, 1, 0:16, :]
        )
        tmp0[2, i] = fz[4 + 2 * i, 0, 0:16, :] + fz[5 + 2 * i, 0, 0:16, :]
    first, second = pl.ds(0, 8, stride=2), pl.ds(1, 8, stride=2)
    f1[8:12, 0, 8:16, :] = 0.125 * (tmp0[0, :, first, :] + tmp0[0, :, second, :])
    f1[8:12, 1, 8:16, :] = 0.125 * tmp0[1, :, first, :]
    f1[8:12, 2, 8:16, :] = 0.125 * (tmp0[2, :, first, :] + tmp0[2, :, second, :])
    f1x_copies = [
        send(
            f1.at[8:12, :, 8:16, :],
            f1.at[8 - 4 * step : 12 - 4 * step, :, 8:16, :],
            f1x_sems,
            slot,
            at_x(step),
        )
        for slot, step in enumerate((-1, 1, -2, 2))
    ]

    row = lax.broadcasted_iota(jnp.int32, (128, 128), 0)
    column = lax.broadcasted_iota(jnp.int32, (128, 128), 1)
    pack = [
        jnp.where((row // 2 + 16) % 64 + 64 * p == column, 1.0, 0.0).astype(F32) for p in range(2)
    ]
    pack_even = [
        jnp.where((row % 2 == 0) & ((row // 2 + 16) % 64 + 64 * p == column), 1.0, 0.0).astype(F32)
        for p in range(2)
    ]
    first4, second4 = pl.ds(0, 4, stride=2), pl.ds(1, 4, stride=2)
    tmp1[0] = dot(f1[8, 0, 8:16, :], pack[0]) + dot(f1[10, 0, 8:16, :], pack[1])
    tmp1[1] = dot(f1[8, 1, 8:16, :] + f1[9, 1, 8:16, :], pack[0]) + dot(
        f1[10, 1, 8:16, :] + f1[11, 1, 8:16, :], pack[1]
    )
    tmp1[2] = dot(f1[8, 2, 8:16, :] + f1[9, 2, 8:16, :], pack_even[0]) + dot(
        f1[10, 2, 8:16, :] + f1[11, 2, 8:16, :], pack_even[1]
    )
    g2f[1, 2, 0] = 0.125 * (tmp1[0, first4, :] + tmp1[0, second4, :])
    g2f[1, 2, 1] = 0.125 * tmp1[1, first4, :]
    g2f[1, 2, 2] = 0.125 * (tmp1[2, first4, :] + tmp1[2, second4, :])

    def gather_x(ref, sems):
        return [
            send(ref.at[1, 2], ref.at[1, (2 - step) % count_x], sems, step - 1, at_x(step))
            for step in range(1, count_x)
        ]

    def gather_y(ref, sems):
        return [
            send(ref.at[1], ref.at[(1 - step) % count_y], sems, step - 1, at_y(step))
            for step in range(1, count_y)
        ]

    gfx_copies = gather_x(g2f, gfx_sems)

    for low, high in chunks(1, 15, 2):
        x_sum = [fx[low:high, t] + fx[low + 1 : high + 1, t] for t in range(2)]
        y_sum = [fy[low:high, t] + roll(fy[low:high, t], -1, 1) for t in range(2)]
        z0, z1 = fz[low:high, 0], fz[low:high, 1]
        inv[low:high, 0] = 1.0 / ((x_sum[0] + y_sum[0]) + (z0 + z1))
        inv[low:high, 1] = 1.0 / ((x_sum[1] + y_sum[1]) + (z1 + roll(z0, -1, 2)))

    place_y(1, y_copies[1])
    for low, high in chunks(1, 15, 4):
        for t in range(2):
            d = inv[low:high, t] * source[low:high, t] * (1.0 / CENTER)
            dd[low:high, t] = d
            xa[low:high, t] = d

    def step_0(old, new, low, high, step, target=None):
        keep_old, keep_new = STEPS[step]
        for lo, hi in chunks(low, high, 2):
            applied = operator_0(old, faces0, lo, hi)
            for t in range(2):
                r = source[lo:hi, t] - applied[t]
                d = keep_old * dd[lo:hi, t] + keep_new * (inv[lo:hi, t] * r)
                if target is None:
                    dd[lo:hi, t] = d
                    new[lo:hi, t] = old[lo:hi, t] + d
                else:
                    target(lo, hi, t, old[lo:hi, t] + d)

    step_0(xa, xb, 2, 14, 0)

    for copy in f1x_copies:
        copy.wait_recv()
    f1y_copies = [
        send(
            f1.at[:, :, 8:16, :],
            f1.at[:, :, 8 - 8 * step : 16 - 8 * step, :],
            f1y_sems,
            slot,
            at_y(step),
        )
        for slot, step in enumerate((-1, 1))
    ]
    step_0(xb, xa, 3, 13, 1)
    best[4:12, :, 0:16, :] = xa[4:12, :, 0:16, :]
    for i in range(4):
        applied = operator_0(xa, faces0, 4 + 2 * i, 6 + 2 * i)
        r = (source[4 + 2 * i : 6 + 2 * i, 0, 0:16, :] - applied[0][:, :16]) + (
            source[4 + 2 * i : 6 + 2 * i, 1, 0:16, :] - applied[1][:, :16]
        )
        tmp0[0, i] = r[0] + r[1]
    b1[8:12, 8:16, :] = 0.125 * (tmp0[0, :, first, :] + tmp0[0, :, second, :])
    b1x_copies = [
        send(
            b1.at[8:12, 8:16, :],
            b1.at[8 - 4 * step : 12 - 4 * step, 8:16, :],
            b1x_sems,
            slot,
            at_x(step),
        )
        for slot, step in enumerate((-1, 1, -2, 2))
    ]
    x_copies.append(send_x(2))
    for copy in gfx_copies:
        copy.wait_recv()
    gfy_copies = gather_y(g2f, gfy_sems)

    for copy in f1y_copies:
        copy.wait_recv()
    for low, high in chunks(1, 19, 6):
        x_sum = f1[low:high, 0] + f1[low + 1 : high + 1, 0]
        y_term, z_term = f1[low:high, 1], f1[low:high, 2]
        y_sum = y_term + roll(y_term, -1, 1)
        inv1[low:high] = 1.0 / ((x_sum + y_sum) + (z_term + roll(z_term, -1, 2)))

    for copy in b1x_copies:
        copy.wait_recv()
    b1y_copies = [
        send(
            b1.at[:, 8:16, :],
            b1.at[:, 8 - 8 * step : 16 - 8 * step, :],
            b1y_sems,
            slot,
            at_y(step),
        )
        for slot, step in enumerate((-1, 1))
    ]
    for copy in x_copies[2]:
        copy.wait_recv()
    y_copies.append(send_y(2))
    for copy in b1y_copies:
        copy.wait_recv()

    for low, high in chunks(1, 19, 6):
        d = inv1[low:high] * b1[low:high] * (1.0 / CENTER)
        d1[low:high] = d
        x1a[low:high] = d

    def step_1(old, new, low, high, step):
        keep_old, keep_new = STEPS[step]
        for lo, hi in chunks(low, high, 4):
            r = b1[lo:hi] - operator_1(old, f1, lo, hi)
            d = keep_old * d1[lo:hi] + keep_new * (inv1[lo:hi] * r)
            d1[lo:hi] = d
            new[lo:hi] = old[lo:hi] + d

    step_1(x1a, x1b, 2, 18, 0)
    step_1(x1b, x1a, 3, 17, 1)
    r = (b1[8:12] - operator_1(x1a, f1, 8, 12))[:, 8:16]
    tmp1[0] = dot(r[0] + r[1], pack[0]) + dot(r[2] + r[3], pack[1])
    g2b[1, 2] = 0.125 * (tmp1[0, first4, :] + tmp1[0, second4, :])
    gbx_copies = gather_x(g2b, gbx_sems)

    for copy in gfy_copies:
        copy.wait_recv()
    for f in range(3):
        for s in range(count_y):
            f2[f, :, 4 * s : 4 * s + 4, :] = g2f[s, :, f]
    faces2 = (f2.at[0], f2.at[1], f2.at[2])
    for low, high in chunks(0, 16, 4):
        terms = rows(faces2[0], low, high + 1)
        turned = roll(terms, 64, 2)
        half = lane_of(terms[1:].shape) < 64
        x_sum = terms[:-1] + jnp.where(half, turned[:-1], turned[1:])
        y_term, z_term = f2[1, low:high], f2[2, low:high]
        y_sum = y_term + roll(y_term, -1, 1)
        inv2[low:high] = 1.0 / ((x_sum + y_sum) + (z_term + roll(z_term, -1, 2)))

        x_low = f2[0, low:high]
        x_low = jnp.where(half, x_low, roll(x_low, 64, 2))
        tmp2[0, low:high] = x_low + roll(x_low, -1, 2)
        y_both = y_term + roll(y_term, 64, 2)
        tmp2[1, low:high] = y_both + roll(y_both, -1, 2)
        tmp2[2, low:high] = z_term + roll(z_term, 64, 2)
    first16, second16 = pl.ds(0, 16, stride=2), pl.ds(1, 16, stride=2)
    f3[0] = 0.125 * (tmp2[0, :, first16, :] + tmp2[0, :, second16, :])
    f3[1] = 0.125 * tmp2[1, :, first16, :]
    f3[2] = 0.125 * (tmp2[2, :, first16, :] + tmp2[2, :, second16, :])
    faces3 = (f3.at[0], f3.at[1], f3.at[2])
    for low, high in chunks(0, 16, 8):
        terms = rows(faces3[0], low, high + 1)
        y_term, z_term = f3[1, low:high], f3[2, low:high]
        inv3[low:high] = 1.0 / (
            (terms[:-1] + terms[1:] + (y_term + roll(y_term, -1, 1)))
            + (z_term + roll(z_term, -2, 2))
        )

    for copy in gbx_copies:
        copy.wait_recv()
    gby_copies = gather_y(g2b, gby_sems)
    place_y(2, y_copies[2])
    for copy in gby_copies:
        copy.wait_recv()
    for s in range(count_y):
        b2[:, 4 * s : 4 * s + 4, :] = g2b[s]

    for low, high in chunks(0, 16, 4):
        d = inv2[low:high] * b2[low:high] * (1.0 / CENTER)
        d2[low:high] = d
        x2a[low:high] = d

    def step_2(old, new, low, high, step):
        keep_old, keep_new = STEPS[step]
        for lo, hi in chunks(low, high, 2):
            r = rows(b2, lo, hi) - operator_2(old, faces2, lo, hi)
            d = keep_old * rows(d2, lo, hi) + keep_new * (rows(inv2, lo, hi) * r)
            put_rows(d2, lo, hi, d)
            put_rows(new, lo, hi, rows(old, lo, hi) + d)

    step_2(x2a, x2b, 0, 16, 0)
    step_2(x2b, x2a, 0, 16, 1)
    for low, high in chunks(0, 16, 2):
        r = b2[low:high] - operator_2(x2a, faces2, low, high)
        r = r + roll(r, 64, 2)
        tmp2[0, low:high] = r + roll(r, -1, 2)
    b3[...] = 0.125 * (tmp2[0, :, first16, :] + tmp2[0, :, second16, :])

    d = inv3[...] * b3[...] * (1.0 / CENTER)
    d3[...] = d
    x3a[...] = d

    def step_3(old, new, low, high, step):
        keep_old, keep_new = STEPS[step]
        for lo, hi in chunks(low, high, 4):
            r = rows(b3, lo, hi) - operator_3(old, faces3, lo, hi)
            d = keep_old * rows(d3, lo, hi) + keep_new * (rows(inv3, lo, hi) * r)
            put_rows(d3, lo, hi, d)
            put_rows(new, lo, hi, rows(old, lo, hi) + d)

    step_3(x3a, x3b, 0, 16, 0)
    step_3(x3b, x3a, 0, 16, 1)

    e = x3a[...]
    e = jnp.where(lane_of(e.shape) % 2 == 0, e, roll(e, 1, 2))
    dup2[:, first16, :] = e
    dup2[:, second16, :] = e
    for low, high in chunks(-3, 8, 4):
        put_rows(x2b, low, high, rows(x2a, low, high) + rows(dup2, low, high))
    for low, high in chunks(-2, 7, 2):
        r = rows(b2, low, high) - operator_2(x2b, faces2, low, high)
        d = rows(inv2, low, high) * r * (1.0 / CENTER)
        put_rows(d2, low, high, d)
        put_rows(x2a, low, high, rows(x2b, low, high) + d)
    step_2(x2a, x2b, -1, 6, 0)
    step_2(x2b, x2a, 0, 5, 1)

    spread = [
        jnp.where((column // 2 + 16) % 64 + 64 * p == row, 1.0, 0.0).astype(F32) for p in range(2)
    ]
    e = x2a[0:5, 0:16, :].reshape(80, 128)
    for p in range(2):
        value = dot(e, spread[p]).reshape(5, 16, 128)
        dup21[p, :, first16, :] = value
        dup21[p, :, second16, :] = value
    for i in range(3, 17):
        x1b[i] = x1a[i] + dup21[(i // 2) % 2, i // 4, 0:24, :]
    for low, high in chunks(4, 16, 4):
        r = b1[low:high] - operator_1(x1b, f1, low, high)
        d = inv1[low:high] * r * (1.0 / CENTER)
        d1[low:high] = d
        x1a[low:high] = x1b[low:high] + d
    step_1(x1a, x1b, 5, 15, 0)
    step_1(x1b, x1a, 6, 14, 1)

    e = x1a[6:14]
    dup1[:, pl.ds(0, 24, stride=2), :] = e
    dup1[:, pl.ds(1, 24, stride=2), :] = e
    lower = lax.broadcasted_iota(jnp.int32, (8, 128), 0) < 4
    for i in range(1, 15):
        j = i // 2
        brick = dup1[j, 16:32, :]
        edge = jnp.where(lower, dup1[j, 32:40, :], dup1[j, 8:16, :])
        for t in range(2):
            xb[i, t, 0:16, :] = best[i, t, 0:16, :] + brick
            xb[i, t, 16:24, :] = best[i, t, 16:24, :] + edge
    for lo, hi in chunks(2, 14, 2):
        applied = operator_0(xb, faces0, lo, hi)
        for t in range(2):
            r = source[lo:hi, t] - applied[t]
            d = inv[lo:hi, t] * r * (1.0 / CENTER)
            dd[lo:hi, t] = d
            xa[lo:hi, t] = xb[lo:hi, t] + d
    step_0(xa, xb, 3, 13, 0)

    def to_own(lo, hi, t, value):
        own[t, lo - 4 : hi - 4] = value[:, 0:16, :]

    step_0(xb, None, 4, 12, 1, to_own)
    join = [
        jnp.where((column == 2 * row + t) & (row < 64), 1.0, 0.0).astype(F32) for t in range(2)
    ]
    result = dot(own[0].reshape(128, 128), join[0]) + dot(own[1].reshape(128, 128), join[1])
    out_ref[...] = result.reshape(8, 16, 128)

    for copy in pending:
        copy.wait_send()


def solution(mesh):
    sizes = (mesh.shape["gx"], mesh.shape["gy"], mesh.shape["gz"])
    count_x, count_y, _ = sizes
    vmem = lambda *shape: pltpu.VMEM(shape, F32)
    sems = lambda count: pltpu.SemaphoreType.DMA((2, count))
    fine = (16, 2, 24, 128)
    level1 = (20, 24, 128)
    level2 = (16, 32, 128)
    level3 = (16, 16, 128)
    scratch = [
        vmem(2, 8, 16, 128),
        vmem(2, 8, 16, 128),
        vmem(2, 2, 4, 16, 128),
        vmem(2, 2, 4, 16, 128),
        vmem(3, *fine),
        vmem(3, 2, 16, 2, 4, 128),
        vmem(3, 2, 16, 2, 4, 128),
        vmem(*fine),
        vmem(*fine),
        vmem(*fine),
        vmem(*fine),
        vmem(*fine),
        vmem(*fine),
        vmem(*fine),
        vmem(3, 4, 16, 128),
        vmem(20, 3, 24, 128),
        vmem(*level1),
        vmem(*level1),
        vmem(*level1),
        vmem(*level1),
        vmem(*level1),
        vmem(3, 8, 128),
        vmem(8, 48, 128),
        vmem(count_y, count_x, 3, 4, 128),
        vmem(count_y, count_x, 4, 128),
        vmem(3, *level2),
        vmem(*level2),
        vmem(*level2),
        vmem(*level2),
        vmem(*level2),
        vmem(*level2),
        vmem(3, *level2),
        vmem(3, *level3),
        vmem(*level3),
        vmem(*level3),
        vmem(*level3),
        vmem(*level3),
        vmem(*level3),
        vmem(*level2),
        vmem(2, 5, 32, 128),
        pltpu.SemaphoreType.DMA((2,)),
        sems(4),
        sems(6),
        sems(6),
        sems(4),
        sems(2),
        sems(4),
        sems(2),
        sems(count_x - 1),
        sems(count_y - 1),
        sems(count_x - 1),
        sems(count_y - 1),
    ]

    def shards(pressure_source, conductivity):
        return pl.pallas_call(
            functools.partial(kernel, sizes),
            out_shape=jax.ShapeDtypeStruct((8, 16, 128), F32),
            in_specs=[pl.BlockSpec(memory_space=pl.ANY)] * 2,
            out_specs=pl.BlockSpec(memory_space=pltpu.VMEM),
            scratch_shapes=scratch,
            compiler_params=pltpu.CompilerParams(
                collective_id=0, has_side_effects=True, vmem_limit_bytes=48 * 1024 * 1024
            ),
        )(pressure_source, conductivity)

    placed = (P("gx", "gy", "gz"), P("gx", "gy", "gz"))
    return jax.shard_map(
        shards, mesh=mesh, in_specs=placed, out_specs=P("gx", "gy", "gz"), check_vma=False
    )
```

```python
import functools

import jax
import jax.numpy as jnp
from jax import lax
from jax.experimental import pallas as pl
from jax.experimental.pallas import tpu as pltpu
from jax.sharding import PartitionSpec as P

MESH = pl.DeviceIdType.MESH
F32 = jnp.float32

CENTER = 1.125
RADIUS = 0.875
RATIO = CENTER / RADIUS
RHO0 = 1.0 / RATIO
RHO1 = 1.0 / (2.0 * RATIO - RHO0)
RHO2 = 1.0 / (2.0 * RATIO - RHO1)
STEPS = ((RHO1 * RHO0, 2.0 * RHO1 / RADIUS), (RHO2 * RHO1, 2.0 * RHO2 / RADIUS))


def roll(value, shift, axis):
    return pltpu.roll(value, shift % value.shape[axis], axis)


def lane_of(shape):
    return lax.broadcasted_iota(jnp.int32, shape, len(shape) - 1)


def select_matrix(target):
    row = lax.broadcasted_iota(jnp.int32, (128, 128), 0)
    column = lax.broadcasted_iota(jnp.int32, (128, 128), 1)
    return jnp.where(row == target(column), 1.0, 0.0).astype(F32)


def dot(a, b):
    return jnp.dot(a, b, precision=lax.Precision.HIGHEST, preferred_element_type=F32)


def harmonic(one_side, other_side):
    return 2.0 * one_side * other_side / (one_side + other_side)


def each(low, high, size, body):
    assert (high - low) % size == 0
    count = (high - low) // size
    if count == 1:
        body(low)
        return

    def one(i, carry):
        body(low + i * size)
        return carry

    lax.fori_loop(0, count, one, 0)


def operator_0(field, faces, low, size):
    face_x, face_y, face_z = faces
    here = pl.ds(low, size)
    result = []
    cells = []
    for t in range(2):
        v = field[pl.ds(low - 1, size + 2), t]
        flux = face_x[pl.ds(low, size + 1), t] * (v[1:] - v[:-1])
        c = v[1:-1]
        g = flux[:-1] - flux[1:]
        flux = face_y[here, t] * (c - roll(c, 1, 1))
        g = g + (flux - roll(flux, -1, 1))
        cells.append(c)
        result.append(g)
    even = face_z[here, 0] * (cells[0] - roll(cells[1], 1, 2))
    odd = face_z[here, 1] * (cells[1] - cells[0])
    return [result[0] + (even - odd), result[1] + (odd - roll(even, -1, 2))]


def operator_1(field, faces, low, size):
    here = pl.ds(low, size)
    v = field[pl.ds(low - 1, size + 2)]
    flux = faces[pl.ds(low, size + 1), 0] * (v[1:] - v[:-1])
    c = v[1:-1]
    g = flux[:-1] - flux[1:]
    flux = faces[here, 1] * (c - roll(c, 1, 1))
    g = g + (flux - roll(flux, -1, 1))
    flux = faces[here, 2] * (c - roll(c, 1, 2))
    return g + (flux - roll(flux, -1, 2))


def rows(ref, low, size):
    return jnp.concatenate(
        [ref[pl.ds(lax.rem(low + (k + 16), 16), 1)] for k in range(size)], axis=0
    )


def put_rows(ref, low, value):
    for k in range(value.shape[0]):
        ref[pl.ds(lax.rem(low + (k + 16), 16), 1)] = value[k : k + 1]


def operator_2(field, faces, low, size):
    face_x, face_y, face_z = faces
    v = rows(field, low - 1, size + 2)
    half = lane_of(v[:-1].shape) < 64
    turned = roll(v, 64, 2)
    flux = rows(face_x, low, size + 1) * (v[1:] - jnp.where(half, turned[:-1], turned[1:]))
    turned = roll(flux, 64, 2)
    g = flux[:-1] - jnp.where(half[1:], turned[:-1], turned[1:])
    c = v[1:-1]
    flux = rows(face_y, low, size) * (c - roll(c, 1, 1))
    g = g + (flux - roll(flux, -1, 1))
    flux = rows(face_z, low, size) * (c - roll(c, 1, 2))
    return g + (flux - roll(flux, -1, 2))


def operator_3(field, faces, low, size):
    face_x, face_y, face_z = faces
    v = rows(field, low - 1, size + 2)
    flux = rows(face_x, low, size + 1) * (v[1:] - v[:-1])
    g = flux[:-1] - flux[1:]
    c = v[1:-1]
    flux = rows(face_y, low, size) * (c - roll(c, 1, 1))
    g = g + (flux - roll(flux, -1, 1))
    flux = rows(face_z, low, size) * (c - roll(c, 2, 2))
    return g + (flux - roll(flux, -2, 2))


def kernel(
    sizes,
    source_hbm,
    cond_hbm,
    out_ref,
    staged,
    own,
    z_send,
    z_recv,
    win,
    y_send,
    y_recv,
    fx,
    fy,
    fz,
    inv,
    xa,
    xb,
    dd,
    tmp0,
    f1,
    b1,
    inv1,
    x1a,
    x1b,
    d1,
    tmp1,
    dup1,
    g2f,
    g2b,
    f2,
    b2,
    inv2,
    x2a,
    x2b,
    d2,
    tmp2,
    f3,
    b3,
    inv3,
    x3a,
    x3b,
    d3,
    dup2,
    dup21,
    in_sem,
    z_sems,
    x_sems,
    y_sems,
    f1x_sems,
    f1y_sems,
    b1x_sems,
    b1y_sems,
    gfx_sems,
    gfy_sems,
    gbx_sems,
    gby_sems,
):
    count_x, count_y, count_z = sizes
    me_x, me_y, me_z = lax.axis_index("gx"), lax.axis_index("gy"), lax.axis_index("gz")

    def at_x(step):
        return {"gx": lax.rem(me_x + (step + count_x), count_x)}

    def at_y(step):
        return {"gy": lax.rem(me_y + (step + count_y), count_y)}

    def at_z(step):
        return {"gz": lax.rem(me_z + (step + count_z), count_z)}

    loads = [
        pltpu.make_async_copy(cond_hbm, staged.at[0], in_sem.at[0]),
        pltpu.make_async_copy(source_hbm, staged.at[1], in_sem.at[1]),
    ]
    for load in loads:
        load.start()

    barrier = pltpu.get_barrier_semaphore()
    partners = [at_z(1), at_z(-1)]
    partners += [at_x(step) for step in range(1, count_x)]
    partners += [at_y(step) for step in range(1, count_y)]
    for partner in partners:
        pl.semaphore_signal(barrier, inc=1, device_id=partner, device_id_type=MESH)

    pending = []

    def send(source, target, sems, slot, device):
        copy = pltpu.make_async_remote_copy(
            src_ref=source,
            dst_ref=target,
            send_sem=sems.at[0, slot],
            recv_sem=sems.at[1, slot],
            device_id=device,
            device_id_type=MESH,
        )
        copy.start()
        pending.append(copy)
        return copy

    keep = select_matrix(lambda l: jnp.where(l < 64, 2 * l, 2 * (l - 64) + 1))
    down_a = select_matrix(
        lambda l: jnp.where(l < 64, -1, jnp.where(l < 96, 2 * (l - 64), 2 * (l - 96) + 1))
    )
    down_b = select_matrix(
        lambda l: jnp.where(l >= 64, -1, jnp.where(l < 32, 2 * l, 2 * (l - 32) + 1))
    )
    up_a = select_matrix(
        lambda l: jnp.where(l < 64, -1, jnp.where(l >= 96, 64 + 2 * (l - 96), 64 + 2 * (l - 64) + 1))
    )
    up_b = select_matrix(
        lambda l: jnp.where(l >= 64, -1, jnp.where(l >= 32, 64 + 2 * (l - 32), 64 + 2 * l + 1))
    )
    z_copies = []
    for f in range(2):
        loads[f].wait()
        cells = staged[f].reshape(128, 128)
        z_send[f, 0] = (dot(cells[:64], down_a) + dot(cells[64:], down_b)).reshape(4, 16, 128)
        z_send[f, 1] = (dot(cells[:64], up_a) + dot(cells[64:], up_b)).reshape(4, 16, 128)
        if f == 0:
            pl.semaphore_wait(barrier, len(partners))
        z_copies.append(
            [
                send(z_send.at[f, way], z_recv.at[f, way], z_sems, 2 * f + way, at_z((-1, 1)[way]))
                for way in range(2)
            ]
        )
        own[f] = dot(cells, keep).reshape(8, 16, 128)

    def send_x(f):
        return [
            send(
                win.at[f, 4:8, :, 0:16, :],
                win.at[f, 12:16, :, 0:16, :],
                x_sems,
                2 * f,
                at_x(-1),
            ),
            send(
                win.at[f, 8:12, :, 0:16, :],
                win.at[f, 0:4, :, 0:16, :],
                x_sems,
                2 * f + 1,
                at_x(1),
            ),
        ]

    def send_y(f):
        y_send[f, 0] = win[f, :, :, 0:4, :]
        y_send[f, 1] = win[f, :, :, 12:16, :]
        return [
            send(y_send.at[f, way], y_recv.at[f, way], y_sems, 2 * f + way, at_y((-1, 1)[way]))
            for way in range(2)
        ]

    def place_y(f, copies):
        for copy in copies:
            copy.wait_recv()
        win[f, :, :, 16:20, :] = y_recv[f, 0]
        win[f, :, :, 20:24, :] = y_recv[f, 1]

    x_copies = []
    for f in range(2):
        for copy in z_copies[f]:
            copy.wait_recv()
        lane = lane_of((4, 16, 128))
        for part in range(2):
            mine = own[f, 4 * part : 4 * part + 4]
            above, below = z_recv[f, 0], z_recv[f, 1]
            for t in range(2):
                turn_above = ((0, 96), (64, 32))[part][t]
                turn_below = ((0, 32), (64, 96))[part][t]
                halo = jnp.where(
                    lane < 96,
                    roll(above, turn_above, 2) if turn_above else above,
                    roll(below, turn_below, 2) if turn_below else below,
                )
                win[f, 4 + 4 * part : 8 + 4 * part, t, 0:16, :] = jnp.where(
                    lane < 64, roll(mine, 64, 2) if t else mine, halo
                )
        x_copies.append(send_x(f))
    y_copies = []
    for f in range(2):
        for copy in x_copies[f]:
            copy.wait_recv()
        y_copies.append(send_y(f))
    place_y(0, y_copies[0])

    cond, source, best = win.at[0], win.at[1], win.at[2]
    faces0 = (fx, fy, fz)

    def fine_faces(low):
        here = pl.ds(low, 2)
        k0, k1 = cond[here, 0], cond[here, 1]
        fx[here, 0] = harmonic(k0, cond[pl.ds(low - 1, 2), 0])
        fx[here, 1] = harmonic(k1, cond[pl.ds(low - 1, 2), 1])
        fy[here, 0] = harmonic(k0, roll(k0, 1, 1))
        fy[here, 1] = harmonic(k1, roll(k1, 1, 1))
        fz[here, 0] = harmonic(k0, roll(k1, 1, 2))
        fz[here, 1] = harmonic(k1, k0)

    each(1, 15, 2, fine_faces)
    fx[15] = harmonic(cond[15], cond[14])

    for i in range(4):
        tmp0[0, i] = fx[4 + 2 * i, 0, 0:16, :] + fx[4 + 2 * i, 1, 0:16, :]
        tmp0[1, i] = (fy[4 + 2 * i, 0, 0:16, :] + fy[4 + 2 * i, 1, 0:16, :]) + (
            fy[5 + 2 * i, 0, 0:16, :] + fy[5 + 2 * i, 1, 0:16, :]
        )
        tmp0[2, i] = fz[4 + 2 * i, 0, 0:16, :] + fz[5 + 2 * i, 0, 0:16, :]
    first, second = pl.ds(0, 8, stride=2), pl.ds(1, 8, stride=2)
    f1[8:12, 0, 8:16, :] = 0.125 * (tmp0[0, :, first, :] + tmp0[0, :, second, :])
    f1[8:12, 1, 8:16, :] = 0.125 * tmp0[1, :, first, :]
    f1[8:12, 2, 8:16, :] = 0.125 * (tmp0[2, :, first, :] + tmp0[2, :, second, :])
    f1x_copies = [
        send(
            f1.at[8:12, :, 8:16, :],
            f1.at[8 - 4 * step : 12 - 4 * step, :, 8:16, :],
            f1x_sems,
            slot,
            at_x(step),
        )
        for slot, step in enumerate((-1, 1, -2, 2))
    ]

    row = lax.broadcasted_iota(jnp.int32, (128, 128), 0)
    column = lax.broadcasted_iota(jnp.int32, (128, 128), 1)
    pack = [
        jnp.where((row // 2 + 16) % 64 + 64 * p == column, 1.0, 0.0).astype(F32) for p in range(2)
    ]
    pack_even = [
        jnp.where((row % 2 == 0) & ((row // 2 + 16) % 64 + 64 * p == column), 1.0, 0.0).astype(F32)
        for p in range(2)
    ]
    first4, second4 = pl.ds(0, 4, stride=2), pl.ds(1, 4, stride=2)
    tmp1[0] = dot(f1[8, 0, 8:16, :], pack[0]) + dot(f1[10, 0, 8:16, :], pack[1])
    tmp1[1] = dot(f1[8, 1, 8:16, :] + f1[9, 1, 8:16, :], pack[0]) + dot(
        f1[10, 1, 8:16, :] + f1[11, 1, 8:16, :], pack[1]
    )
    tmp1[2] = dot(f1[8, 2, 8:16, :] + f1[9, 2, 8:16, :], pack_even[0]) + dot(
        f1[10, 2, 8:16, :] + f1[11, 2, 8:16, :], pack_even[1]
    )
    g2f[1, 2, 0] = 0.125 * (tmp1[0, first4, :] + tmp1[0, second4, :])
    g2f[1, 2, 1] = 0.125 * tmp1[1, first4, :]
    g2f[1, 2, 2] = 0.125 * (tmp1[2, first4, :] + tmp1[2, second4, :])

    def gather_x(ref, sems):
        return [
            send(ref.at[1, 2], ref.at[1, (2 - step) % count_x], sems, step - 1, at_x(step))
            for step in range(1, count_x)
        ]

    def gather_y(ref, sems):
        return [
            send(ref.at[1], ref.at[(1 - step) % count_y], sems, step - 1, at_y(step))
            for step in range(1, count_y)
        ]

    sibling = {"gy": me_y + 1 - 2 * lax.rem(me_y, 2)}
    shift = lax.rem(me_y, 2) * 2 + (count_y - 1)

    def hand_on(ref, sems, place):
        return send(
            ref.at[place],
            ref.at[lax.rem(place + shift, count_y)],
            sems,
            count_y + place,
            sibling,
        )

    def gather_y_shared(ref, sems):
        places = [(1 - step) % count_y for step in range(2, count_y, 2)]
        far = {
            place: send(ref.at[1], ref.at[place], sems, place, at_y(1 - place + count_y))
            for place in places
        }
        return far, [hand_on(ref, sems, 1)]

    def hand_on_all(ref, sems, far, handed):
        for place, copy in far.items():
            copy.wait_recv()
            handed.append(hand_on(ref, sems, place))

    gfx_copies = gather_x(g2f, gfx_sems)

    def inverse_0(low):
        here, after = pl.ds(low, 2), pl.ds(low + 1, 2)
        x_sum = [fx[here, t] + fx[after, t] for t in range(2)]
        y_sum = [fy[here, t] + roll(fy[here, t], -1, 1) for t in range(2)]
        z0, z1 = fz[here, 0], fz[here, 1]
        inv[here, 0] = 1.0 / ((x_sum[0] + y_sum[0]) + (z0 + z1))
        inv[here, 1] = 1.0 / ((x_sum[1] + y_sum[1]) + (z1 + roll(z0, -1, 2)))

    each(1, 15, 2, inverse_0)

    place_y(1, y_copies[1])

    def first_0(low):
        here = pl.ds(low, 2)
        d = inv[here] * source[here] * (1.0 / CENTER)
        dd[here] = d
        xa[here] = d

    each(1, 15, 2, first_0)

    def step_0(old, new, low, high, size, step, target=None):
        keep_old, keep_new = STEPS[step]

        def one(lo):
            here = pl.ds(lo, size)
            applied = operator_0(old, faces0, lo, size)
            for t in range(2):
                r = source[here, t] - applied[t]
                d = keep_old * dd[here, t] + keep_new * (inv[here, t] * r)
                if target is None:
                    dd[here, t] = d
                    new[here, t] = old[here, t] + d
                else:
                    target(lo, t, old[here, t] + d)

        each(low, high, size, one)

    step_0(xa, xb, 2, 14, 4, 0)

    for copy in f1x_copies:
        copy.wait_recv()
    f1y_copies = [
        send(
            f1.at[:, :, 8:16, :],
            f1.at[:, :, 8 - 8 * step : 16 - 8 * step, :],
            f1y_sems,
            slot,
            at_y(step),
        )
        for slot, step in enumerate((-1, 1))
    ]
    step_0(xb, xa, 3, 13, 5, 1)
    best[4:12, :, 0:16, :] = xa[4:12, :, 0:16, :]

    def residual_0(low):
        here = pl.ds(low, 4)
        applied = operator_0(xa, faces0, low, 4)
        r = (source[here, 0, 0:16, :] - applied[0][:, :16]) + (
            source[here, 1, 0:16, :] - applied[1][:, :16]
        )
        half = (low - 4) // 2
        tmp0[0, pl.ds(half, 1)] = r[0:1] + r[1:2]
        tmp0[0, pl.ds(half + 1, 1)] = r[2:3] + r[3:4]

    each(4, 12, 4, residual_0)
    b1[8:12, 8:16, :] = 0.125 * (tmp0[0, :, first, :] + tmp0[0, :, second, :])
    b1x_copies = [
        send(
            b1.at[8:12, 8:16, :],
            b1.at[8 - 4 * step : 12 - 4 * step, 8:16, :],
            b1x_sems,
            slot,
            at_x(step),
        )
        for slot, step in enumerate((-1, 1, -2, 2))
    ]

    for copy in f1y_copies:
        copy.wait_recv()
    def inverse_1(low):
        here = pl.ds(low, 6)
        x_sum = f1[here, 0] + f1[pl.ds(low + 1, 6), 0]
        y_term, z_term = f1[here, 1], f1[here, 2]
        y_sum = y_term + roll(y_term, -1, 1)
        inv1[here] = 1.0 / ((x_sum + y_sum) + (z_term + roll(z_term, -1, 2)))

    each(1, 19, 6, inverse_1)

    for copy in b1x_copies:
        copy.wait_recv()
    b1y_copies = [
        send(
            b1.at[:, 8:16, :],
            b1.at[:, 8 - 8 * step : 16 - 8 * step, :],
            b1y_sems,
            slot,
            at_y(step),
        )
        for slot, step in enumerate((-1, 1))
    ]
    x_copies.append(send_x(2))
    for copy in gfx_copies:
        copy.wait_recv()
    gfy_far, gfy_copies = gather_y_shared(g2f, gfy_sems)
    for copy in b1y_copies:
        copy.wait_recv()


    def first_1(low):
        here = pl.ds(low, 6)
        d = inv1[here] * b1[here] * (1.0 / CENTER)
        d1[here] = d
        x1a[here] = d

    each(1, 19, 6, first_1)

    def step_1(old, new, low, high, size, step):
        keep_old, keep_new = STEPS[step]

        def one(lo):
            here = pl.ds(lo, size)
            r = b1[here] - operator_1(old, f1, lo, size)
            d = keep_old * d1[here] + keep_new * (inv1[here] * r)
            d1[here] = d
            new[here] = old[here] + d

        each(low, high, size, one)

    step_1(x1a, x1b, 2, 18, 4, 0)
    hand_on_all(g2f, gfy_sems, gfy_far, gfy_copies)
    step_1(x1b, x1a, 3, 17, 7, 1)
    r = (b1[8:12] - operator_1(x1a, f1, 8, 4))[:, 8:16]
    tmp1[0] = dot(r[0] + r[1], pack[0]) + dot(r[2] + r[3], pack[1])
    g2b[1, 2] = 0.125 * (tmp1[0, first4, :] + tmp1[0, second4, :])
    gbx_copies = gather_x(g2b, gbx_sems)

    for copy in gfy_copies:
        copy.wait_recv()
    for f in range(3):
        for s in range(count_y):
            f2[f, :, 4 * s : 4 * s + 4, :] = g2f[s, :, f]
    faces2 = (f2.at[0], f2.at[1], f2.at[2])

    def inverse_2(low):
        here = pl.ds(low, 4)
        terms = rows(faces2[0], low, 5)
        turned = roll(terms, 64, 2)
        half = lane_of(terms[1:].shape) < 64
        x_sum = terms[:-1] + jnp.where(half, turned[:-1], turned[1:])
        y_term, z_term = f2[1, here], f2[2, here]
        y_sum = y_term + roll(y_term, -1, 1)
        inv2[here] = 1.0 / ((x_sum + y_sum) + (z_term + roll(z_term, -1, 2)))

        x_low = jnp.where(half, terms[:-1], turned[:-1])
        tmp2[0, here] = x_low + roll(x_low, -1, 2)
        y_both = y_term + roll(y_term, 64, 2)
        tmp2[1, here] = y_both + roll(y_both, -1, 2)
        tmp2[2, here] = z_term + roll(z_term, 64, 2)

    each(0, 16, 4, inverse_2)
    first16, second16 = pl.ds(0, 16, stride=2), pl.ds(1, 16, stride=2)
    f3[0] = 0.125 * (tmp2[0, :, first16, :] + tmp2[0, :, second16, :])
    f3[1] = 0.125 * tmp2[1, :, first16, :]
    f3[2] = 0.125 * (tmp2[2, :, first16, :] + tmp2[2, :, second16, :])
    faces3 = (f3.at[0], f3.at[1], f3.at[2])

    def inverse_3(low):
        here = pl.ds(low, 8)
        terms = rows(faces3[0], low, 9)
        y_term, z_term = f3[1, here], f3[2, here]
        inv3[here] = 1.0 / (
            (terms[:-1] + terms[1:] + (y_term + roll(y_term, -1, 1)))
            + (z_term + roll(z_term, -2, 2))
        )

    each(0, 16, 8, inverse_3)

    for copy in gbx_copies:
        copy.wait_recv()
    gby_copies = gather_y(g2b, gby_sems)
    for copy in x_copies[2]:
        copy.wait_recv()
    y_copies.append(send_y(2))
    for copy in gby_copies:
        copy.wait_recv()
    for s in range(count_y):
        b2[:, 4 * s : 4 * s + 4, :] = g2b[s]


    def first_2(low):
        here = pl.ds(low, 4)
        d = inv2[here] * b2[here] * (1.0 / CENTER)
        d2[here] = d
        x2a[here] = d

    each(0, 16, 4, first_2)

    def step_2(old, new, low, high, size, step):
        keep_old, keep_new = STEPS[step]

        def one(lo):
            r = rows(b2, lo, size) - operator_2(old, faces2, lo, size)
            d = keep_old * rows(d2, lo, size) + keep_new * (rows(inv2, lo, size) * r)
            put_rows(d2, lo, d)
            put_rows(new, lo, rows(old, lo, size) + d)

        each(low, high, size, one)

    step_2(x2a, x2b, 0, 16, 4, 0)
    step_2(x2b, x2a, 0, 16, 4, 1)

    def residual_2(low):
        here = pl.ds(low, 4)
        r = b2[here] - operator_2(x2a, faces2, low, 4)
        r = r + roll(r, 64, 2)
        tmp2[0, here] = r + roll(r, -1, 2)

    each(0, 16, 4, residual_2)
    b3[...] = 0.125 * (tmp2[0, :, first16, :] + tmp2[0, :, second16, :])

    d = inv3[...] * b3[...] * (1.0 / CENTER)
    d3[...] = d
    x3a[...] = d

    def step_3(old, new, step):
        keep_old, keep_new = STEPS[step]

        def one(lo):
            here = pl.ds(lo, 4)
            r = b3[here] - operator_3(old, faces3, lo, 4)
            d = keep_old * d3[here] + keep_new * (inv3[here] * r)
            d3[here] = d
            new[here] = old[here] + d

        each(0, 16, 4, one)

    step_3(x3a, x3b, 0)
    step_3(x3b, x3a, 1)

    e = x3a[...]
    e = jnp.where(lane_of(e.shape) % 2 == 0, e, roll(e, 1, 2))
    dup2[:, first16, :] = e
    dup2[:, second16, :] = e
    x2b[...] = x2a[...] + dup2[...]

    def first_up_2(low):
        r = rows(b2, low, 5) - operator_2(x2b, faces2, low, 5)
        d = rows(inv2, low, 5) * r * (1.0 / CENTER)
        put_rows(d2, low, d)
        put_rows(x2a, low, rows(x2b, low, 5) + d)

    each(-2, 8, 5, first_up_2)
    step_2(x2a, x2b, -1, 7, 4, 0)
    step_2(x2b, x2a, 0, 5, 5, 1)

    spread = [
        jnp.where((column // 2 + 16) % 64 + 64 * p == row, 1.0, 0.0).astype(F32) for p in range(2)
    ]
    e = x2a[0:5, 0:16, :].reshape(80, 128)
    for p in range(2):
        value = dot(e, spread[p]).reshape(5, 16, 128)
        dup21[p, :, first16, :] = value
        dup21[p, :, second16, :] = value

    def add_1(quad):
        for i in range(4):
            x1b[4 * quad + i] = x1a[4 * quad + i] + dup21[i // 2, quad, 0:24, :]

    each(0, 5, 1, add_1)

    def first_up_1(low):
        here = pl.ds(low, 4)
        r = b1[here] - operator_1(x1b, f1, low, 4)
        d = inv1[here] * r * (1.0 / CENTER)
        d1[here] = d
        x1a[here] = x1b[here] + d

    each(4, 16, 4, first_up_1)
    step_1(x1a, x1b, 5, 15, 5, 0)
    step_1(x1b, x1a, 6, 14, 4, 1)

    place_y(2, y_copies[2])
    e = x1a[6:14]
    dup1[:, pl.ds(0, 24, stride=2), :] = e
    dup1[:, pl.ds(1, 24, stride=2), :] = e
    lower = lax.broadcasted_iota(jnp.int32, (8, 128), 0) < 4

    def add_0(pair):
        brick = dup1[pair, 16:32, :]
        edge = jnp.where(lower, dup1[pair, 32:40, :], dup1[pair, 8:16, :])
        for k in range(2):
            i = 2 * pair + k
            for t in range(2):
                xb[i, t, 0:16, :] = best[i, t, 0:16, :] + brick
                xb[i, t, 16:24, :] = best[i, t, 16:24, :] + edge

    each(0, 8, 1, add_0)

    def first_up_0(low):
        here = pl.ds(low, 4)
        applied = operator_0(xb, faces0, low, 4)
        for t in range(2):
            r = source[here, t] - applied[t]
            d = inv[here, t] * r * (1.0 / CENTER)
            dd[here, t] = d
            xa[here, t] = xb[here, t] + d

    each(2, 14, 4, first_up_0)
    step_0(xa, xb, 3, 13, 5, 0)

    def to_own(low, t, value):
        own[t, pl.ds(low - 4, 4)] = value[:, 0:16, :]

    step_0(xb, None, 4, 12, 4, 1, to_own)
    join = [
        jnp.where((column == 2 * row + t) & (row < 64), 1.0, 0.0).astype(F32) for t in range(2)
    ]
    result = dot(own[0].reshape(128, 128), join[0]) + dot(own[1].reshape(128, 128), join[1])
    out_ref[...] = result.reshape(8, 16, 128)

    for copy in pending:
        copy.wait_send()


def solution(mesh):
    sizes = (mesh.shape["gx"], mesh.shape["gy"], mesh.shape["gz"])
    count_x, count_y, _ = sizes
    vmem = lambda *shape: pltpu.VMEM(shape, F32)
    sems = lambda count: pltpu.SemaphoreType.DMA((2, count))
    fine = (16, 2, 24, 128)
    level1 = (20, 24, 128)
    level2 = (16, 32, 128)
    level3 = (16, 16, 128)
    scratch = [
        vmem(2, 8, 16, 128),
        vmem(2, 8, 16, 128),
        vmem(2, 2, 4, 16, 128),
        vmem(2, 2, 4, 16, 128),
        vmem(3, *fine),
        vmem(3, 2, 16, 2, 4, 128),
        vmem(3, 2, 16, 2, 4, 128),
        vmem(*fine),
        vmem(*fine),
        vmem(*fine),
        vmem(*fine),
        vmem(*fine),
        vmem(*fine),
        vmem(*fine),
        vmem(3, 4, 16, 128),
        vmem(20, 3, 24, 128),
        vmem(*level1),
        vmem(*level1),
        vmem(*level1),
        vmem(*level1),
        vmem(*level1),
        vmem(3, 8, 128),
        vmem(8, 48, 128),
        vmem(count_y, count_x, 3, 4, 128),
        vmem(count_y, count_x, 4, 128),
        vmem(3, *level2),
        vmem(*level2),
        vmem(*level2),
        vmem(*level2),
        vmem(*level2),
        vmem(*level2),
        vmem(3, *level2),
        vmem(3, *level3),
        vmem(*level3),
        vmem(*level3),
        vmem(*level3),
        vmem(*level3),
        vmem(*level3),
        vmem(*level2),
        vmem(2, 5, 32, 128),
        pltpu.SemaphoreType.DMA((2,)),
        sems(4),
        sems(6),
        sems(6),
        sems(4),
        sems(2),
        sems(4),
        sems(2),
        sems(count_x - 1),
        sems(2 * count_y),
        sems(count_x - 1),
        sems(count_y - 1),
    ]

    def shards(pressure_source, conductivity):
        return pl.pallas_call(
            functools.partial(kernel, sizes),
            out_shape=jax.ShapeDtypeStruct((8, 16, 128), F32),
            in_specs=[pl.BlockSpec(memory_space=pltpu.HBM)] * 2,
            out_specs=pl.BlockSpec(memory_space=pltpu.VMEM),
            scratch_shapes=scratch,
            compiler_params=pltpu.CompilerParams(
                collective_id=0, has_side_effects=True, vmem_limit_bytes=48 * 1024 * 1024
            ),
        )(pressure_source, conductivity)

    placed = (P("gx", "gy", "gz"), P("gx", "gy", "gz"))
    return jax.shard_map(
        shards, mesh=mesh, in_specs=placed, out_specs=P("gx", "gy", "gz"), check_vma=False
    )
```

```python
import functools

import jax
import jax.numpy as jnp
from jax import lax
from jax.experimental import pallas as pl
from jax.experimental.pallas import tpu as pltpu
from jax.sharding import PartitionSpec as P

MESH = pl.DeviceIdType.MESH
F32 = jnp.float32

CENTER = 1.125
RADIUS = 0.875
RATIO = CENTER / RADIUS
RHO0 = 1.0 / RATIO
RHO1 = 1.0 / (2.0 * RATIO - RHO0)
RHO2 = 1.0 / (2.0 * RATIO - RHO1)
STEPS = ((RHO1 * RHO0, 2.0 * RHO1 / RADIUS), (RHO2 * RHO1, 2.0 * RHO2 / RADIUS))


def roll(value, shift, axis):
    return pltpu.roll(value, shift % value.shape[axis], axis)


def lane_of(shape):
    return lax.broadcasted_iota(jnp.int32, shape, len(shape) - 1)


def select_matrix(target):
    row = lax.broadcasted_iota(jnp.int32, (128, 128), 0)
    column = lax.broadcasted_iota(jnp.int32, (128, 128), 1)
    return jnp.where(row == target(column), 1.0, 0.0).astype(F32)


def dot(a, b):
    return jnp.dot(a, b, precision=lax.Precision.HIGHEST, preferred_element_type=F32)


def harmonic(one_side, other_side):
    return 2.0 * one_side * other_side / (one_side + other_side)


def chunks(low, high, size):
    return [(start, min(start + size, high)) for start in range(low, high, size)]


def operator_0(field, faces, low, high):
    face_x, face_y, face_z = faces
    result = []
    cells = []
    for t in range(2):
        v = field[low - 1 : high + 1, t]
        flux = face_x[low : high + 1, t] * (v[1:] - v[:-1])
        c = v[1:-1]
        g = flux[:-1] - flux[1:]
        flux = face_y[low:high, t] * (c - roll(c, 1, 1))
        g = g + (flux - roll(flux, -1, 1))
        cells.append(c)
        result.append(g)
    even = face_z[low:high, 0] * (cells[0] - roll(cells[1], 1, 2))
    odd = face_z[low:high, 1] * (cells[1] - cells[0])
    return [result[0] + (even - odd), result[1] + (odd - roll(even, -1, 2))]


def operator_1(field, faces, low, high):
    v = field[low - 1 : high + 1]
    flux = faces[low : high + 1, 0] * (v[1:] - v[:-1])
    c = v[1:-1]
    g = flux[:-1] - flux[1:]
    flux = faces[low:high, 1] * (c - roll(c, 1, 1))
    g = g + (flux - roll(flux, -1, 1))
    flux = faces[low:high, 2] * (c - roll(c, 1, 2))
    return g + (flux - roll(flux, -1, 2))


def rows(ref, low, high):
    pieces = []
    at = low
    while at < high:
        start = at % 16
        stop = min(16, start + high - at)
        pieces.append(ref[start:stop])
        at += stop - start
    return pieces[0] if len(pieces) == 1 else jnp.concatenate(pieces, axis=0)


def put_rows(ref, low, high, value):
    at = low
    while at < high:
        start = at % 16
        stop = min(16, start + high - at)
        ref[start:stop] = value[at - low : at - low + stop - start]
        at += stop - start


def operator_2(field, faces, low, high):
    face_x, face_y, face_z = faces
    v = rows(field, low - 1, high + 1)
    half = lane_of(v[:-1].shape) < 64
    turned = roll(v, 64, 2)
    flux = rows(face_x, low, high + 1) * (v[1:] - jnp.where(half, turned[:-1], turned[1:]))
    turned = roll(flux, 64, 2)
    g = flux[:-1] - jnp.where(half[1:], turned[:-1], turned[1:])
    c = v[1:-1]
    flux = rows(face_y, low, high) * (c - roll(c, 1, 1))
    g = g + (flux - roll(flux, -1, 1))
    flux = rows(face_z, low, high) * (c - roll(c, 1, 2))
    return g + (flux - roll(flux, -1, 2))


def operator_3(field, faces, low, high):
    face_x, face_y, face_z = faces
    v = rows(field, low - 1, high + 1)
    flux = rows(face_x, low, high + 1) * (v[1:] - v[:-1])
    g = flux[:-1] - flux[1:]
    c = v[1:-1]
    flux = rows(face_y, low, high) * (c - roll(c, 1, 1))
    g = g + (flux - roll(flux, -1, 1))
    flux = rows(face_z, low, high) * (c - roll(c, 2, 2))
    return g + (flux - roll(flux, -2, 2))


def kernel(
    sizes,
    source_hbm,
    cond_hbm,
    out_ref,
    staged,
    own,
    z_send,
    z_recv,
    win,
    y_send,
    y_recv,
    fx,
    fy,
    fz,
    inv,
    xa,
    xb,
    dd,
    tmp0,
    f1,
    b1,
    inv1,
    x1a,
    x1b,
    d1,
    tmp1,
    dup1,
    g2f,
    g2b,
    f2,
    b2,
    inv2,
    x2a,
    x2b,
    d2,
    tmp2,
    f3,
    b3,
    inv3,
    x3a,
    x3b,
    d3,
    dup2,
    dup21,
    in_sem,
    z_sems,
    x_sems,
    y_sems,
    f1x_sems,
    f1y_sems,
    b1x_sems,
    b1y_sems,
    gfx_sems,
    gfy_sems,
    gbx_sems,
    gby_sems,
):
    count_x, count_y, count_z = sizes
    me_x, me_y, me_z = lax.axis_index("gx"), lax.axis_index("gy"), lax.axis_index("gz")

    def at_x(step):
        return {"gx": lax.rem(me_x + (step + count_x), count_x)}

    def at_y(step):
        return {"gy": lax.rem(me_y + (step + count_y), count_y)}

    def at_z(step):
        return {"gz": lax.rem(me_z + (step + count_z), count_z)}

    loads = [
        pltpu.make_async_copy(cond_hbm, staged.at[0], in_sem.at[0]),
        pltpu.make_async_copy(source_hbm, staged.at[1], in_sem.at[1]),
    ]
    for load in loads:
        load.start()

    barrier = pltpu.get_barrier_semaphore()
    partners = [at_z(1), at_z(-1)]
    partners += [at_x(sign * step) for step in (1, 2, 3, 5, 6) for sign in (1, -1)]
    partners += [at_y(step) for step in range(1, count_y)]
    for partner in partners:
        pl.semaphore_signal(barrier, inc=1, device_id=partner, device_id_type=MESH)

    pending = []

    def drain():
        for copy in pending:
            copy.wait_send()
        pending.clear()

    def send(source, target, sems, slot, device):
        copy = pltpu.make_async_remote_copy(
            src_ref=source,
            dst_ref=target,
            send_sem=sems.at[0, slot],
            recv_sem=sems.at[1, slot],
            device_id=device,
            device_id_type=MESH,
        )
        copy.start()
        pending.append(copy)
        return copy

    keep = select_matrix(lambda l: jnp.where(l < 64, 2 * l, 2 * (l - 64) + 1))
    down_a = select_matrix(
        lambda l: jnp.where(l < 64, -1, jnp.where(l < 96, 2 * (l - 64), 2 * (l - 96) + 1))
    )
    down_b = select_matrix(
        lambda l: jnp.where(l >= 64, -1, jnp.where(l < 32, 2 * l, 2 * (l - 32) + 1))
    )
    up_a = select_matrix(
        lambda l: jnp.where(l < 64, -1, jnp.where(l >= 96, 64 + 2 * (l - 96), 64 + 2 * (l - 64) + 1))
    )
    up_b = select_matrix(
        lambda l: jnp.where(l >= 64, -1, jnp.where(l >= 32, 64 + 2 * (l - 32), 64 + 2 * l + 1))
    )
    z_copies = []
    for f in range(2):
        loads[f].wait()
        cells = staged[f].reshape(128, 128)
        z_send[f, 0] = (dot(cells[:64], down_a) + dot(cells[64:], down_b)).reshape(4, 16, 128)
        z_send[f, 1] = (dot(cells[:64], up_a) + dot(cells[64:], up_b)).reshape(4, 16, 128)
        if f == 0:
            pl.semaphore_wait(barrier, len(partners))
        z_copies.append(
            [
                send(z_send.at[f, way], z_recv.at[f, way], z_sems, 2 * f + way, at_z((-1, 1)[way]))
                for way in range(2)
            ]
        )
        own[f] = dot(cells, keep).reshape(8, 16, 128)

    def send_x(f):
        return [
            send(
                win.at[f, 4:8, :, 0:16, :],
                win.at[f, 12:16, :, 0:16, :],
                x_sems,
                2 * f,
                at_x(-1),
            ),
            send(
                win.at[f, 8:12, :, 0:16, :],
                win.at[f, 0:4, :, 0:16, :],
                x_sems,
                2 * f + 1,
                at_x(1),
            ),
        ]

    def send_y(f):
        y_send[f, 0] = win[f, :, :, 0:4, :]
        y_send[f, 1] = win[f, :, :, 12:16, :]
        return [
            send(y_send.at[f, way], y_recv.at[f, way], y_sems, 2 * f + way, at_y((-1, 1)[way]))
            for way in range(2)
        ]

    def place_y(f, copies):
        for copy in copies:
            copy.wait_recv()
        win[f, :, :, 16:20, :] = y_recv[f, 0]
        win[f, :, :, 20:24, :] = y_recv[f, 1]

    x_copies = []
    for f in range(2):
        for copy in z_copies[f]:
            copy.wait_recv()
        lane = lane_of((4, 16, 128))
        for part in range(2):
            mine = own[f, 4 * part : 4 * part + 4]
            above, below = z_recv[f, 0], z_recv[f, 1]
            for t in range(2):
                turn_above = ((0, 96), (64, 32))[part][t]
                turn_below = ((0, 32), (64, 96))[part][t]
                halo = jnp.where(
                    lane < 96,
                    roll(above, turn_above, 2) if turn_above else above,
                    roll(below, turn_below, 2) if turn_below else below,
                )
                win[f, 4 + 4 * part : 8 + 4 * part, t, 0:16, :] = jnp.where(
                    lane < 64, roll(mine, 64, 2) if t else mine, halo
                )
        x_copies.append(send_x(f))
    y_copies = []
    for f in range(2):
        for copy in x_copies[f]:
            copy.wait_recv()
        y_copies.append(send_y(f))
    place_y(0, y_copies[0])

    cond, source, best = win.at[0], win.at[1], win.at[2]
    faces0 = (fx, fy, fz)
    for low, high in chunks(1, 16, 4):
        for t in range(2):
            k = cond[low - 1 : high, t]
            fx[low:high, t] = harmonic(k[1:], k[:-1])
    for low, high in chunks(1, 15, 4):
        k0, k1 = cond[low:high, 0], cond[low:high, 1]
        fy[low:high, 0] = harmonic(k0, roll(k0, 1, 1))
        fy[low:high, 1] = harmonic(k1, roll(k1, 1, 1))
        fz[low:high, 0] = harmonic(k0, roll(k1, 1, 2))
        fz[low:high, 1] = harmonic(k1, k0)

    for i in range(4):
        tmp0[0, i] = fx[4 + 2 * i, 0, 0:16, :] + fx[4 + 2 * i, 1, 0:16, :]
        tmp0[1, i] = (fy[4 + 2 * i, 0, 0:16, :] + fy[4 + 2 * i, 1, 0:16, :]) + (
            fy[5 + 2 * i, 0, 0:16, :] + fy[5 + 2 * i, 1, 0:16, :]
        )
        tmp0[2, i] = fz[4 + 2 * i, 0, 0:16, :] + fz[5 + 2 * i, 0, 0:16, :]
    first, second = pl.ds(0, 8, stride=2), pl.ds(1, 8, stride=2)
    f1[8:12, 0, 8:16, :] = 0.125 * (tmp0[0, :, first, :] + tmp0[0, :, second, :])
    f1[8:12, 1, 8:16, :] = 0.125 * tmp0[1, :, first, :]
    f1[8:12, 2, 8:16, :] = 0.125 * (tmp0[2, :, first, :] + tmp0[2, :, second, :])
    f1x_copies = [
        send(
            f1.at[8:12, :, 8:16, :],
            f1.at[8 - 4 * step : 12 - 4 * step, :, 8:16, :],
            f1x_sems,
            slot,
            at_x(step),
        )
        for slot, step in enumerate((-1, 1, -2, 2))
    ]

    def spread_x(ref, first, last, sems, steps):
        return [
            send(ref.at[1, first:last], ref.at[1, first - step : last - step], sems, slot, at_x(step))
            for slot, step in enumerate(steps)
        ]

    def gather_y(ref, sems):
        return [
            send(ref.at[1], ref.at[(1 - step) % count_y], sems, step - 1, at_y(step))
            for step in range(1, count_y)
        ]

    sibling = {"gy": me_y + 1 - 2 * lax.rem(me_y, 2)}
    shift = lax.rem(me_y, 2) * 2 + (count_y - 1)

    def hand_on(ref, sems, place):
        return send(
            ref.at[place],
            ref.at[lax.rem(place + shift, count_y)],
            sems,
            count_y + place,
            sibling,
        )

    def gather_y_shared(ref, sems):
        places = [(1 - step) % count_y for step in range(2, count_y, 2)]
        far = {
            place: send(ref.at[1], ref.at[place], sems, place, at_y(1 - place + count_y))
            for place in places
        }
        return far, [hand_on(ref, sems, 1)]

    def hand_on_all(ref, sems, far, handed):
        for place, copy in far.items():
            copy.wait_recv()
            handed.append(hand_on(ref, sems, place))

    for low, high in chunks(1, 15, 2):
        x_sum = [fx[low:high, t] + fx[low + 1 : high + 1, t] for t in range(2)]
        y_sum = [fy[low:high, t] + roll(fy[low:high, t], -1, 1) for t in range(2)]
        z0, z1 = fz[low:high, 0], fz[low:high, 1]
        inv[low:high, 0] = 1.0 / ((x_sum[0] + y_sum[0]) + (z0 + z1))
        inv[low:high, 1] = 1.0 / ((x_sum[1] + y_sum[1]) + (z1 + roll(z0, -1, 2)))

    place_y(1, y_copies[1])
    for low, high in chunks(1, 15, 4):
        for t in range(2):
            d = inv[low:high, t] * source[low:high, t] * (1.0 / CENTER)
            dd[low:high, t] = d
            xa[low:high, t] = d

    def step_0(old, new, low, high, step, target=None):
        keep_old, keep_new = STEPS[step]
        for lo, hi in chunks(low, high, 2):
            applied = operator_0(old, faces0, lo, hi)
            for t in range(2):
                r = source[lo:hi, t] - applied[t]
                d = keep_old * dd[lo:hi, t] + keep_new * (inv[lo:hi, t] * r)
                if target is None:
                    dd[lo:hi, t] = d
                    new[lo:hi, t] = old[lo:hi, t] + d
                else:
                    target(lo, hi, t, old[lo:hi, t] + d)

    step_0(xa, xb, 2, 14, 0)

    for copy in f1x_copies:
        copy.wait_recv()
    f1y_copies = [
        send(
            f1.at[:, :, 8:16, :],
            f1.at[:, :, 8 - 8 * step : 16 - 8 * step, :],
            f1y_sems,
            slot,
            at_y(step),
        )
        for slot, step in enumerate((-1, 1))
    ]
    step_0(xb, xa, 3, 13, 1)
    best[4:12, :, 0:16, :] = xa[4:12, :, 0:16, :]
    for i in range(4):
        applied = operator_0(xa, faces0, 4 + 2 * i, 6 + 2 * i)
        r = (source[4 + 2 * i : 6 + 2 * i, 0, 0:16, :] - applied[0][:, :16]) + (
            source[4 + 2 * i : 6 + 2 * i, 1, 0:16, :] - applied[1][:, :16]
        )
        tmp0[0, i] = r[0] + r[1]
    b1[8:12, 8:16, :] = 0.125 * (tmp0[0, :, first, :] + tmp0[0, :, second, :])
    b1x_copies = [
        send(
            b1.at[8:12, 8:16, :],
            b1.at[8 - 4 * step : 12 - 4 * step, 8:16, :],
            b1x_sems,
            slot,
            at_x(step),
        )
        for slot, step in enumerate((-1, 1, -2, 2))
    ]

    row = lax.broadcasted_iota(jnp.int32, (128, 128), 0)
    column = lax.broadcasted_iota(jnp.int32, (128, 128), 1)
    pack = [
        jnp.where((row // 2 + 16) % 64 + 64 * p == column, 1.0, 0.0).astype(F32) for p in range(2)
    ]
    pack_even = [
        jnp.where((row % 2 == 0) & ((row // 2 + 16) % 64 + 64 * p == column), 1.0, 0.0).astype(F32)
        for p in range(2)
    ]
    first4, second4 = pl.ds(0, 4, stride=2), pl.ds(1, 4, stride=2)

    def packed(pieces, matrices):
        whole = [jnp.concatenate(piece, axis=0) for piece in pieces]
        result = dot(whole[0], matrices[0]) + dot(whole[1], matrices[1])
        return result.reshape(len(pieces[0]), 8, 128)

    g2f[1, 15] = jnp.ones((3, 4, 128), F32)
    g2b[1, 15] = jnp.zeros((4, 128), F32)
    mine = slice(8, 16)
    tmp1[0] = packed([[f1[4 * i + 2 * p, 0, mine, :] for i in range(5)] for p in range(2)], pack)
    for f in (1, 2):
        pieces = [
            [f1[4 * i + 2 * p, f, mine, :] + f1[4 * i + 2 * p + 1, f, mine, :] for i in range(5)]
            for p in range(2)
        ]
        tmp1[f] = packed(pieces, (None, pack, pack_even)[f])
    g2f[1, 5:10, 0] = 0.125 * (tmp1[0, :, first4, :] + tmp1[0, :, second4, :])
    g2f[1, 5:10, 1] = 0.125 * tmp1[1, :, first4, :]
    g2f[1, 5:10, 2] = 0.125 * (tmp1[2, :, first4, :] + tmp1[2, :, second4, :])
    gfx_copies = spread_x(g2f, 5, 10, gfx_sems, (5, -5))

    drain()
    for copy in b1x_copies:
        copy.wait_recv()
    b1y_copies = [
        send(
            b1.at[:, 8:16, :],
            b1.at[:, 8 - 8 * step : 16 - 8 * step, :],
            b1y_sems,
            slot,
            at_y(step),
        )
        for slot, step in enumerate((-1, 1))
    ]
    for copy in f1y_copies:
        copy.wait_recv()
    for low, high in chunks(1, 19, 6):
        x_sum = f1[low:high, 0] + f1[low + 1 : high + 1, 0]
        y_term, z_term = f1[low:high, 1], f1[low:high, 2]
        y_sum = y_term + roll(y_term, -1, 1)
        inv1[low:high] = 1.0 / ((x_sum + y_sum) + (z_term + roll(z_term, -1, 2)))

    for copy in b1y_copies:
        copy.wait_recv()

    for low, high in chunks(1, 19, 6):
        d = inv1[low:high] * b1[low:high] * (1.0 / CENTER)
        d1[low:high] = d
        x1a[low:high] = d

    def step_1(old, new, low, high, step):
        keep_old, keep_new = STEPS[step]
        for lo, hi in chunks(low, high, 4):
            r = b1[lo:hi] - operator_1(old, f1, lo, hi)
            d = keep_old * d1[lo:hi] + keep_new * (inv1[lo:hi] * r)
            d1[lo:hi] = d
            new[lo:hi] = old[lo:hi] + d

    step_1(x1a, x1b, 2, 18, 0)
    for copy in gfx_copies:
        copy.wait_recv()
    gfy_far, gfy_copies = gather_y_shared(g2f, gfy_sems)
    step_1(x1b, x1a, 3, 17, 1)
    r = (b1[4:16] - operator_1(x1a, f1, 4, 16))[:, 8:16]
    tmp1[0, 0:3] = packed(
        [[r[4 * i + 2 * p] + r[4 * i + 2 * p + 1] for i in range(3)] for p in range(2)], pack
    )
    g2b[1, 6:9] = 0.125 * (tmp1[0, 0:3, first4, :] + tmp1[0, 0:3, second4, :])
    gbx_copies = spread_x(g2b, 6, 9, gbx_sems, (3, -3, 6, -6))
    x_copies.append(send_x(2))
    for copy in gbx_copies:
        copy.wait_recv()
    gby_copies = gather_y(g2b, gby_sems)

    hand_on_all(g2f, gfy_sems, gfy_far, gfy_copies)
    for copy in gfy_copies:
        copy.wait_recv()
    for f in range(3):
        for s in range(count_y):
            f2[f, :, 4 * s : 4 * s + 4, :] = g2f[s, :, f]
    faces2 = (f2.at[0], f2.at[1], f2.at[2])
    for low, high in chunks(0, 16, 4):
        terms = rows(faces2[0], low, high + 1)
        turned = roll(terms, 64, 2)
        half = lane_of(terms[1:].shape) < 64
        x_sum = terms[:-1] + jnp.where(half, turned[:-1], turned[1:])
        y_term, z_term = f2[1, low:high], f2[2, low:high]
        y_sum = y_term + roll(y_term, -1, 1)
        inv2[low:high] = 1.0 / ((x_sum + y_sum) + (z_term + roll(z_term, -1, 2)))

        x_low = f2[0, low:high]
        x_low = jnp.where(half, x_low, roll(x_low, 64, 2))
        tmp2[0, low:high] = x_low + roll(x_low, -1, 2)
        y_both = y_term + roll(y_term, 64, 2)
        tmp2[1, low:high] = y_both + roll(y_both, -1, 2)
        tmp2[2, low:high] = z_term + roll(z_term, 64, 2)
    first16, second16 = pl.ds(0, 16, stride=2), pl.ds(1, 16, stride=2)
    f3[0] = 0.125 * (tmp2[0, :, first16, :] + tmp2[0, :, second16, :])
    f3[1] = 0.125 * tmp2[1, :, first16, :]
    f3[2] = 0.125 * (tmp2[2, :, first16, :] + tmp2[2, :, second16, :])
    faces3 = (f3.at[0], f3.at[1], f3.at[2])
    for low, high in chunks(0, 16, 8):
        terms = rows(faces3[0], low, high + 1)
        y_term, z_term = f3[1, low:high], f3[2, low:high]
        inv3[low:high] = 1.0 / (
            (terms[:-1] + terms[1:] + (y_term + roll(y_term, -1, 1)))
            + (z_term + roll(z_term, -2, 2))
        )

    for copy in x_copies[2]:
        copy.wait_recv()
    y_copies.append(send_y(2))
    for copy in gby_copies:
        copy.wait_recv()
    for s in range(count_y):
        b2[:, 4 * s : 4 * s + 4, :] = g2b[s]

    for low, high in chunks(0, 16, 4):
        d = inv2[low:high] * b2[low:high] * (1.0 / CENTER)
        d2[low:high] = d
        x2a[low:high] = d

    def step_2(old, new, low, high, step):
        keep_old, keep_new = STEPS[step]
        for lo, hi in chunks(low, high, 2):
            r = rows(b2, lo, hi) - operator_2(old, faces2, lo, hi)
            d = keep_old * rows(d2, lo, hi) + keep_new * (rows(inv2, lo, hi) * r)
            put_rows(d2, lo, hi, d)
            put_rows(new, lo, hi, rows(old, lo, hi) + d)

    step_2(x2a, x2b, 0, 16, 0)
    step_2(x2b, x2a, 0, 16, 1)
    for low, high in chunks(0, 16, 2):
        r = b2[low:high] - operator_2(x2a, faces2, low, high)
        r = r + roll(r, 64, 2)
        tmp2[0, low:high] = r + roll(r, -1, 2)
    b3[...] = 0.125 * (tmp2[0, :, first16, :] + tmp2[0, :, second16, :])

    d = inv3[...] * b3[...] * (1.0 / CENTER)
    d3[...] = d
    x3a[...] = d

    def step_3(old, new, low, high, step):
        keep_old, keep_new = STEPS[step]
        for lo, hi in chunks(low, high, 4):
            r = rows(b3, lo, hi) - operator_3(old, faces3, lo, hi)
            d = keep_old * rows(d3, lo, hi) + keep_new * (rows(inv3, lo, hi) * r)
            put_rows(d3, lo, hi, d)
            put_rows(new, lo, hi, rows(old, lo, hi) + d)

    step_3(x3a, x3b, 0, 16, 0)
    step_3(x3b, x3a, 0, 16, 1)

    e = x3a[...]
    e = jnp.where(lane_of(e.shape) % 2 == 0, e, roll(e, 1, 2))
    dup2[:, first16, :] = e
    dup2[:, second16, :] = e
    for low, high in chunks(2, 13, 4):
        put_rows(x2b, low, high, rows(x2a, low, high) + rows(dup2, low, high))
    for low, high in chunks(3, 12, 2):
        r = rows(b2, low, high) - operator_2(x2b, faces2, low, high)
        d = rows(inv2, low, high) * r * (1.0 / CENTER)
        put_rows(d2, low, high, d)
        put_rows(x2a, low, high, rows(x2b, low, high) + d)
    step_2(x2a, x2b, 4, 11, 0)
    step_2(x2b, x2a, 5, 10, 1)

    spread = [
        jnp.where((column // 2 + 16) % 64 + 64 * p == row, 1.0, 0.0).astype(F32) for p in range(2)
    ]
    e = x2a[5:10, 0:16, :].reshape(80, 128)
    for p in range(2):
        value = dot(e, spread[p]).reshape(5, 16, 128)
        dup21[p, :, first16, :] = value
        dup21[p, :, second16, :] = value
    for i in range(3, 17):
        x1b[i] = x1a[i] + dup21[(i // 2) % 2, i // 4, 0:24, :]
    for low, high in chunks(4, 16, 4):
        r = b1[low:high] - operator_1(x1b, f1, low, high)
        d = inv1[low:high] * r * (1.0 / CENTER)
        d1[low:high] = d
        x1a[low:high] = x1b[low:high] + d
    step_1(x1a, x1b, 5, 15, 0)
    step_1(x1b, x1a, 6, 14, 1)

    drain()
    place_y(2, y_copies[2])
    e = x1a[6:14]
    dup1[:, pl.ds(0, 24, stride=2), :] = e
    dup1[:, pl.ds(1, 24, stride=2), :] = e
    lower = lax.broadcasted_iota(jnp.int32, (8, 128), 0) < 4
    for i in range(1, 15):
        j = i // 2
        brick = dup1[j, 16:32, :]
        edge = jnp.where(lower, dup1[j, 32:40, :], dup1[j, 8:16, :])
        for t in range(2):
            xb[i, t, 0:16, :] = best[i, t, 0:16, :] + brick
            xb[i, t, 16:24, :] = best[i, t, 16:24, :] + edge
    for lo, hi in chunks(2, 14, 2):
        applied = operator_0(xb, faces0, lo, hi)
        for t in range(2):
            r = source[lo:hi, t] - applied[t]
            d = inv[lo:hi, t] * r * (1.0 / CENTER)
            dd[lo:hi, t] = d
            xa[lo:hi, t] = xb[lo:hi, t] + d
    step_0(xa, xb, 3, 13, 0)

    def to_own(lo, hi, t, value):
        own[t, lo - 4 : hi - 4] = value[:, 0:16, :]

    step_0(xb, None, 4, 12, 1, to_own)
    join = [
        jnp.where((column == 2 * row + t) & (row < 64), 1.0, 0.0).astype(F32) for t in range(2)
    ]
    result = dot(own[0].reshape(128, 128), join[0]) + dot(own[1].reshape(128, 128), join[1])
    out_ref[...] = result.reshape(8, 16, 128)


def solution(mesh):
    sizes = (mesh.shape["gx"], mesh.shape["gy"], mesh.shape["gz"])
    count_x, count_y, _ = sizes
    vmem = lambda *shape: pltpu.VMEM(shape, F32)
    sems = lambda count: pltpu.SemaphoreType.DMA((2, count))
    fine = (16, 2, 24, 128)
    level1 = (20, 24, 128)
    level2 = (16, 32, 128)
    level3 = (16, 16, 128)
    scratch = [
        vmem(2, 8, 16, 128),
        vmem(2, 8, 16, 128),
        vmem(2, 2, 4, 16, 128),
        vmem(2, 2, 4, 16, 128),
        vmem(3, *fine),
        vmem(3, 2, 16, 2, 4, 128),
        vmem(3, 2, 16, 2, 4, 128),
        vmem(*fine),
        vmem(*fine),
        vmem(*fine),
        vmem(*fine),
        vmem(*fine),
        vmem(*fine),
        vmem(*fine),
        vmem(3, 4, 16, 128),
        vmem(20, 3, 24, 128),
        vmem(*level1),
        vmem(*level1),
        vmem(*level1),
        vmem(*level1),
        vmem(*level1),
        vmem(3, 5, 8, 128),
        vmem(8, 48, 128),
        vmem(count_y, count_x, 3, 4, 128),
        vmem(count_y, count_x, 4, 128),
        vmem(3, *level2),
        vmem(*level2),
        vmem(*level2),
        vmem(*level2),
        vmem(*level2),
        vmem(*level2),
        vmem(3, *level2),
        vmem(3, *level3),
        vmem(*level3),
        vmem(*level3),
        vmem(*level3),
        vmem(*level3),
        vmem(*level3),
        vmem(*level2),
        vmem(2, 5, 32, 128),
        pltpu.SemaphoreType.DMA((2,)),
        sems(4),
        sems(6),
        sems(6),
        sems(4),
        sems(2),
        sems(4),
        sems(2),
        sems(2),
        sems(2 * count_y),
        sems(4),
        sems(count_y - 1),
    ]

    def shards(pressure_source, conductivity):
        return pl.pallas_call(
            functools.partial(kernel, sizes),
            out_shape=jax.ShapeDtypeStruct((8, 16, 128), F32),
            in_specs=[pl.BlockSpec(memory_space=pltpu.HBM)] * 2,
            out_specs=pl.BlockSpec(memory_space=pltpu.VMEM),
            scratch_shapes=scratch,
            compiler_params=pltpu.CompilerParams(
                collective_id=0, has_side_effects=True, vmem_limit_bytes=62 * 1024 * 1024
            ),
        )(pressure_source, conductivity)

    placed = (P("gx", "gy", "gz"), P("gx", "gy", "gz"))
    return jax.shard_map(
        shards, mesh=mesh, in_specs=placed, out_specs=P("gx", "gy", "gz"), check_vma=False
    )
```

```python
import functools

import jax
import jax.numpy as jnp
from jax import lax
from jax.experimental import pallas as pl
from jax.experimental.pallas import tpu as pltpu
from jax.sharding import PartitionSpec as P

MESH = pl.DeviceIdType.MESH
F32 = jnp.float32

CENTER = 1.125
RADIUS = 0.875
RATIO = CENTER / RADIUS
RHO0 = 1.0 / RATIO
RHO1 = 1.0 / (2.0 * RATIO - RHO0)
RHO2 = 1.0 / (2.0 * RATIO - RHO1)
STEPS = ((RHO1 * RHO0, 2.0 * RHO1 / RADIUS), (RHO2 * RHO1, 2.0 * RHO2 / RADIUS))


def roll(value, shift, axis):
    return pltpu.roll(value, shift % value.shape[axis], axis)


def lane_of(shape):
    return lax.broadcasted_iota(jnp.int32, shape, len(shape) - 1)


def select_matrix(shape, holds):
    row = lax.broadcasted_iota(jnp.int32, shape, 0)
    column = lax.broadcasted_iota(jnp.int32, shape, 1)
    return jnp.where(holds(row, column), 1.0, 0.0).astype(jnp.bfloat16)


def dot(a, ones):
    high = a.astype(jnp.bfloat16)
    rest = a - high.astype(F32)
    middle = rest.astype(jnp.bfloat16)
    low = (rest - middle.astype(F32)).astype(jnp.bfloat16)
    parts = [jnp.dot(part, ones, preferred_element_type=F32) for part in (low, middle, high)]
    return (parts[0] + parts[1]) + parts[2]


def side_by_side(a, b):
    return jnp.concatenate([a, b], axis=1)


def harmonic(one_side, other_side):
    return 2.0 * one_side * other_side / (one_side + other_side)


def chunks(low, high, size):
    return [(start, min(start + size, high)) for start in range(low, high, size)]


def sweep_0(field, faces, low, high, emit):
    face_x, face_y, face_z = faces
    both = range(2)
    here = [field[low, t] for t in both]
    flux = [face_x[low, t] * (here[t] - field[low - 1, t]) for t in both]
    for i in range(low, high):
        after = [field[i + 1, t] for t in both]
        upper = [face_x[i + 1, t] * (after[t] - here[t]) for t in both]
        result = []
        for t in both:
            side = face_y[i, t] * (here[t] - roll(here[t], 1, 0))
            result.append((flux[t] - upper[t]) + (side - roll(side, -1, 0)))
        even = face_z[i, 0] * (here[0] - roll(here[1], 1, 1))
        odd = face_z[i, 1] * (here[1] - here[0])
        emit(i, [result[0] + (even - odd), result[1] + (odd - roll(even, -1, 1))], here)
        here, flux = after, upper


def sweep_1(field, faces, low, high, emit):
    here = field[low]
    flux = faces[low, 0] * (here - field[low - 1])
    for i in range(low, high):
        after = field[i + 1]
        upper = faces[i + 1, 0] * (after - here)
        side = faces[i, 1] * (here - roll(here, 1, 0))
        result = (flux - upper) + (side - roll(side, -1, 0))
        side = faces[i, 2] * (here - roll(here, 1, 1))
        emit(i, result + (side - roll(side, -1, 1)), here)
        here, flux = after, upper


def sweep_2(field, faces, low, high, emit):
    half = lane_of(field.shape[1:]) < 64
    before, here = roll(field[low - 1], 64, 1), field[low]
    turned = roll(here, 64, 1)
    flux = faces[0, low] * (here - jnp.where(half, before, turned))
    flux_turned = roll(flux, 64, 1)
    for i in range(low, high):
        after = field[i + 1]
        after_turned = roll(after, 64, 1)
        upper = faces[0, i + 1] * (after - jnp.where(half, turned, after_turned))
        upper_turned = roll(upper, 64, 1)
        result = flux - jnp.where(half, flux_turned, upper_turned)
        side = faces[1, i] * (here - roll(here, 1, 0))
        result = result + (side - roll(side, -1, 0))
        side = faces[2, i] * (here - roll(here, 1, 1))
        emit(i, result + (side - roll(side, -1, 1)), here)
        here, turned, flux, flux_turned = after, after_turned, upper, upper_turned


def sweep_3(field, faces, low, high, emit):
    here = field[low]
    flux = faces[0, low] * (here - field[low - 1])
    for i in range(low, high):
        after = field[i + 1]
        upper = faces[0, i + 1] * (after - here)
        side = faces[1, i] * (here - roll(here, 1, 0))
        result = (flux - upper) + (side - roll(side, -1, 0))
        side = faces[2, i] * (here - roll(here, 2, 1))
        emit(i, result + (side - roll(side, -2, 1)), here)
        here, flux = after, upper


def kernel(
    sizes,
    source_hbm,
    cond_hbm,
    out_ref,
    staged,
    own,
    z_send,
    z_recv,
    win,
    y_send,
    y_recv,
    fx,
    fy,
    fz,
    inv,
    xa,
    xb,
    dd,
    tmp0,
    f1,
    b1,
    inv1,
    x1a,
    x1b,
    d1,
    tmp1,
    dup1,
    g2f,
    g2b,
    f2,
    b2,
    inv2,
    x2a,
    x2b,
    d2,
    tmp2,
    f3,
    b3,
    inv3,
    x3a,
    x3b,
    d3,
    dup2,
    dup21,
    in_sem,
    z_sems,
    x_sems,
    y_sems,
    f1x_sems,
    f1y_sems,
    b1x_sems,
    b1y_sems,
    gfx_sems,
    gfy_sems,
    gbx_sems,
    gby_sems,
):
    count_x, count_y, count_z = sizes
    me_x, me_y, me_z = lax.axis_index("gx"), lax.axis_index("gy"), lax.axis_index("gz")

    def at_x(step):
        return {"gx": lax.rem(me_x + (step + count_x), count_x)}

    def at_y(step):
        return {"gy": lax.rem(me_y + (step + count_y), count_y)}

    def at_z(step):
        return {"gz": lax.rem(me_z + (step + count_z), count_z)}

    loads = [
        pltpu.make_async_copy(cond_hbm, staged.at[0], in_sem.at[0]),
        pltpu.make_async_copy(source_hbm, staged.at[1], in_sem.at[1]),
    ]
    for load in loads:
        load.start()

    barrier = pltpu.get_barrier_semaphore()
    partners = [at_z(1), at_z(-1)]
    partners += [at_x(sign * step) for step in (1, 2, 3, 5, 6) for sign in (1, -1)]
    partners += [at_y(step) for step in range(1, count_y)]
    for partner in partners:
        pl.semaphore_signal(barrier, inc=1, device_id=partner, device_id_type=MESH)

    pending = []

    def drain():
        for copy in pending:
            copy.wait_send()
        pending.clear()

    def send(source, target, sems, slot, device):
        copy = pltpu.make_async_remote_copy(
            src_ref=source,
            dst_ref=target,
            send_sem=sems.at[0, slot],
            recv_sem=sems.at[1, slot],
            device_id=device,
            device_id_type=MESH,
        )
        copy.start()
        pending.append(copy)
        return copy

    def kept(row, l):
        return row == jnp.where(l < 64, 2 * l, 2 * (l - 64) + 1)

    def sent(row, l):
        half, q = l // 128, (l % 128) // 32
        z = 2 * (l % 32) + 64 * half + jnp.where(q % 2 == 0, half, 1 - half)
        return row == jnp.where(q >= 2, z, z + 128)

    keep = select_matrix((128, 128), kept)
    pass_on = select_matrix((256, 256), sent)
    z_copies = []
    for f in range(2):
        loads[f].wait()
        cells = staged[f].reshape(128, 128)
        halos = dot(side_by_side(cells[:64], cells[64:]), pass_on)
        z_send[f, 0] = halos[:, :128].reshape(4, 16, 128)
        z_send[f, 1] = halos[:, 128:].reshape(4, 16, 128)
        if f == 0:
            pl.semaphore_wait(barrier, len(partners))
        z_copies.append(
            [
                send(z_send.at[f, way], z_recv.at[f, way], z_sems, 2 * f + way, at_z((-1, 1)[way]))
                for way in range(2)
            ]
        )
        own[f] = dot(cells, keep).reshape(8, 16, 128)

    def send_x(f):
        return [
            send(
                win.at[f, 4:8, :, 0:16, :],
                win.at[f, 12:16, :, 0:16, :],
                x_sems,
                2 * f,
                at_x(-1),
            ),
            send(
                win.at[f, 8:12, :, 0:16, :],
                win.at[f, 0:4, :, 0:16, :],
                x_sems,
                2 * f + 1,
                at_x(1),
            ),
        ]

    def send_y(f):
        y_send[f, 0] = win[f, :, :, 0:4, :]
        y_send[f, 1] = win[f, :, :, 12:16, :]
        return [
            send(y_send.at[f, way], y_recv.at[f, way], y_sems, 2 * f + way, at_y((-1, 1)[way]))
            for way in range(2)
        ]

    def place_y(f, copies):
        for copy in copies:
            copy.wait_recv()
        win[f, :, :, 16:20, :] = y_recv[f, 0]
        win[f, :, :, 20:24, :] = y_recv[f, 1]

    x_copies = []
    for f in range(2):
        for copy in z_copies[f]:
            copy.wait_recv()
        lane = lane_of((4, 16, 128))
        for part in range(2):
            mine = own[f, 4 * part : 4 * part + 4]
            above, below = z_recv[f, 0], z_recv[f, 1]
            for t in range(2):
                turn_above = ((0, 96), (64, 32))[part][t]
                turn_below = ((0, 32), (64, 96))[part][t]
                halo = jnp.where(
                    lane < 96,
                    roll(above, turn_above, 2) if turn_above else above,
                    roll(below, turn_below, 2) if turn_below else below,
                )
                win[f, 4 + 4 * part : 8 + 4 * part, t, 0:16, :] = jnp.where(
                    lane < 64, roll(mine, 64, 2) if t else mine, halo
                )
        x_copies.append(send_x(f))
    y_copies = []
    for f in range(2):
        for copy in x_copies[f]:
            copy.wait_recv()
        y_copies.append(send_y(f))
    place_y(0, y_copies[0])

    cond, source, best = win.at[0], win.at[1], win.at[2]
    faces0 = (fx, fy, fz)
    for low, high in chunks(1, 16, 4):
        for t in range(2):
            k = cond[low - 1 : high, t]
            fx[low:high, t] = harmonic(k[1:], k[:-1])
    for low, high in chunks(1, 15, 4):
        k0, k1 = cond[low:high, 0], cond[low:high, 1]
        fy[low:high, 0] = harmonic(k0, roll(k0, 1, 1))
        fy[low:high, 1] = harmonic(k1, roll(k1, 1, 1))
        fz[low:high, 0] = harmonic(k0, roll(k1, 1, 2))
        fz[low:high, 1] = harmonic(k1, k0)

    for i in range(4):
        tmp0[0, i] = fx[4 + 2 * i, 0, 0:16, :] + fx[4 + 2 * i, 1, 0:16, :]
        tmp0[1, i] = (fy[4 + 2 * i, 0, 0:16, :] + fy[4 + 2 * i, 1, 0:16, :]) + (
            fy[5 + 2 * i, 0, 0:16, :] + fy[5 + 2 * i, 1, 0:16, :]
        )
        tmp0[2, i] = fz[4 + 2 * i, 0, 0:16, :] + fz[5 + 2 * i, 0, 0:16, :]
    first, second = pl.ds(0, 8, stride=2), pl.ds(1, 8, stride=2)
    f1[8:12, 0, 8:16, :] = 0.125 * (tmp0[0, :, first, :] + tmp0[0, :, second, :])
    f1[8:12, 1, 8:16, :] = 0.125 * tmp0[1, :, first, :]
    f1[8:12, 2, 8:16, :] = 0.125 * (tmp0[2, :, first, :] + tmp0[2, :, second, :])
    f1x_copies = [
        send(
            f1.at[8:12, :, 8:16, :],
            f1.at[8 - 4 * step : 12 - 4 * step, :, 8:16, :],
            f1x_sems,
            slot,
            at_x(step),
        )
        for slot, step in enumerate((-1, 1, -2, 2))
    ]

    def spread_x(ref, first, last, sems, steps):
        return [
            send(ref.at[1, first:last], ref.at[1, first - step : last - step], sems, slot, at_x(step))
            for slot, step in enumerate(steps)
        ]

    def gather_y(ref, sems):
        return [
            send(ref.at[1], ref.at[(1 - step) % count_y], sems, step - 1, at_y(step))
            for step in range(1, count_y)
        ]

    sibling = {"gy": me_y + 1 - 2 * lax.rem(me_y, 2)}
    shift = lax.rem(me_y, 2) * 2 + (count_y - 1)

    def hand_on(ref, sems, place):
        return send(
            ref.at[place],
            ref.at[lax.rem(place + shift, count_y)],
            sems,
            count_y + place,
            sibling,
        )

    def gather_y_shared(ref, sems):
        places = [(1 - step) % count_y for step in range(2, count_y, 2)]
        far = {
            place: send(ref.at[1], ref.at[place], sems, place, at_y(1 - place + count_y))
            for place in places
        }
        return far, [hand_on(ref, sems, 1)]

    def hand_on_all(ref, sems, far, handed):
        for place, copy in far.items():
            copy.wait_recv()
            handed.append(hand_on(ref, sems, place))

    for low, high in chunks(1, 15, 2):
        x_sum = [fx[low:high, t] + fx[low + 1 : high + 1, t] for t in range(2)]
        y_sum = [fy[low:high, t] + roll(fy[low:high, t], -1, 1) for t in range(2)]
        z0, z1 = fz[low:high, 0], fz[low:high, 1]
        inv[low:high, 0] = 1.0 / ((x_sum[0] + y_sum[0]) + (z0 + z1))
        inv[low:high, 1] = 1.0 / ((x_sum[1] + y_sum[1]) + (z1 + roll(z0, -1, 2)))

    place_y(1, y_copies[1])
    for i in range(1, 15):
        for t in range(2):
            xa[i, t] = inv[i, t] * source[i, t] * (1.0 / CENTER)

    def step_0(old, new, low, high, step, before, after=None, target=None):
        keep_old, keep_new = STEPS[step]

        def emit(i, applied, here):
            for t in range(2):
                r = source[i, t] - applied[t]
                d = keep_old * before[i, t] + keep_new * (inv[i, t] * r)
                if after is not None:
                    after[i, t] = d
                if target is None:
                    new[i, t] = here[t] + d
                else:
                    target(i, t, here[t] + d)

        sweep_0(old, faces0, low, high, emit)

    step_0(xa, xb, 2, 14, 0, xa, dd)

    for copy in f1x_copies:
        copy.wait_recv()
    f1y_copies = [
        send(
            f1.at[:, :, 8:16, :],
            f1.at[:, :, 8 - 8 * step : 16 - 8 * step, :],
            f1y_sems,
            slot,
            at_y(step),
        )
        for slot, step in enumerate((-1, 1))
    ]
    step_0(xb, xa, 3, 13, 1, dd)
    best[4:12, :, 0:16, :] = xa[4:12, :, 0:16, :]
    sums = []

    def residual_0(i, applied, here):
        r = [source[i, t, 0:16, :] - applied[t][:16] for t in range(2)]
        sums.append(r[0] + r[1])
        if i % 2 == 1:
            tmp0[0, (i - 4) // 2] = sums[-2] + sums[-1]

    sweep_0(xa, faces0, 4, 12, residual_0)
    b1[8:12, 8:16, :] = 0.125 * (tmp0[0, :, first, :] + tmp0[0, :, second, :])
    b1x_copies = [
        send(
            b1.at[8:12, 8:16, :],
            b1.at[8 - 4 * step : 12 - 4 * step, 8:16, :],
            b1x_sems,
            slot,
            at_x(step),
        )
        for slot, step in enumerate((-1, 1, -2, 2))
    ]

    def in_pack(row, column):
        return ((row % 128) // 2 + 16) % 64 + 64 * (row // 128) == column

    pack = select_matrix((256, 128), in_pack)
    pack_even = select_matrix((256, 128), lambda row, l: (row % 2 == 0) & in_pack(row, l))
    first4, second4 = pl.ds(0, 4, stride=2), pl.ds(1, 4, stride=2)

    def packed(pieces, matrix):
        whole = [jnp.concatenate(piece, axis=0) for piece in pieces]
        result = dot(side_by_side(*whole), matrix)
        return result.reshape(len(pieces[0]), 8, 128)

    g2f[1, 15] = jnp.ones((3, 4, 128), F32)
    g2b[1, 15] = jnp.zeros((4, 128), F32)
    mine = slice(8, 16)
    tmp1[0] = packed([[f1[4 * i + 2 * p, 0, mine, :] for i in range(5)] for p in range(2)], pack)
    for f in (1, 2):
        pieces = [
            [f1[4 * i + 2 * p, f, mine, :] + f1[4 * i + 2 * p + 1, f, mine, :] for i in range(5)]
            for p in range(2)
        ]
        tmp1[f] = packed(pieces, (None, pack, pack_even)[f])
    g2f[1, 5:10, 0] = 0.125 * (tmp1[0, :, first4, :] + tmp1[0, :, second4, :])
    g2f[1, 5:10, 1] = 0.125 * tmp1[1, :, first4, :]
    g2f[1, 5:10, 2] = 0.125 * (tmp1[2, :, first4, :] + tmp1[2, :, second4, :])
    gfx_copies = spread_x(g2f, 5, 10, gfx_sems, (5, -5))

    drain()
    for copy in b1x_copies:
        copy.wait_recv()
    b1y_copies = [
        send(
            b1.at[:, 8:16, :],
            b1.at[:, 8 - 8 * step : 16 - 8 * step, :],
            b1y_sems,
            slot,
            at_y(step),
        )
        for slot, step in enumerate((-1, 1))
    ]
    for copy in f1y_copies:
        copy.wait_recv()
    for low, high in chunks(1, 19, 6):
        x_sum = f1[low:high, 0] + f1[low + 1 : high + 1, 0]
        y_term, z_term = f1[low:high, 1], f1[low:high, 2]
        y_sum = y_term + roll(y_term, -1, 1)
        inv1[low:high] = 1.0 / ((x_sum + y_sum) + (z_term + roll(z_term, -1, 2)))

    for copy in b1y_copies:
        copy.wait_recv()

    for i in range(1, 19):
        x1a[i] = inv1[i] * b1[i] * (1.0 / CENTER)

    def step_1(old, new, low, high, step, before, after=None):
        keep_old, keep_new = STEPS[step]

        def emit(i, applied, here):
            r = b1[i] - applied
            d = keep_old * before[i] + keep_new * (inv1[i] * r)
            if after is not None:
                after[i] = d
            new[i] = here + d

        sweep_1(old, f1, low, high, emit)

    step_1(x1a, x1b, 2, 18, 0, x1a, d1)
    for copy in gfx_copies:
        copy.wait_recv()
    gfy_far, gfy_copies = gather_y_shared(g2f, gfy_sems)
    step_1(x1b, x1a, 3, 17, 1, d1)
    r = {}

    def residual_1(i, applied, here):
        r[i - 4] = (b1[i] - applied)[8:16]

    sweep_1(x1a, f1, 4, 16, residual_1)
    tmp1[0, 0:3] = packed(
        [[r[4 * i + 2 * p] + r[4 * i + 2 * p + 1] for i in range(3)] for p in range(2)], pack
    )
    g2b[1, 6:9] = 0.125 * (tmp1[0, 0:3, first4, :] + tmp1[0, 0:3, second4, :])
    gbx_copies = spread_x(g2b, 6, 9, gbx_sems, (3, -3, 6, -6))
    x_copies.append(send_x(2))
    for copy in gbx_copies:
        copy.wait_recv()
    gby_copies = gather_y(g2b, gby_sems)

    hand_on_all(g2f, gfy_sems, gfy_far, gfy_copies)
    for copy in gfy_copies:
        copy.wait_recv()
    for f in range(3):
        for s in range(count_y):
            f2[f, :, 4 * s : 4 * s + 4, :] = g2f[s, :, f]
    for low, high in chunks(0, 15, 3):
        terms = f2[0, low : high + 1]
        turned = roll(terms, 64, 2)
        half = lane_of(terms[1:].shape) < 64
        x_sum = terms[:-1] + jnp.where(half, turned[:-1], turned[1:])
        y_term, z_term = f2[1, low:high], f2[2, low:high]
        y_sum = y_term + roll(y_term, -1, 1)
        inv2[low:high] = 1.0 / ((x_sum + y_sum) + (z_term + roll(z_term, -1, 2)))

        x_low = f2[0, low:high]
        x_low = jnp.where(half, x_low, roll(x_low, 64, 2))
        tmp2[0, low:high] = x_low + roll(x_low, -1, 2)
        y_both = y_term + roll(y_term, 64, 2)
        tmp2[1, low:high] = y_both + roll(y_both, -1, 2)
        tmp2[2, low:high] = z_term + roll(z_term, 64, 2)
    first16, second16 = pl.ds(0, 16, stride=2), pl.ds(1, 16, stride=2)
    f3[0] = 0.125 * (tmp2[0, :, first16, :] + tmp2[0, :, second16, :])
    f3[1] = 0.125 * tmp2[1, :, first16, :]
    f3[2] = 0.125 * (tmp2[2, :, first16, :] + tmp2[2, :, second16, :])
    for low, high in chunks(2, 13, 6):
        terms = f3[0, low : high + 1]
        y_term, z_term = f3[1, low:high], f3[2, low:high]
        inv3[low:high] = 1.0 / (
            (terms[:-1] + terms[1:] + (y_term + roll(y_term, -1, 1)))
            + (z_term + roll(z_term, -2, 2))
        )

    for copy in x_copies[2]:
        copy.wait_recv()
    y_copies.append(send_y(2))
    for copy in gby_copies:
        copy.wait_recv()
    for s in range(count_y):
        b2[:, 4 * s : 4 * s + 4, :] = g2b[s]

    for i in range(15):
        x2a[i] = inv2[i] * b2[i] * (1.0 / CENTER)

    def step_2(old, new, low, high, step, before, after=None):
        keep_old, keep_new = STEPS[step]

        def emit(i, applied, here):
            r = b2[i] - applied
            d = keep_old * before[i] + keep_new * (inv2[i] * r)
            if after is not None:
                after[i] = d
            new[i] = here + d

        sweep_2(old, f2, low, high, emit)

    step_2(x2a, x2b, 1, 14, 0, x2a, d2)
    step_2(x2b, x2a, 1, 14, 1, d2)

    def residual_2(i, applied, here):
        r = b2[i] - applied
        r = r + roll(r, 64, 1)
        tmp2[0, i] = r + roll(r, -1, 1)

    sweep_2(x2a, f2, 2, 13, residual_2)
    b3[2:13] = 0.125 * (tmp2[0, 2:13, first16, :] + tmp2[0, 2:13, second16, :])

    for i in range(2, 13):
        x3a[i] = inv3[i] * b3[i] * (1.0 / CENTER)

    def step_3(old, new, low, high, step, before, after=None):
        keep_old, keep_new = STEPS[step]

        def emit(i, applied, here):
            r = b3[i] - applied
            d = keep_old * before[i] + keep_new * (inv3[i] * r)
            if after is not None:
                after[i] = d
            new[i] = here + d

        sweep_3(old, f3, low, high, emit)

    step_3(x3a, x3b, 3, 12, 0, x3a, d3)
    step_3(x3b, x3a, 4, 11, 1, d3)

    e = x3a[4:11]
    e = jnp.where(lane_of(e.shape) % 2 == 0, e, roll(e, 1, 2))
    dup2[4:11, first16, :] = e
    dup2[4:11, second16, :] = e
    for i in range(4, 11):
        x2b[i] = x2a[i] + dup2[i]
    x2b[3] = x2a[3]
    x2b[11] = x2a[11]

    def first_up_2(i, applied, here):
        d = inv2[i] * (b2[i] - applied) * (1.0 / CENTER)
        d2[i] = d
        x2a[i] = here + d

    sweep_2(x2b, f2, 4, 11, first_up_2)
    step_2(x2a, x2b, 5, 10, 0, d2, d2)
    x2b[4] = x2a[4]
    x2b[10] = x2a[10]
    step_2(x2b, x2a, 5, 10, 1, d2)

    def in_spread(row, column):
        return ((column % 128) // 2 + 16) % 64 + 64 * (column // 128) == row

    e = dot(x2a[5:10, 0:16, :].reshape(80, 128), select_matrix((128, 256), in_spread))
    for p in range(2):
        value = e[:, 128 * p : 128 * p + 128].reshape(5, 16, 128)
        dup21[p, :, first16, :] = value
        dup21[p, :, second16, :] = value
    for i in range(3, 17):
        x1b[i] = x1a[i] + dup21[(i // 2) % 2, i // 4, 0:24, :]

    def first_up_1(i, applied, here):
        d = inv1[i] * (b1[i] - applied) * (1.0 / CENTER)
        d1[i] = d
        x1a[i] = here + d

    sweep_1(x1b, f1, 4, 16, first_up_1)
    step_1(x1a, x1b, 5, 15, 0, d1, d1)
    step_1(x1b, x1a, 6, 14, 1, d1)

    drain()
    place_y(2, y_copies[2])
    e = x1a[6:14]
    dup1[:, pl.ds(0, 24, stride=2), :] = e
    dup1[:, pl.ds(1, 24, stride=2), :] = e
    lower = lax.broadcasted_iota(jnp.int32, (8, 128), 0) < 4
    for i in range(1, 15):
        j = i // 2
        brick = dup1[j, 16:32, :]
        edge = jnp.where(lower, dup1[j, 32:40, :], dup1[j, 8:16, :])
        for t in range(2):
            xb[i, t, 0:16, :] = best[i, t, 0:16, :] + brick
            xb[i, t, 16:24, :] = best[i, t, 16:24, :] + edge

    def first_up_0(i, applied, here):
        for t in range(2):
            d = inv[i, t] * (source[i, t] - applied[t]) * (1.0 / CENTER)
            dd[i, t] = d
            xa[i, t] = here[t] + d

    sweep_0(xb, faces0, 2, 14, first_up_0)
    step_0(xa, xb, 3, 13, 0, dd, dd)

    def to_own(i, t, value):
        own[t, i - 4] = value[0:16]

    step_0(xb, None, 4, 12, 1, dd, None, to_own)

    def joined(row, column):
        return (row % 128 < 64) & (column == 2 * (row % 128) + row // 128)

    cells = side_by_side(own[0].reshape(128, 128), own[1].reshape(128, 128))
    result = dot(cells, select_matrix((256, 128), joined))
    out_ref[...] = result.reshape(8, 16, 128)


def solution(mesh):
    sizes = (mesh.shape["gx"], mesh.shape["gy"], mesh.shape["gz"])
    count_x, count_y, _ = sizes
    vmem = lambda *shape: pltpu.VMEM(shape, F32)
    sems = lambda count: pltpu.SemaphoreType.DMA((2, count))
    fine = (16, 2, 24, 128)
    level1 = (20, 24, 128)
    level2 = (16, 32, 128)
    level3 = (16, 16, 128)
    scratch = [
        vmem(2, 8, 16, 128),
        vmem(2, 8, 16, 128),
        vmem(2, 2, 4, 16, 128),
        vmem(2, 2, 4, 16, 128),
        vmem(3, *fine),
        vmem(3, 2, 16, 2, 4, 128),
        vmem(3, 2, 16, 2, 4, 128),
        vmem(*fine),
        vmem(*fine),
        vmem(*fine),
        vmem(*fine),
        vmem(*fine),
        vmem(*fine),
        vmem(*fine),
        vmem(3, 4, 16, 128),
        vmem(20, 3, 24, 128),
        vmem(*level1),
        vmem(*level1),
        vmem(*level1),
        vmem(*level1),
        vmem(*level1),
        vmem(3, 5, 8, 128),
        vmem(8, 48, 128),
        vmem(count_y, count_x, 3, 4, 128),
        vmem(count_y, count_x, 4, 128),
        vmem(3, *level2),
        vmem(*level2),
        vmem(*level2),
        vmem(*level2),
        vmem(*level2),
        vmem(*level2),
        vmem(3, *level2),
        vmem(3, *level3),
        vmem(*level3),
        vmem(*level3),
        vmem(*level3),
        vmem(*level3),
        vmem(*level3),
        vmem(*level2),
        vmem(2, 5, 32, 128),
        pltpu.SemaphoreType.DMA((2,)),
        sems(4),
        sems(6),
        sems(6),
        sems(4),
        sems(2),
        sems(4),
        sems(2),
        sems(2),
        sems(2 * count_y),
        sems(4),
        sems(count_y - 1),
    ]

    def shards(pressure_source, conductivity):
        return pl.pallas_call(
            functools.partial(kernel, sizes),
            out_shape=jax.ShapeDtypeStruct((8, 16, 128), F32),
            in_specs=[pl.BlockSpec(memory_space=pltpu.HBM)] * 2,
            out_specs=pl.BlockSpec(memory_space=pltpu.VMEM),
            scratch_shapes=scratch,
            compiler_params=pltpu.CompilerParams(
                collective_id=0, has_side_effects=True, vmem_limit_bytes=62 * 1024 * 1024
            ),
        )(pressure_source, conductivity)

    placed = (P("gx", "gy", "gz"), P("gx", "gy", "gz"))
    return jax.shard_map(
        shards, mesh=mesh, in_specs=placed, out_specs=P("gx", "gy", "gz"), check_vma=False
    )
```

```python
import functools

import jax
import jax.numpy as jnp
from jax import lax
from jax.experimental import pallas as pl
from jax.experimental.pallas import tpu as pltpu
from jax.sharding import PartitionSpec as P

MESH = pl.DeviceIdType.MESH
F32 = jnp.float32

CENTER = 1.125
RADIUS = 0.875
RATIO = CENTER / RADIUS
RHO0 = 1.0 / RATIO
RHO1 = 1.0 / (2.0 * RATIO - RHO0)
RHO2 = 1.0 / (2.0 * RATIO - RHO1)
STEPS = ((RHO1 * RHO0, 2.0 * RHO1 / RADIUS), (RHO2 * RHO1, 2.0 * RHO2 / RADIUS))


def roll(value, shift, axis):
    return pltpu.roll(value, shift % value.shape[axis], axis)


def lane_of(shape):
    return lax.broadcasted_iota(jnp.int32, shape, len(shape) - 1)


def select_matrix(shape, holds):
    row = lax.broadcasted_iota(jnp.int32, shape, 0)
    column = lax.broadcasted_iota(jnp.int32, shape, 1)
    return jnp.where(holds(row, column), 1.0, 0.0).astype(jnp.bfloat16)


def dot(a, ones):
    high = a.astype(jnp.bfloat16)
    rest = a - high.astype(F32)
    middle = rest.astype(jnp.bfloat16)
    low = (rest - middle.astype(F32)).astype(jnp.bfloat16)
    parts = [jnp.dot(part, ones, preferred_element_type=F32) for part in (low, middle, high)]
    return (parts[0] + parts[1]) + parts[2]


def side_by_side(a, b):
    return jnp.concatenate([a, b], axis=1)


def harmonic(one_side, other_side):
    return 2.0 * one_side * other_side / (one_side + other_side)


def chunks(low, high, size):
    return [(start, min(start + size, high)) for start in range(low, high, size)]


def sweep_0(field, faces, low, high, emit):
    face_x, face_y, face_z = faces
    both = range(2)
    here = [field[low, t] for t in both]
    flux = [face_x[low, t] * (here[t] - field[low - 1, t]) for t in both]
    for i in range(low, high):
        after = [field[i + 1, t] for t in both]
        upper = [face_x[i + 1, t] * (after[t] - here[t]) for t in both]
        result = []
        for t in both:
            side = face_y[i, t] * (here[t] - roll(here[t], 1, 0))
            result.append((flux[t] - upper[t]) + (side - roll(side, -1, 0)))
        even = face_z[i, 0] * (here[0] - roll(here[1], 1, 1))
        odd = face_z[i, 1] * (here[1] - here[0])
        emit(i, [result[0] + (even - odd), result[1] + (odd - roll(even, -1, 1))], here)
        here, flux = after, upper


def sweep_1(field, faces, low, high, emit):
    here = field[low]
    flux = faces[low, 0] * (here - field[low - 1])
    for i in range(low, high):
        after = field[i + 1]
        upper = faces[i + 1, 0] * (after - here)
        side = faces[i, 1] * (here - roll(here, 1, 0))
        result = (flux - upper) + (side - roll(side, -1, 0))
        side = faces[i, 2] * (here - roll(here, 1, 1))
        emit(i, result + (side - roll(side, -1, 1)), here)
        here, flux = after, upper


def sweep_2(field, faces, low, high, emit):
    half = lane_of(field.shape[1:]) < 64
    before, here = roll(field[low - 1], 64, 1), field[low]
    turned = roll(here, 64, 1)
    flux = faces[0, low] * (here - jnp.where(half, before, turned))
    flux_turned = roll(flux, 64, 1)
    for i in range(low, high):
        after = field[i + 1]
        after_turned = roll(after, 64, 1)
        upper = faces[0, i + 1] * (after - jnp.where(half, turned, after_turned))
        upper_turned = roll(upper, 64, 1)
        result = flux - jnp.where(half, flux_turned, upper_turned)
        side = faces[1, i] * (here - roll(here, 1, 0))
        result = result + (side - roll(side, -1, 0))
        side = faces[2, i] * (here - roll(here, 1, 1))
        emit(i, result + (side - roll(side, -1, 1)), here)
        here, turned, flux, flux_turned = after, after_turned, upper, upper_turned


def sweep_3(field, faces, low, high, emit):
    here = field[low]
    flux = faces[0, low] * (here - field[low - 1])
    for i in range(low, high):
        after = field[i + 1]
        upper = faces[0, i + 1] * (after - here)
        side = faces[1, i] * (here - roll(here, 1, 0))
        result = (flux - upper) + (side - roll(side, -1, 0))
        side = faces[2, i] * (here - roll(here, 2, 1))
        emit(i, result + (side - roll(side, -2, 1)), here)
        here, flux = after, upper


def kernel(
    sizes,
    source_hbm,
    cond_hbm,
    out_ref,
    staged,
    own,
    z_send,
    z_recv,
    win,
    y_send,
    y_recv,
    fx,
    fy,
    fz,
    inv,
    xa,
    xb,
    dd,
    tmp0,
    f1,
    b1,
    inv1,
    x1a,
    x1b,
    d1,
    tmp1,
    dup1,
    g2f,
    g2b,
    f2,
    b2,
    inv2,
    x2a,
    x2b,
    d2,
    tmp2,
    f3,
    b3,
    inv3,
    x3a,
    x3b,
    d3,
    dup2,
    dup21,
    in_sem,
    z_sems,
    x_sems,
    y_sems,
    xy_sems,
    f1x_sems,
    f1y_sems,
    b1x_sems,
    b1y_sems,
    gfx_sems,
    gfy_sems,
    gbx_sems,
    gby_sems,
):
    count_x, count_y, count_z = sizes
    me_x, me_y, me_z = lax.axis_index("gx"), lax.axis_index("gy"), lax.axis_index("gz")

    def at_x(step):
        return {"gx": lax.rem(me_x + (step + count_x), count_x)}

    def at_y(step):
        return {"gy": lax.rem(me_y + (step + count_y), count_y)}

    def at_z(step):
        return {"gz": lax.rem(me_z + (step + count_z), count_z)}

    loads = [
        pltpu.make_async_copy(cond_hbm, staged.at[0], in_sem.at[0]),
        pltpu.make_async_copy(source_hbm, staged.at[1], in_sem.at[1]),
    ]
    for load in loads:
        load.start()

    barrier = pltpu.get_barrier_semaphore()
    partners = [at_z(1), at_z(-1)]
    partners += [at_x(sign * step) for step in (1, 2, 3, 5, 6) for sign in (1, -1)]
    partners += [at_y(step) for step in range(1, count_y)]
    partners += [at_x(dx) | at_y(dy) for dx in (-1, 1) for dy in (-1, 1)]
    for partner in partners:
        pl.semaphore_signal(barrier, inc=1, device_id=partner, device_id_type=MESH)

    pending = []

    def drain():
        for copy in pending:
            copy.wait_send()
        pending.clear()

    def send(source, target, sems, slot, device):
        copy = pltpu.make_async_remote_copy(
            src_ref=source,
            dst_ref=target,
            send_sem=sems.at[0, slot],
            recv_sem=sems.at[1, slot],
            device_id=device,
            device_id_type=MESH,
        )
        copy.start()
        pending.append(copy)
        return copy

    def kept(row, l):
        return row == jnp.where(l < 64, 2 * l, 2 * (l - 64) + 1)

    def sent(row, l):
        half, q = l // 128, (l % 128) // 32
        z = 2 * (l % 32) + 64 * half + jnp.where(q % 2 == 0, half, 1 - half)
        return row == jnp.where(q >= 2, z, z + 128)

    keep = select_matrix((128, 128), kept)
    pass_on = select_matrix((256, 256), sent)
    z_copies = []
    for f in range(2):
        loads[f].wait()
        cells = staged[f].reshape(128, 128)
        halos = dot(side_by_side(cells[:64], cells[64:]), pass_on)
        z_send[f, 0] = halos[:, :128].reshape(4, 16, 128)
        z_send[f, 1] = halos[:, 128:].reshape(4, 16, 128)
        if f == 0:
            pl.semaphore_wait(barrier, len(partners))
        z_copies.append(
            [
                send(z_send.at[f, way], z_recv.at[f, way], z_sems, 2 * f + way, at_z((-1, 1)[way]))
                for way in range(2)
            ]
        )
        own[f] = dot(cells, keep).reshape(8, 16, 128)

    def send_x(f):
        return [
            send(
                win.at[f, 4:8, :, 0:16, :],
                win.at[f, 12:16, :, 0:16, :],
                x_sems,
                2 * f,
                at_x(-1),
            ),
            send(
                win.at[f, 8:12, :, 0:16, :],
                win.at[f, 0:4, :, 0:16, :],
                x_sems,
                2 * f + 1,
                at_x(1),
            ),
        ]

    def send_y(f):
        y_send[f, 0] = win[f, :, :, 0:4, :]
        y_send[f, 1] = win[f, :, :, 12:16, :]
        return [
            send(y_send.at[f, way], y_recv.at[f, way], y_sems, 2 * f + way, at_y((-1, 1)[way]))
            for way in range(2)
        ]

    def send_xy(f):
        copies = send_x(f)
        y_send[f, 0, 4:12] = win[f, 4:12, :, 0:4, :]
        y_send[f, 1, 4:12] = win[f, 4:12, :, 12:16, :]
        for way in range(2):
            for slot, (dx, first, last) in enumerate(((0, 4, 12), (1, 8, 12), (-1, 4, 8))):
                copies.append(
                    send(
                        y_send.at[f, way, first:last],
                        y_recv.at[f, way, first - 8 * dx : last - 8 * dx],
                        xy_sems,
                        6 * f + 3 * way + slot,
                        at_y((-1, 1)[way]) | (at_x(dx) if dx else {}),
                    )
                )
        return copies

    def place_y(f, copies):
        for copy in copies:
            copy.wait_recv()
        win[f, :, :, 16:20, :] = y_recv[f, 0]
        win[f, :, :, 20:24, :] = y_recv[f, 1]

    xy_copies = []
    for f in range(2):
        for copy in z_copies[f]:
            copy.wait_recv()
        lane = lane_of((4, 16, 128))
        for part in range(2):
            mine = own[f, 4 * part : 4 * part + 4]
            above, below = z_recv[f, 0], z_recv[f, 1]
            for t in range(2):
                turn_above = ((0, 96), (64, 32))[part][t]
                turn_below = ((0, 32), (64, 96))[part][t]
                halo = jnp.where(
                    lane < 96,
                    roll(above, turn_above, 2) if turn_above else above,
                    roll(below, turn_below, 2) if turn_below else below,
                )
                win[f, 4 + 4 * part : 8 + 4 * part, t, 0:16, :] = jnp.where(
                    lane < 64, roll(mine, 64, 2) if t else mine, halo
                )
        xy_copies.append(send_xy(f))

    cond, source, best = win.at[0], win.at[1], win.at[2]
    faces0 = (fx, fy, fz)
    brick = slice(0, 16)
    for i in range(4, 12):
        k0, k1 = cond[i, 0, brick, :], cond[i, 1, brick, :]
        fz[i, 0, brick, :] = harmonic(k0, roll(k1, 1, 1))
        fz[i, 1, brick, :] = harmonic(k1, k0)
        if i > 4:
            fx[i, 0, brick, :] = harmonic(k0, cond[i - 1, 0, brick, :])
            fx[i, 1, brick, :] = harmonic(k1, cond[i - 1, 1, brick, :])
    place_y(0, xy_copies[0])
    for i in range(1, 16):
        rest = slice(16, 24) if 4 < i < 12 else slice(0, 24)
        for t in range(2):
            fx[i, t, rest, :] = harmonic(cond[i, t, rest, :], cond[i - 1, t, rest, :])
    for i in range(1, 15):
        k0, k1 = cond[i, 0], cond[i, 1]
        fy[i, 0] = harmonic(k0, roll(k0, 1, 0))
        fy[i, 1] = harmonic(k1, roll(k1, 1, 0))
        rest = slice(16, 24) if 4 <= i < 12 else slice(0, 24)
        k0, k1 = k0[rest], k1[rest]
        fz[i, 0, rest, :] = harmonic(k0, roll(k1, 1, 1))
        fz[i, 1, rest, :] = harmonic(k1, k0)

    for i in range(4):
        tmp0[0, i] = fx[4 + 2 * i, 0, 0:16, :] + fx[4 + 2 * i, 1, 0:16, :]
        tmp0[1, i] = (fy[4 + 2 * i, 0, 0:16, :] + fy[4 + 2 * i, 1, 0:16, :]) + (
            fy[5 + 2 * i, 0, 0:16, :] + fy[5 + 2 * i, 1, 0:16, :]
        )
        tmp0[2, i] = fz[4 + 2 * i, 0, 0:16, :] + fz[5 + 2 * i, 0, 0:16, :]
    first, second = pl.ds(0, 8, stride=2), pl.ds(1, 8, stride=2)
    f1[8:12, 0, 8:16, :] = 0.125 * (tmp0[0, :, first, :] + tmp0[0, :, second, :])
    f1[8:12, 1, 8:16, :] = 0.125 * tmp0[1, :, first, :]
    f1[8:12, 2, 8:16, :] = 0.125 * (tmp0[2, :, first, :] + tmp0[2, :, second, :])
    f1x_copies = [
        send(
            f1.at[8:12, :, 8:16, :],
            f1.at[8 - 4 * step : 12 - 4 * step, :, 8:16, :],
            f1x_sems,
            slot,
            at_x(step),
        )
        for slot, step in enumerate((-1, 1, -2, 2))
    ]

    def spread_x(ref, first, last, sems, steps):
        return [
            send(ref.at[1, first:last], ref.at[1, first - step : last - step], sems, slot, at_x(step))
            for slot, step in enumerate(steps)
        ]

    def gather_y(ref, sems):
        return [
            send(ref.at[1], ref.at[(1 - step) % count_y], sems, step - 1, at_y(step))
            for step in range(1, count_y)
        ]

    sibling = {"gy": me_y + 1 - 2 * lax.rem(me_y, 2)}
    shift = lax.rem(me_y, 2) * 2 + (count_y - 1)

    def hand_on(ref, sems, place):
        return send(
            ref.at[place],
            ref.at[lax.rem(place + shift, count_y)],
            sems,
            count_y + place,
            sibling,
        )

    def gather_y_shared(ref, sems):
        places = [(1 - step) % count_y for step in range(2, count_y, 2)]
        far = {
            place: send(ref.at[1], ref.at[place], sems, place, at_y(1 - place + count_y))
            for place in places
        }
        return far, [hand_on(ref, sems, 1)]

    def hand_on_all(ref, sems, far, handed):
        for place, copy in far.items():
            copy.wait_recv()
            handed.append(hand_on(ref, sems, place))

    for low, high in chunks(1, 15, 2):
        x_sum = [fx[low:high, t] + fx[low + 1 : high + 1, t] for t in range(2)]
        y_sum = [fy[low:high, t] + roll(fy[low:high, t], -1, 1) for t in range(2)]
        z0, z1 = fz[low:high, 0], fz[low:high, 1]
        inv[low:high, 0] = 1.0 / ((x_sum[0] + y_sum[0]) + (z0 + z1))
        inv[low:high, 1] = 1.0 / ((x_sum[1] + y_sum[1]) + (z1 + roll(z0, -1, 2)))

    place_y(1, xy_copies[1])
    for i in range(1, 15):
        for t in range(2):
            xa[i, t] = inv[i, t] * source[i, t] * (1.0 / CENTER)

    def step_0(old, new, low, high, step, before, after=None, target=None):
        keep_old, keep_new = STEPS[step]

        def emit(i, applied, here):
            for t in range(2):
                r = source[i, t] - applied[t]
                d = keep_old * before[i, t] + keep_new * (inv[i, t] * r)
                if after is not None:
                    after[i, t] = d
                if target is None:
                    new[i, t] = here[t] + d
                else:
                    target(i, t, here[t] + d)

        sweep_0(old, faces0, low, high, emit)

    step_0(xa, xb, 2, 14, 0, xa, dd)

    for copy in f1x_copies:
        copy.wait_recv()
    f1y_copies = [
        send(
            f1.at[:, :, 8:16, :],
            f1.at[:, :, 8 - 8 * step : 16 - 8 * step, :],
            f1y_sems,
            slot,
            at_y(step),
        )
        for slot, step in enumerate((-1, 1))
    ]
    step_0(xb, xa, 3, 13, 1, dd)
    best[4:12, :, 0:16, :] = xa[4:12, :, 0:16, :]
    sums = []

    def residual_0(i, applied, here):
        r = [source[i, t, 0:16, :] - applied[t][:16] for t in range(2)]
        sums.append(r[0] + r[1])
        if i % 2 == 1:
            tmp0[0, (i - 4) // 2] = sums[-2] + sums[-1]

    sweep_0(xa, faces0, 4, 12, residual_0)
    b1[8:12, 8:16, :] = 0.125 * (tmp0[0, :, first, :] + tmp0[0, :, second, :])
    b1x_copies = [
        send(
            b1.at[first:last, 8:16, :],
            b1.at[first - 4 * step : last - 4 * step, 8:16, :],
            b1x_sems,
            slot,
            at_x(step),
        )
        for slot, (step, first, last) in enumerate(
            ((-1, 8, 12), (1, 8, 12), (-2, 8, 11), (2, 9, 12))
        )
    ]

    def in_pack(row, column):
        return ((row % 128) // 2 + 16) % 64 + 64 * (row // 128) == column

    pack = select_matrix((256, 128), in_pack)
    pack_even = select_matrix((256, 128), lambda row, l: (row % 2 == 0) & in_pack(row, l))
    first4, second4 = pl.ds(0, 4, stride=2), pl.ds(1, 4, stride=2)

    def packed(pieces, matrix):
        whole = [jnp.concatenate(piece, axis=0) for piece in pieces]
        result = dot(side_by_side(*whole), matrix)
        return result.reshape(len(pieces[0]), 8, 128)

    g2f[1, 15] = jnp.ones((3, 4, 128), F32)
    g2b[1, 15] = jnp.zeros((4, 128), F32)
    mine = slice(8, 16)
    tmp1[0] = packed([[f1[4 * i + 2 * p, 0, mine, :] for i in range(5)] for p in range(2)], pack)
    for f in (1, 2):
        pieces = [
            [f1[4 * i + 2 * p, f, mine, :] + f1[4 * i + 2 * p + 1, f, mine, :] for i in range(5)]
            for p in range(2)
        ]
        tmp1[f] = packed(pieces, (None, pack, pack_even)[f])
    g2f[1, 5:10, 0] = 0.125 * (tmp1[0, :, first4, :] + tmp1[0, :, second4, :])
    g2f[1, 5:10, 1] = 0.125 * tmp1[1, :, first4, :]
    g2f[1, 5:10, 2] = 0.125 * (tmp1[2, :, first4, :] + tmp1[2, :, second4, :])
    gfx_copies = spread_x(g2f, 5, 10, gfx_sems, (5, -5))

    drain()
    for copy in b1x_copies:
        copy.wait_recv()
    b1y_copies = [
        send(
            b1.at[:, 8:16, :],
            b1.at[:, 8 - 8 * step : 16 - 8 * step, :],
            b1y_sems,
            slot,
            at_y(step),
        )
        for slot, step in enumerate((-1, 1))
    ]
    for copy in f1y_copies:
        copy.wait_recv()
    for low, high in chunks(1, 19, 6):
        x_sum = f1[low:high, 0] + f1[low + 1 : high + 1, 0]
        y_term, z_term = f1[low:high, 1], f1[low:high, 2]
        y_sum = y_term + roll(y_term, -1, 1)
        inv1[low:high] = 1.0 / ((x_sum + y_sum) + (z_term + roll(z_term, -1, 2)))

    for copy in b1y_copies:
        copy.wait_recv()

    for i in range(1, 19):
        x1a[i] = inv1[i] * b1[i] * (1.0 / CENTER)

    def step_1(old, new, low, high, step, before, after=None):
        keep_old, keep_new = STEPS[step]

        def emit(i, applied, here):
            r = b1[i] - applied
            d = keep_old * before[i] + keep_new * (inv1[i] * r)
            if after is not None:
                after[i] = d
            new[i] = here + d

        sweep_1(old, f1, low, high, emit)

    step_1(x1a, x1b, 2, 18, 0, x1a, d1)
    for copy in gfx_copies:
        copy.wait_recv()
    gfy_far, gfy_copies = gather_y_shared(g2f, gfy_sems)
    step_1(x1b, x1a, 3, 17, 1, d1)
    r = {}

    def residual_1(i, applied, here):
        r[i - 4] = (b1[i] - applied)[8:16]

    sweep_1(x1a, f1, 4, 16, residual_1)
    tmp1[0, 0:3] = packed(
        [[r[4 * i + 2 * p] + r[4 * i + 2 * p + 1] for i in range(3)] for p in range(2)], pack
    )
    g2b[1, 6:9] = 0.125 * (tmp1[0, 0:3, first4, :] + tmp1[0, 0:3, second4, :])
    gbx_copies = spread_x(g2b, 6, 9, gbx_sems, (3, -3, 6, -6))
    x0_copies = send_x(2)
    for copy in gbx_copies:
        copy.wait_recv()
    gby_copies = gather_y(g2b, gby_sems)

    hand_on_all(g2f, gfy_sems, gfy_far, gfy_copies)
    for copy in gfy_copies:
        copy.wait_recv()
    for f in range(3):
        for s in range(count_y):
            f2[f, :, 4 * s : 4 * s + 4, :] = g2f[s, :, f]
    for low, high in chunks(0, 15, 3):
        terms = f2[0, low : high + 1]
        turned = roll(terms, 64, 2)
        half = lane_of(terms[1:].shape) < 64
        x_sum = terms[:-1] + jnp.where(half, turned[:-1], turned[1:])
        y_term, z_term = f2[1, low:high], f2[2, low:high]
        y_sum = y_term + roll(y_term, -1, 1)
        inv2[low:high] = 1.0 / ((x_sum + y_sum) + (z_term + roll(z_term, -1, 2)))

        x_low = f2[0, low:high]
        x_low = jnp.where(half, x_low, roll(x_low, 64, 2))
        tmp2[0, low:high] = x_low + roll(x_low, -1, 2)
        y_both = y_term + roll(y_term, 64, 2)
        tmp2[1, low:high] = y_both + roll(y_both, -1, 2)
        tmp2[2, low:high] = z_term + roll(z_term, 64, 2)
    first16, second16 = pl.ds(0, 16, stride=2), pl.ds(1, 16, stride=2)
    f3[0] = 0.125 * (tmp2[0, :, first16, :] + tmp2[0, :, second16, :])
    f3[1] = 0.125 * tmp2[1, :, first16, :]
    f3[2] = 0.125 * (tmp2[2, :, first16, :] + tmp2[2, :, second16, :])
    for low, high in chunks(2, 13, 6):
        terms = f3[0, low : high + 1]
        y_term, z_term = f3[1, low:high], f3[2, low:high]
        inv3[low:high] = 1.0 / (
            (terms[:-1] + terms[1:] + (y_term + roll(y_term, -1, 1)))
            + (z_term + roll(z_term, -2, 2))
        )

    for copy in x0_copies:
        copy.wait_recv()
    y0_copies = send_y(2)
    for copy in gby_copies:
        copy.wait_recv()
    for s in range(count_y):
        b2[:, 4 * s : 4 * s + 4, :] = g2b[s]

    for i in range(15):
        x2a[i] = inv2[i] * b2[i] * (1.0 / CENTER)

    def step_2(old, new, low, high, step, before, after=None):
        keep_old, keep_new = STEPS[step]

        def emit(i, applied, here):
            r = b2[i] - applied
            d = keep_old * before[i] + keep_new * (inv2[i] * r)
            if after is not None:
                after[i] = d
            new[i] = here + d

        sweep_2(old, f2, low, high, emit)

    step_2(x2a, x2b, 1, 14, 0, x2a, d2)
    step_2(x2b, x2a, 1, 14, 1, d2)

    def residual_2(i, applied, here):
        r = b2[i] - applied
        r = r + roll(r, 64, 1)
        tmp2[0, i] = r + roll(r, -1, 1)

    sweep_2(x2a, f2, 2, 13, residual_2)
    b3[2:13] = 0.125 * (tmp2[0, 2:13, first16, :] + tmp2[0, 2:13, second16, :])

    for i in range(2, 13):
        x3a[i] = inv3[i] * b3[i] * (1.0 / CENTER)

    def step_3(old, new, low, high, step, before, after=None):
        keep_old, keep_new = STEPS[step]

        def emit(i, applied, here):
            r = b3[i] - applied
            d = keep_old * before[i] + keep_new * (inv3[i] * r)
            if after is not None:
                after[i] = d
            new[i] = here + d

        sweep_3(old, f3, low, high, emit)

    step_3(x3a, x3b, 3, 12, 0, x3a, d3)
    step_3(x3b, x3a, 4, 11, 1, d3)

    e = x3a[4:11]
    e = jnp.where(lane_of(e.shape) % 2 == 0, e, roll(e, 1, 2))
    dup2[4:11, first16, :] = e
    dup2[4:11, second16, :] = e
    for i in range(4, 11):
        x2b[i] = x2a[i] + dup2[i]
    x2b[3] = x2a[3]
    x2b[11] = x2a[11]

    def first_up_2(i, applied, here):
        d = inv2[i] * (b2[i] - applied) * (1.0 / CENTER)
        d2[i] = d
        x2a[i] = here + d

    sweep_2(x2b, f2, 4, 11, first_up_2)
    step_2(x2a, x2b, 5, 10, 0, d2, d2)
    x2b[4] = x2a[4]
    x2b[10] = x2a[10]
    step_2(x2b, x2a, 5, 10, 1, d2)

    def in_spread(row, column):
        return ((column % 128) // 2 + 16) % 64 + 64 * (column // 128) == row

    e = dot(x2a[5:10, 0:16, :].reshape(80, 128), select_matrix((128, 256), in_spread))
    for p in range(2):
        value = e[:, 128 * p : 128 * p + 128].reshape(5, 16, 128)
        dup21[p, :, first16, :] = value
        dup21[p, :, second16, :] = value
    for i in range(3, 17):
        x1b[i] = x1a[i] + dup21[(i // 2) % 2, i // 4, 0:24, :]

    def first_up_1(i, applied, here):
        d = inv1[i] * (b1[i] - applied) * (1.0 / CENTER)
        d1[i] = d
        x1a[i] = here + d

    sweep_1(x1b, f1, 4, 16, first_up_1)
    step_1(x1a, x1b, 5, 15, 0, d1, d1)
    step_1(x1b, x1a, 6, 14, 1, d1)

    drain()
    place_y(2, y0_copies)
    e = x1a[6:14]
    dup1[:, pl.ds(0, 24, stride=2), :] = e
    dup1[:, pl.ds(1, 24, stride=2), :] = e
    lower = lax.broadcasted_iota(jnp.int32, (8, 128), 0) < 4
    for i in range(1, 15):
        j = i // 2
        brick = dup1[j, 16:32, :]
        edge = jnp.where(lower, dup1[j, 32:40, :], dup1[j, 8:16, :])
        for t in range(2):
            xb[i, t, 0:16, :] = best[i, t, 0:16, :] + brick
            xb[i, t, 16:24, :] = best[i, t, 16:24, :] + edge

    def first_up_0(i, applied, here):
        for t in range(2):
            d = inv[i, t] * (source[i, t] - applied[t]) * (1.0 / CENTER)
            dd[i, t] = d
            xa[i, t] = here[t] + d

    sweep_0(xb, faces0, 2, 14, first_up_0)
    step_0(xa, xb, 3, 13, 0, dd, dd)

    def to_own(i, t, value):
        own[t, i - 4] = value[0:16]

    step_0(xb, None, 4, 12, 1, dd, None, to_own)

    def joined(row, column):
        return (row % 128 < 64) & (column == 2 * (row % 128) + row // 128)

    cells = side_by_side(own[0].reshape(128, 128), own[1].reshape(128, 128))
    result = dot(cells, select_matrix((256, 128), joined))
    out_ref[...] = result.reshape(8, 16, 128)


def solution(mesh):
    sizes = (mesh.shape["gx"], mesh.shape["gy"], mesh.shape["gz"])
    count_x, count_y, _ = sizes
    vmem = lambda *shape: pltpu.VMEM(shape, F32)
    sems = lambda count: pltpu.SemaphoreType.DMA((2, count))
    fine = (16, 2, 24, 128)
    level1 = (20, 24, 128)
    level2 = (16, 32, 128)
    level3 = (16, 16, 128)
    scratch = [
        vmem(2, 8, 16, 128),
        vmem(2, 8, 16, 128),
        vmem(2, 2, 4, 16, 128),
        vmem(2, 2, 4, 16, 128),
        vmem(3, *fine),
        vmem(3, 2, 16, 2, 4, 128),
        vmem(3, 2, 16, 2, 4, 128),
        vmem(*fine),
        vmem(*fine),
        vmem(*fine),
        vmem(*fine),
        vmem(*fine),
        vmem(*fine),
        vmem(*fine),
        vmem(3, 4, 16, 128),
        vmem(20, 3, 24, 128),
        vmem(*level1),
        vmem(*level1),
        vmem(*level1),
        vmem(*level1),
        vmem(*level1),
        vmem(3, 5, 8, 128),
        vmem(8, 48, 128),
        vmem(count_y, count_x, 3, 4, 128),
        vmem(count_y, count_x, 4, 128),
        vmem(3, *level2),
        vmem(*level2),
        vmem(*level2),
        vmem(*level2),
        vmem(*level2),
        vmem(*level2),
        vmem(3, *level2),
        vmem(3, *level3),
        vmem(*level3),
        vmem(*level3),
        vmem(*level3),
        vmem(*level3),
        vmem(*level3),
        vmem(*level2),
        vmem(2, 5, 32, 128),
        pltpu.SemaphoreType.DMA((2,)),
        sems(4),
        sems(6),
        sems(6),
        sems(12),
        sems(4),
        sems(2),
        sems(4),
        sems(2),
        sems(2),
        sems(2 * count_y),
        sems(4),
        sems(count_y - 1),
    ]

    def shards(pressure_source, conductivity):
        return pl.pallas_call(
            functools.partial(kernel, sizes),
            out_shape=jax.ShapeDtypeStruct((8, 16, 128), F32),
            in_specs=[pl.BlockSpec(memory_space=pltpu.HBM)] * 2,
            out_specs=pl.BlockSpec(memory_space=pltpu.VMEM),
            scratch_shapes=scratch,
            compiler_params=pltpu.CompilerParams(
                collective_id=0, has_side_effects=True, vmem_limit_bytes=55136 * 1024
            ),
        )(pressure_source, conductivity)

    placed = (P("gx", "gy", "gz"), P("gx", "gy", "gz"))
    return jax.shard_map(
        shards, mesh=mesh, in_specs=placed, out_specs=P("gx", "gy", "gz"), check_vma=False
    )
```

```python
import functools

import jax
import jax.numpy as jnp
from jax import lax
from jax.experimental import pallas as pl
from jax.experimental.pallas import tpu as pltpu
from jax.sharding import PartitionSpec as P

MESH = pl.DeviceIdType.MESH
F32 = jnp.float32

CENTER = 1.125
RADIUS = 0.875
RATIO = CENTER / RADIUS
RHO0 = 1.0 / RATIO
RHO1 = 1.0 / (2.0 * RATIO - RHO0)
RHO2 = 1.0 / (2.0 * RATIO - RHO1)
STEPS = ((RHO1 * RHO0, 2.0 * RHO1 / RADIUS), (RHO2 * RHO1, 2.0 * RHO2 / RADIUS))


def roll(value, shift, axis):
    return pltpu.roll(value, shift % value.shape[axis], axis)


def lane_of(shape):
    return lax.broadcasted_iota(jnp.int32, shape, len(shape) - 1)


def select_matrix(shape, holds):
    row = lax.broadcasted_iota(jnp.int32, shape, 0)
    column = lax.broadcasted_iota(jnp.int32, shape, 1)
    return jnp.where(holds(row, column), 1.0, 0.0).astype(jnp.bfloat16)


def dot(a, ones):
    high = a.astype(jnp.bfloat16)
    rest = a - high.astype(F32)
    middle = rest.astype(jnp.bfloat16)
    low = (rest - middle.astype(F32)).astype(jnp.bfloat16)
    parts = [jnp.dot(part, ones, preferred_element_type=F32) for part in (low, middle, high)]
    return (parts[0] + parts[1]) + parts[2]


def side_by_side(a, b):
    return jnp.concatenate([a, b], axis=1)


def harmonic(one_side, other_side):
    return 2.0 * one_side * other_side / (one_side + other_side)


def chunks(low, high, size):
    return [(start, min(start + size, high)) for start in range(low, high, size)]


def sweep_0(field, faces, low, high, emit):
    face_x, face_y, face_z = faces
    both = range(2)
    here = [field[low, t] for t in both]
    flux = [face_x[low, t] * (here[t] - field[low - 1, t]) for t in both]
    for i in range(low, high):
        after = [field[i + 1, t] for t in both]
        upper = [face_x[i + 1, t] * (after[t] - here[t]) for t in both]
        result = []
        for t in both:
            side = face_y[i, t] * (here[t] - roll(here[t], 1, 0))
            result.append((flux[t] - upper[t]) + (side - roll(side, -1, 0)))
        even = face_z[i, 0] * (here[0] - roll(here[1], 1, 1))
        odd = face_z[i, 1] * (here[1] - here[0])
        emit(i, [result[0] + (even - odd), result[1] + (odd - roll(even, -1, 1))], here)
        here, flux = after, upper


def sweep_1(field, faces, low, high, emit):
    here = field[low]
    flux = faces[low, 0] * (here - field[low - 1])
    for i in range(low, high):
        after = field[i + 1]
        upper = faces[i + 1, 0] * (after - here)
        side = faces[i, 1] * (here - roll(here, 1, 0))
        result = (flux - upper) + (side - roll(side, -1, 0))
        side = faces[i, 2] * (here - roll(here, 1, 1))
        emit(i, result + (side - roll(side, -1, 1)), here)
        here, flux = after, upper


def sweep_2(field, faces, low, high, emit):
    half = lane_of(field.shape[1:]) < 64
    before, here = roll(field[low - 1], 64, 1), field[low]
    turned = roll(here, 64, 1)
    flux = faces[0, low] * (here - jnp.where(half, before, turned))
    flux_turned = roll(flux, 64, 1)
    for i in range(low, high):
        after = field[i + 1]
        after_turned = roll(after, 64, 1)
        upper = faces[0, i + 1] * (after - jnp.where(half, turned, after_turned))
        upper_turned = roll(upper, 64, 1)
        result = flux - jnp.where(half, flux_turned, upper_turned)
        side = faces[1, i] * (here - roll(here, 1, 0))
        result = result + (side - roll(side, -1, 0))
        side = faces[2, i] * (here - roll(here, 1, 1))
        emit(i, result + (side - roll(side, -1, 1)), here)
        here, turned, flux, flux_turned = after, after_turned, upper, upper_turned


def sweep_3(field, faces, low, high, emit):
    here = field[low]
    flux = faces[0, low] * (here - field[low - 1])
    for i in range(low, high):
        after = field[i + 1]
        upper = faces[0, i + 1] * (after - here)
        side = faces[1, i] * (here - roll(here, 1, 0))
        result = (flux - upper) + (side - roll(side, -1, 0))
        side = faces[2, i] * (here - roll(here, 2, 1))
        emit(i, result + (side - roll(side, -2, 1)), here)
        here, flux = after, upper


def kernel(
    sizes,
    source_hbm,
    cond_hbm,
    out_ref,
    staged,
    own,
    z_send,
    z_recv,
    win,
    y_send,
    y_recv,
    fx,
    fy,
    fz,
    inv,
    xa,
    xb,
    dd,
    tmp0,
    f1,
    b1,
    inv1,
    x1a,
    x1b,
    d1,
    tmp1,
    dup1,
    g2f,
    g2b,
    f2,
    b2,
    inv2,
    x2a,
    x2b,
    d2,
    tmp2,
    f3,
    b3,
    inv3,
    x3a,
    x3b,
    d3,
    dup2,
    dup21,
    in_sem,
    z_sems,
    x_sems,
    y_sems,
    xy_sems,
    f1x_sems,
    f1y_sems,
    b1x_sems,
    b1y_sems,
    gfx_sems,
    gfy_sems,
    gbx_sems,
    gby_sems,
):
    count_x, count_y, count_z = sizes
    me_x, me_y, me_z = lax.axis_index("gx"), lax.axis_index("gy"), lax.axis_index("gz")

    def at_x(step):
        return {"gx": lax.rem(me_x + (step + count_x), count_x)}

    def at_y(step):
        return {"gy": lax.rem(me_y + (step + count_y), count_y)}

    def at_z(step):
        return {"gz": lax.rem(me_z + (step + count_z), count_z)}

    loads = [
        pltpu.make_async_copy(cond_hbm, staged.at[0], in_sem.at[0]),
        pltpu.make_async_copy(source_hbm, staged.at[1], in_sem.at[1]),
    ]
    for load in loads:
        load.start()

    barrier = pltpu.get_barrier_semaphore()
    partners = [at_z(1), at_z(-1)]
    partners += [at_x(sign * step) for step in (1, 2, 3, 5, 6) for sign in (1, -1)]
    partners += [at_y(step) for step in range(1, count_y)]
    partners += [at_x(dx) | at_y(dy) for dx in (-1, 1) for dy in (-1, 1)]
    for partner in partners:
        pl.semaphore_signal(barrier, inc=1, device_id=partner, device_id_type=MESH)

    pending = []

    def drain():
        for copy in pending:
            copy.wait_send()
        pending.clear()

    def send(source, target, sems, slot, device):
        copy = pltpu.make_async_remote_copy(
            src_ref=source,
            dst_ref=target,
            send_sem=sems.at[0, slot],
            recv_sem=sems.at[1, slot],
            device_id=device,
            device_id_type=MESH,
        )
        copy.start()
        pending.append(copy)
        return copy

    def kept(row, l):
        return row == jnp.where(l < 64, 2 * l, 2 * (l - 64) + 1)

    def sent(row, l):
        half, q = l // 128, (l % 128) // 32
        z = 2 * (l % 32) + 64 * half + jnp.where(q % 2 == 0, half, 1 - half)
        return row == jnp.where(q >= 2, z, z + 128)

    keep = select_matrix((128, 128), kept)
    pass_on = select_matrix((256, 256), sent)
    z_copies = []
    for f in range(2):
        loads[f].wait()
        cells = staged[f].reshape(128, 128)
        halos = dot(side_by_side(cells[:64], cells[64:]), pass_on)
        z_send[f, 0] = halos[:, :128].reshape(4, 16, 128)
        z_send[f, 1] = halos[:, 128:].reshape(4, 16, 128)
        if f == 0:
            pl.semaphore_wait(barrier, len(partners))
        z_copies.append(
            [
                send(z_send.at[f, way], z_recv.at[f, way], z_sems, 2 * f + way, at_z((-1, 1)[way]))
                for way in range(2)
            ]
        )
        own[f] = dot(cells, keep).reshape(8, 16, 128)

    def send_x(f):
        return [
            send(
                win.at[f, 4:8, :, 0:16, :],
                win.at[f, 12:16, :, 0:16, :],
                x_sems,
                2 * f,
                at_x(-1),
            ),
            send(
                win.at[f, 8:12, :, 0:16, :],
                win.at[f, 0:4, :, 0:16, :],
                x_sems,
                2 * f + 1,
                at_x(1),
            ),
        ]

    def send_y(f):
        y_send[f, 0] = win[f, :, :, 0:4, :]
        y_send[f, 1] = win[f, :, :, 12:16, :]
        return [
            send(y_send.at[f, way], y_recv.at[f, way], y_sems, 2 * f + way, at_y((-1, 1)[way]))
            for way in range(2)
        ]

    def send_xy(f):
        copies = send_x(f)
        y_send[f, 0, 4:12] = win[f, 4:12, :, 0:4, :]
        y_send[f, 1, 4:12] = win[f, 4:12, :, 12:16, :]
        for way in range(2):
            for slot, (dx, first, last) in enumerate(((0, 4, 12), (1, 8, 12), (-1, 4, 8))):
                copies.append(
                    send(
                        y_send.at[f, way, first:last],
                        y_recv.at[f, way, first - 8 * dx : last - 8 * dx],
                        xy_sems,
                        6 * f + 3 * way + slot,
                        at_y((-1, 1)[way]) | (at_x(dx) if dx else {}),
                    )
                )
        return copies

    def place_y(f, copies):
        for copy in copies:
            copy.wait_recv()
        win[f, :, :, 16:20, :] = y_recv[f, 0]
        win[f, :, :, 20:24, :] = y_recv[f, 1]

    xy_copies = []
    for f in range(2):
        for copy in z_copies[f]:
            copy.wait_recv()
        lane = lane_of((4, 16, 128))
        for part in range(2):
            mine = own[f, 4 * part : 4 * part + 4]
            above, below = z_recv[f, 0], z_recv[f, 1]
            for t in range(2):
                turn_above = ((0, 96), (64, 32))[part][t]
                turn_below = ((0, 32), (64, 96))[part][t]
                halo = jnp.where(
                    lane < 96,
                    roll(above, turn_above, 2) if turn_above else above,
                    roll(below, turn_below, 2) if turn_below else below,
                )
                win[f, 4 + 4 * part : 8 + 4 * part, t, 0:16, :] = jnp.where(
                    lane < 64, roll(mine, 64, 2) if t else mine, halo
                )
        xy_copies.append(send_xy(f))

    cond, source, best = win.at[0], win.at[1], win.at[2]
    faces0 = (fx, fy, fz)
    brick = slice(0, 16)
    for i in range(4, 12):
        k0, k1 = cond[i, 0, brick, :], cond[i, 1, brick, :]
        fz[i, 0, brick, :] = harmonic(k0, roll(k1, 1, 1))
        fz[i, 1, brick, :] = harmonic(k1, k0)
        if i > 4:
            fx[i, 0, brick, :] = harmonic(k0, cond[i - 1, 0, brick, :])
            fx[i, 1, brick, :] = harmonic(k1, cond[i - 1, 1, brick, :])
    place_y(0, xy_copies[0])
    for t in range(2):
        fx[4, t, brick, :] = harmonic(cond[4, t, brick, :], cond[3, t, brick, :])
    for i in range(4, 12):
        for t in range(2):
            k = cond[i, t]
            fy[i, t] = harmonic(k, roll(k, 1, 0))

    for i in range(4):
        tmp0[0, i] = fx[4 + 2 * i, 0, 0:16, :] + fx[4 + 2 * i, 1, 0:16, :]
        tmp0[1, i] = (fy[4 + 2 * i, 0, 0:16, :] + fy[4 + 2 * i, 1, 0:16, :]) + (
            fy[5 + 2 * i, 0, 0:16, :] + fy[5 + 2 * i, 1, 0:16, :]
        )
        tmp0[2, i] = fz[4 + 2 * i, 0, 0:16, :] + fz[5 + 2 * i, 0, 0:16, :]
    first, second = pl.ds(0, 8, stride=2), pl.ds(1, 8, stride=2)
    f1[8:12, 0, 8:16, :] = 0.125 * (tmp0[0, :, first, :] + tmp0[0, :, second, :])
    f1[8:12, 1, 8:16, :] = 0.125 * tmp0[1, :, first, :]
    f1[8:12, 2, 8:16, :] = 0.125 * (tmp0[2, :, first, :] + tmp0[2, :, second, :])
    f1x_copies = [
        send(
            f1.at[8:12, :, 8:16, :],
            f1.at[8 - 4 * step : 12 - 4 * step, :, 8:16, :],
            f1x_sems,
            slot,
            at_x(step),
        )
        for slot, step in enumerate((-1, 1, -2, 2))
    ]

    def spread_x(ref, first, last, sems, steps):
        return [
            send(ref.at[1, first:last], ref.at[1, first - step : last - step], sems, slot, at_x(step))
            for slot, step in enumerate(steps)
        ]

    def gather_y(ref, sems):
        return [
            send(ref.at[1], ref.at[(1 - step) % count_y], sems, step - 1, at_y(step))
            for step in range(1, count_y)
        ]

    for i in range(1, 16):
        part = slice(16, 24) if 4 <= i < 12 else slice(0, 24)
        for t in range(2):
            fx[i, t, part, :] = harmonic(cond[i, t, part, :], cond[i - 1, t, part, :])
        if i == 15:
            break
        k0, k1 = cond[i, 0], cond[i, 1]
        if not 4 <= i < 12:
            fy[i, 0] = harmonic(k0, roll(k0, 1, 0))
            fy[i, 1] = harmonic(k1, roll(k1, 1, 0))
        k0, k1 = k0[part], k1[part]
        fz[i, 0, part, :] = harmonic(k0, roll(k1, 1, 1))
        fz[i, 1, part, :] = harmonic(k1, k0)

    sibling = {"gy": me_y + 1 - 2 * lax.rem(me_y, 2)}
    shift = lax.rem(me_y, 2) * 2 + (count_y - 1)

    def hand_on(ref, sems, place):
        return send(
            ref.at[place],
            ref.at[lax.rem(place + shift, count_y)],
            sems,
            count_y + place,
            sibling,
        )

    def gather_y_shared(ref, sems):
        places = [(1 - step) % count_y for step in range(2, count_y, 2)]
        far = {
            place: send(ref.at[1], ref.at[place], sems, place, at_y(1 - place + count_y))
            for place in places
        }
        return far, [hand_on(ref, sems, 1)]

    def hand_on_all(ref, sems, far, handed):
        for place, copy in far.items():
            copy.wait_recv()
            handed.append(hand_on(ref, sems, place))

    for low, high in chunks(1, 15, 2):
        x_sum = [fx[low:high, t] + fx[low + 1 : high + 1, t] for t in range(2)]
        y_sum = [fy[low:high, t] + roll(fy[low:high, t], -1, 1) for t in range(2)]
        z0, z1 = fz[low:high, 0], fz[low:high, 1]
        inv[low:high, 0] = 1.0 / ((x_sum[0] + y_sum[0]) + (z0 + z1))
        inv[low:high, 1] = 1.0 / ((x_sum[1] + y_sum[1]) + (z1 + roll(z0, -1, 2)))

    place_y(1, xy_copies[1])
    for i in range(1, 15):
        for t in range(2):
            xa[i, t] = inv[i, t] * source[i, t] * (1.0 / CENTER)

    def step_0(old, new, low, high, step, before, after=None, target=None):
        keep_old, keep_new = STEPS[step]

        def emit(i, applied, here):
            for t in range(2):
                r = source[i, t] - applied[t]
                d = keep_old * before[i, t] + keep_new * (inv[i, t] * r)
                if after is not None:
                    after[i, t] = d
                if target is None:
                    new[i, t] = here[t] + d
                else:
                    target(i, t, here[t] + d)

        sweep_0(old, faces0, low, high, emit)

    step_0(xa, xb, 2, 14, 0, xa, dd)

    step_0(xb, xa, 3, 13, 1, dd)
    best[4:12, :, 0:16, :] = xa[4:12, :, 0:16, :]
    sums = []

    def residual_0(i, applied, here):
        r = [source[i, t, 0:16, :] - applied[t][:16] for t in range(2)]
        sums.append(r[0] + r[1])
        if i % 2 == 1:
            tmp0[0, (i - 4) // 2] = sums[-2] + sums[-1]

    sweep_0(xa, faces0, 4, 12, residual_0)
    b1[8:12, 8:16, :] = 0.125 * (tmp0[0, :, first, :] + tmp0[0, :, second, :])
    b1x_copies = [
        send(
            b1.at[first:last, 8:16, :],
            b1.at[first - 4 * step : last - 4 * step, 8:16, :],
            b1x_sems,
            slot,
            at_x(step),
        )
        for slot, (step, first, last) in enumerate(
            ((-1, 8, 12), (1, 8, 12), (-2, 8, 11), (2, 9, 12))
        )
    ]


    for copy in f1x_copies:
        copy.wait_recv()
    f1y_copies = [
        send(
            f1.at[:, :, 8:16, :],
            f1.at[:, :, 8 - 8 * step : 16 - 8 * step, :],
            f1y_sems,
            slot,
            at_y(step),
        )
        for slot, step in enumerate((-1, 1))
    ]

    def in_pack(row, column):
        return ((row % 128) // 2 + 16) % 64 + 64 * (row // 128) == column

    pack = select_matrix((256, 128), in_pack)
    pack_even = select_matrix((256, 128), lambda row, l: (row % 2 == 0) & in_pack(row, l))
    first4, second4 = pl.ds(0, 4, stride=2), pl.ds(1, 4, stride=2)

    def packed(pieces, matrix):
        whole = [jnp.concatenate(piece, axis=0) for piece in pieces]
        result = dot(side_by_side(*whole), matrix)
        return result.reshape(len(pieces[0]), 8, 128)

    g2f[1, 15] = jnp.ones((3, 4, 128), F32)
    g2b[1, 15] = jnp.zeros((4, 128), F32)
    mine = slice(8, 16)
    tmp1[0] = packed([[f1[4 * i + 2 * p, 0, mine, :] for i in range(5)] for p in range(2)], pack)
    for f in (1, 2):
        pieces = [
            [f1[4 * i + 2 * p, f, mine, :] + f1[4 * i + 2 * p + 1, f, mine, :] for i in range(5)]
            for p in range(2)
        ]
        tmp1[f] = packed(pieces, (None, pack, pack_even)[f])
    g2f[1, 5:10, 0] = 0.125 * (tmp1[0, :, first4, :] + tmp1[0, :, second4, :])
    g2f[1, 5:10, 1] = 0.125 * tmp1[1, :, first4, :]
    g2f[1, 5:10, 2] = 0.125 * (tmp1[2, :, first4, :] + tmp1[2, :, second4, :])
    gfx_copies = spread_x(g2f, 5, 10, gfx_sems, (5, -5))

    drain()
    for copy in b1x_copies:
        copy.wait_recv()
    b1y_copies = [
        send(
            b1.at[:, 8:16, :],
            b1.at[:, 8 - 8 * step : 16 - 8 * step, :],
            b1y_sems,
            slot,
            at_y(step),
        )
        for slot, step in enumerate((-1, 1))
    ]
    for copy in f1y_copies:
        copy.wait_recv()
    for low, high in chunks(1, 19, 6):
        x_sum = f1[low:high, 0] + f1[low + 1 : high + 1, 0]
        y_term, z_term = f1[low:high, 1], f1[low:high, 2]
        y_sum = y_term + roll(y_term, -1, 1)
        inv1[low:high] = 1.0 / ((x_sum + y_sum) + (z_term + roll(z_term, -1, 2)))

    for copy in b1y_copies:
        copy.wait_recv()

    for i in range(1, 19):
        x1a[i] = inv1[i] * b1[i] * (1.0 / CENTER)

    def step_1(old, new, low, high, step, before, after=None):
        keep_old, keep_new = STEPS[step]

        def emit(i, applied, here):
            r = b1[i] - applied
            d = keep_old * before[i] + keep_new * (inv1[i] * r)
            if after is not None:
                after[i] = d
            new[i] = here + d

        sweep_1(old, f1, low, high, emit)

    step_1(x1a, x1b, 2, 18, 0, x1a, d1)
    for copy in gfx_copies:
        copy.wait_recv()
    gfy_far, gfy_copies = gather_y_shared(g2f, gfy_sems)
    step_1(x1b, x1a, 3, 17, 1, d1)
    r = {}

    def residual_1(i, applied, here):
        r[i - 4] = (b1[i] - applied)[8:16]

    sweep_1(x1a, f1, 4, 16, residual_1)
    tmp1[0, 0:3] = packed(
        [[r[4 * i + 2 * p] + r[4 * i + 2 * p + 1] for i in range(3)] for p in range(2)], pack
    )
    g2b[1, 6:9] = 0.125 * (tmp1[0, 0:3, first4, :] + tmp1[0, 0:3, second4, :])
    gbx_copies = spread_x(g2b, 6, 9, gbx_sems, (3, -3, 6, -6))
    x0_copies = send_x(2)
    for copy in gbx_copies:
        copy.wait_recv()
    gby_copies = gather_y(g2b, gby_sems)

    hand_on_all(g2f, gfy_sems, gfy_far, gfy_copies)
    for copy in gfy_copies:
        copy.wait_recv()
    for f in range(3):
        for s in range(count_y):
            f2[f, :, 4 * s : 4 * s + 4, :] = g2f[s, :, f]
    for low, high in chunks(0, 15, 3):
        terms = f2[0, low : high + 1]
        turned = roll(terms, 64, 2)
        half = lane_of(terms[1:].shape) < 64
        x_sum = terms[:-1] + jnp.where(half, turned[:-1], turned[1:])
        y_term, z_term = f2[1, low:high], f2[2, low:high]
        y_sum = y_term + roll(y_term, -1, 1)
        inv2[low:high] = 1.0 / ((x_sum + y_sum) + (z_term + roll(z_term, -1, 2)))

        x_low = f2[0, low:high]
        x_low = jnp.where(half, x_low, roll(x_low, 64, 2))
        tmp2[0, low:high] = x_low + roll(x_low, -1, 2)
        y_both = y_term + roll(y_term, 64, 2)
        tmp2[1, low:high] = y_both + roll(y_both, -1, 2)
        tmp2[2, low:high] = z_term + roll(z_term, 64, 2)
    first16, second16 = pl.ds(0, 16, stride=2), pl.ds(1, 16, stride=2)
    f3[0] = 0.125 * (tmp2[0, :, first16, :] + tmp2[0, :, second16, :])
    f3[1] = 0.125 * tmp2[1, :, first16, :]
    f3[2] = 0.125 * (tmp2[2, :, first16, :] + tmp2[2, :, second16, :])
    for low, high in chunks(2, 13, 6):
        terms = f3[0, low : high + 1]
        y_term, z_term = f3[1, low:high], f3[2, low:high]
        inv3[low:high] = 1.0 / (
            (terms[:-1] + terms[1:] + (y_term + roll(y_term, -1, 1)))
            + (z_term + roll(z_term, -2, 2))
        )

    for copy in x0_copies:
        copy.wait_recv()
    y0_copies = send_y(2)
    for copy in gby_copies:
        copy.wait_recv()
    for s in range(count_y):
        b2[:, 4 * s : 4 * s + 4, :] = g2b[s]

    for i in range(15):
        x2a[i] = inv2[i] * b2[i] * (1.0 / CENTER)

    def step_2(old, new, low, high, step, before, after=None):
        keep_old, keep_new = STEPS[step]

        def emit(i, applied, here):
            r = b2[i] - applied
            d = keep_old * before[i] + keep_new * (inv2[i] * r)
            if after is not None:
                after[i] = d
            new[i] = here + d

        sweep_2(old, f2, low, high, emit)

    step_2(x2a, x2b, 1, 14, 0, x2a, d2)
    step_2(x2b, x2a, 1, 14, 1, d2)

    def residual_2(i, applied, here):
        r = b2[i] - applied
        r = r + roll(r, 64, 1)
        tmp2[0, i] = r + roll(r, -1, 1)

    sweep_2(x2a, f2, 2, 13, residual_2)
    b3[2:13] = 0.125 * (tmp2[0, 2:13, first16, :] + tmp2[0, 2:13, second16, :])

    for i in range(2, 13):
        x3a[i] = inv3[i] * b3[i] * (1.0 / CENTER)

    def step_3(old, new, low, high, step, before, after=None):
        keep_old, keep_new = STEPS[step]

        def emit(i, applied, here):
            r = b3[i] - applied
            d = keep_old * before[i] + keep_new * (inv3[i] * r)
            if after is not None:
                after[i] = d
            new[i] = here + d

        sweep_3(old, f3, low, high, emit)

    step_3(x3a, x3b, 3, 12, 0, x3a, d3)
    step_3(x3b, x3a, 4, 11, 1, d3)

    e = x3a[4:11]
    e = jnp.where(lane_of(e.shape) % 2 == 0, e, roll(e, 1, 2))
    dup2[4:11, first16, :] = e
    dup2[4:11, second16, :] = e
    for i in range(4, 11):
        x2b[i] = x2a[i] + dup2[i]
    x2b[3] = x2a[3]
    x2b[11] = x2a[11]

    def first_up_2(i, applied, here):
        d = inv2[i] * (b2[i] - applied) * (1.0 / CENTER)
        d2[i] = d
        x2a[i] = here + d

    sweep_2(x2b, f2, 4, 11, first_up_2)
    step_2(x2a, x2b, 5, 10, 0, d2, d2)
    x2b[4] = x2a[4]
    x2b[10] = x2a[10]
    step_2(x2b, x2a, 5, 10, 1, d2)

    def in_spread(row, column):
        return ((column % 128) // 2 + 16) % 64 + 64 * (column // 128) == row

    e = dot(x2a[5:10, 0:16, :].reshape(80, 128), select_matrix((128, 256), in_spread))
    for p in range(2):
        value = e[:, 128 * p : 128 * p + 128].reshape(5, 16, 128)
        dup21[p, :, first16, :] = value
        dup21[p, :, second16, :] = value
    for i in range(3, 17):
        x1b[i] = x1a[i] + dup21[(i // 2) % 2, i // 4, 0:24, :]

    def first_up_1(i, applied, here):
        d = inv1[i] * (b1[i] - applied) * (1.0 / CENTER)
        d1[i] = d
        x1a[i] = here + d

    sweep_1(x1b, f1, 4, 16, first_up_1)
    step_1(x1a, x1b, 5, 15, 0, d1, d1)
    step_1(x1b, x1a, 6, 14, 1, d1)

    drain()
    place_y(2, y0_copies)
    e = x1a[6:14]
    dup1[:, pl.ds(0, 24, stride=2), :] = e
    dup1[:, pl.ds(1, 24, stride=2), :] = e
    lower = lax.broadcasted_iota(jnp.int32, (8, 128), 0) < 4
    for i in range(1, 15):
        j = i // 2
        brick = dup1[j, 16:32, :]
        edge = jnp.where(lower, dup1[j, 32:40, :], dup1[j, 8:16, :])
        for t in range(2):
            xb[i, t, 0:16, :] = best[i, t, 0:16, :] + brick
            xb[i, t, 16:24, :] = best[i, t, 16:24, :] + edge

    def first_up_0(i, applied, here):
        for t in range(2):
            d = inv[i, t] * (source[i, t] - applied[t]) * (1.0 / CENTER)
            dd[i, t] = d
            xa[i, t] = here[t] + d

    sweep_0(xb, faces0, 2, 14, first_up_0)
    step_0(xa, xb, 3, 13, 0, dd, dd)

    def to_own(i, t, value):
        own[t, i - 4] = value[0:16]

    step_0(xb, None, 4, 12, 1, dd, None, to_own)

    def joined(row, column):
        return (row % 128 < 64) & (column == 2 * (row % 128) + row // 128)

    cells = side_by_side(own[0].reshape(128, 128), own[1].reshape(128, 128))
    result = dot(cells, select_matrix((256, 128), joined))
    out_ref[...] = result.reshape(8, 16, 128)


def solution(mesh):
    sizes = (mesh.shape["gx"], mesh.shape["gy"], mesh.shape["gz"])
    count_x, count_y, _ = sizes
    vmem = lambda *shape: pltpu.VMEM(shape, F32)
    sems = lambda count: pltpu.SemaphoreType.DMA((2, count))
    fine = (16, 2, 24, 128)
    level1 = (20, 24, 128)
    level2 = (16, 32, 128)
    level3 = (16, 16, 128)
    scratch = [
        vmem(2, 8, 16, 128),
        vmem(2, 8, 16, 128),
        vmem(2, 2, 4, 16, 128),
        vmem(2, 2, 4, 16, 128),
        vmem(3, *fine),
        vmem(3, 2, 16, 2, 4, 128),
        vmem(3, 2, 16, 2, 4, 128),
        vmem(*fine),
        vmem(*fine),
        vmem(*fine),
        vmem(*fine),
        vmem(*fine),
        vmem(*fine),
        vmem(*fine),
        vmem(3, 4, 16, 128),
        vmem(20, 3, 24, 128),
        vmem(*level1),
        vmem(*level1),
        vmem(*level1),
        vmem(*level1),
        vmem(*level1),
        vmem(3, 5, 8, 128),
        vmem(8, 48, 128),
        vmem(count_y, count_x, 3, 4, 128),
        vmem(count_y, count_x, 4, 128),
        vmem(3, *level2),
        vmem(*level2),
        vmem(*level2),
        vmem(*level2),
        vmem(*level2),
        vmem(*level2),
        vmem(3, *level2),
        vmem(3, *level3),
        vmem(*level3),
        vmem(*level3),
        vmem(*level3),
        vmem(*level3),
        vmem(*level3),
        vmem(*level2),
        vmem(2, 5, 32, 128),
        pltpu.SemaphoreType.DMA((2,)),
        sems(4),
        sems(6),
        sems(6),
        sems(12),
        sems(4),
        sems(2),
        sems(4),
        sems(2),
        sems(2),
        sems(2 * count_y),
        sems(4),
        sems(count_y - 1),
    ]

    def shards(pressure_source, conductivity):
        return pl.pallas_call(
            functools.partial(kernel, sizes),
            out_shape=jax.ShapeDtypeStruct((8, 16, 128), F32),
            in_specs=[pl.BlockSpec(memory_space=pltpu.HBM)] * 2,
            out_specs=pl.BlockSpec(memory_space=pltpu.VMEM),
            scratch_shapes=scratch,
            compiler_params=pltpu.CompilerParams(
                collective_id=0, has_side_effects=True, vmem_limit_bytes=55136 * 1024
            ),
        )(pressure_source, conductivity)

    placed = (P("gx", "gy", "gz"), P("gx", "gy", "gz"))
    return jax.shard_map(
        shards, mesh=mesh, in_specs=placed, out_specs=P("gx", "gy", "gz"), check_vma=False
    )
```

```python
import functools

import jax
import jax.numpy as jnp
from jax import lax
from jax.experimental import pallas as pl
from jax.experimental.pallas import tpu as pltpu
from jax.sharding import PartitionSpec as P

MESH = pl.DeviceIdType.MESH
F32 = jnp.float32

CENTER = 1.125
RADIUS = 0.875
RATIO = CENTER / RADIUS
RHO0 = 1.0 / RATIO
RHO1 = 1.0 / (2.0 * RATIO - RHO0)
RHO2 = 1.0 / (2.0 * RATIO - RHO1)
STEPS = ((RHO1 * RHO0, 2.0 * RHO1 / RADIUS), (RHO2 * RHO1, 2.0 * RHO2 / RADIUS))


def roll(value, shift, axis):
    return pltpu.roll(value, shift % value.shape[axis], axis)


def lane_of(shape):
    return lax.broadcasted_iota(jnp.int32, shape, len(shape) - 1)


def select_matrix(shape, holds):
    row = lax.broadcasted_iota(jnp.int32, shape, 0)
    column = lax.broadcasted_iota(jnp.int32, shape, 1)
    return jnp.where(holds(row, column), 1.0, 0.0).astype(jnp.bfloat16)


def dot(a, ones):
    high = a.astype(jnp.bfloat16)
    rest = a - high.astype(F32)
    middle = rest.astype(jnp.bfloat16)
    low = (rest - middle.astype(F32)).astype(jnp.bfloat16)
    parts = [jnp.dot(part, ones, preferred_element_type=F32) for part in (low, middle, high)]
    return (parts[0] + parts[1]) + parts[2]


def side_by_side(a, b):
    return jnp.concatenate([a, b], axis=1)


def harmonic(one_side, other_side):
    return 2.0 * one_side * other_side / (one_side + other_side)


def chunks(low, high, size):
    return [(start, min(start + size, high)) for start in range(low, high, size)]


def sweep_0(field, faces, low, high, emit):
    face_x, face_y, face_z = faces
    both = range(2)
    here = [field[low, t] for t in both]
    flux = [face_x[low, t] * (here[t] - field[low - 1, t]) for t in both]
    for i in range(low, high):
        after = [field[i + 1, t] for t in both]
        upper = [face_x[i + 1, t] * (after[t] - here[t]) for t in both]
        result = []
        for t in both:
            side = face_y[i, t] * (here[t] - roll(here[t], 1, 0))
            result.append((flux[t] - upper[t]) + (side - roll(side, -1, 0)))
        even = face_z[i, 0] * (here[0] - roll(here[1], 1, 1))
        odd = face_z[i, 1] * (here[1] - here[0])
        emit(i, [result[0] + (even - odd), result[1] + (odd - roll(even, -1, 1))], here)
        here, flux = after, upper


def sweep_1(field, faces, low, high, emit):
    here = field[low]
    flux = faces[low, 0] * (here - field[low - 1])
    for i in range(low, high):
        after = field[i + 1]
        upper = faces[i + 1, 0] * (after - here)
        side = faces[i, 1] * (here - roll(here, 1, 0))
        result = (flux - upper) + (side - roll(side, -1, 0))
        side = faces[i, 2] * (here - roll(here, 1, 1))
        emit(i, result + (side - roll(side, -1, 1)), here)
        here, flux = after, upper


def sweep_2(field, faces, low, high, emit):
    half = lane_of(field.shape[1:]) < 64
    before, here = roll(field[low - 1], 64, 1), field[low]
    turned = roll(here, 64, 1)
    flux = faces[0, low] * (here - jnp.where(half, before, turned))
    flux_turned = roll(flux, 64, 1)
    for i in range(low, high):
        after = field[i + 1]
        after_turned = roll(after, 64, 1)
        upper = faces[0, i + 1] * (after - jnp.where(half, turned, after_turned))
        upper_turned = roll(upper, 64, 1)
        result = flux - jnp.where(half, flux_turned, upper_turned)
        side = faces[1, i] * (here - roll(here, 1, 0))
        result = result + (side - roll(side, -1, 0))
        side = faces[2, i] * (here - roll(here, 1, 1))
        emit(i, result + (side - roll(side, -1, 1)), here)
        here, turned, flux, flux_turned = after, after_turned, upper, upper_turned


def sweep_3(field, faces, low, high, emit):
    here = field[low]
    flux = faces[0, low] * (here - field[low - 1])
    for i in range(low, high):
        after = field[i + 1]
        upper = faces[0, i + 1] * (after - here)
        side = faces[1, i] * (here - roll(here, 1, 0))
        result = (flux - upper) + (side - roll(side, -1, 0))
        side = faces[2, i] * (here - roll(here, 2, 1))
        emit(i, result + (side - roll(side, -2, 1)), here)
        here, flux = after, upper


def kernel(
    sizes,
    source_hbm,
    cond_hbm,
    out_ref,
    staged,
    own,
    z_send,
    z_recv,
    win,
    y_send,
    y_recv,
    fx,
    fy,
    fz,
    inv,
    xa,
    xb,
    dd,
    tmp0,
    f1,
    b1,
    inv1,
    x1a,
    x1b,
    d1,
    tmp1,
    dup1,
    g2f,
    g2b,
    f2,
    b2,
    inv2,
    x2a,
    x2b,
    d2,
    tmp2,
    f3,
    b3,
    inv3,
    x3a,
    x3b,
    d3,
    dup2,
    dup21,
    in_sem,
    z_sems,
    x_sems,
    y_sems,
    xy_sems,
    f1x_sems,
    f1y_sems,
    b1x_sems,
    b1y_sems,
    gfx_sems,
    gfy_sems,
    gbx_sems,
    gby_sems,
):
    count_x, count_y, count_z = sizes
    me_x, me_y, me_z = lax.axis_index("gx"), lax.axis_index("gy"), lax.axis_index("gz")

    def at_x(step):
        return {"gx": lax.rem(me_x + (step + count_x), count_x)}

    def at_y(step):
        return {"gy": lax.rem(me_y + (step + count_y), count_y)}

    def at_z(step):
        return {"gz": lax.rem(me_z + (step + count_z), count_z)}

    loads = [
        pltpu.make_async_copy(cond_hbm, staged.at[0], in_sem.at[0]),
        pltpu.make_async_copy(source_hbm, staged.at[1], in_sem.at[1]),
    ]
    for load in loads:
        load.start()

    barrier = pltpu.get_barrier_semaphore()
    partners = [at_z(1), at_z(-1)]
    partners += [at_x(sign * step) for step in (1, 2, 3, 5, 6) for sign in (1, -1)]
    partners += [at_y(step) for step in range(1, count_y)]
    partners += [at_x(dx) | at_y(dy) for dx in (-1, 1) for dy in (-1, 1)]
    for partner in partners:
        pl.semaphore_signal(barrier, inc=1, device_id=partner, device_id_type=MESH)

    pending = []

    def drain():
        for copy in pending:
            copy.wait_send()
        pending.clear()

    def send(source, target, sems, slot, device):
        copy = pltpu.make_async_remote_copy(
            src_ref=source,
            dst_ref=target,
            send_sem=sems.at[0, slot],
            recv_sem=sems.at[1, slot],
            device_id=device,
            device_id_type=MESH,
        )
        copy.start()
        pending.append(copy)
        return copy

    def kept(row, l):
        return row == jnp.where(l < 64, 2 * l, 2 * l - 127)

    def sent(row, l):
        half, q = l >> 7, (l >> 5) & 3
        z = 2 * (l & 31) + 64 * half + jnp.where((q & 1) == 0, half, 1 - half)
        return row == jnp.where(q >= 2, z, z + 128)

    keep = select_matrix((128, 128), kept)
    pass_on = select_matrix((256, 256), sent)
    z_copies = []
    for f in range(2):
        loads[f].wait()
        cells = staged[f].reshape(128, 128)
        halos = dot(side_by_side(cells[:64], cells[64:]), pass_on)
        z_send[f, 0] = halos[:, :128].reshape(4, 16, 128)
        z_send[f, 1] = halos[:, 128:].reshape(4, 16, 128)
        if f == 0:
            pl.semaphore_wait(barrier, len(partners))
        z_copies.append(
            [
                send(z_send.at[f, way], z_recv.at[f, way], z_sems, 2 * f + way, at_z((-1, 1)[way]))
                for way in range(2)
            ]
        )
        own[f] = dot(cells, keep).reshape(8, 16, 128)

    def send_x(f):
        return [
            send(
                win.at[f, 4:8, :, 0:16, :],
                win.at[f, 12:16, :, 0:16, :],
                x_sems,
                2 * f,
                at_x(-1),
            ),
            send(
                win.at[f, 8:12, :, 0:16, :],
                win.at[f, 0:4, :, 0:16, :],
                x_sems,
                2 * f + 1,
                at_x(1),
            ),
        ]

    def send_y(f):
        y_send[f, 0] = win[f, :, :, 0:4, :]
        y_send[f, 1] = win[f, :, :, 12:16, :]
        return [
            send(y_send.at[f, way], y_recv.at[f, way], y_sems, 2 * f + way, at_y((-1, 1)[way]))
            for way in range(2)
        ]

    def send_xy(f):
        copies = send_x(f)
        y_send[f, 0, 4:12] = win[f, 4:12, :, 0:4, :]
        y_send[f, 1, 4:12] = win[f, 4:12, :, 12:16, :]
        for way in range(2):
            for slot, (dx, first, last) in enumerate(((0, 4, 12), (1, 8, 12), (-1, 4, 8))):
                copies.append(
                    send(
                        y_send.at[f, way, first:last],
                        y_recv.at[f, way, first - 8 * dx : last - 8 * dx],
                        xy_sems,
                        6 * f + 3 * way + slot,
                        at_y((-1, 1)[way]) | (at_x(dx) if dx else {}),
                    )
                )
        return copies

    def place_y(f, copies):
        for copy in copies:
            copy.wait_recv()
        win[f, :, :, 16:20, :] = y_recv[f, 0]
        win[f, :, :, 20:24, :] = y_recv[f, 1]

    xy_copies = []
    for f in range(2):
        for copy in z_copies[f]:
            copy.wait_recv()
        lane = lane_of((4, 16, 128))
        for part in range(2):
            mine = own[f, 4 * part : 4 * part + 4]
            above, below = z_recv[f, 0], z_recv[f, 1]
            for t in range(2):
                turn_above = ((0, 96), (64, 32))[part][t]
                turn_below = ((0, 32), (64, 96))[part][t]
                halo = jnp.where(
                    lane < 96,
                    roll(above, turn_above, 2) if turn_above else above,
                    roll(below, turn_below, 2) if turn_below else below,
                )
                win[f, 4 + 4 * part : 8 + 4 * part, t, 0:16, :] = jnp.where(
                    lane < 64, roll(mine, 64, 2) if t else mine, halo
                )
        xy_copies.append(send_xy(f))

    cond, source, best = win.at[0], win.at[1], win.at[2]
    faces0 = (fx, fy, fz)
    brick = slice(0, 16)
    for i in range(4, 12):
        k0, k1 = cond[i, 0, brick, :], cond[i, 1, brick, :]
        fz[i, 0, brick, :] = harmonic(k0, roll(k1, 1, 1))
        fz[i, 1, brick, :] = harmonic(k1, k0)
        if i > 4:
            fx[i, 0, brick, :] = harmonic(k0, cond[i - 1, 0, brick, :])
            fx[i, 1, brick, :] = harmonic(k1, cond[i - 1, 1, brick, :])
    place_y(0, xy_copies[0])
    for t in range(2):
        fx[4, t, brick, :] = harmonic(cond[4, t, brick, :], cond[3, t, brick, :])
    for i in range(4, 12):
        for t in range(2):
            k = cond[i, t]
            fy[i, t] = harmonic(k, roll(k, 1, 0))

    for i in range(4):
        tmp0[0, i] = fx[4 + 2 * i, 0, 0:16, :] + fx[4 + 2 * i, 1, 0:16, :]
        tmp0[1, i] = (fy[4 + 2 * i, 0, 0:16, :] + fy[4 + 2 * i, 1, 0:16, :]) + (
            fy[5 + 2 * i, 0, 0:16, :] + fy[5 + 2 * i, 1, 0:16, :]
        )
        tmp0[2, i] = fz[4 + 2 * i, 0, 0:16, :] + fz[5 + 2 * i, 0, 0:16, :]
    first, second = pl.ds(0, 8, stride=2), pl.ds(1, 8, stride=2)
    f1[8:12, 0, 8:16, :] = 0.125 * (tmp0[0, :, first, :] + tmp0[0, :, second, :])
    f1[8:12, 1, 8:16, :] = 0.125 * tmp0[1, :, first, :]
    f1[8:12, 2, 8:16, :] = 0.125 * (tmp0[2, :, first, :] + tmp0[2, :, second, :])
    f1x_copies = [
        send(
            f1.at[8:12, :, 8:16, :],
            f1.at[8 - 4 * step : 12 - 4 * step, :, 8:16, :],
            f1x_sems,
            slot,
            at_x(step),
        )
        for slot, step in enumerate((-2, 2, -1, 1))
    ]

    def spread_x(ref, first, last, sems, steps):
        return [
            send(ref.at[1, first:last], ref.at[1, first - step : last - step], sems, slot, at_x(step))
            for slot, step in enumerate(steps)
        ]

    def gather_y(ref, sems):
        return [
            send(ref.at[1], ref.at[(1 - step) % count_y], sems, step - 1, at_y(step))
            for step in sorted(range(1, count_y), key=lambda step: abs(step - count_y // 2))
        ]

    for i in range(1, 16):
        part = slice(16, 24) if 4 <= i < 12 else slice(0, 24)
        for t in range(2):
            fx[i, t, part, :] = harmonic(cond[i, t, part, :], cond[i - 1, t, part, :])
        if i == 15:
            break
        k0, k1 = cond[i, 0], cond[i, 1]
        if not 4 <= i < 12:
            fy[i, 0] = harmonic(k0, roll(k0, 1, 0))
            fy[i, 1] = harmonic(k1, roll(k1, 1, 0))
        k0, k1 = k0[part], k1[part]
        fz[i, 0, part, :] = harmonic(k0, roll(k1, 1, 1))
        fz[i, 1, part, :] = harmonic(k1, k0)

    sibling = {"gy": me_y + 1 - 2 * lax.rem(me_y, 2)}
    shift = lax.rem(me_y, 2) * 2 + (count_y - 1)

    def hand_on(ref, sems, place):
        return send(
            ref.at[place],
            ref.at[lax.rem(place + shift, count_y)],
            sems,
            count_y + place,
            sibling,
        )

    def gather_y_shared(ref, sems):
        places = [(1 - step) % count_y for step in range(2, count_y, 2)]
        far = {
            place: send(ref.at[1], ref.at[place], sems, place, at_y(1 - place + count_y))
            for place in places
        }
        return far, [hand_on(ref, sems, 1)]

    def hand_on_all(ref, sems, far, handed):
        for place, copy in far.items():
            copy.wait_recv()
            handed.append(hand_on(ref, sems, place))

    for low, high in chunks(1, 15, 2):
        x_sum = [fx[low:high, t] + fx[low + 1 : high + 1, t] for t in range(2)]
        y_sum = [fy[low:high, t] + roll(fy[low:high, t], -1, 1) for t in range(2)]
        z0, z1 = fz[low:high, 0], fz[low:high, 1]
        inv[low:high, 0] = 1.0 / ((x_sum[0] + y_sum[0]) + (z0 + z1))
        inv[low:high, 1] = 1.0 / ((x_sum[1] + y_sum[1]) + (z1 + roll(z0, -1, 2)))

    place_y(1, xy_copies[1])
    for i in range(1, 15):
        for t in range(2):
            xa[i, t] = inv[i, t] * source[i, t] * (1.0 / CENTER)

    def step_0(old, new, low, high, step, before, after=None, target=None):
        keep_old, keep_new = STEPS[step]

        def emit(i, applied, here):
            for t in range(2):
                r = source[i, t] - applied[t]
                d = keep_old * before[i, t] + keep_new * (inv[i, t] * r)
                if after is not None:
                    after[i, t] = d
                if target is None:
                    new[i, t] = here[t] + d
                else:
                    target(i, t, here[t] + d)

        sweep_0(old, faces0, low, high, emit)

    step_0(xa, xb, 2, 14, 0, xa, dd)

    step_0(xb, xa, 3, 13, 1, dd)
    best[4:12, :, 0:16, :] = xa[4:12, :, 0:16, :]
    sums = []

    def residual_0(i, applied, here):
        r = [source[i, t, 0:16, :] - applied[t][:16] for t in range(2)]
        sums.append(r[0] + r[1])
        if i % 2 == 1:
            tmp0[0, (i - 4) // 2] = sums[-2] + sums[-1]

    sweep_0(xa, faces0, 4, 12, residual_0)
    b1[8:12, 8:16, :] = 0.125 * (tmp0[0, :, first, :] + tmp0[0, :, second, :])
    b1x_copies = [
        send(
            b1.at[first:last, 8:16, :],
            b1.at[first - 4 * step : last - 4 * step, 8:16, :],
            b1x_sems,
            slot,
            at_x(step),
        )
        for slot, (step, first, last) in enumerate(
            ((-2, 8, 11), (2, 9, 12), (-1, 8, 12), (1, 8, 12))
        )
    ]


    for copy in f1x_copies:
        copy.wait_recv()
    f1y_copies = [
        send(
            f1.at[:, :, 8:16, :],
            f1.at[:, :, 8 - 8 * step : 16 - 8 * step, :],
            f1y_sems,
            slot,
            at_y(step),
        )
        for slot, step in enumerate((-1, 1))
    ]

    def in_pack(row, column):
        return ((((row & 127) >> 1) + 16) & 63) + 64 * (row >> 7) == column

    pack = select_matrix((256, 128), in_pack)
    pack_even = select_matrix((256, 128), lambda row, l: ((row & 1) == 0) & in_pack(row, l))
    first4, second4 = pl.ds(0, 4, stride=2), pl.ds(1, 4, stride=2)

    def packed(pieces, matrix):
        whole = [jnp.concatenate(piece, axis=0) for piece in pieces]
        result = dot(side_by_side(*whole), matrix)
        return result.reshape(len(pieces[0]), 8, 128)

    g2f[1, 15] = jnp.ones((3, 4, 128), F32)
    g2b[1, 15] = jnp.zeros((4, 128), F32)
    mine = slice(8, 16)
    tmp1[0] = packed([[f1[4 * i + 2 * p, 0, mine, :] for i in range(5)] for p in range(2)], pack)
    for f in (1, 2):
        pieces = [
            [f1[4 * i + 2 * p, f, mine, :] + f1[4 * i + 2 * p + 1, f, mine, :] for i in range(5)]
            for p in range(2)
        ]
        tmp1[f] = packed(pieces, (None, pack, pack_even)[f])
    g2f[1, 5:10, 0] = 0.125 * (tmp1[0, :, first4, :] + tmp1[0, :, second4, :])
    g2f[1, 5:10, 1] = 0.125 * tmp1[1, :, first4, :]
    g2f[1, 5:10, 2] = 0.125 * (tmp1[2, :, first4, :] + tmp1[2, :, second4, :])
    gfx_copies = spread_x(g2f, 5, 10, gfx_sems, (5, -5))

    drain()
    for copy in b1x_copies:
        copy.wait_recv()
    b1y_copies = [
        send(
            b1.at[:, 8:16, :],
            b1.at[:, 8 - 8 * step : 16 - 8 * step, :],
            b1y_sems,
            slot,
            at_y(step),
        )
        for slot, step in enumerate((-1, 1))
    ]
    for copy in f1y_copies:
        copy.wait_recv()
    for low, high in chunks(1, 19, 6):
        x_sum = f1[low:high, 0] + f1[low + 1 : high + 1, 0]
        y_term, z_term = f1[low:high, 1], f1[low:high, 2]
        y_sum = y_term + roll(y_term, -1, 1)
        inv1[low:high] = 1.0 / ((x_sum + y_sum) + (z_term + roll(z_term, -1, 2)))

    for copy in b1y_copies:
        copy.wait_recv()

    for i in range(1, 19):
        x1a[i] = inv1[i] * b1[i] * (1.0 / CENTER)

    def step_1(old, new, low, high, step, before, after=None):
        keep_old, keep_new = STEPS[step]

        def emit(i, applied, here):
            r = b1[i] - applied
            d = keep_old * before[i] + keep_new * (inv1[i] * r)
            if after is not None:
                after[i] = d
            new[i] = here + d

        sweep_1(old, f1, low, high, emit)

    step_1(x1a, x1b, 2, 18, 0, x1a, d1)
    for copy in gfx_copies:
        copy.wait_recv()
    gfy_far, gfy_copies = gather_y_shared(g2f, gfy_sems)
    step_1(x1b, x1a, 3, 17, 1, d1)
    r = {}

    def residual_1(i, applied, here):
        r[i - 4] = (b1[i] - applied)[8:16]

    sweep_1(x1a, f1, 4, 16, residual_1)
    tmp1[0, 0:3] = packed(
        [[r[4 * i + 2 * p] + r[4 * i + 2 * p + 1] for i in range(3)] for p in range(2)], pack
    )
    g2b[1, 6:9] = 0.125 * (tmp1[0, 0:3, first4, :] + tmp1[0, 0:3, second4, :])
    gbx_copies = spread_x(g2b, 6, 9, gbx_sems, (6, -6, 3, -3))
    x0_copies = send_x(2)
    for copy in gbx_copies:
        copy.wait_recv()
    gby_copies = gather_y(g2b, gby_sems)

    hand_on_all(g2f, gfy_sems, gfy_far, gfy_copies)
    for copy in gfy_copies:
        copy.wait_recv()
    for f in range(3):
        for s in range(count_y):
            f2[f, :, 4 * s : 4 * s + 4, :] = g2f[s, :, f]
    for low, high in chunks(0, 15, 3):
        terms = f2[0, low : high + 1]
        turned = roll(terms, 64, 2)
        half = lane_of(terms[1:].shape) < 64
        x_sum = terms[:-1] + jnp.where(half, turned[:-1], turned[1:])
        y_term, z_term = f2[1, low:high], f2[2, low:high]
        y_sum = y_term + roll(y_term, -1, 1)
        inv2[low:high] = 1.0 / ((x_sum + y_sum) + (z_term + roll(z_term, -1, 2)))

        x_low = f2[0, low:high]
        x_low = jnp.where(half, x_low, roll(x_low, 64, 2))
        tmp2[0, low:high] = x_low + roll(x_low, -1, 2)
        y_both = y_term + roll(y_term, 64, 2)
        tmp2[1, low:high] = y_both + roll(y_both, -1, 2)
        tmp2[2, low:high] = z_term + roll(z_term, 64, 2)
    first16, second16 = pl.ds(0, 16, stride=2), pl.ds(1, 16, stride=2)
    f3[0] = 0.125 * (tmp2[0, :, first16, :] + tmp2[0, :, second16, :])
    f3[1] = 0.125 * tmp2[1, :, first16, :]
    f3[2] = 0.125 * (tmp2[2, :, first16, :] + tmp2[2, :, second16, :])
    for low, high in chunks(2, 13, 6):
        terms = f3[0, low : high + 1]
        y_term, z_term = f3[1, low:high], f3[2, low:high]
        inv3[low:high] = 1.0 / (
            (terms[:-1] + terms[1:] + (y_term + roll(y_term, -1, 1)))
            + (z_term + roll(z_term, -2, 2))
        )

    for copy in x0_copies:
        copy.wait_recv()
    y0_copies = send_y(2)
    for copy in gby_copies:
        copy.wait_recv()
    for s in range(count_y):
        b2[:, 4 * s : 4 * s + 4, :] = g2b[s]

    for i in range(15):
        x2a[i] = inv2[i] * b2[i] * (1.0 / CENTER)

    def step_2(old, new, low, high, step, before, after=None):
        keep_old, keep_new = STEPS[step]

        def emit(i, applied, here):
            r = b2[i] - applied
            d = keep_old * before[i] + keep_new * (inv2[i] * r)
            if after is not None:
                after[i] = d
            new[i] = here + d

        sweep_2(old, f2, low, high, emit)

    step_2(x2a, x2b, 1, 14, 0, x2a, d2)
    step_2(x2b, x2a, 1, 14, 1, d2)

    def residual_2(i, applied, here):
        r = b2[i] - applied
        r = r + roll(r, 64, 1)
        tmp2[0, i] = r + roll(r, -1, 1)

    sweep_2(x2a, f2, 2, 13, residual_2)
    b3[2:13] = 0.125 * (tmp2[0, 2:13, first16, :] + tmp2[0, 2:13, second16, :])

    for i in range(2, 13):
        x3a[i] = inv3[i] * b3[i] * (1.0 / CENTER)

    def step_3(old, new, low, high, step, before, after=None):
        keep_old, keep_new = STEPS[step]

        def emit(i, applied, here):
            r = b3[i] - applied
            d = keep_old * before[i] + keep_new * (inv3[i] * r)
            if after is not None:
                after[i] = d
            new[i] = here + d

        sweep_3(old, f3, low, high, emit)

    step_3(x3a, x3b, 3, 12, 0, x3a, d3)
    step_3(x3b, x3a, 4, 11, 1, d3)

    e = x3a[4:11]
    e = jnp.where((lane_of(e.shape) & 1) == 0, e, roll(e, 1, 2))
    dup2[4:11, first16, :] = e
    dup2[4:11, second16, :] = e
    for i in range(4, 11):
        x2b[i] = x2a[i] + dup2[i]
    x2b[3] = x2a[3]
    x2b[11] = x2a[11]

    def first_up_2(i, applied, here):
        d = inv2[i] * (b2[i] - applied) * (1.0 / CENTER)
        d2[i] = d
        x2a[i] = here + d

    sweep_2(x2b, f2, 4, 11, first_up_2)
    step_2(x2a, x2b, 5, 10, 0, d2, d2)
    x2b[4] = x2a[4]
    x2b[10] = x2a[10]
    step_2(x2b, x2a, 5, 10, 1, d2)

    def in_spread(row, column):
        return ((((column & 127) >> 1) + 16) & 63) + 64 * (column >> 7) == row

    e = dot(x2a[5:10, 0:16, :].reshape(80, 128), select_matrix((128, 256), in_spread))
    for p in range(2):
        value = e[:, 128 * p : 128 * p + 128].reshape(5, 16, 128)
        dup21[p, :, first16, :] = value
        dup21[p, :, second16, :] = value
    for i in range(3, 17):
        x1b[i] = x1a[i] + dup21[(i // 2) % 2, i // 4, 0:24, :]

    def first_up_1(i, applied, here):
        d = inv1[i] * (b1[i] - applied) * (1.0 / CENTER)
        d1[i] = d
        x1a[i] = here + d

    sweep_1(x1b, f1, 4, 16, first_up_1)
    step_1(x1a, x1b, 5, 15, 0, d1, d1)
    step_1(x1b, x1a, 6, 14, 1, d1)

    drain()
    place_y(2, y0_copies)
    e = x1a[6:14]
    dup1[:, pl.ds(0, 24, stride=2), :] = e
    dup1[:, pl.ds(1, 24, stride=2), :] = e
    lower = lax.broadcasted_iota(jnp.int32, (8, 128), 0) < 4
    for i in range(1, 15):
        j = i // 2
        brick = dup1[j, 16:32, :]
        edge = jnp.where(lower, dup1[j, 32:40, :], dup1[j, 8:16, :])
        for t in range(2):
            xb[i, t, 0:16, :] = best[i, t, 0:16, :] + brick
            xb[i, t, 16:24, :] = best[i, t, 16:24, :] + edge

    def first_up_0(i, applied, here):
        for t in range(2):
            d = inv[i, t] * (source[i, t] - applied[t]) * (1.0 / CENTER)
            dd[i, t] = d
            xa[i, t] = here[t] + d

    sweep_0(xb, faces0, 2, 14, first_up_0)
    step_0(xa, xb, 3, 13, 0, dd, dd)

    def to_own(i, t, value):
        own[t, i - 4] = value[0:16]

    step_0(xb, None, 4, 12, 1, dd, None, to_own)

    def joined(row, column):
        return ((row & 127) < 64) & (column == 2 * (row & 127) + (row >> 7))

    cells = side_by_side(own[0].reshape(128, 128), own[1].reshape(128, 128))
    result = dot(cells, select_matrix((256, 128), joined))
    out_ref[...] = result.reshape(8, 16, 128)


def solution(mesh):
    sizes = (mesh.shape["gx"], mesh.shape["gy"], mesh.shape["gz"])
    count_x, count_y, _ = sizes
    vmem = lambda *shape: pltpu.VMEM(shape, F32)
    sems = lambda count: pltpu.SemaphoreType.DMA((2, count))
    fine = (16, 2, 24, 128)
    level1 = (20, 24, 128)
    level2 = (16, 32, 128)
    level3 = (16, 16, 128)
    scratch = [
        vmem(2, 8, 16, 128),
        vmem(2, 8, 16, 128),
        vmem(2, 2, 4, 16, 128),
        vmem(2, 2, 4, 16, 128),
        vmem(3, *fine),
        vmem(3, 2, 16, 2, 4, 128),
        vmem(3, 2, 16, 2, 4, 128),
        vmem(*fine),
        vmem(*fine),
        vmem(*fine),
        vmem(*fine),
        vmem(*fine),
        vmem(*fine),
        vmem(*fine),
        vmem(3, 4, 16, 128),
        vmem(20, 3, 24, 128),
        vmem(*level1),
        vmem(*level1),
        vmem(*level1),
        vmem(*level1),
        vmem(*level1),
        vmem(3, 5, 8, 128),
        vmem(8, 48, 128),
        vmem(count_y, count_x, 3, 4, 128),
        vmem(count_y, count_x, 4, 128),
        vmem(3, *level2),
        vmem(*level2),
        vmem(*level2),
        vmem(*level2),
        vmem(*level2),
        vmem(*level2),
        vmem(3, *level2),
        vmem(3, *level3),
        vmem(*level3),
        vmem(*level3),
        vmem(*level3),
        vmem(*level3),
        vmem(*level3),
        vmem(*level2),
        vmem(2, 5, 32, 128),
        pltpu.SemaphoreType.DMA((2,)),
        sems(4),
        sems(6),
        sems(6),
        sems(12),
        sems(4),
        sems(2),
        sems(4),
        sems(2),
        sems(2),
        sems(2 * count_y),
        sems(4),
        sems(count_y - 1),
    ]

    def shards(pressure_source, conductivity):
        return pl.pallas_call(
            functools.partial(kernel, sizes),
            out_shape=jax.ShapeDtypeStruct((8, 16, 128), F32),
            in_specs=[pl.BlockSpec(memory_space=pltpu.HBM)] * 2,
            out_specs=pl.BlockSpec(memory_space=pltpu.VMEM),
            scratch_shapes=scratch,
            compiler_params=pltpu.CompilerParams(
                collective_id=0, has_side_effects=True, vmem_limit_bytes=55136 * 1024
            ),
        )(pressure_source, conductivity)

    placed = (P("gx", "gy", "gz"), P("gx", "gy", "gz"))
    return jax.shard_map(
        shards, mesh=mesh, in_specs=placed, out_specs=P("gx", "gy", "gz"), check_vma=False
    )
```

```python
import functools

import jax
import jax.numpy as jnp
from jax import lax
from jax.experimental import pallas as pl
from jax.experimental.pallas import tpu as pltpu
from jax.sharding import PartitionSpec as P

MESH = pl.DeviceIdType.MESH
F32 = jnp.float32

CENTER = 1.125
RADIUS = 0.875
RATIO = CENTER / RADIUS
RHO0 = 1.0 / RATIO
RHO1 = 1.0 / (2.0 * RATIO - RHO0)
RHO2 = 1.0 / (2.0 * RATIO - RHO1)
STEPS = ((RHO1 * RHO0, 2.0 * RHO1 / RADIUS), (RHO2 * RHO1, 2.0 * RHO2 / RADIUS))


def roll(value, shift, axis):
    return pltpu.roll(value, shift % value.shape[axis], axis)


def lane_of(shape):
    return lax.broadcasted_iota(jnp.int32, shape, len(shape) - 1)


def select_matrix(shape, holds):
    row = lax.broadcasted_iota(jnp.int32, shape, 0)
    column = lax.broadcasted_iota(jnp.int32, shape, 1)
    return jnp.where(holds(row, column), 1.0, 0.0).astype(jnp.bfloat16)


def dot(a, ones):
    high = a.astype(jnp.bfloat16)
    rest = a - high.astype(F32)
    middle = rest.astype(jnp.bfloat16)
    low = (rest - middle.astype(F32)).astype(jnp.bfloat16)
    parts = [jnp.dot(part, ones, preferred_element_type=F32) for part in (low, middle, high)]
    return (parts[0] + parts[1]) + parts[2]


def side_by_side(a, b):
    return jnp.concatenate([a, b], axis=1)


def harmonic(one_side, other_side):
    return 2.0 * one_side * other_side / (one_side + other_side)


def chunks(low, high, size):
    return [(start, min(start + size, high)) for start in range(low, high, size)]


def sweep_0(field, faces, low, high, emit):
    face_x, face_y, face_z = faces
    both = range(2)
    here = [field[low, t] for t in both]
    flux = [face_x[low, t] * (here[t] - field[low - 1, t]) for t in both]
    for i in range(low, high):
        after = [field[i + 1, t] for t in both]
        upper = [face_x[i + 1, t] * (after[t] - here[t]) for t in both]
        result = []
        for t in both:
            side = face_y[i, t] * (here[t] - roll(here[t], 1, 0))
            result.append((flux[t] - upper[t]) + (side - roll(side, -1, 0)))
        even = face_z[i, 0] * (here[0] - roll(here[1], 1, 1))
        odd = face_z[i, 1] * (here[1] - here[0])
        emit(i, [result[0] + (even - odd), result[1] + (odd - roll(even, -1, 1))], here)
        here, flux = after, upper


def sweep_1(field, faces, low, high, emit):
    here = field[low]
    flux = faces[low, 0] * (here - field[low - 1])
    for i in range(low, high):
        after = field[i + 1]
        upper = faces[i + 1, 0] * (after - here)
        side = faces[i, 1] * (here - roll(here, 1, 0))
        result = (flux - upper) + (side - roll(side, -1, 0))
        side = faces[i, 2] * (here - roll(here, 1, 1))
        emit(i, result + (side - roll(side, -1, 1)), here)
        here, flux = after, upper


def sweep_2(field, faces, low, high, emit):
    half = lane_of(field.shape[1:]) < 64
    before, here = roll(field[low - 1], 64, 1), field[low]
    turned = roll(here, 64, 1)
    flux = faces[0, low] * (here - jnp.where(half, before, turned))
    flux_turned = roll(flux, 64, 1)
    for i in range(low, high):
        after = field[i + 1]
        after_turned = roll(after, 64, 1)
        upper = faces[0, i + 1] * (after - jnp.where(half, turned, after_turned))
        upper_turned = roll(upper, 64, 1)
        result = flux - jnp.where(half, flux_turned, upper_turned)
        side = faces[1, i] * (here - roll(here, 1, 0))
        result = result + (side - roll(side, -1, 0))
        side = faces[2, i] * (here - roll(here, 1, 1))
        emit(i, result + (side - roll(side, -1, 1)), here)
        here, turned, flux, flux_turned = after, after_turned, upper, upper_turned


def sweep_3(field, faces, low, high, emit):
    here = field[low]
    flux = faces[0, low] * (here - field[low - 1])
    for i in range(low, high):
        after = field[i + 1]
        upper = faces[0, i + 1] * (after - here)
        side = faces[1, i] * (here - roll(here, 1, 0))
        result = (flux - upper) + (side - roll(side, -1, 0))
        side = faces[2, i] * (here - roll(here, 2, 1))
        emit(i, result + (side - roll(side, -2, 1)), here)
        here, flux = after, upper


def kernel(
    sizes,
    source_hbm,
    cond_hbm,
    out_ref,
    staged,
    own,
    z_send,
    z_recv,
    win,
    y_send,
    y_recv,
    fx,
    fy,
    fz,
    inv,
    xa,
    xb,
    dd,
    tmp0,
    f1,
    b1,
    inv1,
    x1a,
    x1b,
    d1,
    tmp1,
    dup1,
    g2f,
    g2b,
    last_y,
    f2,
    b2,
    inv2,
    x2a,
    x2b,
    d2,
    tmp2,
    f3,
    f3_send,
    f3_recv,
    b3_send,
    b3_recv,
    b3,
    inv3,
    x3a,
    x3b,
    d3,
    dup2,
    dup21,
    in_sem,
    z_sems,
    x_sems,
    y_sems,
    xy_sems,
    f1x_sems,
    f1y_sems,
    b1x_sems,
    b1y_sems,
    gfx_sems,
    gfy_sems,
    gbx_sems,
    gby_sems,
    f3_sems,
    b3_sems,
):
    count_x, count_y, count_z = sizes
    me_x, me_y, me_z = lax.axis_index("gx"), lax.axis_index("gy"), lax.axis_index("gz")

    def at_x(step):
        return {"gx": lax.rem(me_x + (step + count_x), count_x)}

    def at_y(step):
        return {"gy": lax.rem(me_y + (step + count_y), count_y)}

    def at_z(step):
        return {"gz": lax.rem(me_z + (step + count_z), count_z)}

    loads = [
        pltpu.make_async_copy(cond_hbm, staged.at[0], in_sem.at[0]),
        pltpu.make_async_copy(source_hbm, staged.at[1], in_sem.at[1]),
    ]
    for load in loads:
        load.start()

    barrier = pltpu.get_barrier_semaphore()
    partners = [at_z(1), at_z(-1)]
    partners += [at_x(sign * step) for step in (1, 2, 3, 5, 6) for sign in (1, -1)]
    partners += [at_y(sign * step) for step in (1, 2, 3) for sign in (1, -1)]
    partners += [at_x(dx) | at_y(dy) for dx in (-1, 1) for dy in (-1, 1)]
    for partner in partners:
        pl.semaphore_signal(barrier, inc=1, device_id=partner, device_id_type=MESH)

    pending = []

    def drain():
        for copy in pending:
            copy.wait_send()
        pending.clear()

    def send(source, target, sems, slot, device):
        copy = pltpu.make_async_remote_copy(
            src_ref=source,
            dst_ref=target,
            send_sem=sems.at[0, slot],
            recv_sem=sems.at[1, slot],
            device_id=device,
            device_id_type=MESH,
        )
        copy.start()
        pending.append(copy)
        return copy

    def kept(row, l):
        return row == jnp.where(l < 64, 2 * l, 2 * l - 127)

    def sent(row, l):
        half, q = l >> 7, (l >> 5) & 3
        z = 2 * (l & 31) + 64 * half + jnp.where((q & 1) == 0, half, 1 - half)
        return row == jnp.where(q >= 2, z, z + 128)

    keep = select_matrix((128, 128), kept)
    pass_on = select_matrix((256, 256), sent)
    z_copies = []
    for f in range(2):
        loads[f].wait()
        cells = staged[f].reshape(128, 128)
        halos = dot(side_by_side(cells[:64], cells[64:]), pass_on)
        z_send[f, 0] = halos[:, :128].reshape(4, 16, 128)
        z_send[f, 1] = halos[:, 128:].reshape(4, 16, 128)
        if f == 0:
            pl.semaphore_wait(barrier, len(partners))
        z_copies.append(
            [
                send(z_send.at[f, way], z_recv.at[f, way], z_sems, 2 * f + way, at_z((-1, 1)[way]))
                for way in range(2)
            ]
        )
        own[f] = dot(cells, keep).reshape(8, 16, 128)

    def send_x(f):
        return [
            send(
                win.at[f, 4:8, :, 0:16, :],
                win.at[f, 12:16, :, 0:16, :],
                x_sems,
                2 * f,
                at_x(-1),
            ),
            send(
                win.at[f, 8:12, :, 0:16, :],
                win.at[f, 0:4, :, 0:16, :],
                x_sems,
                2 * f + 1,
                at_x(1),
            ),
        ]

    def send_y(f):
        y_send[f, 0] = win[f, :, :, 0:4, :]
        y_send[f, 1] = win[f, :, :, 12:16, :]
        return [
            send(y_send.at[f, way], y_recv.at[f, way], y_sems, 2 * f + way, at_y((-1, 1)[way]))
            for way in range(2)
        ]

    def send_xy(f):
        copies = send_x(f)
        y_send[f, 0, 4:12] = win[f, 4:12, :, 0:4, :]
        y_send[f, 1, 4:12] = win[f, 4:12, :, 12:16, :]
        for way in range(2):
            for slot, (dx, first, last) in enumerate(((0, 4, 12), (1, 8, 12), (-1, 4, 8))):
                copies.append(
                    send(
                        y_send.at[f, way, first:last],
                        y_recv.at[f, way, first - 8 * dx : last - 8 * dx],
                        xy_sems,
                        6 * f + 3 * way + slot,
                        at_y((-1, 1)[way]) | (at_x(dx) if dx else {}),
                    )
                )
        return copies

    def place_y(f, copies):
        for copy in copies:
            copy.wait_recv()
        win[f, :, :, 16:20, :] = y_recv[f, 0]
        win[f, :, :, 20:24, :] = y_recv[f, 1]

    xy_copies = []
    for f in range(2):
        for copy in z_copies[f]:
            copy.wait_recv()
        lane = lane_of((4, 16, 128))
        for part in range(2):
            mine = own[f, 4 * part : 4 * part + 4]
            above, below = z_recv[f, 0], z_recv[f, 1]
            for t in range(2):
                turn_above = ((0, 96), (64, 32))[part][t]
                turn_below = ((0, 32), (64, 96))[part][t]
                halo = jnp.where(
                    lane < 96,
                    roll(above, turn_above, 2) if turn_above else above,
                    roll(below, turn_below, 2) if turn_below else below,
                )
                win[f, 4 + 4 * part : 8 + 4 * part, t, 0:16, :] = jnp.where(
                    lane < 64, roll(mine, 64, 2) if t else mine, halo
                )
        xy_copies.append(send_xy(f))

    cond, source, best = win.at[0], win.at[1], win.at[2]
    faces0 = (fx, fy, fz)
    brick = slice(0, 16)
    for i in range(4, 12):
        k0, k1 = cond[i, 0, brick, :], cond[i, 1, brick, :]
        fz[i, 0, brick, :] = harmonic(k0, roll(k1, 1, 1))
        fz[i, 1, brick, :] = harmonic(k1, k0)
        if i > 4:
            fx[i, 0, brick, :] = harmonic(k0, cond[i - 1, 0, brick, :])
            fx[i, 1, brick, :] = harmonic(k1, cond[i - 1, 1, brick, :])
    place_y(0, xy_copies[0])
    for t in range(2):
        fx[4, t, brick, :] = harmonic(cond[4, t, brick, :], cond[3, t, brick, :])
    for i in range(4, 12):
        for t in range(2):
            k = cond[i, t]
            fy[i, t] = harmonic(k, roll(k, 1, 0))

    for i in range(4):
        tmp0[0, i] = fx[4 + 2 * i, 0, 0:16, :] + fx[4 + 2 * i, 1, 0:16, :]
        tmp0[1, i] = (fy[4 + 2 * i, 0, 0:16, :] + fy[4 + 2 * i, 1, 0:16, :]) + (
            fy[5 + 2 * i, 0, 0:16, :] + fy[5 + 2 * i, 1, 0:16, :]
        )
        tmp0[2, i] = fz[4 + 2 * i, 0, 0:16, :] + fz[5 + 2 * i, 0, 0:16, :]
    first, second = pl.ds(0, 8, stride=2), pl.ds(1, 8, stride=2)
    f1[8:12, 0, 8:16, :] = 0.125 * (tmp0[0, :, first, :] + tmp0[0, :, second, :])
    f1[8:12, 1, 8:16, :] = 0.125 * tmp0[1, :, first, :]
    f1[8:12, 2, 8:16, :] = 0.125 * (tmp0[2, :, first, :] + tmp0[2, :, second, :])
    f1x_copies = [
        send(
            f1.at[8:12, :, 8:16, :],
            f1.at[8 - 4 * step : 12 - 4 * step, :, 8:16, :],
            f1x_sems,
            slot,
            at_x(step),
        )
        for slot, step in enumerate((-2, 2, -1, 1))
    ]

    def spread_x(ref, first, last, sems, steps):
        return [
            send(ref.at[2, first:last], ref.at[2, first - step : last - step], sems, slot, at_x(step))
            for slot, step in enumerate(steps)
        ]

    def spread_y(ref, sems):
        return [
            send(ref.at[2], ref.at[2 - step], sems, slot, at_y(step))
            for slot, step in enumerate((2, -2, 1, -1))
        ]

    def pass_rows_3(out, into, sems):
        return [
            send(out.at[way], into.at[way], sems, way, at_y((2, -2)[way])) for way in range(2)
        ]

    for i in range(1, 16):
        part = slice(16, 24) if 4 <= i < 12 else slice(0, 24)
        for t in range(2):
            fx[i, t, part, :] = harmonic(cond[i, t, part, :], cond[i - 1, t, part, :])
        if i == 15:
            break
        k0, k1 = cond[i, 0], cond[i, 1]
        if not 4 <= i < 12:
            fy[i, 0] = harmonic(k0, roll(k0, 1, 0))
            fy[i, 1] = harmonic(k1, roll(k1, 1, 0))
        k0, k1 = k0[part], k1[part]
        fz[i, 0, part, :] = harmonic(k0, roll(k1, 1, 1))
        fz[i, 1, part, :] = harmonic(k1, k0)

    for low, high in chunks(1, 15, 2):
        x_sum = [fx[low:high, t] + fx[low + 1 : high + 1, t] for t in range(2)]
        y_sum = [fy[low:high, t] + roll(fy[low:high, t], -1, 1) for t in range(2)]
        z0, z1 = fz[low:high, 0], fz[low:high, 1]
        inv[low:high, 0] = 1.0 / ((x_sum[0] + y_sum[0]) + (z0 + z1))
        inv[low:high, 1] = 1.0 / ((x_sum[1] + y_sum[1]) + (z1 + roll(z0, -1, 2)))

    place_y(1, xy_copies[1])
    for i in range(1, 15):
        for t in range(2):
            xa[i, t] = inv[i, t] * source[i, t] * (1.0 / CENTER)

    def step_0(old, new, low, high, step, before, after=None, target=None):
        keep_old, keep_new = STEPS[step]

        def emit(i, applied, here):
            for t in range(2):
                r = source[i, t] - applied[t]
                d = keep_old * before[i, t] + keep_new * (inv[i, t] * r)
                if after is not None:
                    after[i, t] = d
                if target is None:
                    new[i, t] = here[t] + d
                else:
                    target(i, t, here[t] + d)

        sweep_0(old, faces0, low, high, emit)

    step_0(xa, xb, 2, 14, 0, xa, dd)

    step_0(xb, xa, 3, 13, 1, dd)
    best[4:12, :, 0:16, :] = xa[4:12, :, 0:16, :]
    sums = []

    def residual_0(i, applied, here):
        r = [source[i, t, 0:16, :] - applied[t][:16] for t in range(2)]
        sums.append(r[0] + r[1])
        if i % 2 == 1:
            tmp0[0, (i - 4) // 2] = sums[-2] + sums[-1]

    sweep_0(xa, faces0, 4, 12, residual_0)
    b1[8:12, 8:16, :] = 0.125 * (tmp0[0, :, first, :] + tmp0[0, :, second, :])
    b1x_copies = [
        send(
            b1.at[first:last, 8:16, :],
            b1.at[first - 4 * step : last - 4 * step, 8:16, :],
            b1x_sems,
            slot,
            at_x(step),
        )
        for slot, (step, first, last) in enumerate(
            ((-2, 8, 11), (2, 9, 12), (-1, 8, 12), (1, 8, 12))
        )
    ]


    for copy in f1x_copies:
        copy.wait_recv()
    f1y_copies = [
        send(
            f1.at[:, :, 8:16, :],
            f1.at[:, :, 8 - 8 * step : 16 - 8 * step, :],
            f1y_sems,
            slot,
            at_y(step),
        )
        for slot, step in enumerate((-1, 1))
    ]

    def in_pack(row, column):
        return ((((row & 127) >> 1) + 16) & 63) + 64 * (row >> 7) == column

    pack = select_matrix((256, 128), in_pack)
    pack_even = select_matrix((256, 128), lambda row, l: ((row & 1) == 0) & in_pack(row, l))
    first4, second4 = pl.ds(0, 4, stride=2), pl.ds(1, 4, stride=2)

    def packed(pieces, matrix):
        whole = [jnp.concatenate(piece, axis=0) for piece in pieces]
        result = dot(side_by_side(*whole), matrix)
        return result.reshape(len(pieces[0]), 8, 128)

    g2f[2, 15] = jnp.ones((3, 4, 128), F32)
    g2b[2, 15] = jnp.zeros((4, 128), F32)
    mine = slice(8, 16)
    tmp1[0] = packed([[f1[4 * i + 2 * p, 0, mine, :] for i in range(5)] for p in range(2)], pack)
    for f in (1, 2):
        pieces = [
            [f1[4 * i + 2 * p, f, mine, :] + f1[4 * i + 2 * p + 1, f, mine, :] for i in range(5)]
            for p in range(2)
        ]
        tmp1[f] = packed(pieces, (None, pack, pack_even)[f])
    g2f[2, 5:10, 0] = 0.125 * (tmp1[0, :, first4, :] + tmp1[0, :, second4, :])
    g2f[2, 5:10, 1] = 0.125 * tmp1[1, :, first4, :]
    g2f[2, 5:10, 2] = 0.125 * (tmp1[2, :, first4, :] + tmp1[2, :, second4, :])
    gfx_copies = spread_x(g2f, 5, 10, gfx_sems, (5, -5))

    drain()
    for copy in b1x_copies:
        copy.wait_recv()
    b1y_copies = [
        send(
            b1.at[:, 8:16, :],
            b1.at[:, 8 - 8 * step : 16 - 8 * step, :],
            b1y_sems,
            slot,
            at_y(step),
        )
        for slot, step in enumerate((-1, 1))
    ]
    for copy in f1y_copies:
        copy.wait_recv()
    for low, high in chunks(1, 19, 6):
        x_sum = f1[low:high, 0] + f1[low + 1 : high + 1, 0]
        y_term, z_term = f1[low:high, 1], f1[low:high, 2]
        y_sum = y_term + roll(y_term, -1, 1)
        inv1[low:high] = 1.0 / ((x_sum + y_sum) + (z_term + roll(z_term, -1, 2)))

    for copy in b1y_copies:
        copy.wait_recv()

    for i in range(1, 19):
        x1a[i] = inv1[i] * b1[i] * (1.0 / CENTER)

    def step_1(old, new, low, high, step, before, after=None):
        keep_old, keep_new = STEPS[step]

        def emit(i, applied, here):
            r = b1[i] - applied
            d = keep_old * before[i] + keep_new * (inv1[i] * r)
            if after is not None:
                after[i] = d
            new[i] = here + d

        sweep_1(old, f1, low, high, emit)

    step_1(x1a, x1b, 2, 18, 0, x1a, d1)
    for copy in gfx_copies:
        copy.wait_recv()
    gfy_copies = spread_y(g2f, gfy_sems)
    gfy_copies.append(send(g2f.at[2, :, 1], last_y, gfy_sems, 4, at_y(-3)))
    step_1(x1b, x1a, 3, 17, 1, d1)
    r = {}

    def residual_1(i, applied, here):
        r[i - 4] = (b1[i] - applied)[8:16]

    sweep_1(x1a, f1, 4, 16, residual_1)
    tmp1[0, 0:3] = packed(
        [[r[4 * i + 2 * p] + r[4 * i + 2 * p + 1] for i in range(3)] for p in range(2)], pack
    )
    g2b[2, 6:9] = 0.125 * (tmp1[0, 0:3, first4, :] + tmp1[0, 0:3, second4, :])
    gbx_copies = spread_x(g2b, 6, 9, gbx_sems, (6, -6, 3, -3))
    x0_copies = send_x(2)
    for copy in gbx_copies:
        copy.wait_recv()
    gby_copies = spread_y(g2b, gby_sems)

    for copy in gfy_copies:
        copy.wait_recv()
    for f in range(3):
        for s in range(5):
            f2[f, :, 4 * s : 4 * s + 4, :] = g2f[s, :, f]
        f2[f, :, 20:24, :] = last_y[...] if f == 1 else jnp.ones((16, 4, 128), F32)
    for low, high in chunks(0, 15, 3):
        terms = f2[0, low : high + 1]
        turned = roll(terms, 64, 2)
        half = lane_of(terms[1:].shape) < 64
        x_sum = terms[:-1] + jnp.where(half, turned[:-1], turned[1:])
        y_term, z_term = f2[1, low:high], f2[2, low:high]
        y_sum = y_term + roll(y_term, -1, 1)
        inv2[low:high] = 1.0 / ((x_sum + y_sum) + (z_term + roll(z_term, -1, 2)))

        x_low = f2[0, low:high]
        x_low = jnp.where(half, x_low, roll(x_low, 64, 2))
        tmp2[0, low:high] = x_low + roll(x_low, -1, 2)
        y_both = y_term + roll(y_term, 64, 2)
        tmp2[1, low:high] = y_both + roll(y_both, -1, 2)
        tmp2[2, low:high] = z_term + roll(z_term, 64, 2)
    first_8, second_8 = pl.ds(4, 8, stride=2), pl.ds(5, 8, stride=2)
    f3[:, :, 8:16, :] = jnp.ones((3, 16, 8, 128), F32)
    f3[0, :, 0:8, :] = 0.125 * (tmp2[0, :, first_8, :] + tmp2[0, :, second_8, :])
    f3[1, :, 0:8, :] = 0.125 * tmp2[1, :, first_8, :]
    f3[2, :, 0:8, :] = 0.125 * (tmp2[2, :, first_8, :] + tmp2[2, :, second_8, :])
    f3_send[0] = f3[:, 2:14, 0:4, :]
    f3_send[1] = f3[:, 2:14, 2:6, :]
    f3_copies = pass_rows_3(f3_send, f3_recv, f3_sems)

    for copy in gby_copies:
        copy.wait_recv()
    for s in range(5):
        b2[:, 4 * s : 4 * s + 4, :] = g2b[s]
    b2[:, 20:24, :] = jnp.zeros((16, 4, 128), F32)

    for i in range(15):
        x2a[i] = inv2[i] * b2[i] * (1.0 / CENTER)

    def step_2(old, new, low, high, step, before, after=None):
        keep_old, keep_new = STEPS[step]

        def emit(i, applied, here):
            r = b2[i] - applied
            d = keep_old * before[i] + keep_new * (inv2[i] * r)
            if after is not None:
                after[i] = d
            new[i] = here + d

        sweep_2(old, f2, low, high, emit)

    step_2(x2a, x2b, 1, 14, 0, x2a, d2)
    step_2(x2b, x2a, 1, 14, 1, d2)

    def residual_2(i, applied, here):
        r = b2[i] - applied
        r = r + roll(r, 64, 1)
        tmp2[0, i] = r + roll(r, -1, 1)

    sweep_2(x2a, f2, 2, 13, residual_2)
    restricted = 0.125 * (tmp2[0, 2:13, first_8, :] + tmp2[0, 2:13, second_8, :])
    b3[2:13, 0:8, :] = restricted
    b3[2:13, 8:16, :] = jnp.zeros((11, 8, 128), F32)
    b3_send[0] = restricted[:, 0:4]
    b3_send[1] = b3[2:13, 2:6, :]
    b3_copies = pass_rows_3(b3_send, b3_recv, b3_sems)

    for copy in x0_copies:
        copy.wait_recv()
    y0_copies = send_y(2)
    for copy in f3_copies:
        copy.wait_recv()
    f3[:, 2:14, 12:16, :] = f3_recv[0]
    f3[:, 2:14, 6:10, :] = f3_recv[1]
    for low, high in chunks(2, 13, 6):
        terms = f3[0, low : high + 1]
        y_term, z_term = f3[1, low:high], f3[2, low:high]
        inv3[low:high] = 1.0 / (
            (terms[:-1] + terms[1:] + (y_term + roll(y_term, -1, 1)))
            + (z_term + roll(z_term, -2, 2))
        )

    for copy in b3_copies:
        copy.wait_recv()
    b3[2:13, 12:16, :] = b3_recv[0]
    b3[2:13, 6:10, :] = b3_recv[1]

    for i in range(2, 13):
        x3a[i] = inv3[i] * b3[i] * (1.0 / CENTER)

    def step_3(old, new, low, high, step, before, after=None):
        keep_old, keep_new = STEPS[step]

        def emit(i, applied, here):
            r = b3[i] - applied
            d = keep_old * before[i] + keep_new * (inv3[i] * r)
            if after is not None:
                after[i] = d
            new[i] = here + d

        sweep_3(old, f3, low, high, emit)

    step_3(x3a, x3b, 3, 12, 0, x3a, d3)
    step_3(x3b, x3a, 4, 11, 1, d3)

    e = x3a[4:11]
    e = jnp.where((lane_of(e.shape) & 1) == 0, e, roll(e, 1, 2))
    e = roll(e, 2, 1)[:, 0:12]
    dup2[4:11, pl.ds(0, 12, stride=2), :] = e
    dup2[4:11, pl.ds(1, 12, stride=2), :] = e
    for i in range(4, 11):
        x2b[i] = x2a[i] + dup2[i]
    x2b[3] = x2a[3]
    x2b[11] = x2a[11]

    def first_up_2(i, applied, here):
        d = inv2[i] * (b2[i] - applied) * (1.0 / CENTER)
        d2[i] = d
        x2a[i] = here + d

    sweep_2(x2b, f2, 4, 11, first_up_2)
    step_2(x2a, x2b, 5, 10, 0, d2, d2)
    x2b[4] = x2a[4]
    x2b[10] = x2a[10]
    step_2(x2b, x2a, 5, 10, 1, d2)

    def in_spread(row, column):
        return ((((column & 127) >> 1) + 16) & 63) + 64 * (column >> 7) == row

    e = dot(x2a[5:10].reshape(120, 128), select_matrix((128, 256), in_spread))
    for p in range(2):
        value = e[:, 128 * p : 128 * p + 128].reshape(5, 24, 128)
        dup21[p, :, pl.ds(0, 24, stride=2), :] = value
        dup21[p, :, pl.ds(1, 24, stride=2), :] = value
    for i in range(3, 17):
        x1b[i] = x1a[i] + dup21[(i // 2) % 2, i // 4, 8:32, :]

    def first_up_1(i, applied, here):
        d = inv1[i] * (b1[i] - applied) * (1.0 / CENTER)
        d1[i] = d
        x1a[i] = here + d

    sweep_1(x1b, f1, 4, 16, first_up_1)
    step_1(x1a, x1b, 5, 15, 0, d1, d1)
    step_1(x1b, x1a, 6, 14, 1, d1)

    drain()
    place_y(2, y0_copies)
    e = x1a[6:14]
    dup1[:, pl.ds(0, 24, stride=2), :] = e
    dup1[:, pl.ds(1, 24, stride=2), :] = e
    lower = lax.broadcasted_iota(jnp.int32, (8, 128), 0) < 4
    for i in range(1, 15):
        j = i // 2
        brick = dup1[j, 16:32, :]
        edge = jnp.where(lower, dup1[j, 32:40, :], dup1[j, 8:16, :])
        for t in range(2):
            xb[i, t, 0:16, :] = best[i, t, 0:16, :] + brick
            xb[i, t, 16:24, :] = best[i, t, 16:24, :] + edge

    def first_up_0(i, applied, here):
        for t in range(2):
            d = inv[i, t] * (source[i, t] - applied[t]) * (1.0 / CENTER)
            dd[i, t] = d
            xa[i, t] = here[t] + d

    sweep_0(xb, faces0, 2, 14, first_up_0)
    step_0(xa, xb, 3, 13, 0, dd, dd)

    def to_own(i, t, value):
        own[t, i - 4] = value[0:16]

    step_0(xb, None, 4, 12, 1, dd, None, to_own)

    def joined(row, column):
        return ((row & 127) < 64) & (column == 2 * (row & 127) + (row >> 7))

    cells = side_by_side(own[0].reshape(128, 128), own[1].reshape(128, 128))
    result = dot(cells, select_matrix((256, 128), joined))
    out_ref[...] = result.reshape(8, 16, 128)


def solution(mesh):
    sizes = (mesh.shape["gx"], mesh.shape["gy"], mesh.shape["gz"])
    count_x = sizes[0]
    vmem = lambda *shape: pltpu.VMEM(shape, F32)
    sems = lambda count: pltpu.SemaphoreType.DMA((2, count))
    fine = (16, 2, 24, 128)
    level1 = (20, 24, 128)
    level2 = (16, 24, 128)
    level3 = (16, 16, 128)
    scratch = [
        vmem(2, 8, 16, 128),
        vmem(2, 8, 16, 128),
        vmem(2, 2, 4, 16, 128),
        vmem(2, 2, 4, 16, 128),
        vmem(3, *fine),
        vmem(3, 2, 16, 2, 4, 128),
        vmem(3, 2, 16, 2, 4, 128),
        vmem(*fine),
        vmem(*fine),
        vmem(*fine),
        vmem(*fine),
        vmem(*fine),
        vmem(*fine),
        vmem(*fine),
        vmem(3, 4, 16, 128),
        vmem(20, 3, 24, 128),
        vmem(*level1),
        vmem(*level1),
        vmem(*level1),
        vmem(*level1),
        vmem(*level1),
        vmem(3, 5, 8, 128),
        vmem(8, 48, 128),
        vmem(5, count_x, 3, 4, 128),
        vmem(5, count_x, 4, 128),
        vmem(count_x, 4, 128),
        vmem(3, *level2),
        vmem(*level2),
        vmem(*level2),
        vmem(*level2),
        vmem(*level2),
        vmem(*level2),
        vmem(3, *level2),
        vmem(3, *level3),
        vmem(2, 3, 12, 4, 128),
        vmem(2, 3, 12, 4, 128),
        vmem(2, 11, 4, 128),
        vmem(2, 11, 4, 128),
        vmem(*level3),
        vmem(*level3),
        vmem(*level3),
        vmem(*level3),
        vmem(*level3),
        vmem(*level2),
        vmem(2, 5, 48, 128),
        pltpu.SemaphoreType.DMA((2,)),
        sems(4),
        sems(6),
        sems(6),
        sems(12),
        sems(4),
        sems(2),
        sems(4),
        sems(2),
        sems(2),
        sems(5),
        sems(4),
        sems(4),
        sems(2),
        sems(2),
    ]

    def shards(pressure_source, conductivity):
        return pl.pallas_call(
            functools.partial(kernel, sizes),
            out_shape=jax.ShapeDtypeStruct((8, 16, 128), F32),
            in_specs=[pl.BlockSpec(memory_space=pltpu.HBM)] * 2,
            out_specs=pl.BlockSpec(memory_space=pltpu.VMEM),
            scratch_shapes=scratch,
            compiler_params=pltpu.CompilerParams(
                collective_id=0, has_side_effects=True, vmem_limit_bytes=55136 * 1024
            ),
        )(pressure_source, conductivity)

    placed = (P("gx", "gy", "gz"), P("gx", "gy", "gz"))
    return jax.shard_map(
        shards, mesh=mesh, in_specs=placed, out_specs=P("gx", "gy", "gz"), check_vma=False
    )
```

```python
import functools

import jax
import jax.numpy as jnp
from jax import lax
from jax.experimental import pallas as pl
from jax.experimental.pallas import tpu as pltpu
from jax.sharding import PartitionSpec as P

MESH = pl.DeviceIdType.MESH
F32 = jnp.float32

CENTER = 1.125
RADIUS = 0.875
RATIO = CENTER / RADIUS
RHO0 = 1.0 / RATIO
RHO1 = 1.0 / (2.0 * RATIO - RHO0)
RHO2 = 1.0 / (2.0 * RATIO - RHO1)
STEPS = ((RHO1 * RHO0, 2.0 * RHO1 / RADIUS), (RHO2 * RHO1, 2.0 * RHO2 / RADIUS))


def roll(value, shift, axis):
    return pltpu.roll(value, shift % value.shape[axis], axis)


def lane_of(shape):
    return lax.broadcasted_iota(jnp.int32, shape, len(shape) - 1)


def select_matrix(shape, holds):
    row = lax.broadcasted_iota(jnp.int32, shape, 0)
    column = lax.broadcasted_iota(jnp.int32, shape, 1)
    return jnp.where(holds(row, column), 1.0, 0.0).astype(jnp.bfloat16)


def dot(a, ones):
    high = a.astype(jnp.bfloat16)
    rest = a - high.astype(F32)
    middle = rest.astype(jnp.bfloat16)
    low = (rest - middle.astype(F32)).astype(jnp.bfloat16)
    parts = [jnp.dot(part, ones, preferred_element_type=F32) for part in (low, middle, high)]
    return (parts[0] + parts[1]) + parts[2]


def side_by_side(a, b):
    return jnp.concatenate([a, b], axis=1)


def harmonic(one_side, other_side):
    return 2.0 * one_side * other_side / (one_side + other_side)


def chunks(low, high, size):
    return [(start, min(start + size, high)) for start in range(low, high, size)]


def sweep_0(field, faces, low, high, emit):
    face_x, face_y, face_z = faces
    both = range(2)
    here = [field[low, t] for t in both]
    flux = [face_x[low, t] * (here[t] - field[low - 1, t]) for t in both]
    for i in range(low, high):
        after = [field[i + 1, t] for t in both]
        upper = [face_x[i + 1, t] * (after[t] - here[t]) for t in both]
        result = []
        for t in both:
            side = face_y[i, t] * (here[t] - roll(here[t], 1, 0))
            result.append((flux[t] - upper[t]) + (side - roll(side, -1, 0)))
        even = face_z[i, 0] * (here[0] - roll(here[1], 1, 1))
        odd = face_z[i, 1] * (here[1] - here[0])
        emit(i, [result[0] + (even - odd), result[1] + (odd - roll(even, -1, 1))], here)
        here, flux = after, upper


def sweep_1(field, faces, low, high, emit):
    here = field[low]
    flux = faces[low, 0] * (here - field[low - 1])
    for i in range(low, high):
        after = field[i + 1]
        upper = faces[i + 1, 0] * (after - here)
        side = faces[i, 1] * (here - roll(here, 1, 0))
        result = (flux - upper) + (side - roll(side, -1, 0))
        side = faces[i, 2] * (here - roll(here, 1, 1))
        emit(i, result + (side - roll(side, -1, 1)), here)
        here, flux = after, upper


def sweep_2(field, faces, low, high, emit):
    half = lane_of(field.shape[1:]) < 64
    before, here = roll(field[low - 1], 64, 1), field[low]
    turned = roll(here, 64, 1)
    flux = faces[0, low] * (here - jnp.where(half, before, turned))
    flux_turned = roll(flux, 64, 1)
    for i in range(low, high):
        after = field[i + 1]
        after_turned = roll(after, 64, 1)
        upper = faces[0, i + 1] * (after - jnp.where(half, turned, after_turned))
        upper_turned = roll(upper, 64, 1)
        result = flux - jnp.where(half, flux_turned, upper_turned)
        side = faces[1, i] * (here - roll(here, 1, 0))
        result = result + (side - roll(side, -1, 0))
        side = faces[2, i] * (here - roll(here, 1, 1))
        emit(i, result + (side - roll(side, -1, 1)), here)
        here, turned, flux, flux_turned = after, after_turned, upper, upper_turned


def sweep_3(field, faces, low, high, emit):
    here = field[low]
    flux = faces[0, low] * (here - field[low - 1])
    for i in range(low, high):
        after = field[i + 1]
        upper = faces[0, i + 1] * (after - here)
        side = faces[1, i] * (here - roll(here, 1, 0))
        result = (flux - upper) + (side - roll(side, -1, 0))
        side = faces[2, i] * (here - roll(here, 2, 1))
        emit(i, result + (side - roll(side, -2, 1)), here)
        here, flux = after, upper


def kernel(
    sizes,
    source_hbm,
    cond_hbm,
    out_ref,
    staged,
    own,
    z_send,
    z_recv,
    win,
    y_send,
    y_recv,
    fx,
    fy,
    fz,
    inv,
    xa,
    xb,
    dd,
    tmp0,
    f1,
    b1,
    inv1,
    x1a,
    x1b,
    d1,
    tmp1,
    dup1,
    g2f,
    g2b,
    f2,
    b2,
    inv2,
    x2a,
    x2b,
    d2,
    tmp2,
    f3,
    b3,
    inv3,
    x3a,
    x3b,
    d3,
    dup2,
    dup21,
    in_sem,
    z_sems,
    x_sems,
    y_sems,
    xy_sems,
    f1x_sems,
    f1y_sems,
    b1_sems,
    gfx_sems,
    gfy_sems,
    gbx_sems,
    gby_sems,
):
    count_x, count_y, count_z = sizes
    me_x, me_y, me_z = lax.axis_index("gx"), lax.axis_index("gy"), lax.axis_index("gz")

    def at_x(step):
        return {"gx": lax.rem(me_x + (step + count_x), count_x)}

    def at_y(step):
        return {"gy": lax.rem(me_y + (step + count_y), count_y)}

    def at_z(step):
        return {"gz": lax.rem(me_z + (step + count_z), count_z)}

    loads = [
        pltpu.make_async_copy(cond_hbm, staged.at[0], in_sem.at[0]),
        pltpu.make_async_copy(source_hbm, staged.at[1], in_sem.at[1]),
    ]
    for load in loads:
        load.start()

    barrier = pltpu.get_barrier_semaphore()
    partners = [at_z(1), at_z(-1)]
    partners += [at_x(sign * step) for step in (1, 2, 3, 5, 6) for sign in (1, -1)]
    partners += [at_y(step) for step in range(1, count_y)]
    partners += [at_x(dx) | at_y(dy) for dx in (-2, -1, 1, 2) for dy in (-1, 1)]
    for partner in partners:
        pl.semaphore_signal(barrier, inc=1, device_id=partner, device_id_type=MESH)

    pending = []

    def drain(count):
        for copy in pending[:count]:
            copy.wait_send()
        del pending[:count]

    def send(source, target, sems, slot, device):
        copy = pltpu.make_async_remote_copy(
            src_ref=source,
            dst_ref=target,
            send_sem=sems.at[0, slot],
            recv_sem=sems.at[1, slot],
            device_id=device,
            device_id_type=MESH,
        )
        copy.start()
        pending.append(copy)
        return copy

    def kept(row, l):
        return row == jnp.where(l < 64, 2 * l, 2 * l - 127)

    def sent(row, l):
        half, q = l >> 7, (l >> 5) & 3
        z = 2 * (l & 31) + 64 * half + jnp.where((q & 1) == 0, half, 1 - half)
        return row == jnp.where(q >= 2, z, z + 128)

    keep = select_matrix((128, 128), kept)
    pass_on = select_matrix((256, 256), sent)
    z_copies = []
    for f in range(2):
        loads[f].wait()
        cells = staged[f].reshape(128, 128)
        halos = dot(side_by_side(cells[:64], cells[64:]), pass_on)
        z_send[f, 0] = halos[:, :128].reshape(4, 16, 128)
        z_send[f, 1] = halos[:, 128:].reshape(4, 16, 128)
        if f == 0:
            pl.semaphore_wait(barrier, len(partners))
        z_copies.append(
            [
                send(z_send.at[f, way], z_recv.at[f, way], z_sems, 2 * f + way, at_z((-1, 1)[way]))
                for way in range(2)
            ]
        )
        own[f] = dot(cells, keep).reshape(8, 16, 128)

    def send_x(f):
        return [
            send(
                win.at[f, 4:8, :, 0:16, :],
                win.at[f, 12:16, :, 0:16, :],
                x_sems,
                2 * f,
                at_x(-1),
            ),
            send(
                win.at[f, 8:12, :, 0:16, :],
                win.at[f, 0:4, :, 0:16, :],
                x_sems,
                2 * f + 1,
                at_x(1),
            ),
        ]

    def send_y(f):
        y_send[f, 0] = win[f, :, :, 0:4, :]
        y_send[f, 1] = win[f, :, :, 12:16, :]
        return [
            send(y_send.at[f, way], y_recv.at[f, way], y_sems, 2 * f + way, at_y((-1, 1)[way]))
            for way in range(2)
        ]

    def send_xy(f):
        copies = send_x(f)
        y_send[f, 0, 4:12] = win[f, 4:12, :, 0:4, :]
        y_send[f, 1, 4:12] = win[f, 4:12, :, 12:16, :]
        for way in range(2):
            for slot, (dx, first, last) in enumerate(((0, 4, 12), (1, 8, 12), (-1, 4, 8))):
                copies.append(
                    send(
                        y_send.at[f, way, first:last],
                        y_recv.at[f, way, first - 8 * dx : last - 8 * dx],
                        xy_sems,
                        6 * f + 3 * way + slot,
                        at_y((-1, 1)[way]) | (at_x(dx) if dx else {}),
                    )
                )
        return copies

    def place_y(f, copies):
        for copy in copies:
            copy.wait_recv()
        win[f, :, :, 16:20, :] = y_recv[f, 0]
        win[f, :, :, 20:24, :] = y_recv[f, 1]

    xy_copies = []
    for f in range(2):
        for copy in z_copies[f]:
            copy.wait_recv()
        lane = lane_of((4, 16, 128))
        for part in range(2):
            mine = own[f, 4 * part : 4 * part + 4]
            above, below = z_recv[f, 0], z_recv[f, 1]
            for t in range(2):
                turn_above = ((0, 96), (64, 32))[part][t]
                turn_below = ((0, 32), (64, 96))[part][t]
                halo = jnp.where(
                    lane < 96,
                    roll(above, turn_above, 2) if turn_above else above,
                    roll(below, turn_below, 2) if turn_below else below,
                )
                win[f, 4 + 4 * part : 8 + 4 * part, t, 0:16, :] = jnp.where(
                    lane < 64, roll(mine, 64, 2) if t else mine, halo
                )
        xy_copies.append(send_xy(f))
    level_0_sends = len(pending)

    cond, source, best = win.at[0], win.at[1], win.at[2]
    faces0 = (fx, fy, fz)
    brick = slice(0, 16)
    for i in range(4, 12):
        k0, k1 = cond[i, 0, brick, :], cond[i, 1, brick, :]
        fz[i, 0, brick, :] = harmonic(k0, roll(k1, 1, 1))
        fz[i, 1, brick, :] = harmonic(k1, k0)
        if i > 4:
            fx[i, 0, brick, :] = harmonic(k0, cond[i - 1, 0, brick, :])
            fx[i, 1, brick, :] = harmonic(k1, cond[i - 1, 1, brick, :])
    place_y(0, xy_copies[0])
    for t in range(2):
        fx[4, t, brick, :] = harmonic(cond[4, t, brick, :], cond[3, t, brick, :])
    for i in range(4, 12):
        for t in range(2):
            k = cond[i, t]
            fy[i, t] = harmonic(k, roll(k, 1, 0))

    for i in range(4):
        tmp0[0, i] = fx[4 + 2 * i, 0, 0:16, :] + fx[4 + 2 * i, 1, 0:16, :]
        tmp0[1, i] = (fy[4 + 2 * i, 0, 0:16, :] + fy[4 + 2 * i, 1, 0:16, :]) + (
            fy[5 + 2 * i, 0, 0:16, :] + fy[5 + 2 * i, 1, 0:16, :]
        )
        tmp0[2, i] = fz[4 + 2 * i, 0, 0:16, :] + fz[5 + 2 * i, 0, 0:16, :]
    first, second = pl.ds(0, 8, stride=2), pl.ds(1, 8, stride=2)
    f1[8:12, 0, 8:16, :] = 0.125 * (tmp0[0, :, first, :] + tmp0[0, :, second, :])
    f1[8:12, 1, 8:16, :] = 0.125 * tmp0[1, :, first, :]
    f1[8:12, 2, 8:16, :] = 0.125 * (tmp0[2, :, first, :] + tmp0[2, :, second, :])
    f1x_copies = [
        send(
            f1.at[8:12, :, 8:16, :],
            f1.at[8 - 4 * step : 12 - 4 * step, :, 8:16, :],
            f1x_sems,
            slot,
            at_x(step),
        )
        for slot, step in enumerate((-2, 2, -1, 1))
    ]

    def send_f1_y(first, last, part):
        return [
            send(
                f1.at[first:last, :, 8:16, :],
                f1.at[first:last, :, 8 - 8 * step : 16 - 8 * step, :],
                f1y_sems,
                2 * part + slot,
                at_y(step),
            )
            for slot, step in enumerate((-1, 1))
        ]

    f1y_copies = send_f1_y(8, 12, 0)
    for i in (0, 19):
        for tile in (slice(0, 8), slice(16, 24)):
            f1[i, :, tile, :] = jnp.ones((3, 8, 128), F32)
    for i in (1, 18):
        for tile in (slice(0, 8), slice(16, 24)):
            b1[i, tile, :] = jnp.zeros((8, 128), F32)

    def spread_x(ref, first, last, sems, steps):
        return [
            send(ref.at[1, first:last], ref.at[1, first - step : last - step], sems, slot, at_x(step))
            for slot, step in enumerate(steps)
        ]

    def gather_y(ref, sems):
        return [
            send(ref.at[1], ref.at[(1 - step) % count_y], sems, step - 1, at_y(step))
            for step in sorted(range(1, count_y), key=lambda step: abs(step - count_y // 2))
        ]

    for i in range(1, 16):
        part = slice(16, 24) if 4 <= i < 12 else slice(0, 24)
        for t in range(2):
            fx[i, t, part, :] = harmonic(cond[i, t, part, :], cond[i - 1, t, part, :])
        if i == 15:
            break
        k0, k1 = cond[i, 0], cond[i, 1]
        if not 4 <= i < 12:
            fy[i, 0] = harmonic(k0, roll(k0, 1, 0))
            fy[i, 1] = harmonic(k1, roll(k1, 1, 0))
        k0, k1 = k0[part], k1[part]
        fz[i, 0, part, :] = harmonic(k0, roll(k1, 1, 1))
        fz[i, 1, part, :] = harmonic(k1, k0)

    sibling = {"gy": me_y + 1 - 2 * lax.rem(me_y, 2)}
    shift = lax.rem(me_y, 2) * 2 + (count_y - 1)

    def hand_on(ref, sems, place):
        return send(
            ref.at[place],
            ref.at[lax.rem(place + shift, count_y)],
            sems,
            count_y + place,
            sibling,
        )

    def gather_y_shared(ref, sems):
        places = [(1 - step) % count_y for step in range(2, count_y, 2)]
        far = {
            place: send(ref.at[1], ref.at[place], sems, place, at_y(1 - place + count_y))
            for place in places
        }
        return far, [hand_on(ref, sems, 1)]

    def hand_on_all(ref, sems, far, handed):
        for place, copy in far.items():
            copy.wait_recv()
            handed.append(hand_on(ref, sems, place))

    for low, high in chunks(1, 15, 2):
        x_sum = [fx[low:high, t] + fx[low + 1 : high + 1, t] for t in range(2)]
        y_sum = [fy[low:high, t] + roll(fy[low:high, t], -1, 1) for t in range(2)]
        z0, z1 = fz[low:high, 0], fz[low:high, 1]
        inv[low:high, 0] = 1.0 / ((x_sum[0] + y_sum[0]) + (z0 + z1))
        inv[low:high, 1] = 1.0 / ((x_sum[1] + y_sum[1]) + (z1 + roll(z0, -1, 2)))

    place_y(1, xy_copies[1])
    for i in range(1, 15):
        for t in range(2):
            xa[i, t] = inv[i, t] * source[i, t] * (1.0 / CENTER)

    def step_0(old, new, low, high, step, before, after=None, target=None):
        keep_old, keep_new = STEPS[step]

        def emit(i, applied, here):
            for t in range(2):
                r = source[i, t] - applied[t]
                d = keep_old * before[i, t] + keep_new * (inv[i, t] * r)
                if after is not None:
                    after[i, t] = d
                if target is None:
                    new[i, t] = here[t] + d
                else:
                    target(i, t, here[t] + d)

        sweep_0(old, faces0, low, high, emit)

    step_0(xa, xb, 2, 14, 0, xa, dd)

    step_0(xb, xa, 3, 13, 1, dd)
    best[4:12, :, 0:16, :] = xa[4:12, :, 0:16, :]
    sums = []

    def residual_0(i, applied, here):
        r = [source[i, t, 0:16, :] - applied[t][:16] for t in range(2)]
        sums.append(r[0] + r[1])
        if i % 2 == 1:
            tmp0[0, (i - 4) // 2] = sums[-2] + sums[-1]

    sweep_0(xa, faces0, 4, 12, residual_0)
    b1[8:12, 8:16, :] = 0.125 * (tmp0[0, :, first, :] + tmp0[0, :, second, :])
    b1_copies = [
        send(
            b1.at[first:last, 8:16, :],
            b1.at[first - 4 * dx : last - 4 * dx, 8 - 8 * dy : 16 - 8 * dy, :],
            b1_sems,
            slot,
            (at_x(dx) if dx else {}) | (at_y(dy) if dy else {}),
        )
        for slot, (dx, dy, first, last) in enumerate(
            (
                (-2, 0, 8, 11),
                (2, 0, 9, 12),
                (-2, -1, 8, 10),
                (-2, 1, 8, 10),
                (2, -1, 10, 12),
                (2, 1, 10, 12),
                (-1, 0, 8, 12),
                (1, 0, 8, 12),
                (-1, -1, 8, 12),
                (-1, 1, 8, 12),
                (1, -1, 8, 12),
                (1, 1, 8, 12),
                (0, -1, 8, 12),
                (0, 1, 8, 12),
            )
        )
    ]


    for copy in f1x_copies:
        copy.wait_recv()
    f1y_copies += send_f1_y(1, 8, 1) + send_f1_y(12, 19, 2)

    def in_pack(row, column):
        return ((((row & 127) >> 1) + 16) & 63) + 64 * (row >> 7) == column

    pack = select_matrix((256, 128), in_pack)
    pack_even = select_matrix((256, 128), lambda row, l: ((row & 1) == 0) & in_pack(row, l))
    first4, second4 = pl.ds(0, 4, stride=2), pl.ds(1, 4, stride=2)

    def packed(pieces, matrix):
        whole = [jnp.concatenate(piece, axis=0) for piece in pieces]
        result = dot(side_by_side(*whole), matrix)
        return result.reshape(len(pieces[0]), 8, 128)

    g2f[1, 15] = jnp.ones((3, 4, 128), F32)
    g2b[1, 15] = jnp.zeros((4, 128), F32)
    mine = slice(8, 16)
    tmp1[0] = packed([[f1[4 * i + 2 * p, 0, mine, :] for i in range(5)] for p in range(2)], pack)
    for f in (1, 2):
        pieces = [
            [f1[4 * i + 2 * p, f, mine, :] + f1[4 * i + 2 * p + 1, f, mine, :] for i in range(5)]
            for p in range(2)
        ]
        tmp1[f] = packed(pieces, (None, pack, pack_even)[f])
    g2f[1, 5:10, 0] = 0.125 * (tmp1[0, :, first4, :] + tmp1[0, :, second4, :])
    g2f[1, 5:10, 1] = 0.125 * tmp1[1, :, first4, :]
    g2f[1, 5:10, 2] = 0.125 * (tmp1[2, :, first4, :] + tmp1[2, :, second4, :])
    gfx_copies = spread_x(g2f, 5, 10, gfx_sems, (5, -5))

    drain(level_0_sends)
    level_1_sends = len(pending)
    for copy in f1y_copies:
        copy.wait_recv()
    for low, high in chunks(1, 19, 6):
        x_sum = f1[low:high, 0] + f1[low + 1 : high + 1, 0]
        y_term, z_term = f1[low:high, 1], f1[low:high, 2]
        y_sum = y_term + roll(y_term, -1, 1)
        inv1[low:high] = 1.0 / ((x_sum + y_sum) + (z_term + roll(z_term, -1, 2)))

    for copy in b1_copies:
        copy.wait_recv()

    for i in range(1, 19):
        x1a[i] = inv1[i] * b1[i] * (1.0 / CENTER)

    def step_1(old, new, low, high, step, before, after=None):
        keep_old, keep_new = STEPS[step]

        def emit(i, applied, here):
            r = b1[i] - applied
            d = keep_old * before[i] + keep_new * (inv1[i] * r)
            if after is not None:
                after[i] = d
            new[i] = here + d

        sweep_1(old, f1, low, high, emit)

    step_1(x1a, x1b, 2, 18, 0, x1a, d1)
    for copy in gfx_copies:
        copy.wait_recv()
    gfy_far, gfy_copies = gather_y_shared(g2f, gfy_sems)
    step_1(x1b, x1a, 3, 17, 1, d1)
    r = {}

    def residual_1(i, applied, here):
        r[i - 4] = (b1[i] - applied)[8:16]

    sweep_1(x1a, f1, 4, 16, residual_1)
    tmp1[0, 0:3] = packed(
        [[r[4 * i + 2 * p] + r[4 * i + 2 * p + 1] for i in range(3)] for p in range(2)], pack
    )
    g2b[1, 6:9] = 0.125 * (tmp1[0, 0:3, first4, :] + tmp1[0, 0:3, second4, :])
    gbx_copies = spread_x(g2b, 6, 9, gbx_sems, (6, -6, 3, -3))
    x0_copies = send_x(2)
    for copy in gbx_copies:
        copy.wait_recv()
    gby_copies = gather_y(g2b, gby_sems)

    hand_on_all(g2f, gfy_sems, gfy_far, gfy_copies)
    for copy in gfy_copies:
        copy.wait_recv()
    for f in range(3):
        for s in range(count_y):
            f2[f, :, 4 * s : 4 * s + 4, :] = g2f[s, :, f]
    for low, high in chunks(0, 15, 3):
        terms = f2[0, low : high + 1]
        turned = roll(terms, 64, 2)
        half = lane_of(terms[1:].shape) < 64
        x_sum = terms[:-1] + jnp.where(half, turned[:-1], turned[1:])
        y_term, z_term = f2[1, low:high], f2[2, low:high]
        y_sum = y_term + roll(y_term, -1, 1)
        inv2[low:high] = 1.0 / ((x_sum + y_sum) + (z_term + roll(z_term, -1, 2)))

        x_low = f2[0, low:high]
        x_low = jnp.where(half, x_low, roll(x_low, 64, 2))
        tmp2[0, low:high] = x_low + roll(x_low, -1, 2)
        y_both = y_term + roll(y_term, 64, 2)
        tmp2[1, low:high] = y_both + roll(y_both, -1, 2)
        tmp2[2, low:high] = z_term + roll(z_term, 64, 2)
    first16, second16 = pl.ds(0, 16, stride=2), pl.ds(1, 16, stride=2)
    f3[0] = 0.125 * (tmp2[0, :, first16, :] + tmp2[0, :, second16, :])
    f3[1] = 0.125 * tmp2[1, :, first16, :]
    f3[2] = 0.125 * (tmp2[2, :, first16, :] + tmp2[2, :, second16, :])
    for low, high in chunks(2, 13, 6):
        terms = f3[0, low : high + 1]
        y_term, z_term = f3[1, low:high], f3[2, low:high]
        inv3[low:high] = 1.0 / (
            (terms[:-1] + terms[1:] + (y_term + roll(y_term, -1, 1)))
            + (z_term + roll(z_term, -2, 2))
        )

    for copy in x0_copies:
        copy.wait_recv()
    y0_copies = send_y(2)
    drain(level_1_sends)
    for copy in gby_copies:
        copy.wait_recv()
    for s in range(count_y):
        b2[:, 4 * s : 4 * s + 4, :] = g2b[s]

    for i in range(15):
        x2a[i] = inv2[i] * b2[i] * (1.0 / CENTER)

    def step_2(old, new, low, high, step, before, after=None):
        keep_old, keep_new = STEPS[step]

        def emit(i, applied, here):
            r = b2[i] - applied
            d = keep_old * before[i] + keep_new * (inv2[i] * r)
            if after is not None:
                after[i] = d
            new[i] = here + d

        sweep_2(old, f2, low, high, emit)

    step_2(x2a, x2b, 1, 14, 0, x2a, d2)
    step_2(x2b, x2a, 1, 14, 1, d2)

    def residual_2(i, applied, here):
        r = b2[i] - applied
        r = r + roll(r, 64, 1)
        tmp2[0, i] = r + roll(r, -1, 1)

    sweep_2(x2a, f2, 2, 13, residual_2)
    b3[2:13] = 0.125 * (tmp2[0, 2:13, first16, :] + tmp2[0, 2:13, second16, :])

    for i in range(2, 13):
        x3a[i] = inv3[i] * b3[i] * (1.0 / CENTER)

    def step_3(old, new, low, high, step, before, after=None):
        keep_old, keep_new = STEPS[step]

        def emit(i, applied, here):
            r = b3[i] - applied
            d = keep_old * before[i] + keep_new * (inv3[i] * r)
            if after is not None:
                after[i] = d
            new[i] = here + d

        sweep_3(old, f3, low, high, emit)

    step_3(x3a, x3b, 3, 12, 0, x3a, d3)
    step_3(x3b, x3a, 4, 11, 1, d3)

    e = x3a[4:11]
    e = jnp.where((lane_of(e.shape) & 1) == 0, e, roll(e, 1, 2))
    dup2[4:11, first16, :] = e
    dup2[4:11, second16, :] = e
    for i in range(4, 11):
        x2b[i] = x2a[i] + dup2[i]
    x2b[3] = x2a[3]
    x2b[11] = x2a[11]

    def first_up_2(i, applied, here):
        d = inv2[i] * (b2[i] - applied) * (1.0 / CENTER)
        d2[i] = d
        x2a[i] = here + d

    sweep_2(x2b, f2, 4, 11, first_up_2)
    step_2(x2a, x2b, 5, 10, 0, d2, d2)
    x2b[4] = x2a[4]
    x2b[10] = x2a[10]
    step_2(x2b, x2a, 5, 10, 1, d2)

    def in_spread(row, column):
        return ((((column & 127) >> 1) + 16) & 63) + 64 * (column >> 7) == row

    e = dot(x2a[5:10, 0:16, :].reshape(80, 128), select_matrix((128, 256), in_spread))
    for p in range(2):
        value = e[:, 128 * p : 128 * p + 128].reshape(5, 16, 128)
        dup21[p, :, first16, :] = value
        dup21[p, :, second16, :] = value
    for i in range(3, 17):
        x1b[i] = x1a[i] + dup21[(i // 2) % 2, i // 4, 0:24, :]

    def first_up_1(i, applied, here):
        d = inv1[i] * (b1[i] - applied) * (1.0 / CENTER)
        d1[i] = d
        x1a[i] = here + d

    sweep_1(x1b, f1, 4, 16, first_up_1)
    step_1(x1a, x1b, 5, 15, 0, d1, d1)
    step_1(x1b, x1a, 6, 14, 1, d1)

    drain(len(pending))
    place_y(2, y0_copies)
    e = x1a[6:14]
    dup1[:, pl.ds(0, 24, stride=2), :] = e
    dup1[:, pl.ds(1, 24, stride=2), :] = e
    lower = lax.broadcasted_iota(jnp.int32, (8, 128), 0) < 4
    for i in range(1, 15):
        j = i // 2
        brick = dup1[j, 16:32, :]
        edge = jnp.where(lower, dup1[j, 32:40, :], dup1[j, 8:16, :])
        for t in range(2):
            xb[i, t, 0:16, :] = best[i, t, 0:16, :] + brick
            xb[i, t, 16:24, :] = best[i, t, 16:24, :] + edge

    def first_up_0(i, applied, here):
        for t in range(2):
            d = inv[i, t] * (source[i, t] - applied[t]) * (1.0 / CENTER)
            dd[i, t] = d
            xa[i, t] = here[t] + d

    sweep_0(xb, faces0, 2, 14, first_up_0)
    step_0(xa, xb, 3, 13, 0, dd, dd)

    def to_own(i, t, value):
        own[t, i - 4] = value[0:16]

    step_0(xb, None, 4, 12, 1, dd, None, to_own)

    def joined(row, column):
        return ((row & 127) < 64) & (column == 2 * (row & 127) + (row >> 7))

    cells = side_by_side(own[0].reshape(128, 128), own[1].reshape(128, 128))
    result = dot(cells, select_matrix((256, 128), joined))
    out_ref[...] = result.reshape(8, 16, 128)


def solution(mesh):
    sizes = (mesh.shape["gx"], mesh.shape["gy"], mesh.shape["gz"])
    count_x, count_y, _ = sizes
    vmem = lambda *shape: pltpu.VMEM(shape, F32)
    sems = lambda count: pltpu.SemaphoreType.DMA((2, count))
    fine = (16, 2, 24, 128)
    level1 = (20, 24, 128)
    level2 = (16, 32, 128)
    level3 = (16, 16, 128)
    scratch = [
        vmem(2, 8, 16, 128),
        vmem(2, 8, 16, 128),
        vmem(2, 2, 4, 16, 128),
        vmem(2, 2, 4, 16, 128),
        vmem(3, *fine),
        vmem(3, 2, 16, 2, 4, 128),
        vmem(3, 2, 16, 2, 4, 128),
        vmem(*fine),
        vmem(*fine),
        vmem(*fine),
        vmem(*fine),
        vmem(*fine),
        vmem(*fine),
        vmem(*fine),
        vmem(3, 4, 16, 128),
        vmem(20, 3, 24, 128),
        vmem(*level1),
        vmem(*level1),
        vmem(*level1),
        vmem(*level1),
        vmem(*level1),
        vmem(3, 5, 8, 128),
        vmem(8, 48, 128),
        vmem(count_y, count_x, 3, 4, 128),
        vmem(count_y, count_x, 4, 128),
        vmem(3, *level2),
        vmem(*level2),
        vmem(*level2),
        vmem(*level2),
        vmem(*level2),
        vmem(*level2),
        vmem(3, *level2),
        vmem(3, *level3),
        vmem(*level3),
        vmem(*level3),
        vmem(*level3),
        vmem(*level3),
        vmem(*level3),
        vmem(*level2),
        vmem(2, 5, 32, 128),
        pltpu.SemaphoreType.DMA((2,)),
        sems(4),
        sems(6),
        sems(6),
        sems(12),
        sems(4),
        sems(6),
        sems(14),
        sems(2),
        sems(2 * count_y),
        sems(4),
        sems(count_y - 1),
    ]

    def shards(pressure_source, conductivity):
        return pl.pallas_call(
            functools.partial(kernel, sizes),
            out_shape=jax.ShapeDtypeStruct((8, 16, 128), F32),
            in_specs=[pl.BlockSpec(memory_space=pltpu.HBM)] * 2,
            out_specs=pl.BlockSpec(memory_space=pltpu.VMEM),
            scratch_shapes=scratch,
            compiler_params=pltpu.CompilerParams(
                collective_id=0, has_side_effects=True, vmem_limit_bytes=55136 * 1024
            ),
        )(pressure_source, conductivity)

    placed = (P("gx", "gy", "gz"), P("gx", "gy", "gz"))
    return jax.shard_map(
        shards, mesh=mesh, in_specs=placed, out_specs=P("gx", "gy", "gz"), check_vma=False
    )
```

```python
import functools

import jax
import jax.numpy as jnp
from jax import lax
from jax.experimental import pallas as pl
from jax.experimental.pallas import tpu as pltpu
from jax.sharding import PartitionSpec as P

MESH = pl.DeviceIdType.MESH
F32 = jnp.float32

CENTER = 1.125
RADIUS = 0.875
RATIO = CENTER / RADIUS
RHO0 = 1.0 / RATIO
RHO1 = 1.0 / (2.0 * RATIO - RHO0)
RHO2 = 1.0 / (2.0 * RATIO - RHO1)
STEPS = ((RHO1 * RHO0, 2.0 * RHO1 / RADIUS), (RHO2 * RHO1, 2.0 * RHO2 / RADIUS))


def roll(value, shift, axis):
    return pltpu.roll(value, shift % value.shape[axis], axis)


def lane_of(shape):
    return lax.broadcasted_iota(jnp.int32, shape, len(shape) - 1)


def select_matrix(shape, holds):
    row = lax.broadcasted_iota(jnp.int32, shape, 0)
    column = lax.broadcasted_iota(jnp.int32, shape, 1)
    return jnp.where(holds(row, column), 1.0, 0.0).astype(jnp.bfloat16)


def dot(a, ones):
    high = a.astype(jnp.bfloat16)
    rest = a - high.astype(F32)
    middle = rest.astype(jnp.bfloat16)
    low = (rest - middle.astype(F32)).astype(jnp.bfloat16)
    parts = [jnp.dot(part, ones, preferred_element_type=F32) for part in (low, middle, high)]
    return (parts[0] + parts[1]) + parts[2]


def side_by_side(a, b):
    return jnp.concatenate([a, b], axis=1)


def harmonic(one_side, other_side):
    return 2.0 * one_side * other_side / (one_side + other_side)


def chunks(low, high, size):
    return [(start, min(start + size, high)) for start in range(low, high, size)]


def sweep_0(field, faces, low, high, emit):
    face_x, face_y, face_z = faces
    both = range(2)
    here = [field[low, t] for t in both]
    flux = [face_x[low, t] * (here[t] - field[low - 1, t]) for t in both]
    for i in range(low, high):
        after = [field[i + 1, t] for t in both]
        upper = [face_x[i + 1, t] * (after[t] - here[t]) for t in both]
        result = []
        for t in both:
            side = face_y[i, t] * (here[t] - roll(here[t], 1, 0))
            result.append((flux[t] - upper[t]) + (side - roll(side, -1, 0)))
        even = face_z[i, 0] * (here[0] - roll(here[1], 1, 1))
        odd = face_z[i, 1] * (here[1] - here[0])
        emit(i, [result[0] + (even - odd), result[1] + (odd - roll(even, -1, 1))], here)
        here, flux = after, upper


def sweep_1(field, faces, low, high, emit):
    here = field[low]
    flux = faces[low, 0] * (here - field[low - 1])
    for i in range(low, high):
        after = field[i + 1]
        upper = faces[i + 1, 0] * (after - here)
        side = faces[i, 1] * (here - roll(here, 1, 0))
        result = (flux - upper) + (side - roll(side, -1, 0))
        side = faces[i, 2] * (here - roll(here, 1, 1))
        emit(i, result + (side - roll(side, -1, 1)), here)
        here, flux = after, upper


def sweep_2(field, faces, low, high, emit):
    half = lane_of(field.shape[1:]) < 64
    before, here = roll(field[low - 1], 64, 1), field[low]
    turned = roll(here, 64, 1)
    flux = faces[0, low] * (here - jnp.where(half, before, turned))
    flux_turned = roll(flux, 64, 1)
    for i in range(low, high):
        after = field[i + 1]
        after_turned = roll(after, 64, 1)
        upper = faces[0, i + 1] * (after - jnp.where(half, turned, after_turned))
        upper_turned = roll(upper, 64, 1)
        result = flux - jnp.where(half, flux_turned, upper_turned)
        side = faces[1, i] * (here - roll(here, 1, 0))
        result = result + (side - roll(side, -1, 0))
        side = faces[2, i] * (here - roll(here, 1, 1))
        emit(i, result + (side - roll(side, -1, 1)), here)
        here, turned, flux, flux_turned = after, after_turned, upper, upper_turned


def sweep_3(field, faces, low, high, emit):
    here = field[low]
    flux = faces[0, low] * (here - field[low - 1])
    for i in range(low, high):
        after = field[i + 1]
        upper = faces[0, i + 1] * (after - here)
        side = faces[1, i] * (here - roll(here, 1, 0))
        result = (flux - upper) + (side - roll(side, -1, 0))
        side = faces[2, i] * (here - roll(here, 2, 1))
        emit(i, result + (side - roll(side, -2, 1)), here)
        here, flux = after, upper


def kernel(
    sizes,
    source_hbm,
    cond_hbm,
    out_ref,
    staged,
    own,
    z_send,
    z_recv,
    win,
    y_send,
    y_recv,
    fx,
    fy,
    fz,
    inv,
    xa,
    xb,
    dd,
    tmp0,
    f1,
    b1,
    inv1,
    x1a,
    x1b,
    d1,
    tmp1,
    dup1,
    g2f,
    g2b,
    f2,
    b2,
    inv2,
    x2a,
    x2b,
    d2,
    tmp2,
    f3,
    b3,
    inv3,
    x3a,
    x3b,
    d3,
    dup2,
    dup21,
    in_sem,
    z_sems,
    x_sems,
    y_sems,
    xy_sems,
    f1x_sems,
    f1y_sems,
    b1x_sems,
    b1y_sems,
    gfx_sems,
    gfy_sems,
    gbx_sems,
    gby_sems,
):
    count_x, count_y, count_z = sizes
    me_x, me_y, me_z = lax.axis_index("gx"), lax.axis_index("gy"), lax.axis_index("gz")

    def at_x(step):
        return {"gx": lax.rem(me_x + (step + count_x), count_x)}

    def at_y(step):
        return {"gy": lax.rem(me_y + (step + count_y), count_y)}

    def at_z(step):
        return {"gz": lax.rem(me_z + (step + count_z), count_z)}

    loads = [
        pltpu.make_async_copy(cond_hbm, staged.at[0], in_sem.at[0]),
        pltpu.make_async_copy(source_hbm, staged.at[1], in_sem.at[1]),
    ]
    for load in loads:
        load.start()

    barrier = pltpu.get_barrier_semaphore()
    partners = [at_z(1), at_z(-1)]
    partners += [at_x(sign * step) for step in (1, 2, 3, 5, 6) for sign in (1, -1)]
    partners += [at_y(step) for step in range(1, count_y)]
    partners += [at_x(dx) | at_y(dy) for dx in (-1, 1) for dy in (-1, 1)]
    for partner in partners:
        pl.semaphore_signal(barrier, inc=1, device_id=partner, device_id_type=MESH)

    pending = []

    def drain(count):
        for copy in pending[:count]:
            copy.wait_send()
        del pending[:count]

    def send(source, target, sems, slot, device):
        copy = pltpu.make_async_remote_copy(
            src_ref=source,
            dst_ref=target,
            send_sem=sems.at[0, slot],
            recv_sem=sems.at[1, slot],
            device_id=device,
            device_id_type=MESH,
        )
        copy.start()
        pending.append(copy)
        return copy

    def kept(row, l):
        return row == jnp.where(l < 64, 2 * l, 2 * l - 127)

    def sent(row, l):
        half, q = l >> 7, (l >> 5) & 3
        z = 2 * (l & 31) + 64 * half + jnp.where((q & 1) == 0, half, 1 - half)
        return row == jnp.where(q >= 2, z, z + 128)

    keep = select_matrix((128, 128), kept)
    pass_on = select_matrix((256, 256), sent)
    z_copies = []
    for f in range(2):
        loads[f].wait()
        cells = staged[f].reshape(128, 128)
        halos = dot(side_by_side(cells[:64], cells[64:]), pass_on)
        z_send[f, 0] = halos[:, :128].reshape(4, 16, 128)
        z_send[f, 1] = halos[:, 128:].reshape(4, 16, 128)
        if f == 0:
            pl.semaphore_wait(barrier, len(partners))
        z_copies.append(
            [
                send(z_send.at[f, way], z_recv.at[f, way], z_sems, 2 * f + way, at_z((-1, 1)[way]))
                for way in range(2)
            ]
        )
        own[f] = dot(cells, keep).reshape(8, 16, 128)

    for way in range(2):
        for i in (0, 1, 14, 15):
            y_recv[1, way, i] = jnp.zeros((2, 4, 128), F32)
            if i in (0, 15):
                y_recv[0, way, i] = jnp.ones((2, 4, 128), F32)

    def send_x(f):
        depth = 4 if f == 0 else 3
        return [
            send(
                win.at[f, 4 : 4 + depth, :, 0:16, :],
                win.at[f, 12 : 12 + depth, :, 0:16, :],
                x_sems,
                2 * f,
                at_x(-1),
            ),
            send(
                win.at[f, 12 - depth : 12, :, 0:16, :],
                win.at[f, 4 - depth : 4, :, 0:16, :],
                x_sems,
                2 * f + 1,
                at_x(1),
            ),
        ]

    def send_y(f):
        y_send[f, 0] = win[f, :, :, 0:4, :]
        y_send[f, 1] = win[f, :, :, 12:16, :]
        return [
            send(
                y_send.at[f, way, 1:15],
                y_recv.at[f, way, 1:15],
                y_sems,
                2 * f + way,
                at_y((-1, 1)[way]),
            )
            for way in range(2)
        ]

    def send_xy(f):
        depth = 3 - f
        copies = send_x(f)
        y_send[f, 0, 4:12] = win[f, 4:12, :, 0:4, :]
        y_send[f, 1, 4:12] = win[f, 4:12, :, 12:16, :]
        for way in range(2):
            for slot, (dx, first, last) in enumerate(
                ((1, 12 - depth, 12), (-1, 4, 4 + depth), (0, 4, 12))
            ):
                copies.append(
                    send(
                        y_send.at[f, way, first:last],
                        y_recv.at[f, way, first - 8 * dx : last - 8 * dx],
                        xy_sems,
                        6 * f + 3 * way + slot,
                        at_y((-1, 1)[way]) | (at_x(dx) if dx else {}),
                    )
                )
        return copies

    def place_y(f, copies):
        for copy in copies:
            copy.wait_recv()
        win[f, :, :, 16:20, :] = y_recv[f, 0]
        win[f, :, :, 20:24, :] = y_recv[f, 1]

    xy_copies = []
    for f in range(2):
        for copy in z_copies[f]:
            copy.wait_recv()
        lane = lane_of((4, 16, 128))
        for part in range(2):
            mine = own[f, 4 * part : 4 * part + 4]
            above, below = z_recv[f, 0], z_recv[f, 1]
            for t in range(2):
                turn_above = ((0, 96), (64, 32))[part][t]
                turn_below = ((0, 32), (64, 96))[part][t]
                halo = jnp.where(
                    lane < 96,
                    roll(above, turn_above, 2) if turn_above else above,
                    roll(below, turn_below, 2) if turn_below else below,
                )
                win[f, 4 + 4 * part : 8 + 4 * part, t, 0:16, :] = jnp.where(
                    lane < 64, roll(mine, 64, 2) if t else mine, halo
                )
        xy_copies.append(send_xy(f))
    level_0_sends = len(pending)

    cond, source, best = win.at[0], win.at[1], win.at[2]
    faces0 = (fx, fy, fz)
    brick = slice(0, 16)
    for i in range(4, 12):
        k0, k1 = cond[i, 0, brick, :], cond[i, 1, brick, :]
        fz[i, 0, brick, :] = harmonic(k0, roll(k1, 1, 1))
        fz[i, 1, brick, :] = harmonic(k1, k0)
        if i > 4:
            fx[i, 0, brick, :] = harmonic(k0, cond[i - 1, 0, brick, :])
            fx[i, 1, brick, :] = harmonic(k1, cond[i - 1, 1, brick, :])
    place_y(0, xy_copies[0])
    for t in range(2):
        fx[4, t, brick, :] = harmonic(cond[4, t, brick, :], cond[3, t, brick, :])
    for i in range(4, 12):
        for t in range(2):
            k = cond[i, t]
            fy[i, t] = harmonic(k, roll(k, 1, 0))

    for i in range(4):
        tmp0[0, i] = fx[4 + 2 * i, 0, 0:16, :] + fx[4 + 2 * i, 1, 0:16, :]
        tmp0[1, i] = (fy[4 + 2 * i, 0, 0:16, :] + fy[4 + 2 * i, 1, 0:16, :]) + (
            fy[5 + 2 * i, 0, 0:16, :] + fy[5 + 2 * i, 1, 0:16, :]
        )
        tmp0[2, i] = fz[4 + 2 * i, 0, 0:16, :] + fz[5 + 2 * i, 0, 0:16, :]
    first, second = pl.ds(0, 8, stride=2), pl.ds(1, 8, stride=2)
    f1[8:12, 0, 8:16, :] = 0.125 * (tmp0[0, :, first, :] + tmp0[0, :, second, :])
    f1[8:12, 1, 8:16, :] = 0.125 * tmp0[1, :, first, :]
    f1[8:12, 2, 8:16, :] = 0.125 * (tmp0[2, :, first, :] + tmp0[2, :, second, :])
    f1x_copies = [
        send(
            f1.at[8:12, :, 8:16, :],
            f1.at[8 - 4 * step : 12 - 4 * step, :, 8:16, :],
            f1x_sems,
            slot,
            at_x(step),
        )
        for slot, step in enumerate((-2, 2, -1, 1))
    ]

    def send_f1_y(first, last, part):
        return [
            send(
                f1.at[first:last, :, 8:16, :],
                f1.at[first:last, :, 8 - 8 * step : 16 - 8 * step, :],
                f1y_sems,
                2 * part + slot,
                at_y(step),
            )
            for slot, step in enumerate((-1, 1))
        ]

    f1y_copies = send_f1_y(8, 12, 0)
    for i in (0, 19):
        for tile in (slice(0, 8), slice(16, 24)):
            f1[i, :, tile, :] = jnp.ones((3, 8, 128), F32)

    def spread_x(ref, first, last, sems, steps):
        return [
            send(ref.at[1, first:last], ref.at[1, first - step : last - step], sems, slot, at_x(step))
            for slot, step in enumerate(steps)
        ]

    def gather_y(ref, sems):
        return [
            send(ref.at[1], ref.at[(1 - step) % count_y], sems, step - 1, at_y(step))
            for step in sorted(range(1, count_y), key=lambda step: abs(step - count_y // 2))
        ]

    for i in range(1, 16):
        part = slice(16, 24) if 4 <= i < 12 else slice(0, 24)
        for t in range(2):
            fx[i, t, part, :] = harmonic(cond[i, t, part, :], cond[i - 1, t, part, :])
        if i == 15:
            break
        k0, k1 = cond[i, 0], cond[i, 1]
        if not 4 <= i < 12:
            fy[i, 0] = harmonic(k0, roll(k0, 1, 0))
            fy[i, 1] = harmonic(k1, roll(k1, 1, 0))
        k0, k1 = k0[part], k1[part]
        fz[i, 0, part, :] = harmonic(k0, roll(k1, 1, 1))
        fz[i, 1, part, :] = harmonic(k1, k0)

    sibling = {"gy": me_y + 1 - 2 * lax.rem(me_y, 2)}
    shift = lax.rem(me_y, 2) * 2 + (count_y - 1)

    def hand_on(ref, sems, place):
        return send(
            ref.at[place],
            ref.at[lax.rem(place + shift, count_y)],
            sems,
            count_y + place,
            sibling,
        )

    def gather_y_shared(ref, sems):
        places = [(1 - step) % count_y for step in range(2, count_y, 2)]
        far = {
            place: send(ref.at[1], ref.at[place], sems, place, at_y(1 - place + count_y))
            for place in places
        }
        return far, [hand_on(ref, sems, 1)]

    def put_faces_2(place):
        for f in range(3):
            f2[f, :, 4 * place : 4 * place + 4, :] = g2f[place, :, f]

    def hand_on_all(ref, sems, far, handed):
        for place, copy in far.items():
            copy.wait_recv()
            handed.append(hand_on(ref, sems, place))
            put_faces_2(place)

    for low, high in chunks(1, 15, 2):
        x_sum = [fx[low:high, t] + fx[low + 1 : high + 1, t] for t in range(2)]
        y_sum = [fy[low:high, t] + roll(fy[low:high, t], -1, 1) for t in range(2)]
        z0, z1 = fz[low:high, 0], fz[low:high, 1]
        inv[low:high, 0] = 1.0 / ((x_sum[0] + y_sum[0]) + (z0 + z1))
        inv[low:high, 1] = 1.0 / ((x_sum[1] + y_sum[1]) + (z1 + roll(z0, -1, 2)))

    place_y(1, xy_copies[1])
    for i in range(1, 15):
        for t in range(2):
            xa[i, t] = inv[i, t] * source[i, t] * (1.0 / CENTER)

    def step_0(old, new, low, high, step, before, after=None, target=None):
        keep_old, keep_new = STEPS[step]

        def emit(i, applied, here):
            for t in range(2):
                r = source[i, t] - applied[t]
                d = keep_old * before[i, t] + keep_new * (inv[i, t] * r)
                if after is not None:
                    after[i, t] = d
                if target is None:
                    new[i, t] = here[t] + d
                else:
                    target(i, t, here[t] + d)

        sweep_0(old, faces0, low, high, emit)

    step_0(xa, xb, 2, 14, 0, xa, dd)

    step_0(xb, xa, 3, 13, 1, dd)
    best[4:12, :, 0:16, :] = xa[4:12, :, 0:16, :]
    sums = []

    def residual_0(i, applied, here):
        r = [source[i, t, 0:16, :] - applied[t][:16] for t in range(2)]
        sums.append(r[0] + r[1])
        if i % 2 == 1:
            tmp0[0, (i - 4) // 2] = sums[-2] + sums[-1]

    sweep_0(xa, faces0, 4, 12, residual_0)
    b1[8:12, 8:16, :] = 0.125 * (tmp0[0, :, first, :] + tmp0[0, :, second, :])
    b1x_copies = [
        send(
            b1.at[first:last, 8:16, :],
            b1.at[first - 4 * step : last - 4 * step, 8:16, :],
            b1x_sems,
            slot,
            at_x(step),
        )
        for slot, (step, first, last) in enumerate(
            ((-2, 8, 11), (2, 9, 12), (-1, 8, 12), (1, 8, 12))
        )
    ]

    for copy in f1x_copies:
        copy.wait_recv()
    f1y_copies += send_f1_y(1, 8, 1) + send_f1_y(12, 19, 2)

    def in_pack(row, column):
        return ((((row & 127) >> 1) + 16) & 63) + 64 * (row >> 7) == column

    pack = select_matrix((256, 128), in_pack)
    pack_even = select_matrix((256, 128), lambda row, l: ((row & 1) == 0) & in_pack(row, l))
    first4, second4 = pl.ds(0, 4, stride=2), pl.ds(1, 4, stride=2)

    def packed(pieces, matrix):
        whole = [jnp.concatenate(piece, axis=0) for piece in pieces]
        result = dot(side_by_side(*whole), matrix)
        return result.reshape(len(pieces[0]), 8, 128)

    g2f[1, 15] = jnp.ones((3, 4, 128), F32)
    g2b[1, 15] = jnp.zeros((4, 128), F32)
    mine = slice(8, 16)
    tmp1[0] = packed([[f1[4 * i + 2 * p, 0, mine, :] for i in range(5)] for p in range(2)], pack)
    for f in (1, 2):
        pieces = [
            [f1[4 * i + 2 * p, f, mine, :] + f1[4 * i + 2 * p + 1, f, mine, :] for i in range(5)]
            for p in range(2)
        ]
        tmp1[f] = packed(pieces, (None, pack, pack_even)[f])
    g2f[1, 5:10, 0] = 0.125 * (tmp1[0, :, first4, :] + tmp1[0, :, second4, :])
    g2f[1, 5:10, 1] = 0.125 * tmp1[1, :, first4, :]
    g2f[1, 5:10, 2] = 0.125 * (tmp1[2, :, first4, :] + tmp1[2, :, second4, :])
    gfx_copies = spread_x(g2f, 5, 10, gfx_sems, (5, -5))

    drain(level_0_sends)
    level_1_sends = len(pending)
    for copy in b1x_copies:
        copy.wait_recv()
    b1y_copies = [
        send(
            b1.at[1:19, 8:16, :],
            b1.at[1:19, 8 - 8 * step : 16 - 8 * step, :],
            b1y_sems,
            slot,
            at_y(step),
        )
        for slot, step in enumerate((-1, 1))
    ]
    for copy in f1y_copies:
        copy.wait_recv()
    for low, high in chunks(1, 19, 6):
        x_sum = f1[low:high, 0] + f1[low + 1 : high + 1, 0]
        y_term, z_term = f1[low:high, 1], f1[low:high, 2]
        y_sum = y_term + roll(y_term, -1, 1)
        inv1[low:high] = 1.0 / ((x_sum + y_sum) + (z_term + roll(z_term, -1, 2)))

    for copy in b1y_copies:
        copy.wait_recv()

    for i in range(1, 19):
        x1a[i] = inv1[i] * b1[i] * (1.0 / CENTER)

    def step_1(old, new, low, high, step, before, after=None):
        keep_old, keep_new = STEPS[step]

        def emit(i, applied, here):
            r = b1[i] - applied
            d = keep_old * before[i] + keep_new * (inv1[i] * r)
            if after is not None:
                after[i] = d
            new[i] = here + d

        sweep_1(old, f1, low, high, emit)

    step_1(x1a, x1b, 2, 18, 0, x1a, d1)
    for copy in gfx_copies:
        copy.wait_recv()
    gfy_far, gfy_copies = gather_y_shared(g2f, gfy_sems)
    step_1(x1b, x1a, 3, 17, 1, d1)
    r = {}

    def residual_1(i, applied, here):
        r[i - 4] = (b1[i] - applied)[8:16]

    sweep_1(x1a, f1, 4, 16, residual_1)
    tmp1[0, 0:3] = packed(
        [[r[4 * i + 2 * p] + r[4 * i + 2 * p + 1] for i in range(3)] for p in range(2)], pack
    )
    g2b[1, 6:9] = 0.125 * (tmp1[0, 0:3, first4, :] + tmp1[0, 0:3, second4, :])
    gbx_copies = spread_x(g2b, 6, 9, gbx_sems, (6, -6, 3, -3))
    x0_copies = send_x(2)
    for copy in gbx_copies:
        copy.wait_recv()
    gby_copies = gather_y(g2b, gby_sems)

    put_faces_2(1)
    hand_on_all(g2f, gfy_sems, gfy_far, gfy_copies)
    for copy in gfy_copies:
        copy.wait_recv()
    for s in range(0, count_y, 2):
        put_faces_2(s)
    for low, high in chunks(0, 15, 3):
        terms = f2[0, low : high + 1]
        turned = roll(terms, 64, 2)
        half = lane_of(terms[1:].shape) < 64
        x_sum = terms[:-1] + jnp.where(half, turned[:-1], turned[1:])
        y_term, z_term = f2[1, low:high], f2[2, low:high]
        y_sum = y_term + roll(y_term, -1, 1)
        inv2[low:high] = 1.0 / ((x_sum + y_sum) + (z_term + roll(z_term, -1, 2)))

        x_low = f2[0, low:high]
        x_low = jnp.where(half, x_low, roll(x_low, 64, 2))
        tmp2[0, low:high] = x_low + roll(x_low, -1, 2)
        y_both = y_term + roll(y_term, 64, 2)
        tmp2[1, low:high] = y_both + roll(y_both, -1, 2)
        tmp2[2, low:high] = z_term + roll(z_term, 64, 2)
    first16, second16 = pl.ds(0, 16, stride=2), pl.ds(1, 16, stride=2)
    f3[0] = 0.125 * (tmp2[0, :, first16, :] + tmp2[0, :, second16, :])
    f3[1] = 0.125 * tmp2[1, :, first16, :]
    f3[2] = 0.125 * (tmp2[2, :, first16, :] + tmp2[2, :, second16, :])
    for low, high in chunks(2, 13, 6):
        terms = f3[0, low : high + 1]
        y_term, z_term = f3[1, low:high], f3[2, low:high]
        inv3[low:high] = 1.0 / (
            (terms[:-1] + terms[1:] + (y_term + roll(y_term, -1, 1)))
            + (z_term + roll(z_term, -2, 2))
        )

    for copy in x0_copies:
        copy.wait_recv()
    y0_copies = send_y(2)
    drain(level_1_sends)
    for copy in gby_copies:
        copy.wait_recv()
    for s in range(count_y):
        b2[:, 4 * s : 4 * s + 4, :] = g2b[s]

    for i in range(15):
        x2a[i] = inv2[i] * b2[i] * (1.0 / CENTER)

    def step_2(old, new, low, high, step, before, after=None):
        keep_old, keep_new = STEPS[step]

        def emit(i, applied, here):
            r = b2[i] - applied
            d = keep_old * before[i] + keep_new * (inv2[i] * r)
            if after is not None:
                after[i] = d
            new[i] = here + d

        sweep_2(old, f2, low, high, emit)

    step_2(x2a, x2b, 1, 14, 0, x2a, d2)
    step_2(x2b, x2a, 1, 14, 1, d2)

    def residual_2(i, applied, here):
        r = b2[i] - applied
        r = r + roll(r, 64, 1)
        tmp2[0, i] = r + roll(r, -1, 1)

    sweep_2(x2a, f2, 2, 13, residual_2)
    b3[2:13] = 0.125 * (tmp2[0, 2:13, first16, :] + tmp2[0, 2:13, second16, :])

    for i in range(2, 13):
        x3a[i] = inv3[i] * b3[i] * (1.0 / CENTER)

    def step_3(old, new, low, high, step, before, after=None):
        keep_old, keep_new = STEPS[step]

        def emit(i, applied, here):
            r = b3[i] - applied
            d = keep_old * before[i] + keep_new * (inv3[i] * r)
            if after is not None:
                after[i] = d
            new[i] = here + d

        sweep_3(old, f3, low, high, emit)

    step_3(x3a, x3b, 3, 12, 0, x3a, d3)
    step_3(x3b, x3a, 4, 11, 1, d3)

    e = x3a[4:11]
    e = jnp.where((lane_of(e.shape) & 1) == 0, e, roll(e, 1, 2))
    dup2[4:11, first16, :] = e
    dup2[4:11, second16, :] = e
    for i in range(4, 11):
        x2b[i] = x2a[i] + dup2[i]
    x2b[3] = x2a[3]
    x2b[11] = x2a[11]

    def first_up_2(i, applied, here):
        d = inv2[i] * (b2[i] - applied) * (1.0 / CENTER)
        d2[i] = d
        x2a[i] = here + d

    sweep_2(x2b, f2, 4, 11, first_up_2)
    step_2(x2a, x2b, 5, 10, 0, d2, d2)
    x2b[4] = x2a[4]
    x2b[10] = x2a[10]
    step_2(x2b, x2a, 5, 10, 1, d2)

    def in_spread(row, column):
        return ((((column & 127) >> 1) + 16) & 63) + 64 * (column >> 7) == row

    e = dot(x2a[5:10, 0:16, :].reshape(80, 128), select_matrix((128, 256), in_spread))
    for p in range(2):
        value = e[:, 128 * p : 128 * p + 128].reshape(5, 16, 128)
        dup21[p, :, first16, :] = value
        dup21[p, :, second16, :] = value
    for i in range(3, 17):
        x1b[i] = x1a[i] + dup21[(i // 2) % 2, i // 4, 0:24, :]

    def first_up_1(i, applied, here):
        d = inv1[i] * (b1[i] - applied) * (1.0 / CENTER)
        d1[i] = d
        x1a[i] = here + d

    sweep_1(x1b, f1, 4, 16, first_up_1)
    step_1(x1a, x1b, 5, 15, 0, d1, d1)
    step_1(x1b, x1a, 6, 14, 1, d1)

    drain(len(pending))
    place_y(2, y0_copies)
    e = x1a[6:14]
    dup1[:, pl.ds(0, 24, stride=2), :] = e
    dup1[:, pl.ds(1, 24, stride=2), :] = e
    lower = lax.broadcasted_iota(jnp.int32, (8, 128), 0) < 4
    for i in range(1, 15):
        j = i // 2
        brick = dup1[j, 16:32, :]
        edge = jnp.where(lower, dup1[j, 32:40, :], dup1[j, 8:16, :])
        for t in range(2):
            xb[i, t, 0:16, :] = best[i, t, 0:16, :] + brick
            xb[i, t, 16:24, :] = best[i, t, 16:24, :] + edge

    def first_up_0(i, applied, here):
        for t in range(2):
            d = inv[i, t] * (source[i, t] - applied[t]) * (1.0 / CENTER)
            dd[i, t] = d
            xa[i, t] = here[t] + d

    sweep_0(xb, faces0, 2, 14, first_up_0)
    step_0(xa, xb, 3, 13, 0, dd, dd)

    def to_own(i, t, value):
        own[t, i - 4] = value[0:16]

    step_0(xb, None, 4, 12, 1, dd, None, to_own)

    def joined(row, column):
        return ((row & 127) < 64) & (column == 2 * (row & 127) + (row >> 7))

    cells = side_by_side(own[0].reshape(128, 128), own[1].reshape(128, 128))
    result = dot(cells, select_matrix((256, 128), joined))
    out_ref[...] = result.reshape(8, 16, 128)


def solution(mesh):
    sizes = (mesh.shape["gx"], mesh.shape["gy"], mesh.shape["gz"])
    count_x, count_y, _ = sizes
    vmem = lambda *shape: pltpu.VMEM(shape, F32)
    sems = lambda count: pltpu.SemaphoreType.DMA((2, count))
    fine = (16, 2, 24, 128)
    level1 = (20, 24, 128)
    level2 = (16, 32, 128)
    level3 = (16, 16, 128)
    scratch = [
        vmem(2, 8, 16, 128),
        vmem(2, 8, 16, 128),
        vmem(2, 2, 4, 16, 128),
        vmem(2, 2, 4, 16, 128),
        vmem(3, *fine),
        vmem(3, 2, 16, 2, 4, 128),
        vmem(3, 2, 16, 2, 4, 128),
        vmem(*fine),
        vmem(*fine),
        vmem(*fine),
        vmem(*fine),
        vmem(*fine),
        vmem(*fine),
        vmem(*fine),
        vmem(3, 4, 16, 128),
        vmem(20, 3, 24, 128),
        vmem(*level1),
        vmem(*level1),
        vmem(*level1),
        vmem(*level1),
        vmem(*level1),
        vmem(3, 5, 8, 128),
        vmem(8, 48, 128),
        vmem(count_y, count_x, 3, 4, 128),
        vmem(count_y, count_x, 4, 128),
        vmem(3, *level2),
        vmem(*level2),
        vmem(*level2),
        vmem(*level2),
        vmem(*level2),
        vmem(*level2),
        vmem(3, *level2),
        vmem(3, *level3),
        vmem(*level3),
        vmem(*level3),
        vmem(*level3),
        vmem(*level3),
        vmem(*level3),
        vmem(*level2),
        vmem(2, 5, 32, 128),
        pltpu.SemaphoreType.DMA((2,)),
        sems(4),
        sems(6),
        sems(6),
        sems(12),
        sems(4),
        sems(6),
        sems(4),
        sems(2),
        sems(2),
        sems(2 * count_y),
        sems(4),
        sems(count_y - 1),
    ]

    def shards(pressure_source, conductivity):
        return pl.pallas_call(
            functools.partial(kernel, sizes),
            out_shape=jax.ShapeDtypeStruct((8, 16, 128), F32),
            in_specs=[pl.BlockSpec(memory_space=pltpu.HBM)] * 2,
            out_specs=pl.BlockSpec(memory_space=pltpu.VMEM),
            scratch_shapes=scratch,
            compiler_params=pltpu.CompilerParams(
                collective_id=0, has_side_effects=True, vmem_limit_bytes=55136 * 1024
            ),
        )(pressure_source, conductivity)

    placed = (P("gx", "gy", "gz"), P("gx", "gy", "gz"))
    return jax.shard_map(
        shards, mesh=mesh, in_specs=placed, out_specs=P("gx", "gy", "gz"), check_vma=False
    )
```

```python
import functools

import jax
import jax.numpy as jnp
from jax import lax
from jax.experimental import pallas as pl
from jax.experimental.pallas import tpu as pltpu
from jax.sharding import PartitionSpec as P

MESH = pl.DeviceIdType.MESH
F32 = jnp.float32

CENTER = 1.125
RADIUS = 0.875
RATIO = CENTER / RADIUS
RHO0 = 1.0 / RATIO
RHO1 = 1.0 / (2.0 * RATIO - RHO0)
RHO2 = 1.0 / (2.0 * RATIO - RHO1)
STEPS = ((RHO1 * RHO0, 2.0 * RHO1 / RADIUS), (RHO2 * RHO1, 2.0 * RHO2 / RADIUS))


def roll(value, shift, axis):
    return pltpu.roll(value, shift % value.shape[axis], axis)


def lane_of(shape):
    return lax.broadcasted_iota(jnp.int32, shape, len(shape) - 1)


def select_matrix(shape, holds):
    row = lax.broadcasted_iota(jnp.int32, shape, 0)
    column = lax.broadcasted_iota(jnp.int32, shape, 1)
    return jnp.where(holds(row, column), 1.0, 0.0).astype(jnp.bfloat16)


def dot(a, ones):
    high = a.astype(jnp.bfloat16)
    rest = a - high.astype(F32)
    middle = rest.astype(jnp.bfloat16)
    low = (rest - middle.astype(F32)).astype(jnp.bfloat16)
    parts = [jnp.dot(part, ones, preferred_element_type=F32) for part in (low, middle, high)]
    return (parts[0] + parts[1]) + parts[2]


def side_by_side(a, b):
    return jnp.concatenate([a, b], axis=1)


def harmonic(one_side, other_side):
    return 2.0 * one_side * other_side / (one_side + other_side)


def chunks(low, high, size):
    return [(start, min(start + size, high)) for start in range(low, high, size)]


def sweep_0(field, faces, low, high, emit):
    face_x, face_y, face_z = faces
    both = range(2)
    here = [field[low, t] for t in both]
    flux = [face_x[low, t] * (here[t] - field[low - 1, t]) for t in both]
    for i in range(low, high):
        after = [field[i + 1, t] for t in both]
        upper = [face_x[i + 1, t] * (after[t] - here[t]) for t in both]
        result = []
        for t in both:
            side = face_y[i, t] * (here[t] - roll(here[t], 1, 0))
            result.append((flux[t] - upper[t]) + (side - roll(side, -1, 0)))
        even = face_z[i, 0] * (here[0] - roll(here[1], 1, 1))
        odd = face_z[i, 1] * (here[1] - here[0])
        emit(i, [result[0] + (even - odd), result[1] + (odd - roll(even, -1, 1))], here)
        here, flux = after, upper


def sweep_1(field, faces, low, high, emit):
    here = field[low]
    flux = faces[low, 0] * (here - field[low - 1])
    for i in range(low, high):
        after = field[i + 1]
        upper = faces[i + 1, 0] * (after - here)
        side = faces[i, 1] * (here - roll(here, 1, 0))
        result = (flux - upper) + (side - roll(side, -1, 0))
        side = faces[i, 2] * (here - roll(here, 1, 1))
        emit(i, result + (side - roll(side, -1, 1)), here)
        here, flux = after, upper


def sweep_2(field, faces, low, high, emit):
    half = lane_of(field.shape[1:]) < 64
    before, here = roll(field[low - 1], 64, 1), field[low]
    turned = roll(here, 64, 1)
    flux = faces[0, low] * (here - jnp.where(half, before, turned))
    flux_turned = roll(flux, 64, 1)
    for i in range(low, high):
        after = field[i + 1]
        after_turned = roll(after, 64, 1)
        upper = faces[0, i + 1] * (after - jnp.where(half, turned, after_turned))
        upper_turned = roll(upper, 64, 1)
        result = flux - jnp.where(half, flux_turned, upper_turned)
        side = faces[1, i] * (here - roll(here, 1, 0))
        result = result + (side - roll(side, -1, 0))
        side = faces[2, i] * (here - roll(here, 1, 1))
        emit(i, result + (side - roll(side, -1, 1)), here)
        here, turned, flux, flux_turned = after, after_turned, upper, upper_turned


def sweep_3(field, faces, low, high, emit):
    here = field[low]
    flux = faces[0, low] * (here - field[low - 1])
    for i in range(low, high):
        after = field[i + 1]
        upper = faces[0, i + 1] * (after - here)
        side = faces[1, i] * (here - roll(here, 1, 0))
        result = (flux - upper) + (side - roll(side, -1, 0))
        side = faces[2, i] * (here - roll(here, 2, 1))
        emit(i, result + (side - roll(side, -2, 1)), here)
        here, flux = after, upper


def kernel(
    sizes,
    source_hbm,
    cond_hbm,
    out_ref,
    staged,
    own,
    z_send,
    z_recv,
    win,
    y_send,
    y_recv,
    fx,
    fy,
    fz,
    inv,
    xa,
    xb,
    dd,
    tmp0,
    f1,
    b1,
    inv1,
    x1a,
    x1b,
    d1,
    tmp1,
    dup1,
    g2f,
    g2b,
    f2,
    b2,
    inv2,
    x2a,
    x2b,
    d2,
    tmp2,
    f3,
    b3,
    inv3,
    x3a,
    x3b,
    d3,
    dup2,
    dup21,
    in_sem,
    z_sems,
    x_sems,
    y_sems,
    xy_sems,
    f1x_sems,
    f1y_sems,
    b1x_sems,
    b1y_sems,
    gfx_sems,
    gfy_sems,
    gbx_sems,
    gby_sems,
):
    count_x, count_y, count_z = sizes
    me_x, me_y, me_z = lax.axis_index("gx"), lax.axis_index("gy"), lax.axis_index("gz")

    def at_x(step):
        return {"gx": lax.rem(me_x + (step + count_x), count_x)}

    def at_y(step):
        return {"gy": lax.rem(me_y + (step + count_y), count_y)}

    def at_z(step):
        return {"gz": lax.rem(me_z + (step + count_z), count_z)}

    loads = [
        pltpu.make_async_copy(cond_hbm, staged.at[0], in_sem.at[0]),
        pltpu.make_async_copy(source_hbm, staged.at[1], in_sem.at[1]),
    ]
    for load in loads:
        load.start()

    barrier = pltpu.get_barrier_semaphore()
    partners = [at_z(1), at_z(-1)]
    partners += [at_x(sign * step) for step in (1, 2, 3, 6) for sign in (1, -1)]
    partners += [at_y(step) for step in range(1, count_y)]
    partners += [at_x(dx) | at_y(dy) for dx in (-1, 1) for dy in (-1, 1)]
    for partner in partners:
        pl.semaphore_signal(barrier, inc=1, device_id=partner, device_id_type=MESH)

    pending = []

    def drain(count):
        for copy in pending[:count]:
            copy.wait_send()
        del pending[:count]

    def send(source, target, sems, slot, device):
        copy = pltpu.make_async_remote_copy(
            src_ref=source,
            dst_ref=target,
            send_sem=sems.at[0, slot],
            recv_sem=sems.at[1, slot],
            device_id=device,
            device_id_type=MESH,
        )
        copy.start()
        pending.append(copy)
        return copy

    def kept(row, l):
        return row == jnp.where(l < 64, 2 * l, 2 * l - 127)

    def sent(row, l):
        half, q = l >> 7, (l >> 5) & 3
        z = 2 * (l & 31) + 64 * half + jnp.where((q & 1) == 0, half, 1 - half)
        return row == jnp.where(q >= 2, z, z + 128)

    keep = select_matrix((128, 128), kept)
    pass_on = select_matrix((256, 256), sent)
    z_copies = []
    for f in range(2):
        loads[f].wait()
        cells = staged[f].reshape(128, 128)
        halos = dot(side_by_side(cells[:64], cells[64:]), pass_on)
        z_send[f, 0] = halos[:, :128].reshape(4, 16, 128)
        z_send[f, 1] = halos[:, 128:].reshape(4, 16, 128)
        if f == 0:
            pl.semaphore_wait(barrier, len(partners))
        z_copies.append(
            [
                send(z_send.at[f, way], z_recv.at[f, way], z_sems, 2 * f + way, at_z((-1, 1)[way]))
                for way in range(2)
            ]
        )
        own[f] = dot(cells, keep).reshape(8, 16, 128)

    for way in range(2):
        for i in (0, 1, 14, 15):
            y_recv[1, way, i] = jnp.zeros((2, 4, 128), F32)
            if i in (0, 15):
                y_recv[0, way, i] = jnp.ones((2, 4, 128), F32)

    def send_x(f):
        depth = 4 if f == 0 else 3
        return [
            send(
                win.at[f, 4 : 4 + depth, :, 0:16, :],
                win.at[f, 12 : 12 + depth, :, 0:16, :],
                x_sems,
                2 * f,
                at_x(-1),
            ),
            send(
                win.at[f, 12 - depth : 12, :, 0:16, :],
                win.at[f, 4 - depth : 4, :, 0:16, :],
                x_sems,
                2 * f + 1,
                at_x(1),
            ),
        ]

    def send_y(f):
        y_send[f, 0] = win[f, :, :, 0:4, :]
        y_send[f, 1] = win[f, :, :, 12:16, :]
        return [
            send(
                y_send.at[f, way, 1:15],
                y_recv.at[f, way, 1:15],
                y_sems,
                2 * f + way,
                at_y((-1, 1)[way]),
            )
            for way in range(2)
        ]

    def send_xy(f):
        depth = 3 - f
        copies = send_x(f)
        y_send[f, 0, 4:12] = win[f, 4:12, :, 0:4, :]
        y_send[f, 1, 4:12] = win[f, 4:12, :, 12:16, :]
        for way in range(2):
            for slot, (dx, first, last) in enumerate(
                ((1, 12 - depth, 12), (-1, 4, 4 + depth), (0, 4, 12))
            ):
                copies.append(
                    send(
                        y_send.at[f, way, first:last],
                        y_recv.at[f, way, first - 8 * dx : last - 8 * dx],
                        xy_sems,
                        6 * f + 3 * way + slot,
                        at_y((-1, 1)[way]) | (at_x(dx) if dx else {}),
                    )
                )
        return copies

    def place_y(f, copies):
        for copy in copies:
            copy.wait_recv()
        win[f, :, :, 16:20, :] = y_recv[f, 0]
        win[f, :, :, 20:24, :] = y_recv[f, 1]

    xy_copies = []
    for f in range(2):
        for copy in z_copies[f]:
            copy.wait_recv()
        lane = lane_of((4, 16, 128))
        for part in range(2):
            mine = own[f, 4 * part : 4 * part + 4]
            above, below = z_recv[f, 0], z_recv[f, 1]
            for t in range(2):
                turn_above = ((0, 96), (64, 32))[part][t]
                turn_below = ((0, 32), (64, 96))[part][t]
                halo = jnp.where(
                    lane < 96,
                    roll(above, turn_above, 2) if turn_above else above,
                    roll(below, turn_below, 2) if turn_below else below,
                )
                win[f, 4 + 4 * part : 8 + 4 * part, t, 0:16, :] = jnp.where(
                    lane < 64, roll(mine, 64, 2) if t else mine, halo
                )
        xy_copies.append(send_xy(f))
    level_0_sends = len(pending)

    cond, source, best = win.at[0], win.at[1], win.at[2]
    faces0 = (fx, fy, fz)
    brick = slice(0, 16)
    for i in range(4, 12):
        k0, k1 = cond[i, 0, brick, :], cond[i, 1, brick, :]
        fz[i, 0, brick, :] = harmonic(k0, roll(k1, 1, 1))
        fz[i, 1, brick, :] = harmonic(k1, k0)
        if i > 4:
            fx[i, 0, brick, :] = harmonic(k0, cond[i - 1, 0, brick, :])
            fx[i, 1, brick, :] = harmonic(k1, cond[i - 1, 1, brick, :])
    place_y(0, xy_copies[0])
    for t in range(2):
        fx[4, t, brick, :] = harmonic(cond[4, t, brick, :], cond[3, t, brick, :])
    for i in range(4, 12):
        for t in range(2):
            k = cond[i, t]
            fy[i, t] = harmonic(k, roll(k, 1, 0))

    for i in range(4):
        tmp0[0, i] = fx[4 + 2 * i, 0, 0:16, :] + fx[4 + 2 * i, 1, 0:16, :]
        tmp0[1, i] = (fy[4 + 2 * i, 0, 0:16, :] + fy[4 + 2 * i, 1, 0:16, :]) + (
            fy[5 + 2 * i, 0, 0:16, :] + fy[5 + 2 * i, 1, 0:16, :]
        )
        tmp0[2, i] = fz[4 + 2 * i, 0, 0:16, :] + fz[5 + 2 * i, 0, 0:16, :]
    first, second = pl.ds(0, 8, stride=2), pl.ds(1, 8, stride=2)
    f1[8:12, 0, 8:16, :] = 0.125 * (tmp0[0, :, first, :] + tmp0[0, :, second, :])
    f1[8:12, 1, 8:16, :] = 0.125 * tmp0[1, :, first, :]
    f1[8:12, 2, 8:16, :] = 0.125 * (tmp0[2, :, first, :] + tmp0[2, :, second, :])
    f1x_copies = [
        send(
            f1.at[first:last, :, 8:16, :],
            f1.at[first - 4 * step : last - 4 * step, :, 8:16, :],
            f1x_sems,
            slot,
            at_x(step),
        )
        for slot, (step, first, last) in enumerate(
            ((-1, 8, 12), (1, 8, 12), (-2, 8, 12), (2, 9, 12))
        )
    ]

    def send_f1_y(first, last, part):
        return [
            send(
                f1.at[first:last, :, 8:16, :],
                f1.at[first:last, :, 8 - 8 * step : 16 - 8 * step, :],
                f1y_sems,
                2 * part + slot,
                at_y(step),
            )
            for slot, step in enumerate((-1, 1))
        ]

    f1y_copies = send_f1_y(8, 12, 0)
    for i in (0, 19):
        for tile in (slice(0, 8), slice(16, 24)):
            f1[i, :, tile, :] = jnp.ones((3, 8, 128), F32)

    def spread_x(ref, first, last, sems, steps):
        return [
            send(ref.at[1, first:last], ref.at[1, first - step : last - step], sems, slot, at_x(step))
            for slot, step in enumerate(steps)
        ]

    def gather_y(ref, sems):
        return [
            send(ref.at[1], ref.at[(1 - step) % count_y], sems, step - 1, at_y(step))
            for step in sorted(range(1, count_y), key=lambda step: abs(step - count_y // 2))
        ]

    for i in range(1, 16):
        part = slice(16, 24) if 4 <= i < 12 else slice(0, 24)
        for t in range(2):
            fx[i, t, part, :] = harmonic(cond[i, t, part, :], cond[i - 1, t, part, :])
        if i == 15:
            break
        k0, k1 = cond[i, 0], cond[i, 1]
        if not 4 <= i < 12:
            fy[i, 0] = harmonic(k0, roll(k0, 1, 0))
            fy[i, 1] = harmonic(k1, roll(k1, 1, 0))
        k0, k1 = k0[part], k1[part]
        fz[i, 0, part, :] = harmonic(k0, roll(k1, 1, 1))
        fz[i, 1, part, :] = harmonic(k1, k0)

    sibling = {"gy": me_y + 1 - 2 * lax.rem(me_y, 2)}
    shift = lax.rem(me_y, 2) * 2 + (count_y - 1)

    def hand_on(ref, sems, place):
        return send(
            ref.at[place],
            ref.at[lax.rem(place + shift, count_y)],
            sems,
            count_y + place,
            sibling,
        )

    def gather_y_shared(ref, sems):
        places = [(1 - step) % count_y for step in range(2, count_y, 2)]
        far = {
            place: send(ref.at[1], ref.at[place], sems, place, at_y(1 - place + count_y))
            for place in places
        }
        return far, [hand_on(ref, sems, 1)]

    def put_faces_2(place):
        for f in range(3):
            f2[f, :, 4 * place : 4 * place + 4, :] = g2f[place, :, f]

    def hand_on_all(ref, sems, far, handed):
        for place, copy in far.items():
            copy.wait_recv()
            handed.append(hand_on(ref, sems, place))
            put_faces_2(place)

    for low, high in chunks(1, 15, 2):
        x_sum = [fx[low:high, t] + fx[low + 1 : high + 1, t] for t in range(2)]
        y_sum = [fy[low:high, t] + roll(fy[low:high, t], -1, 1) for t in range(2)]
        z0, z1 = fz[low:high, 0], fz[low:high, 1]
        inv[low:high, 0] = 1.0 / ((x_sum[0] + y_sum[0]) + (z0 + z1))
        inv[low:high, 1] = 1.0 / ((x_sum[1] + y_sum[1]) + (z1 + roll(z0, -1, 2)))

    place_y(1, xy_copies[1])
    for i in range(1, 15):
        for t in range(2):
            xa[i, t] = inv[i, t] * source[i, t] * (1.0 / CENTER)

    def step_0(old, new, low, high, step, before, after=None, target=None):
        keep_old, keep_new = STEPS[step]

        def emit(i, applied, here):
            for t in range(2):
                r = source[i, t] - applied[t]
                d = keep_old * before[i, t] + keep_new * (inv[i, t] * r)
                if after is not None:
                    after[i, t] = d
                if target is None:
                    new[i, t] = here[t] + d
                else:
                    target(i, t, here[t] + d)

        sweep_0(old, faces0, low, high, emit)

    step_0(xa, xb, 2, 14, 0, xa, dd)

    for copy in f1x_copies[:2]:
        copy.wait_recv()
    f1y_copies += send_f1_y(4, 8, 1) + send_f1_y(12, 16, 2)
    step_0(xb, xa, 3, 13, 1, dd)
    best[4:12, :, 0:16, :] = xa[4:12, :, 0:16, :]
    sums = []

    def residual_0(i, applied, here):
        r = [source[i, t, 0:16, :] - applied[t][:16] for t in range(2)]
        sums.append(r[0] + r[1])
        if i % 2 == 1:
            tmp0[0, (i - 4) // 2] = sums[-2] + sums[-1]

    sweep_0(xa, faces0, 4, 12, residual_0)
    b1[8:12, 8:16, :] = 0.125 * (tmp0[0, :, first, :] + tmp0[0, :, second, :])
    b1x_copies = [
        send(
            b1.at[first:last, 8:16, :],
            b1.at[first - 4 * step : last - 4 * step, 8:16, :],
            b1x_sems,
            slot,
            at_x(step),
        )
        for slot, (step, first, last) in enumerate(
            ((-2, 8, 11), (2, 9, 12), (-1, 8, 12), (1, 8, 12))
        )
    ]

    def in_pack(row, column):
        return ((((row & 127) >> 1) + 16) & 63) + 64 * (row >> 7) == column

    pack = select_matrix((256, 128), in_pack)
    pack_even = select_matrix((256, 128), lambda row, l: ((row & 1) == 0) & in_pack(row, l))
    first4, second4 = pl.ds(0, 4, stride=2), pl.ds(1, 4, stride=2)

    def packed(pieces, matrix):
        whole = [jnp.concatenate(piece, axis=0) for piece in pieces]
        result = dot(side_by_side(*whole), matrix)
        return result.reshape(len(pieces[0]), 8, 128)

    g2f[1, 15] = jnp.ones((3, 4, 128), F32)
    g2b[1, 15] = jnp.zeros((4, 128), F32)
    mine = slice(8, 16)
    tmp1[0] = packed([[f1[4 * i + 2 * p, 0, mine, :] for i in (1, 2, 3)] for p in range(2)], pack)
    for f in (1, 2):
        pieces = [
            [f1[4 * i + 2 * p, f, mine, :] + f1[4 * i + 2 * p + 1, f, mine, :] for i in (1, 2, 3)]
            for p in range(2)
        ]
        tmp1[f] = packed(pieces, (None, pack, pack_even)[f])
    g2f[1, 6:9, 0] = 0.125 * (tmp1[0, :, first4, :] + tmp1[0, :, second4, :])
    g2f[1, 6:9, 1] = 0.125 * tmp1[1, :, first4, :]
    g2f[1, 6:9, 2] = 0.125 * (tmp1[2, :, first4, :] + tmp1[2, :, second4, :])
    gfx_copies = spread_x(g2f, 6, 9, gfx_sems, (6, -6, 3, -3))
    for copy in f1x_copies[2:]:
        copy.wait_recv()
    f1y_copies += send_f1_y(1, 4, 3) + send_f1_y(16, 19, 4)

    drain(level_0_sends)
    level_1_sends = len(pending)
    for copy in b1x_copies:
        copy.wait_recv()
    b1y_copies = [
        send(
            b1.at[1:19, 8:16, :],
            b1.at[1:19, 8 - 8 * step : 16 - 8 * step, :],
            b1y_sems,
            slot,
            at_y(step),
        )
        for slot, step in enumerate((-1, 1))
    ]
    for copy in f1y_copies:
        copy.wait_recv()
    for low, high in chunks(1, 19, 6):
        x_sum = f1[low:high, 0] + f1[low + 1 : high + 1, 0]
        y_term, z_term = f1[low:high, 1], f1[low:high, 2]
        y_sum = y_term + roll(y_term, -1, 1)
        inv1[low:high] = 1.0 / ((x_sum + y_sum) + (z_term + roll(z_term, -1, 2)))

    for copy in b1y_copies:
        copy.wait_recv()

    for i in range(1, 19):
        x1a[i] = inv1[i] * b1[i] * (1.0 / CENTER)

    def step_1(old, new, low, high, step, before, after=None):
        keep_old, keep_new = STEPS[step]

        def emit(i, applied, here):
            r = b1[i] - applied
            d = keep_old * before[i] + keep_new * (inv1[i] * r)
            if after is not None:
                after[i] = d
            new[i] = here + d

        sweep_1(old, f1, low, high, emit)

    step_1(x1a, x1b, 2, 18, 0, x1a, d1)
    for copy in gfx_copies:
        copy.wait_recv()
    gfy_far, gfy_copies = gather_y_shared(g2f, gfy_sems)
    step_1(x1b, x1a, 3, 17, 1, d1)
    r = {}

    def residual_1(i, applied, here):
        r[i - 4] = (b1[i] - applied)[8:16]

    sweep_1(x1a, f1, 4, 16, residual_1)
    tmp1[0] = packed(
        [[r[4 * i + 2 * p] + r[4 * i + 2 * p + 1] for i in range(3)] for p in range(2)], pack
    )
    g2b[1, 6:9] = 0.125 * (tmp1[0, :, first4, :] + tmp1[0, :, second4, :])
    gbx_copies = spread_x(g2b, 6, 9, gbx_sems, (6, -6, 3, -3))
    x0_copies = send_x(2)
    for copy in gbx_copies:
        copy.wait_recv()
    gby_copies = gather_y(g2b, gby_sems)

    put_faces_2(1)
    hand_on_all(g2f, gfy_sems, gfy_far, gfy_copies)
    for copy in gfy_copies:
        copy.wait_recv()
    for s in range(0, count_y, 2):
        put_faces_2(s)
    for low, high in chunks(0, 15, 3):
        terms = f2[0, low : high + 1]
        turned = roll(terms, 64, 2)
        half = lane_of(terms[1:].shape) < 64
        x_sum = terms[:-1] + jnp.where(half, turned[:-1], turned[1:])
        y_term, z_term = f2[1, low:high], f2[2, low:high]
        y_sum = y_term + roll(y_term, -1, 1)
        inv2[low:high] = 1.0 / ((x_sum + y_sum) + (z_term + roll(z_term, -1, 2)))

        x_low = f2[0, low:high]
        x_low = jnp.where(half, x_low, roll(x_low, 64, 2))
        tmp2[0, low:high] = x_low + roll(x_low, -1, 2)
        y_both = y_term + roll(y_term, 64, 2)
        tmp2[1, low:high] = y_both + roll(y_both, -1, 2)
        tmp2[2, low:high] = z_term + roll(z_term, 64, 2)
    first16, second16 = pl.ds(0, 16, stride=2), pl.ds(1, 16, stride=2)
    f3[0] = 0.125 * (tmp2[0, :, first16, :] + tmp2[0, :, second16, :])
    f3[1] = 0.125 * tmp2[1, :, first16, :]
    f3[2] = 0.125 * (tmp2[2, :, first16, :] + tmp2[2, :, second16, :])
    for low, high in chunks(2, 13, 6):
        terms = f3[0, low : high + 1]
        y_term, z_term = f3[1, low:high], f3[2, low:high]
        inv3[low:high] = 1.0 / (
            (terms[:-1] + terms[1:] + (y_term + roll(y_term, -1, 1)))
            + (z_term + roll(z_term, -2, 2))
        )

    for copy in x0_copies:
        copy.wait_recv()
    y0_copies = send_y(2)
    drain(level_1_sends)
    for copy in gby_copies:
        copy.wait_recv()
    for s in range(count_y):
        b2[:, 4 * s : 4 * s + 4, :] = g2b[s]

    for i in range(15):
        x2a[i] = inv2[i] * b2[i] * (1.0 / CENTER)

    def step_2(old, new, low, high, step, before, after=None):
        keep_old, keep_new = STEPS[step]

        def emit(i, applied, here):
            r = b2[i] - applied
            d = keep_old * before[i] + keep_new * (inv2[i] * r)
            if after is not None:
                after[i] = d
            new[i] = here + d

        sweep_2(old, f2, low, high, emit)

    step_2(x2a, x2b, 1, 14, 0, x2a, d2)
    step_2(x2b, x2a, 1, 14, 1, d2)

    def residual_2(i, applied, here):
        r = b2[i] - applied
        r = r + roll(r, 64, 1)
        tmp2[0, i] = r + roll(r, -1, 1)

    sweep_2(x2a, f2, 2, 13, residual_2)
    b3[2:13] = 0.125 * (tmp2[0, 2:13, first16, :] + tmp2[0, 2:13, second16, :])

    for i in range(2, 13):
        x3a[i] = inv3[i] * b3[i] * (1.0 / CENTER)

    def step_3(old, new, low, high, step, before, after=None):
        keep_old, keep_new = STEPS[step]

        def emit(i, applied, here):
            r = b3[i] - applied
            d = keep_old * before[i] + keep_new * (inv3[i] * r)
            if after is not None:
                after[i] = d
            new[i] = here + d

        sweep_3(old, f3, low, high, emit)

    step_3(x3a, x3b, 3, 12, 0, x3a, d3)
    step_3(x3b, x3a, 4, 11, 1, d3)

    e = x3a[4:11]
    e = jnp.where((lane_of(e.shape) & 1) == 0, e, roll(e, 1, 2))
    dup2[4:11, first16, :] = e
    dup2[4:11, second16, :] = e
    for i in range(4, 11):
        x2b[i] = x2a[i] + dup2[i]
    x2b[3] = x2a[3]
    x2b[11] = x2a[11]

    def first_up_2(i, applied, here):
        d = inv2[i] * (b2[i] - applied) * (1.0 / CENTER)
        d2[i] = d
        x2a[i] = here + d

    sweep_2(x2b, f2, 4, 11, first_up_2)
    step_2(x2a, x2b, 5, 10, 0, d2, d2)
    x2b[4] = x2a[4]
    x2b[10] = x2a[10]
    step_2(x2b, x2a, 5, 10, 1, d2)

    def in_spread(row, column):
        return ((((column & 127) >> 1) + 16) & 63) + 64 * (column >> 7) == row

    e = dot(x2a[5:10, 0:16, :].reshape(80, 128), select_matrix((128, 256), in_spread))
    for p in range(2):
        value = e[:, 128 * p : 128 * p + 128].reshape(5, 16, 128)
        dup21[p, :, first16, :] = value
        dup21[p, :, second16, :] = value
    for i in range(3, 17):
        x1b[i] = x1a[i] + dup21[(i // 2) % 2, i // 4, 0:24, :]

    def first_up_1(i, applied, here):
        d = inv1[i] * (b1[i] - applied) * (1.0 / CENTER)
        d1[i] = d
        x1a[i] = here + d

    sweep_1(x1b, f1, 4, 16, first_up_1)
    step_1(x1a, x1b, 5, 15, 0, d1, d1)
    step_1(x1b, x1a, 6, 14, 1, d1)

    drain(len(pending))
    place_y(2, y0_copies)
    e = x1a[6:14]
    dup1[:, pl.ds(0, 24, stride=2), :] = e
    dup1[:, pl.ds(1, 24, stride=2), :] = e
    lower = lax.broadcasted_iota(jnp.int32, (8, 128), 0) < 4
    for i in range(1, 15):
        j = i // 2
        brick = dup1[j, 16:32, :]
        edge = jnp.where(lower, dup1[j, 32:40, :], dup1[j, 8:16, :])
        for t in range(2):
            xb[i, t, 0:16, :] = best[i, t, 0:16, :] + brick
            xb[i, t, 16:24, :] = best[i, t, 16:24, :] + edge

    def first_up_0(i, applied, here):
        for t in range(2):
            d = inv[i, t] * (source[i, t] - applied[t]) * (1.0 / CENTER)
            dd[i, t] = d
            xa[i, t] = here[t] + d

    sweep_0(xb, faces0, 2, 14, first_up_0)
    step_0(xa, xb, 3, 13, 0, dd, dd)

    def to_own(i, t, value):
        own[t, i - 4] = value[0:16]

    step_0(xb, None, 4, 12, 1, dd, None, to_own)

    def joined(row, column):
        return ((row & 127) < 64) & (column == 2 * (row & 127) + (row >> 7))

    cells = side_by_side(own[0].reshape(128, 128), own[1].reshape(128, 128))
    result = dot(cells, select_matrix((256, 128), joined))
    out_ref[...] = result.reshape(8, 16, 128)


def solution(mesh):
    sizes = (mesh.shape["gx"], mesh.shape["gy"], mesh.shape["gz"])
    count_x, count_y, _ = sizes
    vmem = lambda *shape: pltpu.VMEM(shape, F32)
    sems = lambda count: pltpu.SemaphoreType.DMA((2, count))
    fine = (16, 2, 24, 128)
    level1 = (20, 24, 128)
    level2 = (16, 32, 128)
    level3 = (16, 16, 128)
    scratch = [
        vmem(2, 8, 16, 128),
        vmem(2, 8, 16, 128),
        vmem(2, 2, 4, 16, 128),
        vmem(2, 2, 4, 16, 128),
        vmem(3, *fine),
        vmem(3, 2, 16, 2, 4, 128),
        vmem(3, 2, 16, 2, 4, 128),
        vmem(*fine),
        vmem(*fine),
        vmem(*fine),
        vmem(*fine),
        vmem(*fine),
        vmem(*fine),
        vmem(*fine),
        vmem(3, 4, 16, 128),
        vmem(20, 3, 24, 128),
        vmem(*level1),
        vmem(*level1),
        vmem(*level1),
        vmem(*level1),
        vmem(*level1),
        vmem(3, 3, 8, 128),
        vmem(8, 48, 128),
        vmem(count_y, count_x, 3, 4, 128),
        vmem(count_y, count_x, 4, 128),
        vmem(3, *level2),
        vmem(*level2),
        vmem(*level2),
        vmem(*level2),
        vmem(*level2),
        vmem(*level2),
        vmem(3, *level2),
        vmem(3, *level3),
        vmem(*level3),
        vmem(*level3),
        vmem(*level3),
        vmem(*level3),
        vmem(*level3),
        vmem(*level2),
        vmem(2, 5, 32, 128),
        pltpu.SemaphoreType.DMA((2,)),
        sems(4),
        sems(6),
        sems(6),
        sems(12),
        sems(4),
        sems(10),
        sems(4),
        sems(2),
        sems(4),
        sems(2 * count_y),
        sems(4),
        sems(count_y - 1),
    ]

    def shards(pressure_source, conductivity):
        return pl.pallas_call(
            functools.partial(kernel, sizes),
            out_shape=jax.ShapeDtypeStruct((8, 16, 128), F32),
            in_specs=[pl.BlockSpec(memory_space=pltpu.HBM)] * 2,
            out_specs=pl.BlockSpec(memory_space=pltpu.VMEM),
            scratch_shapes=scratch,
            compiler_params=pltpu.CompilerParams(
                collective_id=0, has_side_effects=True, vmem_limit_bytes=55136 * 1024
            ),
        )(pressure_source, conductivity)

    placed = (P("gx", "gy", "gz"), P("gx", "gy", "gz"))
    return jax.shard_map(
        shards, mesh=mesh, in_specs=placed, out_specs=P("gx", "gy", "gz"), check_vma=False
    )
```

```python
import functools

import jax
import jax.numpy as jnp
from jax import lax
from jax.experimental import pallas as pl
from jax.experimental.pallas import tpu as pltpu
from jax.sharding import PartitionSpec as P

MESH = pl.DeviceIdType.MESH
F32 = jnp.float32

CENTER = 1.125
RADIUS = 0.875
RATIO = CENTER / RADIUS
RHO0 = 1.0 / RATIO
RHO1 = 1.0 / (2.0 * RATIO - RHO0)
RHO2 = 1.0 / (2.0 * RATIO - RHO1)
STEPS = ((RHO1 * RHO0, 2.0 * RHO1 / RADIUS), (RHO2 * RHO1, 2.0 * RHO2 / RADIUS))


def roll(value, shift, axis):
    return pltpu.roll(value, shift % value.shape[axis], axis)


def lane_of(shape):
    return lax.broadcasted_iota(jnp.int32, shape, len(shape) - 1)


def select_matrix(shape, holds):
    row = lax.broadcasted_iota(jnp.int32, shape, 0)
    column = lax.broadcasted_iota(jnp.int32, shape, 1)
    return jnp.where(holds(row, column), 1.0, 0.0).astype(jnp.bfloat16)


def dot(a, ones):
    high = a.astype(jnp.bfloat16)
    rest = a - high.astype(F32)
    middle = rest.astype(jnp.bfloat16)
    low = (rest - middle.astype(F32)).astype(jnp.bfloat16)
    parts = [jnp.dot(part, ones, preferred_element_type=F32) for part in (low, middle, high)]
    return (parts[0] + parts[1]) + parts[2]


def side_by_side(a, b):
    return jnp.concatenate([a, b], axis=1)


def harmonic(one_side, other_side):
    return 2.0 * one_side * other_side / (one_side + other_side)


def chunks(low, high, size):
    return [(start, min(start + size, high)) for start in range(low, high, size)]


def sweep_0(field, faces, low, high, emit):
    face_x, face_y, face_z = faces
    both = range(2)
    here = [field[low, t] for t in both]
    flux = [face_x[low, t] * (here[t] - field[low - 1, t]) for t in both]
    for i in range(low, high):
        after = [field[i + 1, t] for t in both]
        upper = [face_x[i + 1, t] * (after[t] - here[t]) for t in both]
        result = []
        for t in both:
            side = face_y[i, t] * (here[t] - roll(here[t], 1, 0))
            result.append((flux[t] - upper[t]) + (side - roll(side, -1, 0)))
        even = face_z[i, 0] * (here[0] - roll(here[1], 1, 1))
        odd = face_z[i, 1] * (here[1] - here[0])
        emit(i, [result[0] + (even - odd), result[1] + (odd - roll(even, -1, 1))], here)
        here, flux = after, upper


def sweep_1(field, faces, low, high, emit):
    here = field[low]
    flux = faces[low, 0] * (here - field[low - 1])
    for i in range(low, high):
        after = field[i + 1]
        upper = faces[i + 1, 0] * (after - here)
        side = faces[i, 1] * (here - roll(here, 1, 0))
        result = (flux - upper) + (side - roll(side, -1, 0))
        side = faces[i, 2] * (here - roll(here, 1, 1))
        emit(i, result + (side - roll(side, -1, 1)), here)
        here, flux = after, upper


def sweep_2(field, faces, low, high, emit):
    half = lane_of(field.shape[1:]) < 64
    before, here = roll(field[low - 1], 64, 1), field[low]
    turned = roll(here, 64, 1)
    flux = faces[0, low] * (here - jnp.where(half, before, turned))
    flux_turned = roll(flux, 64, 1)
    for i in range(low, high):
        after = field[i + 1]
        after_turned = roll(after, 64, 1)
        upper = faces[0, i + 1] * (after - jnp.where(half, turned, after_turned))
        upper_turned = roll(upper, 64, 1)
        result = flux - jnp.where(half, flux_turned, upper_turned)
        side = faces[1, i] * (here - roll(here, 1, 0))
        result = result + (side - roll(side, -1, 0))
        side = faces[2, i] * (here - roll(here, 1, 1))
        emit(i, result + (side - roll(side, -1, 1)), here)
        here, turned, flux, flux_turned = after, after_turned, upper, upper_turned


def sweep_3(field, faces, low, high, emit):
    here = field[low]
    flux = faces[0, low] * (here - field[low - 1])
    for i in range(low, high):
        after = field[i + 1]
        upper = faces[0, i + 1] * (after - here)
        side = faces[1, i] * (here - roll(here, 1, 0))
        result = (flux - upper) + (side - roll(side, -1, 0))
        side = faces[2, i] * (here - roll(here, 2, 1))
        emit(i, result + (side - roll(side, -2, 1)), here)
        here, flux = after, upper


def kernel(
    sizes,
    source_hbm,
    cond_hbm,
    out_ref,
    staged,
    own,
    z_send,
    z_recv,
    win,
    y_send,
    y_recv,
    fx,
    fy,
    fz,
    inv,
    xa,
    xb,
    dd,
    tmp0,
    f1,
    b1,
    inv1,
    x1a,
    x1b,
    d1,
    tmp1,
    dup1,
    g2f,
    g2b,
    f2,
    b2,
    inv2,
    x2a,
    x2b,
    d2,
    tmp2,
    f3,
    b3,
    inv3,
    x3a,
    x3b,
    d3,
    dup2,
    dup21,
    in_sem,
    z_sems,
    x_sems,
    y_sems,
    xy_sems,
    f1x_sems,
    f1y_sems,
    b1x_sems,
    b1y_sems,
    gfx_sems,
    gfy_sems,
    gbx_sems,
    gby_sems,
):
    count_x, count_y, count_z = sizes
    me_x, me_y, me_z = lax.axis_index("gx"), lax.axis_index("gy"), lax.axis_index("gz")

    def at_x(step):
        return {"gx": lax.rem(me_x + (step + count_x), count_x)}

    def at_y(step):
        return {"gy": lax.rem(me_y + (step + count_y), count_y)}

    def at_z(step):
        return {"gz": lax.rem(me_z + (step + count_z), count_z)}

    loads = [
        pltpu.make_async_copy(cond_hbm, staged.at[0], in_sem.at[0]),
        pltpu.make_async_copy(source_hbm, staged.at[1], in_sem.at[1]),
    ]
    for load in loads:
        load.start()

    barrier = pltpu.get_barrier_semaphore()
    partners = [at_z(1), at_z(-1)]
    partners += [at_x(sign * step) for step in (1, 2, 3, 5, 6) for sign in (1, -1)]
    partners += [at_y(step) for step in range(1, count_y)]
    partners += [at_x(dx) | at_y(dy) for dx in (-1, 1) for dy in (-1, 1)]
    for partner in partners:
        pl.semaphore_signal(barrier, inc=1, device_id=partner, device_id_type=MESH)

    pending = []

    def drain(count):
        for copy in pending[:count]:
            copy.wait_send()
        del pending[:count]

    def send(source, target, sems, slot, device):
        copy = pltpu.make_async_remote_copy(
            src_ref=source,
            dst_ref=target,
            send_sem=sems.at[0, slot],
            recv_sem=sems.at[1, slot],
            device_id=device,
            device_id_type=MESH,
        )
        copy.start()
        pending.append(copy)
        return copy

    def kept(row, l):
        return row == jnp.where(l < 64, 2 * l, 2 * l - 127)

    def sent(row, l):
        half, q = l >> 7, (l >> 5) & 3
        z = 2 * (l & 31) + 64 * half + jnp.where((q & 1) == 0, half, 1 - half)
        return row == jnp.where(q >= 2, z, z + 128)

    keep = select_matrix((128, 128), kept)
    pass_on = select_matrix((256, 256), sent)
    z_copies = []
    for f in range(2):
        loads[f].wait()
        cells = staged[f].reshape(128, 128)
        halos = dot(side_by_side(cells[:64], cells[64:]), pass_on)
        z_send[f, 0] = halos[:, :128].reshape(4, 16, 128)
        z_send[f, 1] = halos[:, 128:].reshape(4, 16, 128)
        if f == 0:
            pl.semaphore_wait(barrier, len(partners))
        z_copies.append(
            [
                send(z_send.at[f, way], z_recv.at[f, way], z_sems, 2 * f + way, at_z((-1, 1)[way]))
                for way in range(2)
            ]
        )
        own[f] = dot(cells, keep).reshape(8, 16, 128)

    for way in range(2):
        for i in (0, 15):
            y_recv[0, way, i] = jnp.ones((2, 4, 128), F32)
            y_recv[1, way, i] = jnp.zeros((2, 4, 128), F32)

    def send_x(f):
        depth = 4 if f == 0 else 3
        return [
            send(
                win.at[f, 4 : 4 + depth, :, 0:16, :],
                win.at[f, 12 : 12 + depth, :, 0:16, :],
                x_sems,
                2 * f,
                at_x(-1),
            ),
            send(
                win.at[f, 12 - depth : 12, :, 0:16, :],
                win.at[f, 4 - depth : 4, :, 0:16, :],
                x_sems,
                2 * f + 1,
                at_x(1),
            ),
        ]

    def send_y(f):
        y_send[f, 0] = win[f, :, :, 0:4, :]
        y_send[f, 1] = win[f, :, :, 12:16, :]
        return [
            send(
                y_send.at[f, way, 1:15],
                y_recv.at[f, way, 1:15],
                y_sems,
                2 * f + way,
                at_y((-1, 1)[way]),
            )
            for way in range(2)
        ]

    def send_xy(f):
        copies = send_x(f)
        y_send[f, 0, 4:12] = win[f, 4:12, :, 0:4, :]
        y_send[f, 1, 4:12] = win[f, 4:12, :, 12:16, :]
        for way in range(2):
            copies.append(
                send(
                    y_send.at[f, way, 4:12],
                    y_recv.at[f, way, 4:12],
                    xy_sems,
                    2 * f + way,
                    at_y((-1, 1)[way]),
                )
            )
        return copies

    def send_corners():
        return [
            send(
                y_send.at[0:2, way, first:last],
                y_recv.at[0:2, way, first - 8 * dx : last - 8 * dx],
                xy_sems,
                4 + 2 * way + slot,
                at_y((-1, 1)[way]) | at_x(dx),
            )
            for way in range(2)
            for slot, (dx, first, last) in enumerate(((1, 9, 12), (-1, 4, 7)))
        ]

    def place_y(f, first, last):
        win[f, first:last, :, 16:20, :] = y_recv[f, 0, first:last]
        win[f, first:last, :, 20:24, :] = y_recv[f, 1, first:last]

    xy_copies = []
    for f in range(2):
        for copy in z_copies[f]:
            copy.wait_recv()
        lane = lane_of((4, 16, 128))
        for part in range(2):
            mine = own[f, 4 * part : 4 * part + 4]
            above, below = z_recv[f, 0], z_recv[f, 1]
            for t in range(2):
                turn_above = ((0, 96), (64, 32))[part][t]
                turn_below = ((0, 32), (64, 96))[part][t]
                halo = jnp.where(
                    lane < 96,
                    roll(above, turn_above, 2) if turn_above else above,
                    roll(below, turn_below, 2) if turn_below else below,
                )
                win[f, 4 + 4 * part : 8 + 4 * part, t, 0:16, :] = jnp.where(
                    lane < 64, roll(mine, 64, 2) if t else mine, halo
                )
        xy_copies.append(send_xy(f))
    corners = send_corners()
    level_0_sends = len(pending)

    cond, source, best = win.at[0], win.at[1], win.at[2]
    faces0 = (fx, fy, fz)
    brick = slice(0, 16)
    for i in range(4, 12):
        k0, k1 = cond[i, 0, brick, :], cond[i, 1, brick, :]
        fz[i, 0, brick, :] = harmonic(k0, roll(k1, 1, 1))
        fz[i, 1, brick, :] = harmonic(k1, k0)
        if i > 4:
            fx[i, 0, brick, :] = harmonic(k0, cond[i - 1, 0, brick, :])
            fx[i, 1, brick, :] = harmonic(k1, cond[i - 1, 1, brick, :])
    for copy in xy_copies[0]:
        copy.wait_recv()
    place_y(0, 4, 12)
    for t in range(2):
        fx[4, t, brick, :] = harmonic(cond[4, t, brick, :], cond[3, t, brick, :])
    for i in range(4, 12):
        for t in range(2):
            k = cond[i, t]
            fy[i, t] = harmonic(k, roll(k, 1, 0))

    for i in range(4):
        tmp0[0, i] = fx[4 + 2 * i, 0, 0:16, :] + fx[4 + 2 * i, 1, 0:16, :]
        tmp0[1, i] = (fy[4 + 2 * i, 0, 0:16, :] + fy[4 + 2 * i, 1, 0:16, :]) + (
            fy[5 + 2 * i, 0, 0:16, :] + fy[5 + 2 * i, 1, 0:16, :]
        )
        tmp0[2, i] = fz[4 + 2 * i, 0, 0:16, :] + fz[5 + 2 * i, 0, 0:16, :]
    first, second = pl.ds(0, 8, stride=2), pl.ds(1, 8, stride=2)
    f1[8:12, 0, 8:16, :] = 0.125 * (tmp0[0, :, first, :] + tmp0[0, :, second, :])
    f1[8:12, 1, 8:16, :] = 0.125 * tmp0[1, :, first, :]
    f1[8:12, 2, 8:16, :] = 0.125 * (tmp0[2, :, first, :] + tmp0[2, :, second, :])
    f1x_copies = [
        send(
            f1.at[8:12, :, 8:16, :],
            f1.at[8 - 4 * step : 12 - 4 * step, :, 8:16, :],
            f1x_sems,
            slot,
            at_x(step),
        )
        for slot, step in enumerate((-2, 2, -1, 1))
    ]

    for i in (0, 19):
        for tile in (slice(0, 8), slice(16, 24)):
            f1[i, :, tile, :] = jnp.ones((3, 8, 128), F32)

    def spread_x(ref, first, last, sems, steps):
        return [
            send(ref.at[1, first:last], ref.at[1, first - step : last - step], sems, slot, at_x(step))
            for slot, step in enumerate(steps)
        ]

    def gather_y(ref, sems):
        return [
            send(ref.at[1], ref.at[(1 - step) % count_y], sems, step - 1, at_y(step))
            for step in sorted(range(1, count_y), key=lambda step: abs(step - count_y // 2))
        ]

    for copy in corners:
        copy.wait_recv()
    place_y(0, 0, 4)
    place_y(0, 12, 16)
    for i in range(1, 16):
        part = slice(16, 24) if 4 <= i < 12 else slice(0, 24)
        for t in range(2):
            fx[i, t, part, :] = harmonic(cond[i, t, part, :], cond[i - 1, t, part, :])
        if i == 15:
            break
        k0, k1 = cond[i, 0], cond[i, 1]
        if not 4 <= i < 12:
            fy[i, 0] = harmonic(k0, roll(k0, 1, 0))
            fy[i, 1] = harmonic(k1, roll(k1, 1, 0))
        k0, k1 = k0[part], k1[part]
        fz[i, 0, part, :] = harmonic(k0, roll(k1, 1, 1))
        fz[i, 1, part, :] = harmonic(k1, k0)

    sibling = {"gy": me_y + 1 - 2 * lax.rem(me_y, 2)}
    shift = lax.rem(me_y, 2) * 2 + (count_y - 1)

    def hand_on(ref, sems, place):
        return send(
            ref.at[place],
            ref.at[lax.rem(place + shift, count_y)],
            sems,
            count_y + place,
            sibling,
        )

    def gather_y_shared(ref, sems):
        places = [(1 - step) % count_y for step in range(2, count_y, 2)]
        far = {
            place: send(ref.at[1], ref.at[place], sems, place, at_y(1 - place + count_y))
            for place in places
        }
        return far, [hand_on(ref, sems, 1)]

    def put_faces_2(place):
        for f in range(3):
            f2[f, :, 4 * place : 4 * place + 4, :] = g2f[place, :, f]

    def hand_on_all(ref, sems, far, handed):
        for place, copy in far.items():
            copy.wait_recv()
            handed.append(hand_on(ref, sems, place))
            put_faces_2(place)

    for low, high in chunks(1, 15, 2):
        x_sum = [fx[low:high, t] + fx[low + 1 : high + 1, t] for t in range(2)]
        y_sum = [fy[low:high, t] + roll(fy[low:high, t], -1, 1) for t in range(2)]
        z0, z1 = fz[low:high, 0], fz[low:high, 1]
        inv[low:high, 0] = 1.0 / ((x_sum[0] + y_sum[0]) + (z0 + z1))
        inv[low:high, 1] = 1.0 / ((x_sum[1] + y_sum[1]) + (z1 + roll(z0, -1, 2)))

    for copy in xy_copies[1]:
        copy.wait_recv()
    place_y(1, 0, 16)
    for i in range(1, 15):
        for t in range(2):
            xa[i, t] = inv[i, t] * source[i, t] * (1.0 / CENTER)

    def step_0(old, new, low, high, step, before, after=None, target=None):
        keep_old, keep_new = STEPS[step]

        def emit(i, applied, here):
            for t in range(2):
                r = source[i, t] - applied[t]
                d = keep_old * before[i, t] + keep_new * (inv[i, t] * r)
                if after is not None:
                    after[i, t] = d
                if target is None:
                    new[i, t] = here[t] + d
                else:
                    target(i, t, here[t] + d)

        sweep_0(old, faces0, low, high, emit)

    step_0(xa, xb, 2, 14, 0, xa, dd)

    step_0(xb, xa, 3, 13, 1, dd)
    best[4:12, :, 0:16, :] = xa[4:12, :, 0:16, :]
    sums = []

    def residual_0(i, applied, here):
        r = [source[i, t, 0:16, :] - applied[t][:16] for t in range(2)]
        sums.append(r[0] + r[1])
        if i % 2 == 1:
            tmp0[0, (i - 4) // 2] = sums[-2] + sums[-1]

    sweep_0(xa, faces0, 4, 12, residual_0)
    b1[8:12, 8:16, :] = 0.125 * (tmp0[0, :, first, :] + tmp0[0, :, second, :])
    b1x_copies = [
        send(
            b1.at[first:last, 8:16, :],
            b1.at[first - 4 * step : last - 4 * step, 8:16, :],
            b1x_sems,
            slot,
            at_x(step),
        )
        for slot, (step, first, last) in enumerate(
            ((-2, 8, 11), (2, 9, 12), (-1, 8, 12), (1, 8, 12))
        )
    ]

    for copy in f1x_copies:
        copy.wait_recv()
    f1y_copies = [
        send(
            f1.at[1:19, :, 8:16, :],
            f1.at[1:19, :, 8 - 8 * step : 16 - 8 * step, :],
            f1y_sems,
            slot,
            at_y(step),
        )
        for slot, step in enumerate((-1, 1))
    ]

    def in_pack(row, column):
        return ((((row & 127) >> 1) + 16) & 63) + 64 * (row >> 7) == column

    pack = select_matrix((256, 128), in_pack)
    pack_even = select_matrix((256, 128), lambda row, l: ((row & 1) == 0) & in_pack(row, l))
    first4, second4 = pl.ds(0, 4, stride=2), pl.ds(1, 4, stride=2)

    def packed(pieces, matrix):
        whole = [jnp.concatenate(piece, axis=0) for piece in pieces]
        result = dot(side_by_side(*whole), matrix)
        return result.reshape(len(pieces[0]), 8, 128)

    g2f[1, 15] = jnp.ones((3, 4, 128), F32)
    g2b[1, 15] = jnp.zeros((4, 128), F32)
    mine = slice(8, 16)
    tmp1[0] = packed([[f1[4 * i + 2 * p, 0, mine, :] for i in range(5)] for p in range(2)], pack)
    for f in (1, 2):
        pieces = [
            [f1[4 * i + 2 * p, f, mine, :] + f1[4 * i + 2 * p + 1, f, mine, :] for i in range(5)]
            for p in range(2)
        ]
        tmp1[f] = packed(pieces, (None, pack, pack_even)[f])
    g2f[1, 5:10, 0] = 0.125 * (tmp1[0, :, first4, :] + tmp1[0, :, second4, :])
    g2f[1, 5:10, 1] = 0.125 * tmp1[1, :, first4, :]
    g2f[1, 5:10, 2] = 0.125 * (tmp1[2, :, first4, :] + tmp1[2, :, second4, :])
    gfx_copies = spread_x(g2f, 5, 10, gfx_sems, (5, -5))

    drain(level_0_sends)
    level_1_sends = len(pending)
    for copy in b1x_copies:
        copy.wait_recv()
    b1y_copies = [
        send(
            b1.at[1:19, 8:16, :],
            b1.at[1:19, 8 - 8 * step : 16 - 8 * step, :],
            b1y_sems,
            slot,
            at_y(step),
        )
        for slot, step in enumerate((-1, 1))
    ]
    for copy in f1y_copies:
        copy.wait_recv()
    for low, high in chunks(1, 19, 6):
        x_sum = f1[low:high, 0] + f1[low + 1 : high + 1, 0]
        y_term, z_term = f1[low:high, 1], f1[low:high, 2]
        y_sum = y_term + roll(y_term, -1, 1)
        inv1[low:high] = 1.0 / ((x_sum + y_sum) + (z_term + roll(z_term, -1, 2)))

    for copy in b1y_copies:
        copy.wait_recv()

    for i in range(1, 19):
        x1a[i] = inv1[i] * b1[i] * (1.0 / CENTER)

    def step_1(old, new, low, high, step, before, after=None):
        keep_old, keep_new = STEPS[step]

        def emit(i, applied, here):
            r = b1[i] - applied
            d = keep_old * before[i] + keep_new * (inv1[i] * r)
            if after is not None:
                after[i] = d
            new[i] = here + d

        sweep_1(old, f1, low, high, emit)

    step_1(x1a, x1b, 2, 18, 0, x1a, d1)
    for copy in gfx_copies:
        copy.wait_recv()
    gfy_far, gfy_copies = gather_y_shared(g2f, gfy_sems)
    step_1(x1b, x1a, 3, 17, 1, d1)
    r = {}

    def residual_1(i, applied, here):
        r[i - 4] = (b1[i] - applied)[8:16]

    sweep_1(x1a, f1, 4, 16, residual_1)
    tmp1[0, 0:3] = packed(
        [[r[4 * i + 2 * p] + r[4 * i + 2 * p + 1] for i in range(3)] for p in range(2)], pack
    )
    g2b[1, 6:9] = 0.125 * (tmp1[0, 0:3, first4, :] + tmp1[0, 0:3, second4, :])
    gbx_copies = spread_x(g2b, 6, 9, gbx_sems, (6, -6, 3, -3))
    x0_copies = send_x(2)
    for copy in gbx_copies:
        copy.wait_recv()
    gby_copies = gather_y(g2b, gby_sems)

    put_faces_2(1)
    hand_on_all(g2f, gfy_sems, gfy_far, gfy_copies)
    for copy in gfy_copies:
        copy.wait_recv()
    for s in range(0, count_y, 2):
        put_faces_2(s)
    for low, high in chunks(0, 15, 3):
        terms = f2[0, low : high + 1]
        turned = roll(terms, 64, 2)
        half = lane_of(terms[1:].shape) < 64
        x_sum = terms[:-1] + jnp.where(half, turned[:-1], turned[1:])
        y_term, z_term = f2[1, low:high], f2[2, low:high]
        y_sum = y_term + roll(y_term, -1, 1)
        inv2[low:high] = 1.0 / ((x_sum + y_sum) + (z_term + roll(z_term, -1, 2)))

        x_low = f2[0, low:high]
        x_low = jnp.where(half, x_low, roll(x_low, 64, 2))
        tmp2[0, low:high] = x_low + roll(x_low, -1, 2)
        y_both = y_term + roll(y_term, 64, 2)
        tmp2[1, low:high] = y_both + roll(y_both, -1, 2)
        tmp2[2, low:high] = z_term + roll(z_term, 64, 2)
    first16, second16 = pl.ds(0, 16, stride=2), pl.ds(1, 16, stride=2)
    f3[0] = 0.125 * (tmp2[0, :, first16, :] + tmp2[0, :, second16, :])
    f3[1] = 0.125 * tmp2[1, :, first16, :]
    f3[2] = 0.125 * (tmp2[2, :, first16, :] + tmp2[2, :, second16, :])
    for low, high in chunks(2, 13, 6):
        terms = f3[0, low : high + 1]
        y_term, z_term = f3[1, low:high], f3[2, low:high]
        inv3[low:high] = 1.0 / (
            (terms[:-1] + terms[1:] + (y_term + roll(y_term, -1, 1)))
            + (z_term + roll(z_term, -2, 2))
        )

    for copy in x0_copies:
        copy.wait_recv()
    y0_copies = send_y(2)
    drain(level_1_sends)
    for copy in gby_copies:
        copy.wait_recv()
    for s in range(count_y):
        b2[:, 4 * s : 4 * s + 4, :] = g2b[s]

    for i in range(15):
        x2a[i] = inv2[i] * b2[i] * (1.0 / CENTER)

    def step_2(old, new, low, high, step, before, after=None):
        keep_old, keep_new = STEPS[step]

        def emit(i, applied, here):
            r = b2[i] - applied
            d = keep_old * before[i] + keep_new * (inv2[i] * r)
            if after is not None:
                after[i] = d
            new[i] = here + d

        sweep_2(old, f2, low, high, emit)

    step_2(x2a, x2b, 1, 14, 0, x2a, d2)
    step_2(x2b, x2a, 1, 14, 1, d2)

    def residual_2(i, applied, here):
        r = b2[i] - applied
        r = r + roll(r, 64, 1)
        tmp2[0, i] = r + roll(r, -1, 1)

    sweep_2(x2a, f2, 2, 13, residual_2)
    b3[2:13] = 0.125 * (tmp2[0, 2:13, first16, :] + tmp2[0, 2:13, second16, :])

    for i in range(2, 13):
        x3a[i] = inv3[i] * b3[i] * (1.0 / CENTER)

    def step_3(old, new, low, high, step, before, after=None):
        keep_old, keep_new = STEPS[step]

        def emit(i, applied, here):
            r = b3[i] - applied
            d = keep_old * before[i] + keep_new * (inv3[i] * r)
            if after is not None:
                after[i] = d
            new[i] = here + d

        sweep_3(old, f3, low, high, emit)

    step_3(x3a, x3b, 3, 12, 0, x3a, d3)
    step_3(x3b, x3a, 4, 11, 1, d3)

    e = x3a[4:11]
    e = jnp.where((lane_of(e.shape) & 1) == 0, e, roll(e, 1, 2))
    dup2[4:11, first16, :] = e
    dup2[4:11, second16, :] = e
    for i in range(4, 11):
        x2b[i] = x2a[i] + dup2[i]
    x2b[3] = x2a[3]
    x2b[11] = x2a[11]

    def first_up_2(i, applied, here):
        d = inv2[i] * (b2[i] - applied) * (1.0 / CENTER)
        d2[i] = d
        x2a[i] = here + d

    sweep_2(x2b, f2, 4, 11, first_up_2)
    step_2(x2a, x2b, 5, 10, 0, d2, d2)
    x2b[4] = x2a[4]
    x2b[10] = x2a[10]
    step_2(x2b, x2a, 5, 10, 1, d2)

    def in_spread(row, column):
        return ((((column & 127) >> 1) + 16) & 63) + 64 * (column >> 7) == row

    e = dot(x2a[5:10, 0:16, :].reshape(80, 128), select_matrix((128, 256), in_spread))
    for p in range(2):
        value = e[:, 128 * p : 128 * p + 128].reshape(5, 16, 128)
        dup21[p, :, first16, :] = value
        dup21[p, :, second16, :] = value
    for i in range(3, 17):
        x1b[i] = x1a[i] + dup21[(i // 2) % 2, i // 4, 0:24, :]

    def first_up_1(i, applied, here):
        d = inv1[i] * (b1[i] - applied) * (1.0 / CENTER)
        d1[i] = d
        x1a[i] = here + d

    sweep_1(x1b, f1, 4, 16, first_up_1)
    step_1(x1a, x1b, 5, 15, 0, d1, d1)
    step_1(x1b, x1a, 6, 14, 1, d1)

    drain(len(pending))
    for copy in y0_copies:
        copy.wait_recv()
    place_y(2, 0, 16)
    e = x1a[6:14]
    dup1[:, pl.ds(0, 24, stride=2), :] = e
    dup1[:, pl.ds(1, 24, stride=2), :] = e
    lower = lax.broadcasted_iota(jnp.int32, (8, 128), 0) < 4
    for i in range(1, 15):
        j = i // 2
        brick = dup1[j, 16:32, :]
        edge = jnp.where(lower, dup1[j, 32:40, :], dup1[j, 8:16, :])
        for t in range(2):
            xb[i, t, 0:16, :] = best[i, t, 0:16, :] + brick
            xb[i, t, 16:24, :] = best[i, t, 16:24, :] + edge

    def first_up_0(i, applied, here):
        for t in range(2):
            d = inv[i, t] * (source[i, t] - applied[t]) * (1.0 / CENTER)
            dd[i, t] = d
            xa[i, t] = here[t] + d

    sweep_0(xb, faces0, 2, 14, first_up_0)
    step_0(xa, xb, 3, 13, 0, dd, dd)

    def to_own(i, t, value):
        own[t, i - 4] = value[0:16]

    step_0(xb, None, 4, 12, 1, dd, None, to_own)

    def joined(row, column):
        return ((row & 127) < 64) & (column == 2 * (row & 127) + (row >> 7))

    cells = side_by_side(own[0].reshape(128, 128), own[1].reshape(128, 128))
    result = dot(cells, select_matrix((256, 128), joined))
    out_ref[...] = result.reshape(8, 16, 128)


def solution(mesh):
    sizes = (mesh.shape["gx"], mesh.shape["gy"], mesh.shape["gz"])
    count_x, count_y, _ = sizes
    vmem = lambda *shape: pltpu.VMEM(shape, F32)
    sems = lambda count: pltpu.SemaphoreType.DMA((2, count))
    fine = (16, 2, 24, 128)
    level1 = (20, 24, 128)
    level2 = (16, 32, 128)
    level3 = (16, 16, 128)
    scratch = [
        vmem(2, 8, 16, 128),
        vmem(2, 8, 16, 128),
        vmem(2, 2, 4, 16, 128),
        vmem(2, 2, 4, 16, 128),
        vmem(3, *fine),
        vmem(3, 2, 16, 2, 4, 128),
        vmem(3, 2, 16, 2, 4, 128),
        vmem(*fine),
        vmem(*fine),
        vmem(*fine),
        vmem(*fine),
        vmem(*fine),
        vmem(*fine),
        vmem(*fine),
        vmem(3, 4, 16, 128),
        vmem(20, 3, 24, 128),
        vmem(*level1),
        vmem(*level1),
        vmem(*level1),
        vmem(*level1),
        vmem(*level1),
        vmem(3, 5, 8, 128),
        vmem(8, 48, 128),
        vmem(count_y, count_x, 3, 4, 128),
        vmem(count_y, count_x, 4, 128),
        vmem(3, *level2),
        vmem(*level2),
        vmem(*level2),
        vmem(*level2),
        vmem(*level2),
        vmem(*level2),
        vmem(3, *level2),
        vmem(3, *level3),
        vmem(*level3),
        vmem(*level3),
        vmem(*level3),
        vmem(*level3),
        vmem(*level3),
        vmem(*level2),
        vmem(2, 5, 32, 128),
        pltpu.SemaphoreType.DMA((2,)),
        sems(4),
        sems(6),
        sems(6),
        sems(8),
        sems(4),
        sems(2),
        sems(4),
        sems(2),
        sems(2),
        sems(2 * count_y),
        sems(4),
        sems(count_y - 1),
    ]

    def shards(pressure_source, conductivity):
        return pl.pallas_call(
            functools.partial(kernel, sizes),
            out_shape=jax.ShapeDtypeStruct((8, 16, 128), F32),
            in_specs=[pl.BlockSpec(memory_space=pltpu.HBM)] * 2,
            out_specs=pl.BlockSpec(memory_space=pltpu.VMEM),
            scratch_shapes=scratch,
            compiler_params=pltpu.CompilerParams(
                collective_id=0, has_side_effects=True, vmem_limit_bytes=55136 * 1024
            ),
        )(pressure_source, conductivity)

    placed = (P("gx", "gy", "gz"), P("gx", "gy", "gz"))
    return jax.shard_map(
        shards, mesh=mesh, in_specs=placed, out_specs=P("gx", "gy", "gz"), check_vma=False
    )
```

```python
import functools

import jax
import jax.numpy as jnp
from jax import lax
from jax.experimental import pallas as pl
from jax.experimental.pallas import tpu as pltpu
from jax.sharding import PartitionSpec as P

MESH = pl.DeviceIdType.MESH
F32 = jnp.float32

CENTER = 1.125
RADIUS = 0.875
RATIO = CENTER / RADIUS
RHO0 = 1.0 / RATIO
RHO1 = 1.0 / (2.0 * RATIO - RHO0)
RHO2 = 1.0 / (2.0 * RATIO - RHO1)
STEPS = ((RHO1 * RHO0, 2.0 * RHO1 / RADIUS), (RHO2 * RHO1, 2.0 * RHO2 / RADIUS))


def roll(value, shift, axis):
    return pltpu.roll(value, shift % value.shape[axis], axis)


def lane_of(shape):
    return lax.broadcasted_iota(jnp.int32, shape, len(shape) - 1)


def select_matrix(shape, holds):
    row = lax.broadcasted_iota(jnp.int32, shape, 0)
    column = lax.broadcasted_iota(jnp.int32, shape, 1)
    return jnp.where(holds(row, column), 1.0, 0.0).astype(jnp.bfloat16)


def dot(a, ones):
    high = a.astype(jnp.bfloat16)
    rest = a - high.astype(F32)
    middle = rest.astype(jnp.bfloat16)
    low = (rest - middle.astype(F32)).astype(jnp.bfloat16)
    parts = [jnp.dot(part, ones, preferred_element_type=F32) for part in (low, middle, high)]
    return (parts[0] + parts[1]) + parts[2]


def side_by_side(a, b):
    return jnp.concatenate([a, b], axis=1)


def harmonic(one_side, other_side):
    return 2.0 * one_side * other_side / (one_side + other_side)


def chunks(low, high, size):
    return [(start, min(start + size, high)) for start in range(low, high, size)]


def sweep_0(field, faces, low, high, emit):
    face_x, face_y, face_z = faces
    both = range(2)
    here = [field[low, t] for t in both]
    flux = [face_x[low, t] * (here[t] - field[low - 1, t]) for t in both]
    for i in range(low, high):
        after = [field[i + 1, t] for t in both]
        upper = [face_x[i + 1, t] * (after[t] - here[t]) for t in both]
        result = []
        for t in both:
            side = face_y[i, t] * (here[t] - roll(here[t], 1, 0))
            result.append((flux[t] - upper[t]) + (side - roll(side, -1, 0)))
        even = face_z[i, 0] * (here[0] - roll(here[1], 1, 1))
        odd = face_z[i, 1] * (here[1] - here[0])
        emit(i, [result[0] + (even - odd), result[1] + (odd - roll(even, -1, 1))], here)
        here, flux = after, upper


def sweep_1(field, faces, low, high, emit):
    here = field[low]
    flux = faces[low, 0] * (here - field[low - 1])
    for i in range(low, high):
        after = field[i + 1]
        upper = faces[i + 1, 0] * (after - here)
        side = faces[i, 1] * (here - roll(here, 1, 0))
        result = (flux - upper) + (side - roll(side, -1, 0))
        side = faces[i, 2] * (here - roll(here, 1, 1))
        emit(i, result + (side - roll(side, -1, 1)), here)
        here, flux = after, upper


def sweep_2(field, faces, low, high, emit):
    half = lane_of(field.shape[1:]) < 64
    before, here = roll(field[low - 1], 64, 1), field[low]
    turned = roll(here, 64, 1)
    flux = faces[0, low] * (here - jnp.where(half, before, turned))
    flux_turned = roll(flux, 64, 1)
    for i in range(low, high):
        after = field[i + 1]
        after_turned = roll(after, 64, 1)
        upper = faces[0, i + 1] * (after - jnp.where(half, turned, after_turned))
        upper_turned = roll(upper, 64, 1)
        result = flux - jnp.where(half, flux_turned, upper_turned)
        side = faces[1, i] * (here - roll(here, 1, 0))
        result = result + (side - roll(side, -1, 0))
        side = faces[2, i] * (here - roll(here, 1, 1))
        emit(i, result + (side - roll(side, -1, 1)), here)
        here, turned, flux, flux_turned = after, after_turned, upper, upper_turned


def sweep_3(field, faces, low, high, emit):
    here = field[low]
    flux = faces[0, low] * (here - field[low - 1])
    for i in range(low, high):
        after = field[i + 1]
        upper = faces[0, i + 1] * (after - here)
        side = faces[1, i] * (here - roll(here, 1, 0))
        result = (flux - upper) + (side - roll(side, -1, 0))
        side = faces[2, i] * (here - roll(here, 2, 1))
        emit(i, result + (side - roll(side, -2, 1)), here)
        here, flux = after, upper


def kernel(
    sizes,
    source_hbm,
    cond_hbm,
    out_ref,
    staged,
    own,
    z_send,
    z_recv,
    win,
    y_send,
    y_recv,
    fx,
    fy,
    fz,
    inv,
    xa,
    xb,
    dd,
    tmp0,
    f1,
    b1,
    inv1,
    x1a,
    x1b,
    d1,
    tmp1,
    dup1,
    g2f,
    g2b,
    f2,
    b2,
    inv2,
    x2a,
    x2b,
    d2,
    tmp2,
    f3,
    b3,
    inv3,
    x3a,
    x3b,
    d3,
    dup2,
    dup21,
    in_sem,
    z_sems,
    x_sems,
    y_sems,
    xy_sems,
    f1x_sems,
    f1y_sems,
    b1x_sems,
    b1y_sems,
    gfx_sems,
    gfy_sems,
    gbx_sems,
    gby_sems,
):
    count_x, count_y, count_z = sizes
    me_x, me_y, me_z = lax.axis_index("gx"), lax.axis_index("gy"), lax.axis_index("gz")

    def at_x(step):
        return {"gx": lax.rem(me_x + (step + count_x), count_x)}

    def at_y(step):
        return {"gy": lax.rem(me_y + (step + count_y), count_y)}

    def at_z(step):
        return {"gz": lax.rem(me_z + (step + count_z), count_z)}

    loads = [
        pltpu.make_async_copy(cond_hbm, staged.at[0], in_sem.at[0]),
        pltpu.make_async_copy(source_hbm, staged.at[1], in_sem.at[1]),
    ]
    for load in loads:
        load.start()

    barrier = pltpu.get_barrier_semaphore()
    partners = [at_z(1), at_z(-1)]
    partners += [at_x(sign * step) for step in (1, 2, 3, 5, 6) for sign in (1, -1)]
    partners += [at_y(step) for step in range(1, count_y)]
    partners += [at_x(dx) | at_y(dy) for dx in (-1, 1) for dy in (-1, 1)]
    for partner in partners:
        pl.semaphore_signal(barrier, inc=1, device_id=partner, device_id_type=MESH)

    pending = []

    def drain(count):
        for copy in pending[:count]:
            copy.wait_send()
        del pending[:count]

    def send(source, target, sems, slot, device):
        copy = pltpu.make_async_remote_copy(
            src_ref=source,
            dst_ref=target,
            send_sem=sems.at[0, slot],
            recv_sem=sems.at[1, slot],
            device_id=device,
            device_id_type=MESH,
        )
        copy.start()
        pending.append(copy)
        return copy

    def kept(row, l):
        return row == jnp.where(l < 64, 2 * l, 2 * l - 127)

    def sent(row, l):
        half, q = l >> 7, (l >> 5) & 3
        z = 2 * (l & 31) + 64 * half + jnp.where((q & 1) == 0, half, 1 - half)
        return row == jnp.where(q >= 2, z, z + 128)

    keep = select_matrix((128, 128), kept)
    pass_on = select_matrix((256, 256), sent)
    z_copies = []
    for f in range(2):
        loads[f].wait()
        cells = staged[f].reshape(128, 128)
        halos = dot(side_by_side(cells[:64], cells[64:]), pass_on)
        z_send[f, 0] = halos[:, :128].reshape(4, 16, 128)
        z_send[f, 1] = halos[:, 128:].reshape(4, 16, 128)
        if f == 0:
            pl.semaphore_wait(barrier, len(partners))
        z_copies.append(
            [
                send(z_send.at[f, way], z_recv.at[f, way], z_sems, 2 * f + way, at_z((-1, 1)[way]))
                for way in range(2)
            ]
        )

    for f in range(2):
        own[f] = dot(staged[f].reshape(128, 128), keep).reshape(8, 16, 128)

    for way in range(2):
        for i in (0, 15):
            y_recv[0, way, i] = jnp.ones((2, 4, 128), F32)
            y_recv[1, way, i] = jnp.zeros((2, 4, 128), F32)

    def send_x(f):
        depth = 4 if f == 0 else 3
        return [
            send(
                win.at[f, 4 : 4 + depth, :, 0:16, :],
                win.at[f, 12 : 12 + depth, :, 0:16, :],
                x_sems,
                2 * f,
                at_x(-1),
            ),
            send(
                win.at[f, 12 - depth : 12, :, 0:16, :],
                win.at[f, 4 - depth : 4, :, 0:16, :],
                x_sems,
                2 * f + 1,
                at_x(1),
            ),
        ]

    def send_y(f):
        y_send[f, 0] = win[f, :, :, 0:4, :]
        y_send[f, 1] = win[f, :, :, 12:16, :]
        return [
            send(
                y_send.at[f, way, 1:15],
                y_recv.at[f, way, 1:15],
                y_sems,
                2 * f + way,
                at_y((-1, 1)[way]),
            )
            for way in range(2)
        ]

    def send_xy(f):
        copies = send_x(f)
        y_send[f, 0, 4:12] = win[f, 4:12, :, 0:4, :]
        y_send[f, 1, 4:12] = win[f, 4:12, :, 12:16, :]
        for way in range(2):
            copies.append(
                send(
                    y_send.at[f, way, 4:12],
                    y_recv.at[f, way, 4:12],
                    xy_sems,
                    2 * f + way,
                    at_y((-1, 1)[way]),
                )
            )
        return copies

    def send_corners():
        return [
            send(
                y_send.at[0:2, way, first:last],
                y_recv.at[0:2, way, first - 8 * dx : last - 8 * dx],
                xy_sems,
                4 + 2 * way + slot,
                at_y((-1, 1)[way]) | at_x(dx),
            )
            for way in range(2)
            for slot, (dx, first, last) in enumerate(((1, 9, 12), (-1, 4, 7)))
        ]

    def place_y(f, first, last):
        win[f, first:last, :, 16:20, :] = y_recv[f, 0, first:last]
        win[f, first:last, :, 20:24, :] = y_recv[f, 1, first:last]

    xy_copies = []
    for f in range(2):
        for copy in z_copies[f]:
            copy.wait_recv()
        lane = lane_of((4, 16, 128))
        for part in range(2):
            mine = own[f, 4 * part : 4 * part + 4]
            above, below = z_recv[f, 0], z_recv[f, 1]
            for t in range(2):
                turn_above = ((0, 96), (64, 32))[part][t]
                turn_below = ((0, 32), (64, 96))[part][t]
                halo = jnp.where(
                    lane < 96,
                    roll(above, turn_above, 2) if turn_above else above,
                    roll(below, turn_below, 2) if turn_below else below,
                )
                win[f, 4 + 4 * part : 8 + 4 * part, t, 0:16, :] = jnp.where(
                    lane < 64, roll(mine, 64, 2) if t else mine, halo
                )
        xy_copies.append(send_xy(f))
    corners = send_corners()
    level_0_sends = len(pending)

    cond, source, best = win.at[0], win.at[1], win.at[2]
    faces0 = (fx, fy, fz)
    brick = slice(0, 16)
    for i in range(4, 12):
        k0, k1 = cond[i, 0, brick, :], cond[i, 1, brick, :]
        fz[i, 0, brick, :] = harmonic(k0, roll(k1, 1, 1))
        fz[i, 1, brick, :] = harmonic(k1, k0)
        if i > 4:
            fx[i, 0, brick, :] = harmonic(k0, cond[i - 1, 0, brick, :])
            fx[i, 1, brick, :] = harmonic(k1, cond[i - 1, 1, brick, :])
    for copy in xy_copies[0]:
        copy.wait_recv()
    place_y(0, 4, 12)
    for t in range(2):
        fx[4, t, brick, :] = harmonic(cond[4, t, brick, :], cond[3, t, brick, :])
    for i in range(4, 12):
        for t in range(2):
            k = cond[i, t]
            fy[i, t] = harmonic(k, roll(k, 1, 0))

    for i in range(4):
        tmp0[0, i] = fx[4 + 2 * i, 0, 0:16, :] + fx[4 + 2 * i, 1, 0:16, :]
        tmp0[1, i] = (fy[4 + 2 * i, 0, 0:16, :] + fy[4 + 2 * i, 1, 0:16, :]) + (
            fy[5 + 2 * i, 0, 0:16, :] + fy[5 + 2 * i, 1, 0:16, :]
        )
        tmp0[2, i] = fz[4 + 2 * i, 0, 0:16, :] + fz[5 + 2 * i, 0, 0:16, :]
    first, second = pl.ds(0, 8, stride=2), pl.ds(1, 8, stride=2)
    f1[8:12, 0, 8:16, :] = 0.125 * (tmp0[0, :, first, :] + tmp0[0, :, second, :])
    f1[8:12, 1, 8:16, :] = 0.125 * tmp0[1, :, first, :]
    f1[8:12, 2, 8:16, :] = 0.125 * (tmp0[2, :, first, :] + tmp0[2, :, second, :])
    f1x_copies = [
        send(
            f1.at[8:12, :, 8:16, :],
            f1.at[8 - 4 * step : 12 - 4 * step, :, 8:16, :],
            f1x_sems,
            slot,
            at_x(step),
        )
        for slot, step in enumerate((-2, 2, -1, 1))
    ]

    for i in (0, 19):
        for tile in (slice(0, 8), slice(16, 24)):
            f1[i, :, tile, :] = jnp.ones((3, 8, 128), F32)

    def spread_x(ref, first, last, sems, steps):
        return [
            send(ref.at[1, first:last], ref.at[1, first - step : last - step], sems, slot, at_x(step))
            for slot, step in enumerate(steps)
        ]

    def gather_y(ref, sems):
        return [
            send(ref.at[1], ref.at[(1 - step) % count_y], sems, step - 1, at_y(step))
            for step in sorted(range(1, count_y), key=lambda step: abs(step - count_y // 2))
        ]

    for copy in corners:
        copy.wait_recv()
    place_y(0, 0, 4)
    place_y(0, 12, 16)
    for i in range(1, 16):
        part = slice(16, 24) if 4 <= i < 12 else slice(0, 24)
        for t in range(2):
            fx[i, t, part, :] = harmonic(cond[i, t, part, :], cond[i - 1, t, part, :])
        if i == 15:
            break
        k0, k1 = cond[i, 0], cond[i, 1]
        if not 4 <= i < 12:
            fy[i, 0] = harmonic(k0, roll(k0, 1, 0))
            fy[i, 1] = harmonic(k1, roll(k1, 1, 0))
        k0, k1 = k0[part], k1[part]
        fz[i, 0, part, :] = harmonic(k0, roll(k1, 1, 1))
        fz[i, 1, part, :] = harmonic(k1, k0)

    sibling = {"gy": me_y + 1 - 2 * lax.rem(me_y, 2)}
    shift = lax.rem(me_y, 2) * 2 + (count_y - 1)

    def hand_on(ref, sems, place):
        return send(
            ref.at[place],
            ref.at[lax.rem(place + shift, count_y)],
            sems,
            count_y + place,
            sibling,
        )

    def gather_y_shared(ref, sems):
        places = [(1 - step) % count_y for step in range(2, count_y, 2)]
        far = {
            place: send(ref.at[1], ref.at[place], sems, place, at_y(1 - place + count_y))
            for place in places
        }
        return far, [hand_on(ref, sems, 1)]

    def put_faces_2(place):
        for f in range(3):
            f2[f, :, 4 * place : 4 * place + 4, :] = g2f[place, :, f]

    def hand_on_all(ref, sems, far, handed):
        for place, copy in far.items():
            copy.wait_recv()
            handed.append(hand_on(ref, sems, place))
            put_faces_2(place)

    for low, high in chunks(1, 15, 2):
        x_sum = [fx[low:high, t] + fx[low + 1 : high + 1, t] for t in range(2)]
        y_sum = [fy[low:high, t] + roll(fy[low:high, t], -1, 1) for t in range(2)]
        z0, z1 = fz[low:high, 0], fz[low:high, 1]
        inv[low:high, 0] = 1.0 / ((x_sum[0] + y_sum[0]) + (z0 + z1))
        inv[low:high, 1] = 1.0 / ((x_sum[1] + y_sum[1]) + (z1 + roll(z0, -1, 2)))

    for copy in xy_copies[1]:
        copy.wait_recv()
    place_y(1, 0, 16)
    for i in range(1, 15):
        for t in range(2):
            xa[i, t] = inv[i, t] * source[i, t] * (1.0 / CENTER)

    def step_0(old, new, low, high, step, before, after=None, target=None):
        keep_old, keep_new = STEPS[step]

        def emit(i, applied, here):
            for t in range(2):
                r = source[i, t] - applied[t]
                d = keep_old * before[i, t] + keep_new * (inv[i, t] * r)
                if after is not None:
                    after[i, t] = d
                if target is None:
                    new[i, t] = here[t] + d
                else:
                    target(i, t, here[t] + d)

        sweep_0(old, faces0, low, high, emit)

    step_0(xa, xb, 2, 14, 0, xa, dd)

    step_0(xb, xa, 3, 13, 1, dd)
    best[4:12, :, 0:16, :] = xa[4:12, :, 0:16, :]
    sums = []

    def residual_0(i, applied, here):
        r = [source[i, t, 0:16, :] - applied[t][:16] for t in range(2)]
        sums.append(r[0] + r[1])
        if i % 2 == 1:
            tmp0[0, (i - 4) // 2] = sums[-2] + sums[-1]

    sweep_0(xa, faces0, 4, 12, residual_0)
    b1[8:12, 8:16, :] = 0.125 * (tmp0[0, :, first, :] + tmp0[0, :, second, :])
    b1x_copies = [
        send(
            b1.at[first:last, 8:16, :],
            b1.at[first - 4 * step : last - 4 * step, 8:16, :],
            b1x_sems,
            slot,
            at_x(step),
        )
        for slot, (step, first, last) in enumerate(
            ((-2, 8, 11), (2, 9, 12), (-1, 8, 12), (1, 8, 12))
        )
    ]

    for copy in f1x_copies:
        copy.wait_recv()
    f1y_copies = [
        send(
            f1.at[1:19, :, 8:16, :],
            f1.at[1:19, :, 8 - 8 * step : 16 - 8 * step, :],
            f1y_sems,
            slot,
            at_y(step),
        )
        for slot, step in enumerate((-1, 1))
    ]

    def in_pack(row, column):
        return ((((row & 127) >> 1) + 16) & 63) + 64 * (row >> 7) == column

    pack = select_matrix((256, 128), in_pack)
    pack_even = select_matrix((256, 128), lambda row, l: ((row & 1) == 0) & in_pack(row, l))
    first4, second4 = pl.ds(0, 4, stride=2), pl.ds(1, 4, stride=2)

    def packed(pieces, matrix):
        whole = [jnp.concatenate(piece, axis=0) for piece in pieces]
        result = dot(side_by_side(*whole), matrix)
        return result.reshape(len(pieces[0]), 8, 128)

    g2f[1, 15] = jnp.ones((3, 4, 128), F32)
    g2b[1, 15] = jnp.zeros((4, 128), F32)
    mine = slice(8, 16)
    tmp1[0] = packed([[f1[4 * i + 2 * p, 0, mine, :] for i in range(5)] for p in range(2)], pack)
    for f in (1, 2):
        pieces = [
            [f1[4 * i + 2 * p, f, mine, :] + f1[4 * i + 2 * p + 1, f, mine, :] for i in range(5)]
            for p in range(2)
        ]
        tmp1[f] = packed(pieces, (None, pack, pack_even)[f])
    g2f[1, 5:10, 0] = 0.125 * (tmp1[0, :, first4, :] + tmp1[0, :, second4, :])
    g2f[1, 5:10, 1] = 0.125 * tmp1[1, :, first4, :]
    g2f[1, 5:10, 2] = 0.125 * (tmp1[2, :, first4, :] + tmp1[2, :, second4, :])
    gfx_copies = spread_x(g2f, 5, 10, gfx_sems, (5, -5))

    drain(level_0_sends)
    level_1_sends = len(pending)
    for copy in b1x_copies:
        copy.wait_recv()
    b1y_copies = [
        send(
            b1.at[1:19, 8:16, :],
            b1.at[1:19, 8 - 8 * step : 16 - 8 * step, :],
            b1y_sems,
            slot,
            at_y(step),
        )
        for slot, step in enumerate((-1, 1))
    ]
    for copy in f1y_copies:
        copy.wait_recv()
    for low, high in chunks(1, 19, 6):
        x_sum = f1[low:high, 0] + f1[low + 1 : high + 1, 0]
        y_term, z_term = f1[low:high, 1], f1[low:high, 2]
        y_sum = y_term + roll(y_term, -1, 1)
        inv1[low:high] = 1.0 / ((x_sum + y_sum) + (z_term + roll(z_term, -1, 2)))

    for copy in b1y_copies:
        copy.wait_recv()

    for i in range(1, 19):
        x1a[i] = inv1[i] * b1[i] * (1.0 / CENTER)

    def step_1(old, new, low, high, step, before, after=None):
        keep_old, keep_new = STEPS[step]

        def emit(i, applied, here):
            r = b1[i] - applied
            d = keep_old * before[i] + keep_new * (inv1[i] * r)
            if after is not None:
                after[i] = d
            new[i] = here + d

        sweep_1(old, f1, low, high, emit)

    step_1(x1a, x1b, 2, 18, 0, x1a, d1)
    for copy in gfx_copies:
        copy.wait_recv()
    gfy_far, gfy_copies = gather_y_shared(g2f, gfy_sems)
    step_1(x1b, x1a, 3, 17, 1, d1)
    r = {}

    def residual_1(i, applied, here):
        r[i - 4] = (b1[i] - applied)[8:16]

    sweep_1(x1a, f1, 4, 16, residual_1)
    tmp1[0, 0:3] = packed(
        [[r[4 * i + 2 * p] + r[4 * i + 2 * p + 1] for i in range(3)] for p in range(2)], pack
    )
    g2b[1, 6:9] = 0.125 * (tmp1[0, 0:3, first4, :] + tmp1[0, 0:3, second4, :])
    gbx_copies = spread_x(g2b, 6, 9, gbx_sems, (6, -6, 3, -3))
    x0_copies = send_x(2)
    for copy in gbx_copies:
        copy.wait_recv()
    gby_copies = gather_y(g2b, gby_sems)

    put_faces_2(1)
    hand_on_all(g2f, gfy_sems, gfy_far, gfy_copies)
    for copy in gfy_copies:
        copy.wait_recv()
    for s in range(0, count_y, 2):
        put_faces_2(s)
    for low, high in chunks(0, 15, 3):
        terms = f2[0, low : high + 1]
        turned = roll(terms, 64, 2)
        half = lane_of(terms[1:].shape) < 64
        x_sum = terms[:-1] + jnp.where(half, turned[:-1], turned[1:])
        y_term, z_term = f2[1, low:high], f2[2, low:high]
        y_sum = y_term + roll(y_term, -1, 1)
        inv2[low:high] = 1.0 / ((x_sum + y_sum) + (z_term + roll(z_term, -1, 2)))

        x_low = f2[0, low:high]
        x_low = jnp.where(half, x_low, roll(x_low, 64, 2))
        tmp2[0, low:high] = x_low + roll(x_low, -1, 2)
        y_both = y_term + roll(y_term, 64, 2)
        tmp2[1, low:high] = y_both + roll(y_both, -1, 2)
        tmp2[2, low:high] = z_term + roll(z_term, 64, 2)
    first16, second16 = pl.ds(0, 16, stride=2), pl.ds(1, 16, stride=2)
    f3[0] = 0.125 * (tmp2[0, :, first16, :] + tmp2[0, :, second16, :])
    f3[1] = 0.125 * tmp2[1, :, first16, :]
    f3[2] = 0.125 * (tmp2[2, :, first16, :] + tmp2[2, :, second16, :])
    for low, high in chunks(2, 13, 6):
        terms = f3[0, low : high + 1]
        y_term, z_term = f3[1, low:high], f3[2, low:high]
        inv3[low:high] = 1.0 / (
            (terms[:-1] + terms[1:] + (y_term + roll(y_term, -1, 1)))
            + (z_term + roll(z_term, -2, 2))
        )

    for copy in x0_copies:
        copy.wait_recv()
    y0_copies = send_y(2)
    drain(level_1_sends)
    for copy in gby_copies:
        copy.wait_recv()
    for s in range(count_y):
        b2[:, 4 * s : 4 * s + 4, :] = g2b[s]

    for i in range(15):
        x2a[i] = inv2[i] * b2[i] * (1.0 / CENTER)

    def step_2(old, new, low, high, step, before, after=None):
        keep_old, keep_new = STEPS[step]

        def emit(i, applied, here):
            r = b2[i] - applied
            d = keep_old * before[i] + keep_new * (inv2[i] * r)
            if after is not None:
                after[i] = d
            new[i] = here + d

        sweep_2(old, f2, low, high, emit)

    step_2(x2a, x2b, 1, 14, 0, x2a, d2)
    step_2(x2b, x2a, 1, 14, 1, d2)

    def residual_2(i, applied, here):
        r = b2[i] - applied
        r = r + roll(r, 64, 1)
        tmp2[0, i] = r + roll(r, -1, 1)

    sweep_2(x2a, f2, 2, 13, residual_2)
    b3[2:13] = 0.125 * (tmp2[0, 2:13, first16, :] + tmp2[0, 2:13, second16, :])

    for i in range(2, 13):
        x3a[i] = inv3[i] * b3[i] * (1.0 / CENTER)

    def step_3(old, new, low, high, step, before, after=None):
        keep_old, keep_new = STEPS[step]

        def emit(i, applied, here):
            r = b3[i] - applied
            d = keep_old * before[i] + keep_new * (inv3[i] * r)
            if after is not None:
                after[i] = d
            new[i] = here + d

        sweep_3(old, f3, low, high, emit)

    step_3(x3a, x3b, 3, 12, 0, x3a, d3)
    step_3(x3b, x3a, 4, 11, 1, d3)

    e = x3a[4:11]
    e = jnp.where((lane_of(e.shape) & 1) == 0, e, roll(e, 1, 2))
    dup2[4:11, first16, :] = e
    dup2[4:11, second16, :] = e
    for i in range(4, 11):
        x2b[i] = x2a[i] + dup2[i]
    x2b[3] = x2a[3]
    x2b[11] = x2a[11]

    def first_up_2(i, applied, here):
        d = inv2[i] * (b2[i] - applied) * (1.0 / CENTER)
        d2[i] = d
        x2a[i] = here + d

    sweep_2(x2b, f2, 4, 11, first_up_2)
    step_2(x2a, x2b, 5, 10, 0, d2, d2)
    x2b[4] = x2a[4]
    x2b[10] = x2a[10]
    step_2(x2b, x2a, 5, 10, 1, d2)

    def in_spread(row, column):
        return ((((column & 127) >> 1) + 16) & 63) + 64 * (column >> 7) == row

    e = dot(x2a[5:10, 0:16, :].reshape(80, 128), select_matrix((128, 256), in_spread))
    for p in range(2):
        value = e[:, 128 * p : 128 * p + 128].reshape(5, 16, 128)
        dup21[p, :, first16, :] = value
        dup21[p, :, second16, :] = value
    for i in range(3, 17):
        x1b[i] = x1a[i] + dup21[(i // 2) % 2, i // 4, 0:24, :]

    def first_up_1(i, applied, here):
        d = inv1[i] * (b1[i] - applied) * (1.0 / CENTER)
        d1[i] = d
        x1a[i] = here + d

    sweep_1(x1b, f1, 4, 16, first_up_1)
    step_1(x1a, x1b, 5, 15, 0, d1, d1)
    step_1(x1b, x1a, 6, 14, 1, d1)

    drain(len(pending))
    for copy in y0_copies:
        copy.wait_recv()
    place_y(2, 0, 16)
    e = x1a[6:14]
    dup1[:, pl.ds(0, 24, stride=2), :] = e
    dup1[:, pl.ds(1, 24, stride=2), :] = e
    lower = lax.broadcasted_iota(jnp.int32, (8, 128), 0) < 4
    for i in range(1, 15):
        j = i // 2
        brick = dup1[j, 16:32, :]
        edge = jnp.where(lower, dup1[j, 32:40, :], dup1[j, 8:16, :])
        for t in range(2):
            xb[i, t, 0:16, :] = best[i, t, 0:16, :] + brick
            xb[i, t, 16:24, :] = best[i, t, 16:24, :] + edge

    def first_up_0(i, applied, here):
        for t in range(2):
            d = inv[i, t] * (source[i, t] - applied[t]) * (1.0 / CENTER)
            dd[i, t] = d
            xa[i, t] = here[t] + d

    sweep_0(xb, faces0, 2, 14, first_up_0)
    step_0(xa, xb, 3, 13, 0, dd, dd)

    def to_own(i, t, value):
        own[t, i - 4] = value[0:16]

    step_0(xb, None, 4, 12, 1, dd, None, to_own)

    def joined(row, column):
        return ((row & 127) < 64) & (column == 2 * (row & 127) + (row >> 7))

    cells = side_by_side(own[0].reshape(128, 128), own[1].reshape(128, 128))
    result = dot(cells, select_matrix((256, 128), joined))
    out_ref[...] = result.reshape(8, 16, 128)


def solution(mesh):
    sizes = (mesh.shape["gx"], mesh.shape["gy"], mesh.shape["gz"])
    count_x, count_y, _ = sizes
    vmem = lambda *shape: pltpu.VMEM(shape, F32)
    sems = lambda count: pltpu.SemaphoreType.DMA((2, count))
    fine = (16, 2, 24, 128)
    level1 = (20, 24, 128)
    level2 = (16, 32, 128)
    level3 = (16, 16, 128)
    scratch = [
        vmem(2, 8, 16, 128),
        vmem(2, 8, 16, 128),
        vmem(2, 2, 4, 16, 128),
        vmem(2, 2, 4, 16, 128),
        vmem(3, *fine),
        vmem(3, 2, 16, 2, 4, 128),
        vmem(3, 2, 16, 2, 4, 128),
        vmem(*fine),
        vmem(*fine),
        vmem(*fine),
        vmem(*fine),
        vmem(*fine),
        vmem(*fine),
        vmem(*fine),
        vmem(3, 4, 16, 128),
        vmem(20, 3, 24, 128),
        vmem(*level1),
        vmem(*level1),
        vmem(*level1),
        vmem(*level1),
        vmem(*level1),
        vmem(3, 5, 8, 128),
        vmem(8, 48, 128),
        vmem(count_y, count_x, 3, 4, 128),
        vmem(count_y, count_x, 4, 128),
        vmem(3, *level2),
        vmem(*level2),
        vmem(*level2),
        vmem(*level2),
        vmem(*level2),
        vmem(*level2),
        vmem(3, *level2),
        vmem(3, *level3),
        vmem(*level3),
        vmem(*level3),
        vmem(*level3),
        vmem(*level3),
        vmem(*level3),
        vmem(*level2),
        vmem(2, 5, 32, 128),
        pltpu.SemaphoreType.DMA((2,)),
        sems(4),
        sems(6),
        sems(6),
        sems(8),
        sems(4),
        sems(2),
        sems(4),
        sems(2),
        sems(2),
        sems(2 * count_y),
        sems(4),
        sems(count_y - 1),
    ]

    def shards(pressure_source, conductivity):
        return pl.pallas_call(
            functools.partial(kernel, sizes),
            out_shape=jax.ShapeDtypeStruct((8, 16, 128), F32),
            in_specs=[pl.BlockSpec(memory_space=pltpu.HBM)] * 2,
            out_specs=pl.BlockSpec(memory_space=pltpu.VMEM),
            scratch_shapes=scratch,
            compiler_params=pltpu.CompilerParams(
                collective_id=0, has_side_effects=True, vmem_limit_bytes=55136 * 1024
            ),
        )(pressure_source, conductivity)

    placed = (P("gx", "gy", "gz"), P("gx", "gy", "gz"))
    return jax.shard_map(
        shards, mesh=mesh, in_specs=placed, out_specs=P("gx", "gy", "gz"), check_vma=False
    )
```
